32 devices in a mesh: rep: 4 (over y, core), shard: 8 (over z, x).
Axes of the slice: x: 2, y: 2, z: 4, core: 2. Of those that a mesh axis runs over, the one named last changes fastest.
Arguments:
- hidden_in: bfloat16 [8192, 1536], P(('rep', 'shard')), may hold values from -6 to 6
- segments: int32 [32, 256], P(('rep', 'shard')), may hold values from 0 to 63, never falling along the last dimension, each value on 1 to 128 neighbouring positions
- routes: int32 [8192, 4], P(('rep', 'shard')), may hold values from 0 to 7, all different within a row; in each aligned block of 256 rows (0 to 255, 256 to 511, ...) at most 192 rows name the same one
- gate_weights: float32 [8192, 4], P(('rep', 'shard')), may hold values from 0.2 to 0.6
- grad_out: bfloat16 [8192, 1536], P(('rep', 'shard')), may hold values from -6 to 6
- attn_gain: bfloat16 [1536], P('shard'), may hold values from 0.5 to 1.5
- query_weight: bfloat16 [1536, 1536], P('shard'), may hold values from -0.3125 to 0.3125
- key_weight: bfloat16 [1536, 256], P('shard'), may hold values from -0.15625 to 0.15625
- value_weight: bfloat16 [1536, 256], P('shard'), may hold values from -0.15625 to 0.15625
- output_weight: bfloat16 [1536, 1536], P('shard'), may hold values from -0.875 to 0.875
- ffn_gain: bfloat16 [1536], P('shard'), may hold values from 0.5 to 1.5
- gate_weight: bfloat16 [8, 1536, 768], P(None, 'shard'), may hold values from -0.15625 to 0.15625
- up_weight: bfloat16 [8, 1536, 768], P(None, 'shard'), may hold values from -0.15625 to 0.15625
- down_weight: bfloat16 [8, 768, 1536], P(None, 'shard'), may hold values from -0.4375 to 0.4375
Outputs:
- layer_out: bfloat16 [8192, 1536], P(('rep', 'shard'))
- grad_in: bfloat16 [8192, 1536], P(('rep', 'shard'))
- grad_attn_gain: float32 [1536], P('shard')
- grad_query_weight: float32 [1536, 1536], P('shard')
- grad_key_weight: float32 [1536, 256], P('shard')
- grad_value_weight: float32 [1536, 256], P('shard')
- grad_output_weight: float32 [1536, 1536], P('shard')
- grad_ffn_gain: float32 [1536], P('shard')
- grad_gate_weight: float32 [8, 1536, 768], P(None, 'shard')
- grad_up_weight: float32 [8, 1536, 768], P(None, 'shard')
- grad_down_weight: float32 [8, 768, 1536], P(None, 'shard')
The draws below stay inside these ranges and needn't reach their ends.
Inputs may be any that keep to these rules, and one draw needn't show every extreme that they name: `routes`: in the 256 rows of one sequence no expert is named by more than 192 rows; a row's experts differ. `segments`: document numbers never fall along a sequence; a document holds 1 to 128 tokens.
All inputs are finite; a program needn't handle non-finite values.
Results may differ from the reference program's by a relative error of at most 0.014.
Values may be sent and summed in bfloat16 or wider, within the bound.
A program may use at most 320 MiB of HBM per device.

```python
import math
import jax
import jax.numpy as jnp
import numpy as np
from jax import lax

D = 1536
HEADS = 12
KV_HEADS = 2
HEAD_DIM = 128
FF = 768
TOP = 4
EXPERTS = 8
TOK_DEV = 256
CAP = 192
SEG_MOST = 128
DOCS = 64
SEQS = 32
TOKENS = 8192


def shard_levels(rng, extent, cuts, least, top_value):
    gain, own = 1.0, jax.random.fold_in(rng, 6)
    for dim, parts in cuts:
        draws = jnp.exp(jax.random.uniform(jax.random.fold_in(own, dim), (parts,), jnp.float32, least / len(cuts), top_value / len(cuts)))
        gain = gain * jnp.repeat(draws, extent[dim] // parts).reshape([-1 if axis == dim else 1 for axis in range(len(extent))])
    return gain


def split_up(count, total, reach, skew):
    weights = [(1 << 20) // math.isqrt(grade ** skew) + 1 for grade in range(2, count + 1)]
    surplus, counts = total - reach - (count - 1), [1] * (count - 1)
    while surplus > 0:
        movable = [i for i in range(count - 1) if counts[i] < reach]
        mass, remaining = sum([weights[i] for i in movable]), surplus
        for i in movable:
            extra = min(reach - counts[i], max(1, remaining * weights[i] // mass), surplus)
            counts[i] = counts[i] + extra
            surplus = surplus - extra
    return np.array([reach] + counts)


def ragged(own_key, amount, total, most, slope):
    if amount == 2:
        one = jax.random.randint(own_key, (), max(1, total - most), min(most, total - 1) + 1)
        return jnp.stack([one, total - one])
    tallies = jnp.asarray(split_up(amount, total, most, slope), jnp.int32)
    pairs = (amount - 1) // 2
    giver, taker = tallies[1:1 + 2 * pairs:2], tallies[2:2 + 2 * pairs:2]
    slack = jnp.minimum(giver - 1, most - taker)
    passed = jax.random.randint(jax.random.fold_in(own_key, 1), (pairs,), 0, 1 << 20) % (slack + 1)
    tallies = tallies.at[1:1 + 2 * pairs:2].set(giver - passed).at[2:2 + 2 * pairs:2].set(taker + passed)
    return tallies[jax.random.permutation(jax.random.fold_in(own_key, 2), amount)]


def assign_block(rng, own, number, rows, count, top, reach, slope):
    sequence = jax.random.permutation(rng, count)
    heavy_load, usual = load_shares(count, rows * top, reach, slope, True), load_shares(count, rows * top, reach, slope, False)
    places = jnp.arange(count)

    def named(lengths, rotation):
        used = int((lengths > 0).sum())
        fixed = max(1, used // 4)
        moved = fixed + (places - fixed + rotation * (used - fixed)) % max(1, count - fixed)
        return jnp.zeros((count,), jnp.int32).at[sequence[jnp.where(places < fixed, places, moved)]].set(jnp.asarray(lengths, jnp.int32))

    lengths = jnp.where(number % 4 == 0, named(heavy_load, number // 4), named(usual, number - number // 4 - 1))
    mixed = jax.random.permutation(jax.random.fold_in(own, 3), count)
    giver, receiver = mixed[0:count // 2 * 2:2], mixed[1:count // 2 * 2:2]
    slack = jnp.minimum(lengths[giver] - 1, reach - lengths[receiver]) // 2
    slack = jnp.where((giver == sequence[0]) | (receiver == sequence[0]) | (lengths[receiver] == 0), 0, jnp.maximum(slack, 0))
    moved = jax.random.randint(jax.random.fold_in(own, 4), (count // 2,), 0, 1 << 20) % (slack + 1)
    lengths = lengths.at[giver].add(-moved).at[receiver].add(moved)
    labels = jnp.searchsorted(jnp.cumsum(lengths), jnp.arange(rows * top), side="right").astype(jnp.int32)
    table = labels.reshape(top, rows).T
    table = table[jax.random.permutation(jax.random.fold_in(own, 1), rows)]
    rotation = jax.random.randint(jax.random.fold_in(own, 2), (rows, 1), 0, top)
    return jnp.take_along_axis(table, (jnp.arange(top)[None, :] + rotation) % top, axis=1)


def load_shares(count, total, bound, lean, full):
    loads = [(1 << 20) // math.isqrt(standing ** lean) + 1 for standing in range(1, count + 1)]
    largest = bound if full else min(bound, max(-(-total // count), total * loads[0] // sum(loads)))
    least = 1 if total - largest >= count - 1 else 0
    holding, spare = [largest] + [least] * (count - 1), total - largest - least * (count - 1)
    while spare > 0:
        candidates = [i for i in range(1, count) if holding[i] < largest] or [i for i in range(1, count) if holding[i] < bound]
        mass, left = sum([loads[i] for i in candidates]), spare
        for i in candidates:
            more = min(bound - holding[i], max(1, left * loads[i] // mass), spare)
            holding[i] = holding[i] + more
            spare = spare - more
    return np.array(holding)


def gaussian(key, extent, spread, limit, split=(), kind=jnp.bfloat16):
    loudness = shard_levels(key, extent, split, -0.22, 0.18) if split else 1.0
    result = jax.random.normal(key, extent, jnp.float32) * spread * loudness
    return jnp.minimum(jnp.maximum(result, -limit), limit).astype(kind)


def setup_inputs(seed: int = 0) -> dict:
    keys = jax.random.split(jax.random.key(seed), 15)
    hidden_in = gaussian(keys[0], (TOKENS, D), 1.0, 6.0, ((0, 32),))
    segments = jax.vmap(lambda own: jnp.searchsorted(jnp.cumsum(ragged(own, DOCS, TOK_DEV, SEG_MOST, 2)), jnp.arange(TOK_DEV), side="right"))(jax.random.split(keys[1], SEQS)).reshape((SEQS, TOK_DEV)).astype(jnp.int32)
    routes_keys = jax.random.split(jax.random.fold_in(keys[2], 1), TOKENS // TOK_DEV)
    routes_turns = jax.random.permutation(jax.random.fold_in(keys[2], 3), TOKENS // TOK_DEV)
    routes = jax.vmap(lambda own, number: assign_block(jax.random.fold_in(keys[2], 2), own, number, TOK_DEV, EXPERTS, TOP, CAP, 2))(routes_keys, routes_turns).reshape((TOKENS, TOP))
    gate_weights = jnp.clip(0.2 + 0.400000021 * jax.random.uniform(keys[3], (TOKENS, TOP), jnp.float32) ** shard_levels(keys[3], (TOKENS, TOP), ((0, 32),), -0.2, 0.2), 0.2, 0.6)
    grad_out = gaussian(keys[4], (TOKENS, D), 1.0, 6.0, ((0, 32),))
    attn_gain = jnp.clip(1.0 + 0.1 * jax.random.normal(keys[5], (D,), jnp.float32), 0.5, 1.5).astype(jnp.bfloat16)
    query_weight = gaussian(keys[6], (D, HEADS * HEAD_DIM), (D // 4) ** -0.5, 0.3125, ((0, 8),))
    key_weight = gaussian(keys[7], (D, KV_HEADS * HEAD_DIM), D ** -0.5, 0.15625, ((0, 8),))
    value_weight = gaussian(keys[8], (D, KV_HEADS * HEAD_DIM), D ** -0.5, 0.15625, ((0, 8),))
    output_weight = gaussian(keys[9], (HEADS * HEAD_DIM, D), (HEADS * HEAD_DIM // 32) ** -0.5, 0.875, ((0, 8),))
    ffn_gain = jnp.clip(1.0 + 0.1 * jax.random.normal(keys[10], (D,), jnp.float32), 0.5, 1.5).astype(jnp.bfloat16)
    gate_weight = gaussian(keys[11], (EXPERTS, D, FF), D ** -0.5, 0.15625, ((1, 8),))
    up_weight = gaussian(keys[12], (EXPERTS, D, FF), D ** -0.5, 0.15625, ((1, 8),))
    down_weight = gaussian(keys[13], (EXPERTS, FF, D), (FF // 4) ** -0.5, 0.4375, ((1, 8),))
    return {"hidden_in": hidden_in, "segments": segments, "routes": routes, "gate_weights": gate_weights, "grad_out": grad_out, "attn_gain": attn_gain, "query_weight": query_weight, "key_weight": key_weight, "value_weight": value_weight, "output_weight": output_weight, "ffn_gain": ffn_gain, "gate_weight": gate_weight, "up_weight": up_weight, "down_weight": down_weight}


epsilon = 1e-06
rotary_base = 1000000.0
masked_score = -1e+30
highest = lax.Precision.HIGHEST

@jax.custom_vjp
def low(v):
    return lax.optimization_barrier(v.astype(jnp.bfloat16)).astype(jnp.float32)

@jax.custom_vjp
def low_back(v):
    return v

def low_keep(v):
    return (low(v), None)

def low_pass(kept, grad):
    return (grad,)

def back_keep(v):
    return (v, None)

def back_low(kept, grad):
    return (low(grad),)
low.defvjp(low_keep, low_pass)
low_back.defvjp(back_keep, back_low)

def rms_norm(values, scale_gain):
    return values * lax.rsqrt(lax.optimization_barrier(jnp.mean(values * values, axis=-1, keepdims=True)) + epsilon) * scale_gain

def rotary_tables(length, head_width):
    half_width = head_width // 2
    frequency = rotary_base ** (-2.0 * jnp.arange(half_width, dtype=jnp.float32) / head_width)
    angles = jnp.arange(length, dtype=jnp.float32)[:, None] * frequency[None, :]
    return (jnp.cos(angles)[:, None, :], jnp.sin(angles)[:, None, :])

def rotate(values, cosine, sine_table):
    half_width = values.shape[-1] // 2
    first_half = values[..., :half_width]
    second_half = values[..., half_width:]
    return jnp.concatenate([first_half * cosine - second_half * sine_table, second_half * cosine + first_half * sine_table], axis=-1)

def dispatch(routes, experts, capacity):
    flat_routes = routes.reshape(-1).astype(jnp.int32)
    onehot = (flat_routes[:, None] == jnp.arange(experts, dtype=jnp.int32)[None, :]).astype(jnp.int32)
    slot_rank = lax.optimization_barrier(jnp.sum((jnp.cumsum(onehot, axis=0) - 1) * onehot, axis=1)).astype(jnp.int32)
    owners = (jnp.arange(flat_routes.shape[0], dtype=jnp.int32) // routes.shape[1]).astype(jnp.int32)
    slot_table = jnp.zeros((experts, capacity), jnp.int32).at[flat_routes, slot_rank].set(owners)
    slot_index = (flat_routes * capacity + slot_rank).astype(jnp.int32).reshape(routes.shape)
    return (slot_table, slot_index)

def sequence_forward(item, weight_list):
    inputs, segment, routes, gate_share = item
    attn_gain, query_weight, key_weight, value_weight, output_weight, ffn_gain, gate_weight, up_weight, down_weight = weight_list
    length = inputs.shape[0]
    normed = low(rms_norm(inputs, attn_gain))
    query_raw = low_back(jnp.dot(normed, query_weight, precision=highest))
    key_raw = low_back(jnp.dot(normed, key_weight, precision=highest))
    value_heads = low(low_back(jnp.dot(normed, value_weight, precision=highest))).reshape(length, KV_HEADS, HEAD_DIM)
    cosine, sine_table = rotary_tables(length, HEAD_DIM)
    rotated_queries = low(rotate(query_raw.reshape(length, HEADS, HEAD_DIM), cosine, sine_table))
    rotated_keys = low(rotate(key_raw.reshape(length, KV_HEADS, HEAD_DIM), cosine, sine_table))
    grouped = rotated_queries.reshape(length, KV_HEADS, HEADS // KV_HEADS, HEAD_DIM)
    scores = jnp.einsum('ikgd,jkd->kgij', grouped, rotated_keys, precision=highest) * HEAD_DIM ** (-0.5)
    position = jnp.arange(length, dtype=jnp.int32)
    allowed = (position[:, None] >= position[None, :]) & (segment[:, None] == segment[None, :])
    scores = low_back(jnp.where(allowed, scores, masked_score))
    probability = jax.nn.softmax(scores, axis=-1)
    attended = jnp.einsum('kgij,jkd->ikgd', low(probability), value_heads, precision=highest).reshape(length, HEADS * HEAD_DIM)
    attended = low(low_back(attended))
    mixed = inputs + low_back(jnp.dot(attended, output_weight, precision=highest))
    normed_two = low(rms_norm(mixed, ffn_gain))
    slot_table, slot_index = dispatch(routes, EXPERTS, CAP)
    gathered_rows = normed_two[slot_table]
    gate_proj = low_back(jnp.einsum('ecd,edf->ecf', gathered_rows, gate_weight, precision=highest))
    up_proj = low_back(jnp.einsum('ecd,edf->ecf', gathered_rows, up_weight, precision=highest))
    hidden_act = low(jax.nn.silu(gate_proj) * up_proj)
    expert_out = low_back(jnp.einsum('ecf,efd->ecd', hidden_act, down_weight, precision=highest)).reshape(EXPERTS * CAP, D)
    picked = expert_out[slot_index]
    return mixed + lax.optimization_barrier(jnp.sum(gate_share[:, :, None] * picked, axis=1))

def reference(hidden_in, segments, routes, gate_weights, grad_out, attn_gain, query_weight, key_weight, value_weight, output_weight, ffn_gain, gate_weight, up_weight, down_weight):
    weights = tuple((member.astype(jnp.float32) for member in (attn_gain, query_weight, key_weight, value_weight, output_weight, ffn_gain, gate_weight, up_weight, down_weight)))
    runner = jax.checkpoint(sequence_forward)
    stacked = (segments, routes.reshape(SEQS, TOK_DEV, TOP), gate_weights.astype(jnp.float32).reshape(SEQS, TOK_DEV, TOP))

    def forward(inputs, *weight_list):

        def one_sequence(item):
            return runner(item, weight_list)
        return lax.map(one_sequence, (inputs.reshape(SEQS, TOK_DEV, D),) + stacked).reshape(TOKENS, D)
    layer_out, pullback = jax.vjp(forward, hidden_in.astype(jnp.float32), *weights)
    gradients = pullback(grad_out.astype(jnp.float32))
    return (layer_out.astype(jnp.bfloat16), gradients[0].astype(jnp.bfloat16), gradients[1], gradients[2], gradients[3], gradients[4], gradients[5], gradients[6], gradients[7], gradients[8], gradients[9])
```

```python
import jax
import jax.numpy as jnp
from jax import lax
from jax.sharding import Mesh
from jax.sharding import PartitionSpec as P

HEADS = 12
KV_HEADS = 2
HEAD_DIM = 128
EXPERTS = 8

epsilon = 1e-06
rotary_base = 1000000.0
masked_score = -1e30

F32 = jnp.float32
BF16 = jnp.bfloat16


def norm_back(values, scale_gain, upstream):
    inverse = lax.rsqrt(jnp.mean(values * values, axis=-1, keepdims=True) + epsilon)
    normal = values * inverse
    gain_grad = jnp.sum(upstream * normal, axis=0)
    scaled = upstream * scale_gain
    value_grad = inverse * (scaled - normal * jnp.mean(scaled * normal, axis=-1, keepdims=True))
    return (value_grad, gain_grad)


def rms_norm(values, scale_gain):
    return (
        values * lax.rsqrt(jnp.mean(values * values, axis=-1, keepdims=True) + epsilon) * scale_gain
    )


def rotary_tables(length, head_width):
    half_width = head_width // 2
    frequency = rotary_base ** (-2.0 * jnp.arange(half_width, dtype=jnp.float32) / head_width)
    angles = jnp.arange(length, dtype=jnp.float32)[:, None] * frequency[None, :]
    return (jnp.cos(angles)[:, None, :], jnp.sin(angles)[:, None, :])


def rotate(values, cosine, sine_table):
    half_width = values.shape[-1] // 2
    first_half = values[..., :half_width]
    second_half = values[..., half_width:]
    return jnp.concatenate(
        [
            first_half * cosine - second_half * sine_table,
            second_half * cosine + first_half * sine_table,
        ],
        axis=-1,
    )


def dot(a, b, dims):
    return lax.dot_general(a, b, (dims, ((), ())), preferred_element_type=F32)


def swap(value, axes):
    count = 2 ** len(axes)
    return lax.ppermute(value, axes, [(i, count - 1 - i) for i in range(count)])


def ordered(mine, other, place):
    first = jnp.where(place == 0, mine, other)
    second = jnp.where(place == 0, other, mine)
    return jnp.stack([first, second])


def line_steps(depth):
    up = [(i, i + 1) for i in range(depth - 1)]
    down = [(i + 1, i) for i in range(depth - 1)]
    return up, down


def line_gather(block, depth, place):
    up, down = line_steps(depth)
    below, above = [], []
    a = b = block
    for _ in range(depth - 1):
        a = lax.ppermute(a, "z", up)
        b = lax.ppermute(b, "z", down)
        below.append(a)
        above.append(b)
    around = jnp.stack(below[::-1] + [block] + above)
    return lax.dynamic_slice_in_dim(around, depth - 1 - place, depth, 0)


def line_scatter(blocks, depth, place):
    up, down = line_steps(depth)

    def at(index):
        return lax.dynamic_index_in_dim(blocks, jnp.clip(index, 0, depth - 1), 0, keepdims=False)

    a = b = None
    for step in range(1, depth):
        send_a = at(depth - step + place)
        send_b = at(place - 1 - (depth - 1) + step - 0)
        if a is not None:
            send_a = (send_a.astype(F32) + a.astype(F32)).astype(BF16)
            send_b = (send_b.astype(F32) + b.astype(F32)).astype(BF16)
        a = lax.ppermute(send_a, "z", up)
        b = lax.ppermute(send_b, "z", down)
    total = at(place).astype(F32)
    if a is not None:
        total = total + a.astype(F32) + b.astype(F32)
    return total


def slab_gather(block):
    by_x = swap(block, ("x",))
    by_y = swap(block, ("y",))
    by_xy = swap(block, ("y", "x"))
    chips = jnp.stack([block, by_y, by_x, by_xy])
    mate = swap(chips, ("c",))
    return jnp.stack([chips, mate], axis=1)


def slab_return(parts):
    mate = swap(parts[:, 1], ("c",))
    both = parts[:, 0].astype(F32) + mate.astype(F32)
    low = both.astype(BF16)
    by_y = swap(low[1], ("y",))
    by_x = swap(low[2], ("x",))
    by_xy = swap(low[3], ("y", "x"))
    return both[0] + by_x.astype(F32) + by_y.astype(F32) + by_xy.astype(F32)


def make_shards(sizes):
    depth = sizes["z"]

    def shards(
        hidden_in,
        segments,
        routes,
        gate_weights,
        grad_out,
        attn_gain,
        query_weight,
        key_weight,
        value_weight,
        output_weight,
        ffn_gain,
        gate_weight,
        up_weight,
        down_weight,
    ):
        length, width = hidden_in.shape
        groups = HEADS // KV_HEADS
        factor = HEAD_DIM ** (-0.5)
        x, y, c, z = (lax.axis_index(n) for n in ("x", "y", "c", "z"))
        expert = 4 * x + 2 * y + c
        mine = 2 * y + c

        gains = jnp.stack([attn_gain, ffn_gain], axis=1)
        gains = jnp.pad(gains, ((0, 0), (0, 126)))
        packed = jnp.concatenate(
            [query_weight, key_weight, value_weight, output_weight, gains], axis=1
        )
        rows, columns = packed.shape
        quarter = rows // 4
        block = lax.dynamic_slice_in_dim(packed, mine * quarter, quarter, 0)
        held = line_gather(block, depth, z)
        held = ordered(held, swap(held, ("x",)), x)
        held = ordered(held, swap(held, ("y",)), y)
        held = ordered(held, swap(held, ("c",)), c)
        held = held.transpose(3, 2, 1, 0, 4, 5).reshape(width, columns)
        qkv = HEADS * HEAD_DIM + 2 * KV_HEADS * HEAD_DIM
        qkv_full = held[:, :qkv]
        output_full = held[:, qkv : qkv + width]
        gain_first = held[:, qkv + width].astype(F32)
        gain_second = held[:, qkv + width + 1].astype(F32)

        def expert_gather(weight):
            own = lax.dynamic_index_in_dim(weight, expert, 0, keepdims=False)
            away = lax.dynamic_index_in_dim(weight, expert ^ 4, 0, keepdims=False)
            pair = ordered(own, swap(away, ("x",)), x)
            full = line_gather(pair, depth, z)
            return full.reshape(-1, full.shape[-1])

        gate_full = expert_gather(gate_weight)
        up_full = expert_gather(up_weight)
        down_full = expert_gather(down_weight)

        onehot = routes[:, :, None] == jnp.arange(EXPERTS, dtype=jnp.int32)
        shares = jnp.sum(jnp.where(onehot, gate_weights[:, :, None], 0.0), axis=1)
        shares = slab_gather(shares).reshape(-1, EXPERTS)
        share = jnp.sum(
            jnp.where(jnp.arange(EXPERTS) == expert, shares, 0.0), axis=1, keepdims=True
        )
        grads = slab_gather(grad_out).reshape(-1, width)

        inputs = hidden_in.astype(F32)
        normed = rms_norm(inputs, gain_first).astype(BF16)
        projected = dot(normed, qkv_full, ((1,), (0,)))
        query_raw = projected[:, : HEADS * HEAD_DIM]
        key_raw = projected[:, HEADS * HEAD_DIM : HEADS * HEAD_DIM + KV_HEADS * HEAD_DIM]
        value_heads = projected[:, HEADS * HEAD_DIM + KV_HEADS * HEAD_DIM :]
        value_heads = value_heads.astype(BF16).reshape(length, KV_HEADS, HEAD_DIM)
        cosine, sine_table = rotary_tables(length, HEAD_DIM)
        rotated_queries = rotate(
            query_raw.reshape(length, HEADS, HEAD_DIM), cosine, sine_table
        ).astype(BF16)
        rotated_keys = rotate(
            key_raw.reshape(length, KV_HEADS, HEAD_DIM), cosine, sine_table
        ).astype(BF16)
        grouped = rotated_queries.reshape(length, KV_HEADS, groups, HEAD_DIM)
        segment = segments[0]
        position = jnp.arange(length, dtype=jnp.int32)
        allowed = (position[:, None] >= position[None, :]) & (segment[:, None] == segment[None, :])
        scores = (
            jnp.einsum("ikgd,jkd->kgij", grouped, rotated_keys, preferred_element_type=F32) * factor
        )
        scores = jnp.where(allowed, scores, masked_score)
        top_score = jnp.max(scores, axis=-1, keepdims=True)
        exponent_terms = jnp.exp(scores - top_score)
        probability = exponent_terms / jnp.sum(exponent_terms, axis=-1, keepdims=True)
        probability_low = probability.astype(BF16)
        attended = jnp.einsum(
            "kgij,jkd->ikgd", probability_low, value_heads, preferred_element_type=F32
        )
        attended = attended.reshape(length, HEADS * HEAD_DIM).astype(BF16)
        mixed = inputs + dot(attended, output_full, ((1,), (0,)))
        normed_two = rms_norm(mixed, gain_second).astype(BF16)

        rows_in = slab_gather(normed_two).reshape(-1, width)
        gate_proj = dot(rows_in, gate_full, ((1,), (0,)))
        up_proj = dot(rows_in, up_full, ((1,), (0,)))
        sigmoid_gate = jax.nn.sigmoid(gate_proj)
        silu_gate = gate_proj * sigmoid_gate
        hidden_act = (silu_gate * up_proj).astype(BF16)
        expert_grad = (share * grads.astype(F32)).astype(BF16)
        down_grad = dot(hidden_act, expert_grad, ((0,), (0,))).astype(BF16)
        expert_out = dot(hidden_act, down_full, ((1,), (0,)))
        expert_part = (share * expert_out).astype(BF16).reshape(4, 2, length, width)
        hidden_grad = dot(expert_grad, down_full, ((1,), (1,)))
        gate_grad = (
            hidden_grad * up_proj * sigmoid_gate * (1.0 + gate_proj * (1.0 - sigmoid_gate))
        ).astype(BF16)
        up_grad = (hidden_grad * silu_gate).astype(BF16)
        rows_grad = dot(gate_grad, gate_full, ((1,), (1,))) + dot(up_grad, up_full, ((1,), (1,)))
        rows_grad = rows_grad.astype(BF16).reshape(4, 2, length, width)
        gate_weight_grad = dot(rows_in, gate_grad, ((0,), (0,))).astype(BF16)
        up_weight_grad = dot(rows_in, up_grad, ((0,), (0,))).astype(BF16)

        layer_out = (mixed + slab_return(expert_part)).astype(BF16)
        normed_two_grad = slab_return(rows_grad)

        def over_outer(value):
            return lax.psum(value, "o") if sizes["o"] > 1 else value

        def expert_scatter(grad):
            shard = grad.shape[0] // (2 * depth)
            blocks = grad.reshape(depth, 2, shard, grad.shape[1])
            total = over_outer(line_scatter(blocks, depth, z)).astype(BF16)
            own = lax.dynamic_index_in_dim(total, x, 0, keepdims=False)
            away = lax.dynamic_index_in_dim(total, 1 - x, 0, keepdims=False)
            four = ordered(own, swap(away, ("x",)), x)[:, None]
            four = ordered(four, swap(four, ("y",)), y)
            four = ordered(four, swap(four, ("c",)), c)
            return four.transpose(2, 1, 0, 3, 4, 5).reshape(EXPERTS, shard, -1).astype(F32)

        total_down = expert_scatter(down_grad)
        total_gate = expert_scatter(gate_weight_grad)
        total_up = expert_scatter(up_weight_grad)

        upstream = grad_out.astype(F32)
        mixed_part, ffn_gain_grad = norm_back(mixed, gain_second, normed_two_grad)
        mixed_grad = upstream + mixed_part
        mixed_low = mixed_grad.astype(BF16)
        output_weight_grad = dot(attended, mixed_low, ((0,), (0,)))
        attended_grad = dot(mixed_low, output_full, ((1,), (1,)))
        attended_grad = attended_grad.astype(BF16).reshape(length, KV_HEADS, groups, HEAD_DIM)
        prob_grad = jnp.einsum(
            "ikgd,jkd->kgij", attended_grad, value_heads, preferred_element_type=F32
        )
        value_grad = jnp.einsum(
            "kgij,ikgd->jkd", probability_low, attended_grad, preferred_element_type=F32
        )
        value_grad = value_grad.astype(BF16).reshape(length, KV_HEADS * HEAD_DIM)
        score_grad = (
            probability * (prob_grad - jnp.sum(probability * prob_grad, axis=-1, keepdims=True))
        ).astype(BF16)
        query_rot_grad = (
            jnp.einsum("kgij,jkd->ikgd", score_grad, rotated_keys, preferred_element_type=F32)
            * factor
        )
        key_rot_grad = (
            jnp.einsum("kgij,ikgd->jkd", score_grad, grouped, preferred_element_type=F32) * factor
        )
        query_raw_grad = rotate(
            query_rot_grad.reshape(length, HEADS, HEAD_DIM), cosine, -sine_table
        )
        query_raw_grad = query_raw_grad.astype(BF16).reshape(length, HEADS * HEAD_DIM)
        key_raw_grad = (
            rotate(key_rot_grad, cosine, -sine_table)
            .astype(BF16)
            .reshape(length, KV_HEADS * HEAD_DIM)
        )
        qkv_grad = jnp.concatenate([query_raw_grad, key_raw_grad, value_grad], axis=1)
        normed_grad = dot(qkv_grad, qkv_full, ((1,), (1,)))
        qkv_weight_grad = dot(normed, qkv_grad, ((0,), (0,)))
        input_part, attn_gain_grad = norm_back(inputs, gain_first, normed_grad)
        grad_in = (mixed_grad + input_part).astype(BF16)

        gain_grads = jnp.stack([attn_gain_grad, ffn_gain_grad], axis=1)
        gain_grads = jnp.pad(gain_grads, ((0, 0), (0, 126)))
        packed_grad = jnp.concatenate(
            [qkv_weight_grad, output_weight_grad, gain_grads], axis=1
        ).astype(BF16)
        parts = packed_grad.reshape(depth, 2, 2, 2, quarter, columns)
        parts = parts.transpose(3, 1, 2, 0, 4, 5)

        def pick(value, place):
            return lax.dynamic_index_in_dim(value, place, 0, keepdims=False)

        def halve(value, axis, place):
            other = swap(pick(value, 1 - place), (axis,))
            return (pick(value, place).astype(F32) + other.astype(F32)).astype(BF16)

        parts = halve(parts, "c", c)
        parts = halve(parts, "x", x)
        parts = halve(parts, "y", y)
        total = over_outer(line_scatter(parts, depth, z)).astype(BF16)
        total = ordered(total, swap(total, ("c",)), c)
        total = ordered(total, swap(total, ("y",)), y).reshape(rows, columns).astype(F32)
        kv = KV_HEADS * HEAD_DIM
        return (
            layer_out,
            grad_in,
            total[:, qkv + width],
            total[:, : qkv - 2 * kv],
            total[:, qkv - 2 * kv : qkv - kv],
            total[:, qkv - kv : qkv],
            total[:, qkv : qkv + width],
            total[:, qkv + width + 1],
            total_gate,
            total_up,
            total_down,
        )

    return shards


def solution(mesh):
    reps, shard_count = mesh.shape["rep"], mesh.shape["shard"]
    sizes = {"o": reps // 4, "y": 2, "c": 2, "z": shard_count // 2, "x": 2}
    fine = Mesh(mesh.devices.reshape(tuple(sizes.values())), tuple(sizes))
    tokens = P(("o", "y", "c", "z", "x"), None)
    first, second = P(("z", "x")), P(None, ("z", "x"), None)
    matrix = P(("z", "x"), None)
    return jax.shard_map(
        make_shards(sizes),
        mesh=fine,
        in_specs=(
            (tokens,) * 5 + (first, matrix, matrix, matrix, matrix, first) + (second,) * 3
        ),
        out_specs=(
            (tokens,) * 2 + (first, matrix, matrix, matrix, matrix, first) + (second,) * 3
        ),
        check_vma=False,
    )
```

```python
import functools

import jax
import jax.numpy as jnp
from jax import lax
from jax.experimental import pallas as pl
from jax.experimental.pallas import tpu as pltpu
from jax.sharding import Mesh
from jax.sharding import PartitionSpec as P

HEADS = 12
KV_HEADS = 2
GROUP = HEADS // KV_HEADS
HEAD_DIM = 128
EXPERTS = 8
LANES = 128

epsilon = 1e-06
rotary_base = 1000000.0
masked_score = -1e30

F32 = jnp.float32
BF16 = jnp.bfloat16
MESH = pl.DeviceIdType.MESH
VMEM_LIMIT = 60 * 2**20


def dot(a, b, dims):
    return lax.dot_general(a, b, (dims, ((), ())), preferred_element_type=F32)


def dot_nn(a, b):
    return dot(a, b, ((1,), (0,)))


def dot_nt(a, b):
    return dot(a, b, ((1,), (1,)))


def dot_tn(a, b):
    return dot(a, b, ((0,), (0,)))


def guarded(cond, body):
    if cond is None:
        body()
    else:
        pl.when(cond)(body)


def both(first, second):
    if first is None:
        return second
    if second is None:
        return first
    return jnp.logical_and(first, second)


class Net:
    def __init__(self, send_sems, recv_sems, local_sems, core):
        self.send_sems, self.recv_sems, self.local_sems = send_sems, recv_sems, local_sems
        self.away = {"c": 1 - core}
        self.slots, self.sends, self.locals, self.count, self.done = {}, {}, {}, 0, set()

    def slot(self, key):
        return self.slots.setdefault(key, len(self.slots))

    def send(self, key, src, dst, device, cond=None):
        recv, index = self.slot(key), self.count
        self.count += 1

        def build():
            return pltpu.make_async_remote_copy(
                src_ref=src(),
                dst_ref=dst(),
                send_sem=self.send_sems.at[index],
                recv_sem=self.recv_sems.at[recv],
                device_id=device,
                device_id_type=MESH,
            )

        guarded(cond, lambda: build().start())
        self.sends[key] = (cond, build)

    def sent(self, key):
        cond, build = self.sends.pop(key)
        guarded(cond, lambda: build().wait_send())

    def arrive(self, key, dst, cond=None):
        recv = self.slot(key)

        def wait():
            pltpu.make_async_remote_copy(
                src_ref=dst(),
                dst_ref=dst(),
                send_sem=self.send_sems.at[0],
                recv_sem=self.recv_sems.at[recv],
                device_id=self.away,
                device_id_type=MESH,
            ).wait_recv()

        guarded(cond, wait)

    def local(self, key, src, dst):
        index = len(self.locals)
        copy = pltpu.make_async_copy(src, dst, self.local_sems.at[index])
        copy.start()
        self.locals[key] = copy

    def ready(self, key):
        if key not in self.done:
            self.done.add(key)
            self.locals[key].wait()

    def drain(self):
        for key in list(self.sends):
            self.sent(key)
        for key in self.locals:
            self.ready(key)


def greet(depth, coords):
    x, y, c, z = coords
    barrier = pltpu.get_barrier_semaphore()
    for device in ({"y": 1 - y}, {"y": 1 - y, "x": 1 - x}, {"c": 1 - c}):
        pl.semaphore_signal(barrier, inc=1, device_id=device, device_id_type=MESH)
    for zi in range(depth):
        for xi in range(2):

            def tell(zi=zi, xi=xi):
                pl.semaphore_signal(
                    barrier,
                    inc=1,
                    device_id={"z": jnp.int32(zi), "x": jnp.int32(xi)},
                    device_id_type=MESH,
                )

            pl.when(jnp.logical_or(z != zi, x != xi))(tell)
    pl.semaphore_wait(barrier, 3 + 2 * depth - 1)


def along(depth, z):
    return (
        ("up", {"z": z + 1}, z + 1 < depth, lambda k: z - k, lambda k: z - k >= 0),
        ("down", {"z": z - 1}, z > 0, lambda k: z + k, lambda k: z + k < depth),
    )


class SlabGather:
    def __init__(self, net, name, coords, dst):
        self.net, self.name, self.dst = net, name, dst
        x, y, c, _ = coords
        self.chips = (
            (1, {"y": 1 - y}),
            (2, {"x": 1 - x}),
            (3, {"y": 1 - y, "x": 1 - x}),
        )
        self.mate = {"c": 1 - c}

    def put(self, slot, src, device):
        self.net.send(
            (self.name, slot), lambda: src, lambda: self.dst.at[slot], device
        )

    def start(self, src):
        for chip, device in self.chips:
            self.put(2 * chip, src, device)
        self.put(1, src, self.mate)
        self.net.local((self.name, "own"), src, self.dst.at[0])

    def forward(self):
        for chip, _ in self.chips:
            self.net.arrive((self.name, 2 * chip), lambda: self.dst.at[2 * chip])
            self.put(2 * chip + 1, self.dst.at[2 * chip], self.mate)

    def finish(self):
        self.net.ready((self.name, "own"))
        for slot in (1, 3, 5, 7):
            self.net.arrive((self.name, slot), lambda: self.dst.at[slot])


class AttentionGather:
    def __init__(self, net, name, depth, coords, src, dst):
        self.net, self.name, self.depth, self.coords, self.src, self.dst = (
            net, name, depth, coords, src, dst,
        )
        self.rows, self.columns = src.shape[0], src.shape[1] // 4

    def lanes(self, yi, ci):
        return pl.ds(pl.multiple_of((2 * yi + ci) * self.columns, LANES), self.columns)

    def block(self, zi, xi, yi, ci):
        rows = pl.ds(pl.multiple_of((zi * 2 + xi) * self.rows, self.rows), self.rows)
        return lambda: self.dst.at[rows, self.lanes(yi, ci)]

    def put(self, key, place, device, cond=None, src=None):
        block = self.block(*place)
        self.net.send((self.name,) + key, src or block, block, device, cond)

    def wait(self, key, place, cond=None):
        self.net.arrive((self.name,) + key, self.block(*place), cond)

    def start(self):
        x, y, c, z = self.coords
        own = lambda: self.src.at[:, self.lanes(y, c)]
        cross = lambda: self.src.at[:, self.lanes(1 - y, c)]
        for tag, device, more, _, _ in along(self.depth, z):
            self.put(("z", tag, 1), (z, x, y, c), device, more, own)
        self.put(("x", "same"), (z, x, y, c), {"x": 1 - x}, None, own)
        self.put(("x", "cross"), (z, x, 1 - y, c), {"x": 1 - x}, None, cross)
        rows = pl.ds(pl.multiple_of((z * 2 + x) * self.rows, self.rows), self.rows)
        self.net.local((self.name, "own"), self.src, self.dst.at[rows, :])

    def pass_z(self, k):
        x, y, c, z = self.coords
        for tag, device, more, origin, there in along(self.depth, z):
            place, cond = (origin(k), x, y, c), there(k)
            self.wait(("z", tag, k), place, cond)
            if k + 1 < self.depth:
                self.put(("z", tag, k + 1), place, device, both(cond, more))
            self.put(("x", tag, k), place, {"x": 1 - x}, cond)
            self.put(("y", tag, k, 0), place, {"y": 1 - y}, cond)
            self.put(("c", tag, k, 0), place, {"c": 1 - c}, cond)

    def pass_x(self, k):
        x, y, c, z = self.coords
        if k == 0:
            for tag, yi in (("same", y), ("cross", 1 - y)):
                place = (z, 1 - x, yi, c)
                self.wait(("x", tag), place)
                self.put(("c", tag), place, {"c": 1 - c})
            return
        for tag, _, _, origin, there in along(self.depth, z):
            place, cond = (origin(k), 1 - x, y, c), there(k)
            self.wait(("x", tag, k), place, cond)
            self.put(("y", tag, k, 1), place, {"y": 1 - y}, cond)
            self.put(("c", tag, k, 1), place, {"c": 1 - c}, cond)

    def pass_y(self, k):
        x, y, c, z = self.coords
        for tag, _, _, origin, there in along(self.depth, z):
            cond = there(k)
            for j, xi in ((0, x), (1, 1 - x)):
                place = (origin(k), xi, 1 - y, c)
                self.wait(("y", tag, k, j), place, cond)
                self.put(("c", tag, k, 2 + j), place, {"c": 1 - c}, cond)

    def finish(self):
        x, y, c, z = self.coords
        self.net.ready((self.name, "own"))
        for tag, yi in (("same", y), ("cross", 1 - y)):
            self.wait(("c", tag), (z, 1 - x, yi, 1 - c))
        for k in range(1, self.depth):
            for tag, _, _, origin, there in along(self.depth, z):
                for j, (xi, yi) in enumerate(((x, y), (1 - x, y), (x, 1 - y), (1 - x, 1 - y))):
                    self.wait(("c", tag, k, j), (origin(k), xi, yi, 1 - c), there(k))


class ExpertGather:
    def __init__(self, net, name, depth, coords, src, dst):
        self.net, self.name, self.depth, self.coords, self.src, self.dst = (
            net, name, depth, coords, src, dst,
        )
        self.rows = src.shape[1]

    def block(self, zi, xi):
        rows = pl.ds(pl.multiple_of((zi * 2 + xi) * self.rows, self.rows), self.rows)
        return lambda: self.dst.at[rows, :]

    def put(self, key, place, device, cond=None, src=None):
        block = self.block(*place)
        self.net.send((self.name,) + key, src or block, block, device, cond)

    def start(self):
        x, y, c, z = self.coords
        own = self.src.at[4 * x + 2 * y + c]
        for tag, device, more, _, _ in along(self.depth, z):
            self.put(("z", tag, 1, 0), (z, x), device, more, lambda: own)
        away = self.src.at[4 * (1 - x) + 2 * y + c]
        self.put(("x",), (z, x), {"x": 1 - x}, None, lambda: away)
        self.net.local((self.name, "own"), own, self.block(z, x)())

    def pass_x(self):
        x, y, c, z = self.coords
        self.net.arrive((self.name, "x"), self.block(z, 1 - x))
        for tag, device, more, _, _ in along(self.depth, z):
            self.put(("z", tag, 1, 1), (z, 1 - x), device, more)

    def pass_z(self, k):
        x, y, c, z = self.coords
        for j, xi in ((0, x), (1, 1 - x)):
            for tag, device, more, origin, there in along(self.depth, z):
                place, cond = (origin(k), xi), there(k)
                self.net.arrive((self.name, "z", tag, k, j), self.block(*place), cond)
                if k + 1 < self.depth:
                    self.put(("z", tag, k + 1, j), place, device, both(cond, more))

    def finish(self):
        self.net.ready((self.name, "own"))


def inverse_rms(values):
    return lax.rsqrt(jnp.mean(values * values, axis=-1, keepdims=True) + epsilon)


def turn(values, cosine, sine):
    return values * cosine + pltpu.roll(values, HEAD_DIM // 2, axis=1) * sine


def forward_kernel(depth, shard_rows, *refs):
    (
        hidden, mask, cosine, sine, gains_in, wq_in, wo_in, gate_in, up_in, down_in, grad_in, share_in,
        wq, wo, gains, gate, up, down, rows, grads, shares,
        queries, keys, values, probability, attended, mixed, gain_rows,
        wq_here, wo_here, normed_two, gains_here, send_sems, recv_sems, local_sems,
    ) = refs
    coords = x, y, c, z = tuple(lax.axis_index(n) for n in ("x", "y", "c", "z"))
    net = Net(send_sems, recv_sems, local_sems, c)
    greet(depth, coords)

    attn = [
        AttentionGather(net, "wq", depth, coords, wq_in, wq),
        AttentionGather(net, "wo", depth, coords, wo_in, wo),
    ]
    gate_up = [
        ExpertGather(net, "gate", depth, coords, gate_in, gate),
        ExpertGather(net, "up", depth, coords, up_in, up),
    ]
    down_one = ExpertGather(net, "down", depth, coords, down_in, down)

    me = z * 2 + x
    base = [net.slot(("gains", s)) for s in range(2 * depth)][0]
    net.local("gains", gains_in, gains.at[me])

    def gain_copy(s, index):
        return pltpu.make_async_remote_copy(
            src_ref=gains_in,
            dst_ref=gains.at[me],
            send_sem=send_sems.at[index],
            recv_sem=recv_sems.at[base + me],
            device_id={"z": jnp.int32(s // 2), "x": jnp.int32(s % 2)},
            device_id_type=MESH,
        )

    gain_sends = []
    for s in range(2 * depth):
        index = net.count
        net.count += 1
        gain_sends.append((s, index))
        pl.when(me != s)(lambda: gain_copy(s, index).start())

    for one in attn:
        one.start()
    for one in gate_up:
        one.start()
    for k in range(1, depth):
        for one in attn:
            one.pass_z(k)
    attn[0].pass_x(0)
    attn[1].pass_x(0)
    for k in range(1, depth):
        for one in attn:
            one.pass_x(k)
    for one in gate_up:
        one.pass_x()
    share_net = SlabGather(net, "share", coords, shares)
    share_net.start(share_in)
    grad_net = SlabGather(net, "grad", coords, grads)
    grad_net.start(grad_in)
    for k in range(1, depth):
        for one in attn:
            one.pass_y(k)
    for one in gate_up:
        one.pass_z(1)
    down_one.start()
    attn[0].finish()
    net.local("wq here", wq, wq_here)
    for s in range(2 * depth):
        pl.when(me != s)(
            lambda: net.arrive(("gains", s), lambda: gains.at[s])
        )
    net.ready("gains")

    net.local("gains here", gains, gains_here)
    net.ready("gains here")
    wide = None
    for s in range(2 * depth):
        rest = jnp.zeros((8, hidden.shape[1] - gains.shape[2]), F32)
        piece = jnp.concatenate([gains_here[s], rest], axis=1)
        piece = piece if s == 0 else pltpu.roll(piece, s * shard_rows, axis=1)
        wide = piece if wide is None else wide + piece
    gain_rows[...] = wide

    inputs = hidden[...].astype(F32)
    normed = (inputs * inverse_rms(inputs) * gain_rows[0:1, :]).astype(BF16)
    cos, sin = cosine[...], sine[...]
    net.ready("wq here")
    step = 512
    length = hidden.shape[0]
    for start in range(0, wq.shape[1], step):
        part = dot_nn(normed, wq_here[:, start : start + step])
        for at in range(start, start + step, HEAD_DIM):
            head, one = at // HEAD_DIM, part[:, at - start : at - start + HEAD_DIM]
            if head < HEADS:
                queries[head * length : (head + 1) * length, :] = turn(one, cos, sin).astype(BF16)
            elif head < HEADS + KV_HEADS:
                at_row = (head - HEADS) * length
                keys[at_row : at_row + length, :] = turn(one, cos, sin).astype(BF16)
            else:
                at_row = (head - HEADS - KV_HEADS) * length
                values[at_row : at_row + length, :] = one.astype(BF16)
    share_net.forward()
    grad_net.forward()
    for one in gate_up:
        for k in range(2, depth):
            one.pass_z(k)
    down_one.pass_x()
    attn[1].finish()
    net.local("wo here", wo, wo_here)
    factor = HEAD_DIM ** (-0.5)
    allowed = mask[...] > 0.0
    for head in range(HEADS):
        kv = head // GROUP
        here = slice(head * length, (head + 1) * length)
        there = slice(kv * length, (kv + 1) * length)
        scores = dot_nt(queries[here, :], keys[there, :]) * factor
        scores = jnp.where(allowed, scores, masked_score)
        terms = jnp.exp(scores - jnp.max(scores, axis=-1, keepdims=True))
        chance = terms / jnp.sum(terms, axis=-1, keepdims=True)
        probability[here, :] = chance
        attended[:, head * HEAD_DIM : (head + 1) * HEAD_DIM] = dot_nn(
            chance.astype(BF16), values[there, :]
        ).astype(BF16)
    net.ready("wo here")
    for start in range(0, wo.shape[1], step):
        there = slice(start, start + step)
        mixed[:, there] = hidden[:, there].astype(F32) + dot_nn(attended[...], wo_here[:, there])
    total = mixed[...]
    normed_two[...] = (total * inverse_rms(total) * gain_rows[1:2, :]).astype(BF16)
    row_net = SlabGather(net, "rows", coords, rows)
    row_net.start(normed_two)
    down_one.pass_z(1)
    row_net.forward()
    for k in range(2, depth):
        down_one.pass_z(k)
    share_net.finish()
    grad_net.finish()
    row_net.finish()
    for one in gate_up + [down_one]:
        one.finish()
    for s, index in gain_sends:
        pl.when(me != s)(lambda: gain_copy(s, index).wait_send())
    net.drain()
    assert net.count <= send_sems.shape[0] and len(net.slots) <= recv_sems.shape[0]


def forward_call(depth, shard_rows, *args):
    hidden, mask, cosine, sine, gains_in, wq_in, wo_in, gate_in, up_in, down_in, grad_in, share_in = args
    length, width = hidden.shape
    shards = 2 * depth
    here, there = pl.BlockSpec(memory_space=pltpu.VMEM), pl.BlockSpec(memory_space=pltpu.HBM)

    def shape(*dims, dtype=BF16):
        return jax.ShapeDtypeStruct(dims, dtype)

    wide = wq_in.shape[1]
    out_shape = [
        shape(width, wide), shape(width, width), shape(shards, *gains_in.shape, dtype=F32),
        shape(shards * gate_in.shape[1], gate_in.shape[2]),
        shape(shards * up_in.shape[1], up_in.shape[2]),
        shape(shards * down_in.shape[1], down_in.shape[2]),
        shape(EXPERTS, length, width), shape(EXPERTS, length, width),
        shape(EXPERTS, length, LANES, dtype=F32),
        shape(HEADS * length, HEAD_DIM), shape(KV_HEADS * length, HEAD_DIM),
        shape(KV_HEADS * length, HEAD_DIM), shape(HEADS * length, length, dtype=F32),
        shape(length, width), shape(length, width, dtype=F32), shape(8, width, dtype=F32),
    ]
    sends = 24 * depth * 2 + 80
    return pl.pallas_call(
        functools.partial(forward_kernel, depth, shard_rows),
        out_shape=out_shape,
        in_specs=[here] * 4 + [there] * 8,
        out_specs=[there] * 9 + [here] * 7,
        scratch_shapes=[
            pltpu.VMEM((width, wide), BF16),
            pltpu.VMEM((width, width), BF16),
            pltpu.VMEM((length, width), BF16),
            pltpu.VMEM((shards, *gains_in.shape), F32),
            pltpu.SemaphoreType.DMA((sends,)),
            pltpu.SemaphoreType.DMA((sends,)),
            pltpu.SemaphoreType.DMA((16,)),
        ],
        compiler_params=pltpu.CompilerParams(
            collective_id=1, has_side_effects=True, vmem_limit_bytes=VMEM_LIMIT
        ),
    )(*args)


def norm_back(values, scale_gain, upstream):
    inverse = lax.rsqrt(jnp.mean(values * values, axis=-1, keepdims=True) + epsilon)
    normal = values * inverse
    gain_grad = jnp.sum(upstream * normal, axis=0)
    scaled = upstream * scale_gain
    value_grad = inverse * (scaled - normal * jnp.mean(scaled * normal, axis=-1, keepdims=True))
    return (value_grad, gain_grad)


def rms_norm(values, scale_gain):
    return (
        values * lax.rsqrt(jnp.mean(values * values, axis=-1, keepdims=True) + epsilon) * scale_gain
    )


def rotary_tables(length, head_width):
    half_width = head_width // 2
    frequency = rotary_base ** (-2.0 * jnp.arange(half_width, dtype=jnp.float32) / head_width)
    angles = jnp.arange(length, dtype=jnp.float32)[:, None] * frequency[None, :]
    return (jnp.cos(angles)[:, None, :], jnp.sin(angles)[:, None, :])


def rotate(values, cosine, sine_table):
    half_width = values.shape[-1] // 2
    first_half = values[..., :half_width]
    second_half = values[..., half_width:]
    return jnp.concatenate(
        [
            first_half * cosine - second_half * sine_table,
            second_half * cosine + first_half * sine_table,
        ],
        axis=-1,
    )


def swap(value, axes):
    count = 2 ** len(axes)
    return lax.ppermute(value, axes, [(i, count - 1 - i) for i in range(count)])


def ordered(mine, other, place):
    first = jnp.where(place == 0, mine, other)
    second = jnp.where(place == 0, other, mine)
    return jnp.stack([first, second])


def line_steps(depth):
    up = [(i, i + 1) for i in range(depth - 1)]
    down = [(i + 1, i) for i in range(depth - 1)]
    return up, down


def line_gather(block, depth, place):
    up, down = line_steps(depth)
    below, above = [], []
    a = b = block
    for _ in range(depth - 1):
        a = lax.ppermute(a, "z", up)
        b = lax.ppermute(b, "z", down)
        below.append(a)
        above.append(b)
    around = jnp.stack(below[::-1] + [block] + above)
    return lax.dynamic_slice_in_dim(around, depth - 1 - place, depth, 0)


def line_scatter(blocks, depth, place):
    up, down = line_steps(depth)

    def at(index):
        return lax.dynamic_index_in_dim(blocks, jnp.clip(index, 0, depth - 1), 0, keepdims=False)

    a = b = None
    for step in range(1, depth):
        send_a = at(depth - step + place)
        send_b = at(place - 1 - (depth - 1) + step - 0)
        if a is not None:
            send_a = (send_a.astype(F32) + a.astype(F32)).astype(BF16)
            send_b = (send_b.astype(F32) + b.astype(F32)).astype(BF16)
        a = lax.ppermute(send_a, "z", up)
        b = lax.ppermute(send_b, "z", down)
    total = at(place).astype(F32)
    if a is not None:
        total = total + a.astype(F32) + b.astype(F32)
    return total


def slab_gather(block):
    by_x = swap(block, ("x",))
    by_y = swap(block, ("y",))
    by_xy = swap(block, ("y", "x"))
    chips = jnp.stack([block, by_y, by_x, by_xy])
    mate = swap(chips, ("c",))
    return jnp.stack([chips, mate], axis=1)


def slab_return(parts):
    mate = swap(parts[:, 1], ("c",))
    both = parts[:, 0].astype(F32) + mate.astype(F32)
    low = both.astype(BF16)
    by_y = swap(low[1], ("y",))
    by_x = swap(low[2], ("x",))
    by_xy = swap(low[3], ("y", "x"))
    return both[0] + by_x.astype(F32) + by_y.astype(F32) + by_xy.astype(F32)


def make_shards(sizes):
    depth = sizes["z"]

    def shards(
        hidden_in,
        segments,
        routes,
        gate_weights,
        grad_out,
        attn_gain,
        query_weight,
        key_weight,
        value_weight,
        output_weight,
        ffn_gain,
        gate_weight,
        up_weight,
        down_weight,
    ):
        length, width = hidden_in.shape
        groups = HEADS // KV_HEADS
        factor = HEAD_DIM ** (-0.5)
        x, y, c, z = (lax.axis_index(n) for n in ("x", "y", "c", "z"))
        expert = 4 * x + 2 * y + c
        gains = jnp.stack([attn_gain, ffn_gain]).astype(F32)
        shard_rows = gains.shape[1]
        lanes = -(-shard_rows // LANES) * LANES
        gains = jnp.pad(gains, ((0, 6), (0, lanes - shard_rows)))
        wq_in = jnp.concatenate([query_weight, key_weight, value_weight], axis=1)
        onehot = routes[:, :, None] == jnp.arange(LANES, dtype=jnp.int32)
        shares = jnp.sum(jnp.where(onehot, gate_weights[:, :, None], 0.0), axis=1)
        segment = segments[0]
        position = jnp.arange(length, dtype=jnp.int32)
        allowed = (position[:, None] >= position[None, :]) & (segment[:, None] == segment[None, :])
        cosine, sine_table = rotary_tables(length, HEAD_DIM)
        cos_wide = jnp.concatenate([cosine[:, 0], cosine[:, 0]], axis=1)
        sin_wide = jnp.concatenate([-sine_table[:, 0], sine_table[:, 0]], axis=1)
        (
            qkv_full, output_full, _, gate_full, up_full, down_full, rows_in, grads, shares,
            queries, keys, value_rows, probability, attended, mixed, gain_rows,
        ) = forward_call(
            depth, shard_rows, hidden_in, allowed.astype(F32), cos_wide, sin_wide, gains,
            wq_in, output_weight, gate_weight, up_weight, down_weight, grad_out, shares,
        )
        gain_first, gain_second = gain_rows[0], gain_rows[1]
        share = jnp.sum(
            jnp.where(jnp.arange(LANES) == expert, shares, 0.0), axis=2
        ).reshape(-1, 1)
        rows_in, grads = rows_in.reshape(-1, width), grads.reshape(-1, width)
        inputs = hidden_in.astype(F32)
        normed = rms_norm(inputs, gain_first).astype(BF16)
        probability = probability.reshape(KV_HEADS, groups, length, length)
        probability_low = probability.astype(BF16)
        grouped = queries.reshape(KV_HEADS, groups, length, HEAD_DIM).transpose(2, 0, 1, 3)
        rotated_keys = keys.reshape(KV_HEADS, length, HEAD_DIM).transpose(1, 0, 2)
        value_heads = value_rows.reshape(KV_HEADS, length, HEAD_DIM).transpose(1, 0, 2)
        mine = 2 * y + c
        rows = shard_rows
        quarter = rows // 4
        qkv = wq_in.shape[1]
        columns = qkv + width + 128

        gate_proj = dot(rows_in, gate_full, ((1,), (0,)))
        up_proj = dot(rows_in, up_full, ((1,), (0,)))
        sigmoid_gate = jax.nn.sigmoid(gate_proj)
        silu_gate = gate_proj * sigmoid_gate
        hidden_act = (silu_gate * up_proj).astype(BF16)
        expert_grad = (share * grads.astype(F32)).astype(BF16)
        down_grad = dot(hidden_act, expert_grad, ((0,), (0,))).astype(BF16)
        expert_out = dot(hidden_act, down_full, ((1,), (0,)))
        expert_part = (share * expert_out).astype(BF16).reshape(4, 2, length, width)
        hidden_grad = dot(expert_grad, down_full, ((1,), (1,)))
        gate_grad = (
            hidden_grad * up_proj * sigmoid_gate * (1.0 + gate_proj * (1.0 - sigmoid_gate))
        ).astype(BF16)
        up_grad = (hidden_grad * silu_gate).astype(BF16)
        rows_grad = dot(gate_grad, gate_full, ((1,), (1,))) + dot(up_grad, up_full, ((1,), (1,)))
        rows_grad = rows_grad.astype(BF16).reshape(4, 2, length, width)
        gate_weight_grad = dot(rows_in, gate_grad, ((0,), (0,))).astype(BF16)
        up_weight_grad = dot(rows_in, up_grad, ((0,), (0,))).astype(BF16)

        layer_out = (mixed + slab_return(expert_part)).astype(BF16)
        normed_two_grad = slab_return(rows_grad)

        def over_outer(value):
            return lax.psum(value, "o") if sizes["o"] > 1 else value

        def expert_scatter(grad):
            shard = grad.shape[0] // (2 * depth)
            blocks = grad.reshape(depth, 2, shard, grad.shape[1])
            total = over_outer(line_scatter(blocks, depth, z)).astype(BF16)
            own = lax.dynamic_index_in_dim(total, x, 0, keepdims=False)
            away = lax.dynamic_index_in_dim(total, 1 - x, 0, keepdims=False)
            four = ordered(own, swap(away, ("x",)), x)[:, None]
            four = ordered(four, swap(four, ("y",)), y)
            four = ordered(four, swap(four, ("c",)), c)
            return four.transpose(2, 1, 0, 3, 4, 5).reshape(EXPERTS, shard, -1).astype(F32)

        total_down = expert_scatter(down_grad)
        total_gate = expert_scatter(gate_weight_grad)
        total_up = expert_scatter(up_weight_grad)

        upstream = grad_out.astype(F32)
        mixed_part, ffn_gain_grad = norm_back(mixed, gain_second, normed_two_grad)
        mixed_grad = upstream + mixed_part
        mixed_low = mixed_grad.astype(BF16)
        output_weight_grad = dot(attended, mixed_low, ((0,), (0,)))
        attended_grad = dot(mixed_low, output_full, ((1,), (1,)))
        attended_grad = attended_grad.astype(BF16).reshape(length, KV_HEADS, groups, HEAD_DIM)
        prob_grad = jnp.einsum(
            "ikgd,jkd->kgij", attended_grad, value_heads, preferred_element_type=F32
        )
        value_grad = jnp.einsum(
            "kgij,ikgd->jkd", probability_low, attended_grad, preferred_element_type=F32
        )
        value_grad = value_grad.astype(BF16).reshape(length, KV_HEADS * HEAD_DIM)
        score_grad = (
            probability * (prob_grad - jnp.sum(probability * prob_grad, axis=-1, keepdims=True))
        ).astype(BF16)
        query_rot_grad = (
            jnp.einsum("kgij,jkd->ikgd", score_grad, rotated_keys, preferred_element_type=F32)
            * factor
        )
        key_rot_grad = (
            jnp.einsum("kgij,ikgd->jkd", score_grad, grouped, preferred_element_type=F32) * factor
        )
        query_raw_grad = rotate(
            query_rot_grad.reshape(length, HEADS, HEAD_DIM), cosine, -sine_table
        )
        query_raw_grad = query_raw_grad.astype(BF16).reshape(length, HEADS * HEAD_DIM)
        key_raw_grad = (
            rotate(key_rot_grad, cosine, -sine_table)
            .astype(BF16)
            .reshape(length, KV_HEADS * HEAD_DIM)
        )
        qkv_grad = jnp.concatenate([query_raw_grad, key_raw_grad, value_grad], axis=1)
        normed_grad = dot(qkv_grad, qkv_full, ((1,), (1,)))
        qkv_weight_grad = dot(normed, qkv_grad, ((0,), (0,)))
        input_part, attn_gain_grad = norm_back(inputs, gain_first, normed_grad)
        grad_in = (mixed_grad + input_part).astype(BF16)

        gain_grads = jnp.stack([attn_gain_grad, ffn_gain_grad], axis=1)
        gain_grads = jnp.pad(gain_grads, ((0, 0), (0, 126)))
        packed_grad = jnp.concatenate(
            [qkv_weight_grad, output_weight_grad, gain_grads], axis=1
        ).astype(BF16)
        parts = packed_grad.reshape(depth, 2, 2, 2, quarter, columns)
        parts = parts.transpose(3, 1, 2, 0, 4, 5)

        def pick(value, place):
            return lax.dynamic_index_in_dim(value, place, 0, keepdims=False)

        def halve(value, axis, place):
            other = swap(pick(value, 1 - place), (axis,))
            return (pick(value, place).astype(F32) + other.astype(F32)).astype(BF16)

        parts = halve(parts, "c", c)
        parts = halve(parts, "x", x)
        parts = halve(parts, "y", y)
        total = over_outer(line_scatter(parts, depth, z)).astype(BF16)
        total = ordered(total, swap(total, ("c",)), c)
        total = ordered(total, swap(total, ("y",)), y).reshape(rows, columns).astype(F32)
        kv = KV_HEADS * HEAD_DIM
        return (
            layer_out,
            grad_in,
            total[:, qkv + width],
            total[:, : qkv - 2 * kv],
            total[:, qkv - 2 * kv : qkv - kv],
            total[:, qkv - kv : qkv],
            total[:, qkv : qkv + width],
            total[:, qkv + width + 1],
            total_gate,
            total_up,
            total_down,
        )

    return shards


def solution(mesh):
    reps, shard_count = mesh.shape["rep"], mesh.shape["shard"]
    sizes = {"o": reps // 4, "y": 2, "c": 2, "z": shard_count // 2, "x": 2}
    fine = Mesh(mesh.devices.reshape(tuple(sizes.values())), tuple(sizes))
    tokens = P(("o", "y", "c", "z", "x"), None)
    first, second = P(("z", "x")), P(None, ("z", "x"), None)
    matrix = P(("z", "x"), None)
    return jax.shard_map(
        make_shards(sizes),
        mesh=fine,
        in_specs=(
            (tokens,) * 5 + (first, matrix, matrix, matrix, matrix, first) + (second,) * 3
        ),
        out_specs=(
            (tokens,) * 2 + (first, matrix, matrix, matrix, matrix, first) + (second,) * 3
        ),
        check_vma=False,
    )
```

```python
import functools

import jax
import jax.numpy as jnp
from jax import lax
from jax.experimental import pallas as pl
from jax.experimental.pallas import tpu as pltpu
from jax.sharding import Mesh
from jax.sharding import PartitionSpec as P

HEADS = 12
KV_HEADS = 2
GROUP = HEADS // KV_HEADS
HEAD_DIM = 128
EXPERTS = 8
LANES = 128

epsilon = 1e-06
rotary_base = 1000000.0
masked_score = -1e30

F32 = jnp.float32
BF16 = jnp.bfloat16
MESH = pl.DeviceIdType.MESH
VMEM_LIMIT = 62 * 2**20


def dot(a, b, dims):
    return lax.dot_general(a, b, (dims, ((), ())), preferred_element_type=F32)


def dot_nn(a, b):
    return dot(a, b, ((1,), (0,)))


def dot_nt(a, b):
    return dot(a, b, ((1,), (1,)))


def dot_tn(a, b):
    return dot(a, b, ((0,), (0,)))


def guarded(cond, body):
    if cond is None:
        body()
    else:
        pl.when(cond)(body)


def both(first, second):
    if first is None:
        return second
    if second is None:
        return first
    return jnp.logical_and(first, second)


class Net:
    def __init__(self, send_sems, recv_sems, local_sems, core):
        self.send_sems, self.recv_sems, self.local_sems = send_sems, recv_sems, local_sems
        self.away = {"c": 1 - core}
        self.slots, self.sends, self.locals, self.count, self.done = {}, {}, {}, 0, set()

    def slot(self, key):
        return self.slots.setdefault(key, len(self.slots))

    def send(self, key, src, dst, device, cond=None, slot=None):
        recv, index = self.slot(slot or key), self.count
        self.count += 1

        def build():
            return pltpu.make_async_remote_copy(
                src_ref=src(),
                dst_ref=dst(),
                send_sem=self.send_sems.at[index],
                recv_sem=self.recv_sems.at[recv],
                device_id=device,
                device_id_type=MESH,
            )

        guarded(cond, lambda: build().start())
        self.sends[key] = (cond, build)

    def sent(self, key):
        cond, build = self.sends.pop(key)
        guarded(cond, lambda: build().wait_send())

    def arrive(self, key, dst, cond=None):
        recv = self.slot(key)

        def wait():
            pltpu.make_async_remote_copy(
                src_ref=dst(),
                dst_ref=dst(),
                send_sem=self.send_sems.at[0],
                recv_sem=self.recv_sems.at[recv],
                device_id=self.away,
                device_id_type=MESH,
            ).wait_recv()

        guarded(cond, wait)

    def local(self, key, src, dst):
        index = len(self.locals)
        copy = pltpu.make_async_copy(src, dst, self.local_sems.at[index])
        copy.start()
        self.locals[key] = copy

    def ready(self, key):
        if key not in self.done:
            self.done.add(key)
            self.locals[key].wait()

    def drain(self):
        for key in list(self.sends):
            self.sent(key)
        for key in self.locals:
            self.ready(key)


def greet(depth, coords):
    x, y, c, z = coords
    barrier = pltpu.get_barrier_semaphore()
    for device in ({"y": 1 - y}, {"y": 1 - y, "x": 1 - x}, {"c": 1 - c}):
        pl.semaphore_signal(barrier, inc=1, device_id=device, device_id_type=MESH)
    for zi in range(depth):
        for xi in range(2):

            def tell(zi=zi, xi=xi):
                pl.semaphore_signal(
                    barrier,
                    inc=1,
                    device_id={"z": jnp.int32(zi), "x": jnp.int32(xi)},
                    device_id_type=MESH,
                )

            pl.when(jnp.logical_or(z != zi, x != xi))(tell)
    pl.semaphore_wait(barrier, 3 + 2 * depth - 1)


def along(depth, z):
    return (
        ("up", {"z": z + 1}, z + 1 < depth, lambda k: z - k, lambda k: z - k >= 0),
        ("down", {"z": z - 1}, z > 0, lambda k: z + k, lambda k: z + k < depth),
    )


class SlabGather:
    def __init__(self, net, name, coords, dst):
        self.net, self.name, self.dst = net, name, dst
        x, y, c, _ = coords
        self.chips = (
            (1, {"y": 1 - y}),
            (2, {"x": 1 - x}),
            (3, {"y": 1 - y, "x": 1 - x}),
        )
        self.mate = {"c": 1 - c}

    def put(self, slot, src, device):
        self.net.send(
            (self.name, slot), lambda: src, lambda: self.dst.at[slot], device
        )

    def start(self, src):
        for chip, device in self.chips:
            self.put(2 * chip, src, device)
        self.put(1, src, self.mate)
        self.net.local((self.name, "own"), src, self.dst.at[0])

    def forward(self):
        for chip, _ in self.chips:
            self.net.arrive((self.name, 2 * chip), lambda: self.dst.at[2 * chip])
            self.put(2 * chip + 1, self.dst.at[2 * chip], self.mate)

    def finish(self):
        self.net.ready((self.name, "own"))
        for slot in (1, 3, 5, 7):
            self.net.arrive((self.name, slot), lambda: self.dst.at[slot])


class AttentionGather:
    def __init__(self, net, name, depth, coords, src, dst):
        self.net, self.name, self.depth, self.coords, self.src, self.dst = (
            net, name, depth, coords, src, dst,
        )
        self.rows, self.columns = src.shape[0], src.shape[1] // 4

    def lanes(self, yi, ci):
        return pl.ds(pl.multiple_of((2 * yi + ci) * self.columns, LANES), self.columns)

    def block(self, zi, xi, yi, ci):
        rows = pl.ds(pl.multiple_of((zi * 2 + xi) * self.rows, self.rows), self.rows)
        return lambda: self.dst.at[rows, self.lanes(yi, ci)]

    def put(self, key, place, device, cond=None, src=None):
        block = self.block(*place)
        self.net.send((self.name,) + key, src or block, block, device, cond)

    def wait(self, key, place, cond=None):
        self.net.arrive((self.name,) + key, self.block(*place), cond)

    def start(self):
        x, y, c, z = self.coords
        own = lambda: self.src.at[:, self.lanes(y, c)]
        cross = lambda: self.src.at[:, self.lanes(1 - y, c)]
        for tag, device, more, _, _ in along(self.depth, z):
            self.put(("z", tag, 1), (z, x, y, c), device, more, own)
        self.put(("x", "same"), (z, x, y, c), {"x": 1 - x}, None, own)
        self.put(("x", "cross"), (z, x, 1 - y, c), {"x": 1 - x}, None, cross)
        rows = pl.ds(pl.multiple_of((z * 2 + x) * self.rows, self.rows), self.rows)
        self.net.local((self.name, "own"), self.src, self.dst.at[rows, :])

    def pass_z(self, k):
        x, y, c, z = self.coords
        for tag, device, more, origin, there in along(self.depth, z):
            place, cond = (origin(k), x, y, c), there(k)
            self.wait(("z", tag, k), place, cond)
            if k + 1 < self.depth:
                self.put(("z", tag, k + 1), place, device, both(cond, more))
            self.put(("x", tag, k), place, {"x": 1 - x}, cond)
            self.put(("y", tag, k, 0), place, {"y": 1 - y}, cond)
            self.put(("c", tag, k, 0), place, {"c": 1 - c}, cond)

    def pass_x(self, k):
        x, y, c, z = self.coords
        if k == 0:
            for tag, yi in (("same", y), ("cross", 1 - y)):
                place = (z, 1 - x, yi, c)
                self.wait(("x", tag), place)
                self.put(("c", tag), place, {"c": 1 - c})
            return
        for tag, _, _, origin, there in along(self.depth, z):
            place, cond = (origin(k), 1 - x, y, c), there(k)
            self.wait(("x", tag, k), place, cond)
            self.put(("y", tag, k, 1), place, {"y": 1 - y}, cond)
            self.put(("c", tag, k, 1), place, {"c": 1 - c}, cond)

    def pass_y(self, k):
        x, y, c, z = self.coords
        for tag, _, _, origin, there in along(self.depth, z):
            cond = there(k)
            for j, xi in ((0, x), (1, 1 - x)):
                place = (origin(k), xi, 1 - y, c)
                self.wait(("y", tag, k, j), place, cond)
                self.put(("c", tag, k, 2 + j), place, {"c": 1 - c}, cond)

    def finish(self):
        x, y, c, z = self.coords
        self.net.ready((self.name, "own"))
        for tag, yi in (("same", y), ("cross", 1 - y)):
            self.wait(("c", tag), (z, 1 - x, yi, 1 - c))
        for k in range(1, self.depth):
            for tag, _, _, origin, there in along(self.depth, z):
                for j, (xi, yi) in enumerate(((x, y), (1 - x, y), (x, 1 - y), (1 - x, 1 - y))):
                    self.wait(("c", tag, k, j), (origin(k), xi, yi, 1 - c), there(k))


class ExpertGather:
    def __init__(self, net, name, depth, coords, src, dst):
        self.net, self.name, self.depth, self.coords, self.src, self.dst = (
            net, name, depth, coords, src, dst,
        )
        self.rows = src.shape[1]

    def block(self, zi, xi):
        rows = pl.ds(pl.multiple_of((zi * 2 + xi) * self.rows, self.rows), self.rows)
        return lambda: self.dst.at[rows, :]

    def put(self, key, place, device, cond=None, src=None):
        block = self.block(*place)
        self.net.send((self.name,) + key, src or block, block, device, cond)

    def start(self):
        x, y, c, z = self.coords
        own = self.src.at[4 * x + 2 * y + c]
        for tag, device, more, _, _ in along(self.depth, z):
            self.put(("z", tag, 1, 0), (z, x), device, more, lambda: own)
        away = self.src.at[4 * (1 - x) + 2 * y + c]
        self.put(("x",), (z, x), {"x": 1 - x}, None, lambda: away)
        self.net.local((self.name, "own"), own, self.block(z, x)())

    def pass_x(self):
        x, y, c, z = self.coords
        self.net.arrive((self.name, "x"), self.block(z, 1 - x))
        for tag, device, more, _, _ in along(self.depth, z):
            self.put(("z", tag, 1, 1), (z, 1 - x), device, more)

    def pass_z(self, k):
        x, y, c, z = self.coords
        for j, xi in ((0, x), (1, 1 - x)):
            for tag, device, more, origin, there in along(self.depth, z):
                place, cond = (origin(k), xi), there(k)
                self.net.arrive((self.name, "z", tag, k, j), self.block(*place), cond)
                if k + 1 < self.depth:
                    self.put(("z", tag, k + 1, j), place, device, both(cond, more))

    def finish(self):
        self.net.ready((self.name, "own"))


def inverse_rms(values):
    return lax.rsqrt(jnp.mean(values * values, axis=-1, keepdims=True) + epsilon)


def turn(values, cosine, sine):
    return values * cosine + pltpu.roll(values, HEAD_DIM // 2, axis=1) * sine


def forward_kernel(depth, shard_rows, *refs):
    (
        hidden, mask, cosine, sine, gains_in, wq_in, wo_in, gate_in, up_in, down_in, grad_in, share_in,
        wq, wo, gains, gate, up, down, rows, grads, shares,
        queries, keys, values, probability, attended, mixed, gain_rows,
        wq_here, wo_here, normed_two, gains_here, send_sems, recv_sems, local_sems,
    ) = refs
    coords = x, y, c, z = tuple(lax.axis_index(n) for n in ("x", "y", "c", "z"))
    net = Net(send_sems, recv_sems, local_sems, c)
    greet(depth, coords)

    attn = [
        AttentionGather(net, "wq", depth, coords, wq_in, wq),
        AttentionGather(net, "wo", depth, coords, wo_in, wo),
    ]
    gate_up = [
        ExpertGather(net, "gate", depth, coords, gate_in, gate),
        ExpertGather(net, "up", depth, coords, up_in, up),
    ]
    down_one = ExpertGather(net, "down", depth, coords, down_in, down)

    me = z * 2 + x
    base = [net.slot(("gains", s)) for s in range(2 * depth)][0]
    net.local("gains", gains_in, gains.at[me])

    def gain_copy(s, index):
        return pltpu.make_async_remote_copy(
            src_ref=gains_in,
            dst_ref=gains.at[me],
            send_sem=send_sems.at[index],
            recv_sem=recv_sems.at[base + me],
            device_id={"z": jnp.int32(s // 2), "x": jnp.int32(s % 2)},
            device_id_type=MESH,
        )

    gain_sends = []
    for s in range(2 * depth):
        index = net.count
        net.count += 1
        gain_sends.append((s, index))
        pl.when(me != s)(lambda: gain_copy(s, index).start())

    for one in attn:
        one.start()
    for one in gate_up:
        one.start()
    for k in range(1, depth):
        for one in attn:
            one.pass_z(k)
    attn[0].pass_x(0)
    attn[1].pass_x(0)
    for k in range(1, depth):
        for one in attn:
            one.pass_x(k)
    for one in gate_up:
        one.pass_x()
    share_net = SlabGather(net, "share", coords, shares)
    share_net.start(share_in)
    grad_net = SlabGather(net, "grad", coords, grads)
    grad_net.start(grad_in)
    for k in range(1, depth):
        for one in attn:
            one.pass_y(k)
    for one in gate_up:
        one.pass_z(1)
    down_one.start()
    attn[0].finish()
    net.local("wq here", wq, wq_here)
    for s in range(2 * depth):
        pl.when(me != s)(
            lambda: net.arrive(("gains", s), lambda: gains.at[s])
        )
    net.ready("gains")

    net.local("gains here", gains, gains_here)
    net.ready("gains here")
    wide = None
    for s in range(2 * depth):
        rest = jnp.zeros((8, hidden.shape[1] - gains.shape[2]), F32)
        piece = jnp.concatenate([gains_here[s], rest], axis=1)
        piece = piece if s == 0 else pltpu.roll(piece, s * shard_rows, axis=1)
        wide = piece if wide is None else wide + piece
    gain_rows[...] = wide

    inputs = hidden[...].astype(F32)
    normed = (inputs * inverse_rms(inputs) * gain_rows[0:1, :]).astype(BF16)
    cos, sin = cosine[...], sine[...]
    net.ready("wq here")
    step = 512
    length = hidden.shape[0]
    for start in range(0, wq.shape[1], step):
        part = dot_nn(normed, wq_here[:, start : start + step])
        for at in range(start, start + step, HEAD_DIM):
            head, one = at // HEAD_DIM, part[:, at - start : at - start + HEAD_DIM]
            if head < HEADS:
                queries[head * length : (head + 1) * length, :] = turn(one, cos, sin).astype(BF16)
            elif head < HEADS + KV_HEADS:
                at_row = (head - HEADS) * length
                keys[at_row : at_row + length, :] = turn(one, cos, sin).astype(BF16)
            else:
                at_row = (head - HEADS - KV_HEADS) * length
                values[at_row : at_row + length, :] = one.astype(BF16)
    share_net.forward()
    grad_net.forward()
    for one in gate_up:
        for k in range(2, depth):
            one.pass_z(k)
    down_one.pass_x()
    attn[1].finish()
    net.local("wo here", wo, wo_here)
    factor = HEAD_DIM ** (-0.5)
    allowed = mask[...] > 0.0
    for head in range(HEADS):
        kv = head // GROUP
        here = slice(head * length, (head + 1) * length)
        there = slice(kv * length, (kv + 1) * length)
        scores = dot_nt(queries[here, :], keys[there, :]) * factor
        scores = jnp.where(allowed, scores, masked_score)
        terms = jnp.exp(scores - jnp.max(scores, axis=-1, keepdims=True))
        chance = terms / jnp.sum(terms, axis=-1, keepdims=True)
        probability[here, :] = chance
        attended[:, head * HEAD_DIM : (head + 1) * HEAD_DIM] = dot_nn(
            chance.astype(BF16), values[there, :]
        ).astype(BF16)
    net.ready("wo here")
    for start in range(0, wo.shape[1], step):
        there = slice(start, start + step)
        mixed[:, there] = hidden[:, there].astype(F32) + dot_nn(attended[...], wo_here[:, there])
    total = mixed[...]
    normed_two[...] = (total * inverse_rms(total) * gain_rows[1:2, :]).astype(BF16)
    row_net = SlabGather(net, "rows", coords, rows)
    row_net.start(normed_two)
    down_one.pass_z(1)
    row_net.forward()
    for k in range(2, depth):
        down_one.pass_z(k)
    share_net.finish()
    grad_net.finish()
    row_net.finish()
    for one in gate_up + [down_one]:
        one.finish()
    for s, index in gain_sends:
        pl.when(me != s)(lambda: gain_copy(s, index).wait_send())
    net.drain()
    assert net.count <= send_sems.shape[0] and len(net.slots) <= recv_sems.shape[0]


def forward_call(depth, shard_rows, *args):
    hidden, mask, cosine, sine, gains_in, wq_in, wo_in, gate_in, up_in, down_in, grad_in, share_in = args
    length, width = hidden.shape
    shards = 2 * depth
    here, there = pl.BlockSpec(memory_space=pltpu.VMEM), pl.BlockSpec(memory_space=pltpu.HBM)

    def shape(*dims, dtype=BF16):
        return jax.ShapeDtypeStruct(dims, dtype)

    wide = wq_in.shape[1]
    out_shape = [
        shape(width, wide), shape(width, width), shape(shards, *gains_in.shape, dtype=F32),
        shape(shards * gate_in.shape[1], gate_in.shape[2]),
        shape(shards * up_in.shape[1], up_in.shape[2]),
        shape(shards * down_in.shape[1], down_in.shape[2]),
        shape(EXPERTS, length, width), shape(EXPERTS, length, width),
        shape(EXPERTS, length, LANES, dtype=F32),
        shape(HEADS * length, HEAD_DIM), shape(KV_HEADS * length, HEAD_DIM),
        shape(KV_HEADS * length, HEAD_DIM), shape(HEADS * length, length, dtype=F32),
        shape(length, width), shape(length, width, dtype=F32), shape(8, width, dtype=F32),
    ]
    sends = 24 * depth * 2 + 80
    return pl.pallas_call(
        functools.partial(forward_kernel, depth, shard_rows),
        out_shape=out_shape,
        in_specs=[here] * 4 + [there] * 8,
        out_specs=[there] * 9 + [here] * 7,
        scratch_shapes=[
            pltpu.VMEM((width, wide), BF16),
            pltpu.VMEM((width, width), BF16),
            pltpu.VMEM((length, width), BF16),
            pltpu.VMEM((shards, *gains_in.shape), F32),
            pltpu.SemaphoreType.DMA((sends,)),
            pltpu.SemaphoreType.DMA((sends,)),
            pltpu.SemaphoreType.DMA((16,)),
        ],
        compiler_params=pltpu.CompilerParams(
            collective_id=1, has_side_effects=True, vmem_limit_bytes=VMEM_LIMIT
        ),
    )(*args)


class SlabReturn:
    def __init__(self, net, name, coords, parts, length, mates, chips, load):
        self.net, self.name, self.parts, self.length = net, name, parts, length
        self.mates, self.landed, self.load = mates, chips, load
        x, y, c, _ = coords
        self.away = {1: {"y": 1 - y}, 2: {"x": 1 - x}, 3: {"y": 1 - y, "x": 1 - x}}
        self.mate = {"c": 1 - c}

    def part(self, slot):
        return self.parts.at[slot * self.length : (slot + 1) * self.length, :]

    def to_mate(self, chip):
        self.net.send(
            (self.name, "mate", chip),
            lambda: self.part(2 * chip + 1),
            lambda: self.mates.at[chip],
            self.mate,
        )

    def fetch_mate(self, chip):
        self.net.arrive((self.name, "mate", chip), lambda: self.mates.at[chip])
        self.net.local((self.name, "load", chip), self.mates.at[chip], self.load.at[chip])

    def to_chip(self, chip):
        self.net.ready((self.name, "load", chip))
        part = self.part(2 * chip)
        accumulate(part, part, self.load.at[chip])
        self.net.send(
            (self.name, "chip", chip),
            lambda: part,
            lambda: self.landed.at[chip - 1],
            self.away[chip],
        )

    def total(self, out, *more):
        self.fetch_mate(0)
        for chip in (1, 2, 3):
            self.net.arrive((self.name, "chip", chip), lambda: self.landed.at[chip - 1])
            self.net.local((self.name, "last", chip), self.landed.at[chip - 1], self.load.at[chip])
        self.net.ready((self.name, "load", 0))
        for chip in (1, 2, 3):
            self.net.ready((self.name, "last", chip))
        accumulate(out, self.part(0), *(self.load.at[chip] for chip in range(4)), *more)

    def sent(self):
        for chip in range(4):
            self.net.sent((self.name, "mate", chip))
            if chip:
                self.net.sent((self.name, "chip", chip))


def accumulate(out, *terms):
    total, columns = out.shape
    step = 32 if columns < 1024 and total % 32 == 0 else 16

    @pl.loop(0, total // step)
    def _(i):
        here = pl.ds(pl.multiple_of(i * step, step), step)
        value = terms[0][here, :].astype(F32)
        for term in terms[1:]:
            value = value + term[here, :].astype(F32)
        out[here, :] = value.astype(out.dtype)


def clear(out):
    @pl.loop(0, out.shape[0] // 16)
    def _(i):
        here = pl.ds(pl.multiple_of(i * 16, 16), 16)
        out[here, :] = jnp.zeros((16, out.shape[1]), out.dtype)


class LineScatter:
    def __init__(self, net, name, depth, z, block, landed, load):
        self.net, self.name, self.depth, self.z = net, name, depth, z
        self.block, self.landed, self.load = block, landed, load

        steps = range(1, depth)
        up = {s: (depth - s + z, z == 0, jnp.logical_and(z >= 1, z <= s - 1)) for s in steps}
        back = depth - 1 - z
        down = {s: (z + s - depth, back == 0, jnp.logical_and(back >= 1, back <= s - 1)) for s in steps}
        self.ways = (
            ("up", {"z": z + 1}, 0, z >= 1, z < 1, up),
            ("down", {"z": z - 1}, 1, back >= 1, back < 1, down),
        )

    def send(self, key, device, way, s, t, cond):
        self.net.send(
            key,
            lambda: self.block(t),
            lambda: self.landed.at[way, s - 1],
            device,
            cond,
            slot=(self.name, key[1], s),
        )

    def start(self):
        for s in range(1, self.depth):
            for tag, device, way, _, _, steps in self.ways:
                target, first, _ = steps[s]
                self.send((self.name, tag, s), device, way, s, target, first)

    def term(self, way, s):
        return self.landed.at[way, s - 1] if self.load is None else self.load.at[way]

    def take(self, tag, way, s):
        self.net.arrive((self.name, tag, s), lambda: self.landed.at[way, s - 1])
        if self.load is not None:
            pltpu.sync_copy(self.landed.at[way, s - 1], self.load.at[way])

    def step(self, s):
        for tag, device, way, _, _, steps in self.ways:
            t, _, cond = steps[s]

            def body():
                self.take(tag, way, s - 1)
                block = self.block(t)
                accumulate(block, block, self.term(way, s - 1))

            pl.when(cond)(body)
            self.send((self.name, tag, s, "on"), device, way, s, t, cond)

    def finish(self, *outs):
        last = self.depth - 1
        for tag, _, way, fed, unfed, _ in self.ways:
            pl.when(fed)(lambda: self.take(tag, way, last))
            pl.when(unfed)(lambda: clear(self.term(way, last)))
        rows = outs[0].shape[0]
        for i, out in enumerate(outs):
            here = pl.ds(i * rows, rows)
            accumulate(
                out, *(term.at[here, :] for term in (self.block(self.z), self.term(0, last), self.term(1, last)))
            )


class ExpertShare:
    def __init__(self, net, name, coords, result, dst):
        self.net, self.name, self.coords, self.result, self.dst = net, name, coords, result, dst
        x, y, c, _ = coords
        self.expert = 4 * x + 2 * y + c
        self.across = {4: {"x": 1 - x}, 2: {"y": 1 - y}, 1: {"c": 1 - c}}

    def place(self, flip):
        x, y, c, _ = self.coords
        fx = 1 - x if flip & 4 else x
        fy = 1 - y if flip & 2 else y
        fc = 1 - c if flip & 1 else c
        return self.dst.at[4 * fx + 2 * fy + fc]

    def put(self, flip, src, axis):
        self.net.send(
            (self.name, axis | flip), src, lambda: self.place(flip), self.across[axis]
        )

    def wait(self, flip):
        self.net.arrive((self.name, flip), lambda: self.place(flip))

    def start(self):
        x = self.coords[0]
        own = lambda: self.result.at[x]
        self.put(0, lambda: self.result.at[1 - x], 4)
        self.put(0, own, 2)
        self.put(0, own, 1)
        self.net.local((self.name, "own"), own(), self.place(0))

    def pass_x(self):
        self.wait(4)
        self.put(4, lambda: self.place(4), 2)
        self.put(4, lambda: self.place(4), 1)

    def pass_y(self):
        for flip in (2, 6):
            self.wait(flip)
            self.put(flip, lambda: self.place(flip), 1)

    def finish(self):
        self.net.ready((self.name, "own"))
        for flip in (1, 5, 3, 7):
            self.wait(flip)


class AttentionScatter:
    def __init__(self, net, name, depth, coords, grad, mates, chips, lines, dst, mate_load, chip_load, blocks, low):
        self.net, self.name, self.depth, self.coords = net, name, depth, coords
        self.grad, self.mates, self.chips, self.dst = grad, mates, chips, dst
        self.blocks, self.low = blocks, low
        self.columns = columns = grad.shape[1] // 4
        self.rows = grad.shape[0] // (2 * depth)
        self.mate_load, self.chip_load = mate_load.at[:, :columns], chip_load.at[:, :, :, :columns]
        x, y, c, z = coords
        self.away = (
            (1, x, 1 - y, {"y": 1 - y}),
            (2, 1 - x, y, {"x": 1 - x}),
            (3, 1 - x, 1 - y, {"y": 1 - y, "x": 1 - x}),
        )
        self.line = LineScatter(net, name + " line", depth, z, lambda t: blocks.at[t], lines, None)

    def lanes(self, yi, ci):
        return pl.ds(pl.multiple_of((2 * yi + ci) * self.columns, LANES), self.columns)

    def part(self, zi, xi, yi):
        rows = pl.ds(pl.multiple_of((zi * 2 + xi) * self.rows, self.rows), self.rows)
        return self.grad.at[rows, self.lanes(yi, self.coords[2])]

    def to_mate(self, j, yi):
        c = self.coords[2]
        self.net.send(
            (self.name, "c", j),
            lambda: self.grad.at[:, self.lanes(yi, 1 - c)],
            lambda: self.mates.at[j],
            {"c": 1 - c},
        )

    def to_chip(self, chip, zi, xi, yi, device):
        self.net.send(
            (self.name, chip, zi),
            lambda: self.part(zi, xi, yi),
            lambda: self.chips.at[chip - 1, zi],
            device,
        )

    def start(self):
        y = self.coords[1]
        self.to_mate(1, 1 - y)
        self.to_mate(0, y)

    def pass_c(self):
        x, y, c, z = self.coords
        for j, yi in ((1, 1 - y), (0, y)):
            self.net.arrive((self.name, "c", j), lambda: self.mates.at[j])
            pltpu.sync_copy(self.mates.at[j], self.mate_load)
            mine = self.grad.at[:, self.lanes(yi, c)]
            accumulate(mine, mine, self.mate_load)
            for chip, xi, yj, device in self.away:
                if (chip in (1, 3)) == (j == 1):
                    for zi in range(self.depth):
                        self.to_chip(chip, zi, xi, yj, device)

    def pass_chips(self):
        x, y, c, z = self.coords
        for chip, _, _, _ in self.away:
            for zi in range(self.depth):
                self.net.arrive((self.name, chip, zi), lambda: self.chips.at[chip - 1, zi])
            self.net.local(
                (self.name, "load", chip), self.chips.at[chip - 1], self.chip_load.at[chip - 1]
            )
        for chip, _, _, _ in self.away:
            self.net.ready((self.name, "load", chip))
        for zi in range(self.depth):
            accumulate(
                self.blocks.at[zi],
                self.part(zi, x, y),
                *(self.chip_load.at[chip, zi] for chip in range(3)),
            )
        self.line.start()

    def total(self):
        x, y, c, z = self.coords
        self.line.finish(self.low)
        mine = 2 * y + c
        self.net.local((self.name, "own"), self.low, self.dst.at[mine])
        for key, device in (("ty", {"y": 1 - y}), ("tc", {"c": 1 - c})):
            self.net.send(
                (self.name, key), lambda: self.low, lambda: self.dst.at[mine], device
            )

    def pass_y(self):
        x, y, c, z = self.coords
        there = 2 * (1 - y) + c
        self.net.arrive((self.name, "ty"), lambda: self.dst.at[there])
        self.net.send(
            (self.name, "tyc"), lambda: self.dst.at[there], lambda: self.dst.at[there], {"c": 1 - c}
        )

    def finish(self):
        x, y, c, z = self.coords
        self.net.ready((self.name, "own"))
        self.net.arrive((self.name, "tc"), lambda: self.dst.at[2 * y + 1 - c])
        self.net.arrive((self.name, "tyc"), lambda: self.dst.at[2 * (1 - y) + 1 - c])


def norm_back(values, gain, upstream):
    inverse = inverse_rms(values)
    normal = values * inverse
    gain_grad = jnp.sum(upstream * normal, axis=0, keepdims=True)
    scaled = upstream * gain
    return (
        inverse * (scaled - normal * jnp.mean(scaled * normal, axis=-1, keepdims=True)),
        gain_grad,
    )


def backward_kernel(depth, *refs):
    (
        hidden, grad_out, cosine, sine, gain_rows, queries, keys, values, attended, mixed,
        probability, rows_in, grads_in, shares_in, gate_in, up_in, down_in, wq_in, wo_in,
        layer_out, grad_in, gain_total,
        gate_total, up_total, down_total, wq_total, wo_total,
        row_mates, row_chips, out_mates, out_chips,
        gate_lines, up_lines, down_lines, wq_mates, wq_chips, wo_mates, wo_chips,
        rows, grads, wide, down_grad, returned, wide_load, down_load, wide_low, down_low,
        mate_load, chip_load, wq_lines, wo_lines, wq_blocks, wo_blocks, wq_low, wo_low, gain_swap,
        send_sems, recv_sems, local_sems,
    ) = refs
    coords = x, y, c, z = tuple(lax.axis_index(n) for n in ("x", "y", "c", "z"))
    expert = 4 * x + 2 * y + c
    net = Net(send_sems, recv_sems, local_sems, c)
    length, width = hidden.shape
    hidden_units = gate_in.shape[1]
    greet(depth, coords)

    def line(name, block, landed, load):
        return LineScatter(net, name, depth, z, block, landed, load)

    def wide_block(first):
        size = 2 * (width // (2 * depth))
        return lambda t: wide.at[
            pl.ds(pl.multiple_of(t * size, size), size), pl.ds(first, hidden_units)
        ]

    def down_block(t):
        size = 2 * (hidden_units // (2 * depth))
        return down_grad.at[pl.ds(pl.multiple_of(t * size, size), size), :]

    gate_line = line("gate", wide_block(0), gate_lines, wide_load)
    up_line = line("up", wide_block(hidden_units), up_lines, wide_load)
    down_line = line("down", down_block, down_lines, down_load)
    row_back = SlabReturn(net, "rows", coords, grads, length, row_mates, row_chips, returned)
    out_back = SlabReturn(net, "outs", coords, rows, length, out_mates, out_chips, returned)

    def shared_out(name, line, low, dst):
        def go():
            line.finish(low.at[0], low.at[1])
            share = ExpertShare(net, name + " share", coords, low, dst)
            share.start()
            return share

        return go

    down_done = shared_out("down", down_line, down_low, down_total)
    gate_done = shared_out("gate", gate_line, wide_low.at[0], gate_total)
    up_done = shared_out("up", up_line, wide_low.at[1], up_total)
    tile = 256

    def experts(down, hidden_act, both_grads, shares):
        net.local("rows", rows_in, rows)
        net.local("gate", gate_in, wide.at[:, :hidden_units])
        net.local("up", up_in, wide.at[:, hidden_units:])
        net.local("shares", shares_in, shares)
        net.local("grads", grads_in, grads)
        net.local("down", down_in, down)
        for name in ("rows", "gate", "up", "shares", "grads", "down"):
            net.ready(name)
        lane = lax.broadcasted_iota(jnp.int32, (length, LANES), 1)

        def share_of(r):
            return jnp.sum(jnp.where(lane == expert, shares[r], 0.0), axis=1, keepdims=True)

        @pl.loop(0, EXPERTS)
        def _(r):
            here = pl.ds(pl.multiple_of(r * length, length), length)
            grads[here, :] = (share_of(r) * grads[here, :].astype(F32)).astype(BF16)
            for j in range(0, hidden_units, tile):
                gate = dot_nn(rows[here, :], wide[:, j : j + tile])
                up = dot_nn(rows[here, :], wide[:, hidden_units + j : hidden_units + j + tile])
                back = dot_nt(grads[here, :], down[j : j + tile, :])
                sigmoid = 1.0 / (1.0 + jnp.exp(-gate))
                silu = gate * sigmoid
                hidden_act[here, j : j + tile] = (silu * up).astype(BF16)
                both_grads[here, j : j + tile] = (
                    back * up * sigmoid * (1.0 + gate * (1.0 - sigmoid))
                ).astype(BF16)
                both_grads[here, hidden_units + j : hidden_units + j + tile] = (
                    back * silu
                ).astype(BF16)

        @pl.loop(0, hidden_units // tile)
        def _(i):
            at = pl.ds(pl.multiple_of(i * tile, tile), tile)
            for j in range(0, width, 512):
                down_grad[at, j : j + 512] = dot_tn(hidden_act[:, at], grads[:, j : j + 512]).astype(BF16)

        down_line.start()

        def row_grad(slot):
            here = slice(slot * length, (slot + 1) * length)
            for j in range(0, width, 512):
                grads[here, j : j + 512] = dot_nt(both_grads[here, :], wide[j : j + 512, :]).astype(BF16)

        for chip in (1, 2, 3, 0):
            row_grad(2 * chip + 1)
            row_back.to_mate(chip)
        for chip in (1, 2, 3):
            row_grad(2 * chip)
            row_back.fetch_mate(chip)
            row_back.to_chip(chip)
        row_grad(0)

        @pl.loop(0, width // tile)
        def _(i):
            at = pl.ds(pl.multiple_of(i * tile, tile), tile)
            for j in range(0, 2 * hidden_units, 512):
                wide[at, j : j + 512] = dot_tn(rows[:, at], both_grads[:, j : j + 512]).astype(BF16)

        gate_line.start()
        up_line.start()
        for s in range(2, depth):
            down_line.step(s)

        def out_rows(slot):
            here = slice(slot * length, (slot + 1) * length)
            share = share_of(slot)
            for j in range(0, width, 512):
                rows[here, j : j + 512] = (
                    share * dot_nn(hidden_act[here, :], down[:, j : j + 512])
                ).astype(BF16)

        for chip in (1, 2, 3, 0):
            out_rows(2 * chip + 1)
            out_back.to_mate(chip)
        for chip in (1, 2, 3):
            out_rows(2 * chip)
            out_back.fetch_mate(chip)
            out_back.to_chip(chip)
        out_rows(0)

    pl.run_scoped(
        experts,
        pltpu.VMEM((hidden_units, width), BF16),
        pltpu.VMEM((EXPERTS * length, hidden_units), BF16),
        pltpu.VMEM((EXPERTS * length, 2 * hidden_units), BF16),
        pltpu.VMEM((EXPERTS, length, LANES), F32),
    )

    def attention(weight, chances, wq_grad, upstream_two, mixed_grad, mixed_low, attended_grad, qkv_grad):
        net.local("wo here", wo_in, weight.at[:, :width])
        net.local("chance 0", probability.at[: GROUP * length], chances)
        row_back.total(upstream_two)
        gain_swap[0] = jnp.zeros(gain_swap.shape[1:], F32)
        step = 16

        @pl.loop(0, length // step)
        def _(i):
            here = pl.ds(pl.multiple_of(i * step, step), step)
            part, gain_two = norm_back(mixed[here, :], gain_rows[1:2, :], upstream_two[here, :])
            total = grad_out[here, :].astype(F32) + part
            mixed_grad[here, :] = total
            mixed_low[here, :] = total.astype(BF16)
            gain_swap[0, 1:2, :] += gain_two

        row_back.sent()
        for i in range(0, width, tile):
            for j in range(0, width, 512):
                grads[i : i + tile, j : j + 512] = dot_tn(
                    attended[:, i : i + tile], mixed_low[:, j : j + 512]
                ).astype(BF16)
        wo_net = AttentionScatter(
            net, "wo", depth, coords, grads.at[:width, :], wo_mates, wo_chips, wo_lines, wo_total,
            mate_load, chip_load, wo_blocks, wo_low,
        )
        wo_net.start()
        net.ready("wo here")
        for i in range(0, width, 512):
            attended_grad[:, i : i + 512] = dot_nt(
                mixed_low[...], weight[i : i + 512, :width]
            ).astype(BF16)
        net.local("wq here", wq_in, weight)
        down_share = down_done()
        wo_net.pass_c()
        for s in range(2, depth):
            gate_line.step(s)
        cos, sin = cosine[...], -sine[...]
        factor = HEAD_DIM ** (-0.5)
        for kv in range(KV_HEADS):
            net.ready("chance %d" % kv)
            there = slice(kv * length, (kv + 1) * length)
            value_sum = key_sum = None
            for g in range(GROUP):
                head = kv * GROUP + g
                here = slice(head * length, (head + 1) * length)
                cols = slice(head * HEAD_DIM, (head + 1) * HEAD_DIM)
                chance = chances[g * length : (g + 1) * length, :]
                back = attended_grad[:, cols]
                prob_grad = dot_nt(back, values[there, :])
                value_part = dot_tn(chance.astype(BF16), back)
                inner = jnp.sum(chance * prob_grad, axis=-1, keepdims=True)
                score_grad = (chance * (prob_grad - inner)).astype(BF16)
                query_grad = dot_nn(score_grad, keys[there, :]) * factor
                key_part = dot_tn(score_grad, queries[here, :])
                qkv_grad[:, cols] = turn(query_grad, cos, sin).astype(BF16)
                value_sum = value_part if value_sum is None else value_sum + value_part
                key_sum = key_part if key_sum is None else key_sum + key_part
            if kv + 1 < KV_HEADS:
                size = GROUP * length
                net.local("chance %d" % (kv + 1), probability.at[(kv + 1) * size : (kv + 2) * size], chances)
            first = (HEADS + kv) * HEAD_DIM
            qkv_grad[:, first : first + HEAD_DIM] = turn(key_sum * factor, cos, sin).astype(BF16)
            first = first + KV_HEADS * HEAD_DIM
            qkv_grad[:, first : first + HEAD_DIM] = value_sum.astype(BF16)
        down_share.pass_x()
        @pl.loop(0, length // step)
        def _(i):
            here = pl.ds(pl.multiple_of(i * step, step), step)
            one = hidden[here, :].astype(F32)
            mixed_low[here, :] = (one * inverse_rms(one) * gain_rows[0:1, :]).astype(BF16)

        for i in range(0, width, tile):
            for j in range(0, wq_grad.shape[1], 512):
                wq_grad[i : i + tile, j : j + 512] = dot_tn(
                    mixed_low[:, i : i + tile], qkv_grad[:, j : j + 512]
                ).astype(BF16)
        wq_net = AttentionScatter(
            net, "wq", depth, coords, wq_grad, wq_mates, wq_chips, wq_lines, wq_total,
            mate_load, chip_load, wq_blocks, wq_low,
        )
        wq_net.start()
        net.ready("wq here")
        for i in range(0, width, 512):
            upstream_two[:, i : i + 512] = dot_nt(qkv_grad[...], weight[i : i + 512, :])

        @pl.loop(0, length // step)
        def _(i):
            here = pl.ds(pl.multiple_of(i * step, step), step)
            part, gain_one = norm_back(
                hidden[here, :].astype(F32), gain_rows[0:1, :], upstream_two[here, :]
            )
            grad_in[here, :] = (mixed_grad[here, :] + part).astype(BF16)
            gain_swap[0, 0:1, :] += gain_one

        wq_net.pass_c()
        wo_net.pass_chips()
        for i, (axis, device) in enumerate(
            (("c", {"c": 1 - c}), ("x", {"x": 1 - x}), ("y", {"y": 1 - y}))
        ):
            source, target = gain_swap.at[2 * i], gain_swap.at[2 * i + 1]
            gain_send(("gain", axis), source, target, device)
            net.arrive(("gain", axis), lambda: target)
            gain_swap[2 * i + 2] = gain_swap[2 * i] + gain_swap[2 * i + 1]
        for far in range(1, depth):
            gain_send(("gain", "up", far), gain_swap.at[6], gain_swap.at[5 + 2 * far], {"z": z + far}, z + far < depth)
            gain_send(("gain", "down", far), gain_swap.at[6], gain_swap.at[6 + 2 * far], {"z": z - far}, z - far >= 0)
        for s in range(2, depth):
            up_line.step(s)
        for s in range(2, depth):
            wo_net.line.step(s)
        out_back.total(layer_out, mixed)
        wq_net.pass_chips()
        gate_share = gate_done()
        down_share.pass_y()
        wo_net.total()
        for s in range(2, depth):
            wq_net.line.step(s)
        up_share = up_done()
        gate_share.pass_x()
        wo_net.pass_y()
        gain_total[...] = gain_swap[6]
        for far in range(1, depth):
            for tag, slot, cond in (
                ("up", 5 + 2 * far, z - far >= 0), ("down", 6 + 2 * far, z + far < depth)
            ):

                def take():
                    net.arrive(("gain", tag, far), lambda: gain_swap.at[slot])
                    gain_total[...] += gain_swap[slot]

                pl.when(cond)(take)
        wq_net.total()
        up_share.pass_x()
        gate_share.pass_y()
        wq_net.pass_y()
        up_share.pass_y()
        for one in (down_share, gate_share, up_share, wo_net, wq_net):
            one.finish()
        net.drain()

    def gain_send(key, source, target, device, cond=None):
        net.send(key, lambda: source, lambda: target, device, cond)

    pl.run_scoped(
        attention,
        pltpu.VMEM(wq_in.shape, BF16),
        pltpu.VMEM((GROUP * length, length), F32),
        pltpu.VMEM(wq_in.shape, BF16),
        pltpu.VMEM((length, width), F32),
        pltpu.VMEM((length, width), F32),
        pltpu.VMEM((length, width), BF16),
        pltpu.VMEM((length, width), BF16),
        pltpu.VMEM((length, wq_in.shape[1]), BF16),
    )
    assert net.count <= send_sems.shape[0] and len(net.slots) <= recv_sems.shape[0]
    assert len(net.locals) <= local_sems.shape[0]


def backward_call(depth, shard_rows, *args):
    hidden, wq_in, gate_in, down_in = args[0], args[17], args[14], args[16]
    length, width = hidden.shape
    wide, units = wq_in.shape[1], gate_in.shape[1]
    shards, down_rows = 2 * depth, units // (2 * depth)
    here, there = pl.BlockSpec(memory_space=pltpu.VMEM), pl.BlockSpec(memory_space=pltpu.HBM)

    def shape(*dims, dtype=BF16):
        return jax.ShapeDtypeStruct(dims, dtype)

    out_shape = [
        shape(length, width), shape(length, width), shape(8, width, dtype=F32),
        shape(EXPERTS, shard_rows, units), shape(EXPERTS, shard_rows, units),
        shape(EXPERTS, down_rows, width),
        shape(4, shard_rows, wide // 4), shape(4, shard_rows, width // 4),
        shape(4, length, width), shape(3, length, width),
        shape(4, length, width), shape(3, length, width),
        shape(2, depth - 1, 2 * shard_rows, units), shape(2, depth - 1, 2 * shard_rows, units),
        shape(2, depth - 1, 2 * down_rows, width),
        shape(2, width, wide // 4), shape(3, depth, shard_rows, wide // 4),
        shape(2, width, width // 4), shape(3, depth, shard_rows, width // 4),
    ]
    sends = 60 * depth + 160
    return pl.pallas_call(
        functools.partial(backward_kernel, depth),
        out_shape=out_shape,
        in_specs=[here] * 10 + [there] * 9,
        out_specs=[here] * 3 + [there] * 16,
        scratch_shapes=[
            pltpu.VMEM((EXPERTS * length, width), BF16),
            pltpu.VMEM((EXPERTS * length, width), BF16),
            pltpu.VMEM((width, 2 * units), BF16),
            pltpu.VMEM((units, width), BF16),
            pltpu.VMEM((4, length, width), BF16),
            pltpu.VMEM((2, 2 * shard_rows, units), BF16),
            pltpu.VMEM((2, 2 * down_rows, width), BF16),
            pltpu.VMEM((2, 2, shard_rows, units), BF16),
            pltpu.VMEM((2, down_rows, width), BF16),
            pltpu.VMEM((width, wide // 4), BF16),
            pltpu.VMEM((3, depth, shard_rows, wide // 4), BF16),
            pltpu.VMEM((2, depth - 1, shard_rows, wide // 4), BF16),
            pltpu.VMEM((2, depth - 1, shard_rows, width // 4), BF16),
            pltpu.VMEM((depth, shard_rows, wide // 4), BF16),
            pltpu.VMEM((depth, shard_rows, width // 4), BF16),
            pltpu.VMEM((shard_rows, wide // 4), BF16),
            pltpu.VMEM((shard_rows, width // 4), BF16),
            pltpu.VMEM((5 + 2 * depth, 8, width), F32),
            pltpu.SemaphoreType.DMA((sends,)),
            pltpu.SemaphoreType.DMA((sends,)),
            pltpu.SemaphoreType.DMA((64,)),
        ],
        compiler_params=pltpu.CompilerParams(
            collective_id=2, has_side_effects=True, vmem_limit_bytes=VMEM_LIMIT
        ),
    )(*args)


def rotary_tables(length, head_width):
    half_width = head_width // 2
    frequency = rotary_base ** (-2.0 * jnp.arange(half_width, dtype=jnp.float32) / head_width)
    angles = jnp.arange(length, dtype=jnp.float32)[:, None] * frequency[None, :]
    cosine, sine = jnp.cos(angles), jnp.sin(angles)
    return (
        jnp.concatenate([cosine, cosine], axis=1),
        jnp.concatenate([-sine, sine], axis=1),
    )


def make_shards(sizes):
    depth = sizes["z"]

    def shards(
        hidden_in,
        segments,
        routes,
        gate_weights,
        grad_out,
        attn_gain,
        query_weight,
        key_weight,
        value_weight,
        output_weight,
        ffn_gain,
        gate_weight,
        up_weight,
        down_weight,
    ):
        length, width = hidden_in.shape
        gains = jnp.stack([attn_gain, ffn_gain]).astype(F32)
        shard_rows = gains.shape[1]
        lanes = -(-shard_rows // LANES) * LANES
        gains = jnp.pad(gains, ((0, 6), (0, lanes - shard_rows)))
        wq_in = jnp.concatenate([query_weight, key_weight, value_weight], axis=1)
        onehot = routes[:, :, None] == jnp.arange(LANES, dtype=jnp.int32)
        shares = jnp.sum(jnp.where(onehot, gate_weights[:, :, None], 0.0), axis=1)
        segment = segments[0]
        position = jnp.arange(length, dtype=jnp.int32)
        allowed = (position[:, None] >= position[None, :]) & (segment[:, None] == segment[None, :])
        cosine, sine = rotary_tables(length, HEAD_DIM)
        (
            wq, wo, _, gate, up, down, rows, grads, shares,
            queries, keys, values, probability, attended, mixed, gain_rows,
        ) = forward_call(
            depth, shard_rows, hidden_in, allowed.astype(F32), cosine, sine, gains,
            wq_in, output_weight, gate_weight, up_weight, down_weight, grad_out, shares,
        )
        layer_out, grad_in, gain_total, gate_total, up_total, down_total, wq_total, wo_total = (
            backward_call(
                depth, shard_rows, hidden_in, grad_out, cosine, sine, gain_rows, queries, keys,
                values, attended, mixed, probability,
                rows.reshape(-1, width), grads.reshape(-1, width), shares,
                gate, up, down, wq, wo,
            )[:8]
        )
        z, x = lax.axis_index("z"), lax.axis_index("x")
        gain_total = lax.dynamic_slice_in_dim(gain_total, (z * 2 + x) * shard_rows, shard_rows, 1)

        def whole(value):
            value = value.astype(F32)
            return lax.psum(value, "o") if sizes["o"] > 1 else value

        def side_by_side(value):
            return value.transpose(1, 0, 2).reshape(shard_rows, -1)

        wq_total, wo_total = side_by_side(whole(wq_total)), side_by_side(whole(wo_total))
        queries_end = HEADS * HEAD_DIM
        keys_end = queries_end + KV_HEADS * HEAD_DIM
        gain_total = whole(gain_total)
        return (
            layer_out,
            grad_in,
            gain_total[0],
            wq_total[:, :queries_end],
            wq_total[:, queries_end:keys_end],
            wq_total[:, keys_end:],
            wo_total,
            gain_total[1],
            whole(gate_total),
            whole(up_total),
            whole(down_total),
        )

    return shards


def solution(mesh):
    reps, shard_count = mesh.shape["rep"], mesh.shape["shard"]
    sizes = {"o": reps // 4, "y": 2, "c": 2, "z": shard_count // 2, "x": 2}
    fine = Mesh(mesh.devices.reshape(tuple(sizes.values())), tuple(sizes))
    tokens = P(("o", "y", "c", "z", "x"), None)
    first, second = P(("z", "x")), P(None, ("z", "x"), None)
    matrix = P(("z", "x"), None)
    return jax.shard_map(
        make_shards(sizes),
        mesh=fine,
        in_specs=(
            (tokens,) * 5 + (first, matrix, matrix, matrix, matrix, first) + (second,) * 3
        ),
        out_specs=(
            (tokens,) * 2 + (first, matrix, matrix, matrix, matrix, first) + (second,) * 3
        ),
        check_vma=False,
    )
```

```python
import functools

import jax
import jax.numpy as jnp
from jax import lax
from jax.experimental import pallas as pl
from jax.experimental.pallas import tpu as pltpu
from jax.sharding import Mesh
from jax.sharding import PartitionSpec as P

HEADS = 12
KV_HEADS = 2
GROUP = HEADS // KV_HEADS
HEAD_DIM = 128
EXPERTS = 8
LANES = 128

epsilon = 1e-06
rotary_base = 1000000.0
masked_score = -1e30

F32 = jnp.float32
BF16 = jnp.bfloat16
MESH = pl.DeviceIdType.MESH
VMEM_LIMIT = 62 * 2**20


def dot(a, b, dims):
    return lax.dot_general(a, b, (dims, ((), ())), preferred_element_type=F32)


def dot_nn(a, b):
    return dot(a, b, ((1,), (0,)))


def dot_nt(a, b):
    return dot(a, b, ((1,), (1,)))


def dot_tn(a, b):
    return dot(a, b, ((0,), (0,)))


def guarded(cond, body):
    if cond is None:
        body()
    else:
        pl.when(cond)(body)


def both(first, second):
    if first is None:
        return second
    if second is None:
        return first
    return jnp.logical_and(first, second)


class Net:
    def __init__(self, send_sems, recv_sems, local_sems, core):
        self.send_sems, self.recv_sems, self.local_sems = send_sems, recv_sems, local_sems
        self.away = {"c": 1 - core}
        self.slots, self.sends, self.locals, self.count, self.done = {}, {}, {}, 0, set()

    def slot(self, key):
        return self.slots.setdefault(key, len(self.slots))

    def send(self, key, src, dst, device, cond=None, slot=None):
        recv, index = self.slot(slot or key), self.count
        self.count += 1

        def build():
            return pltpu.make_async_remote_copy(
                src_ref=src(),
                dst_ref=dst(),
                send_sem=self.send_sems.at[index],
                recv_sem=self.recv_sems.at[recv],
                device_id=device,
                device_id_type=MESH,
            )

        guarded(cond, lambda: build().start())
        self.sends[key] = (cond, build)

    def sent(self, key):
        cond, build = self.sends.pop(key)
        guarded(cond, lambda: build().wait_send())

    def arrive(self, key, dst, cond=None):
        recv = self.slot(key)

        def wait():
            pltpu.make_async_remote_copy(
                src_ref=dst(),
                dst_ref=dst(),
                send_sem=self.send_sems.at[0],
                recv_sem=self.recv_sems.at[recv],
                device_id=self.away,
                device_id_type=MESH,
            ).wait_recv()

        guarded(cond, wait)

    def local(self, key, src, dst):
        index = len(self.locals)
        copy = pltpu.make_async_copy(src, dst, self.local_sems.at[index])
        copy.start()
        self.locals[key] = copy

    def ready(self, key):
        if key not in self.done:
            self.done.add(key)
            self.locals[key].wait()

    def drain(self):
        for key in list(self.sends):
            self.sent(key)
        for key in self.locals:
            self.ready(key)


def greet(depth, coords):
    x, y, c, z = coords
    barrier = pltpu.get_barrier_semaphore()
    for device in ({"y": 1 - y}, {"y": 1 - y, "x": 1 - x}, {"c": 1 - c}):
        pl.semaphore_signal(barrier, inc=1, device_id=device, device_id_type=MESH)
    for zi in range(depth):
        for xi in range(2):

            def tell(zi=zi, xi=xi):
                pl.semaphore_signal(
                    barrier,
                    inc=1,
                    device_id={"z": jnp.int32(zi), "x": jnp.int32(xi)},
                    device_id_type=MESH,
                )

            pl.when(jnp.logical_or(z != zi, x != xi))(tell)
    pl.semaphore_wait(barrier, 3 + 2 * depth - 1)


def along(depth, z):
    return (
        ("up", {"z": z + 1}, z + 1 < depth, lambda k: z - k, lambda k: z - k >= 0),
        ("down", {"z": z - 1}, z > 0, lambda k: z + k, lambda k: z + k < depth),
    )


class SlabGather:
    def __init__(self, net, name, coords, dst, length):
        self.net, self.name, self.dst, self.length = net, name, dst, length
        x, y, c, _ = coords
        self.to_x, self.to_y, self.to_mate = {"x": 1 - x}, {"y": 1 - y}, {"c": 1 - c}

    def slot(self, slot, half=None):
        first, size = slot * self.length, self.length
        if half is not None:
            size = size // 2
            first = first + half * size
        return self.dst.at[first : first + size, :]

    def put(self, slot, src, device, half=None):
        self.net.send(
            (self.name, slot, half), lambda: src, lambda: self.slot(slot, half), device
        )

    def wait(self, slot, half=None):
        self.net.arrive((self.name, slot, half), lambda: self.slot(slot, half))

    def start(self, src):
        self.put(2, src, self.to_y)
        self.put(4, src, self.to_x)
        self.put(1, src, self.to_mate)

    def forward(self):
        self.wait(2)
        self.put(6, self.slot(2, 0), self.to_x, 0)
        self.put(3, self.slot(2), self.to_mate)
        self.wait(4)
        self.put(6, self.slot(4, 1), self.to_y, 1)
        self.put(5, self.slot(4), self.to_mate)

    def forward_far(self):
        for half in range(2):
            self.wait(6, half)
            self.put(7, self.slot(6, half), self.to_mate, half)

    def sent(self):
        for slot, half in ((2, None), (4, None), (1, None), (6, 0), (6, 1), (3, None), (5, None), (7, 0), (7, 1)):
            self.net.sent((self.name, slot, half))


class AttentionGather:
    def __init__(self, net, name, depth, coords, src, dst):
        self.net, self.name, self.depth, self.src, self.dst = net, name, depth, src, dst
        self.x, self.y, self.c, self.z = x, y, c, z = coords
        self.nx, self.ny, self.nc = 1 - x, 1 - y, 1 - c
        self.rows, self.columns = src.shape[0], src.shape[1] // 4
        self.to_x, self.to_y, self.to_mate = {"x": self.nx}, {"y": self.ny}, {"c": self.nc}
        self.ways = [
            (tag, device, more, {k: (origin(k), there(k), both(there(k), more)) for k in range(1, depth)})
            for tag, device, more, origin, there in along(depth, z)
        ]

    def lanes(self, yi, ci):
        return pl.ds(pl.multiple_of((2 * yi + ci) * self.columns, LANES), self.columns)

    def block(self, zi, xi, yi, ci):
        return lambda: self.dst.at[
            pl.ds(pl.multiple_of((zi * 2 + xi) * self.rows, self.rows), self.rows), self.lanes(yi, ci)
        ]

    def put(self, key, place, device, cond=None, src=None):
        block = self.block(*place)
        self.net.send((self.name,) + key, src or block, block, device, cond)

    def wait(self, key, place, cond=None):
        self.net.arrive((self.name,) + key, self.block(*place), cond)

    def start(self):
        x, y, c, z = self.x, self.y, self.c, self.z
        own = lambda: self.src.at[:, self.lanes(y, c)]
        cross = lambda: self.src.at[:, self.lanes(self.ny, c)]
        for tag, device, more, _ in self.ways:
            self.put(("z", tag, 1), (z, x, y, c), device, more, own)
        rows = pl.ds(pl.multiple_of((z * 2 + x) * self.rows, self.rows), self.rows)
        self.net.local((self.name, "own"), self.src, self.dst.at[rows, :])
        self.put(("x", "same"), (z, x, y, c), self.to_x, None, own)
        self.put(("x", "cross"), (z, x, self.ny, c), self.to_x, None, cross)

    def pass_z(self, k):
        for tag, device, _, steps in self.ways:
            origin, cond, on = steps[k]
            place = (origin, self.x, self.y, self.c)
            self.wait(("z", tag, k), place, cond)
            if k + 1 < self.depth:
                self.put(("z", tag, k + 1), place, device, on)
            self.put(("x", tag, k), place, self.to_x, cond)
            self.put(("y", tag, k, 0), place, self.to_y, cond)
            self.put(("c", tag, k, 0), place, self.to_mate, cond)

    def pass_x(self, k):
        if k == 0:
            for tag, yi in (("same", self.y), ("cross", self.ny)):
                place = (self.z, self.nx, yi, self.c)
                self.wait(("x", tag), place)
                self.put(("c", tag), place, self.to_mate)
            return
        for tag, _, _, steps in self.ways:
            origin, cond, _ = steps[k]
            place = (origin, self.nx, self.y, self.c)
            self.wait(("x", tag, k), place, cond)
            self.put(("y", tag, k, 1), place, self.to_y, cond)
            self.put(("c", tag, k, 1), place, self.to_mate, cond)

    def pass_y(self, k):
        for tag, _, _, steps in self.ways:
            origin, cond, _ = steps[k]
            for j, xi in ((0, self.x), (1, self.nx)):
                place = (origin, xi, self.ny, self.c)
                self.wait(("y", tag, k, j), place, cond)
                self.put(("c", tag, k, 2 + j), place, self.to_mate, cond)

    def finish(self):
        self.net.ready((self.name, "own"))
        for tag, yi in (("same", self.y), ("cross", self.ny)):
            self.wait(("c", tag), (self.z, self.nx, yi, self.nc))
        for k in range(1, self.depth):
            for tag, _, _, steps in self.ways:
                origin, cond, _ = steps[k]
                for j, (xi, yi) in enumerate(
                    ((self.x, self.y), (self.nx, self.y), (self.x, self.ny), (self.nx, self.ny))
                ):
                    self.wait(("c", tag, k, j), (origin, xi, yi, self.nc), cond)


class ExpertGather:
    def __init__(self, net, name, depth, coords, src, dst):
        self.net, self.name, self.depth, self.coords, self.src, self.dst = (
            net, name, depth, coords, src, dst,
        )
        self.rows = src.shape[1]
        x, y, c, z = coords
        self.own, self.away = 4 * x + 2 * y + c, 4 * (1 - x) + 2 * y + c
        self.xs = (x, 1 - x)
        self.to_x = {"x": self.xs[1]}
        self.ways = [
            (tag, device, more, {
                k: (origin(k), there(k), both(there(k), more), both(there(k), jnp.logical_not(more)))
                for k in range(1, depth)
            })
            for tag, device, more, origin, there in along(depth, z)
        ]

    def block(self, zi, xi):
        return lambda: self.dst.at[
            pl.ds(pl.multiple_of((zi * 2 + xi) * self.rows, self.rows), self.rows), :
        ]

    def put(self, key, place, device, cond=None, src=None):
        block = self.block(*place)
        self.net.send((self.name,) + key, src or block, block, device, cond)

    def start(self):
        x, _, _, z = self.coords
        for tag, device, more, _ in self.ways:
            self.put(("z", tag, 1, 0), (z, x), device, more, lambda: self.src.at[self.own])
        self.net.local((self.name, "own"), self.src.at[self.own], self.block(z, x)())

    def start_x(self):
        x, _, _, z = self.coords
        self.put(("x",), (z, x), self.to_x, None, lambda: self.src.at[self.away])

    def pass_x(self):
        x, _, _, z = self.coords
        self.net.arrive((self.name, "x"), self.block(z, self.xs[1]))
        for tag, device, more, _ in self.ways:
            self.put(("z", tag, 1, 1), (z, self.xs[1]), device, more)

    def pass_z(self, k, j):
        if k + 1 >= self.depth:
            return
        for tag, device, _, steps in self.ways:
            origin, _, on, _ = steps[k]
            place = (origin, self.xs[j])
            self.net.arrive((self.name, "z", tag, k, j), self.block(*place), on)
            self.put(("z", tag, k + 1, j), place, device, on)

    def finish(self):
        self.net.ready((self.name, "own"))
        for k in range(1, self.depth):
            for j in range(2):
                for tag, _, _, steps in self.ways:
                    origin, there, _, last = steps[k]
                    cond = there if k + 1 >= self.depth else last
                    self.net.arrive(
                        (self.name, "z", tag, k, j), self.block(origin, self.xs[j]), cond
                    )

    def sent(self):
        self.net.sent((self.name, "x"))
        for k in range(1, self.depth):
            for j in range(2):
                for tag, _, _, _ in self.ways:
                    self.net.sent((self.name, "z", tag, k, j))


def inverse_rms(values):
    return lax.rsqrt(jnp.mean(values * values, axis=-1, keepdims=True) + epsilon)


def turn(values, cosine, sine):
    return values * cosine + pltpu.roll(values, HEAD_DIM // 2, axis=1) * sine


class SlabReturn:
    def __init__(self, net, name, coords, parts, length, mates, fars, chips, load):
        self.net, self.name, self.parts, self.length = net, name, parts, length
        self.mates, self.fars, self.landed, self.load = mates, fars, chips, load
        x, y, c, _ = coords
        self.to_x, self.to_y, self.to_core = {"x": 1 - x}, {"y": 1 - y}, {"c": 1 - c}

    def part(self, slot, half=None):
        first, size = slot * self.length, self.length
        if half is not None:
            size = size // 2
            first = first + half * size
        return self.parts.at[first : first + size, :]

    def half(self, half):
        return pl.ds(half * (self.length // 2), self.length // 2)

    def to_mate(self, chip):
        self.net.send(
            (self.name, "mate", chip),
            lambda: self.part(2 * chip + 1),
            lambda: self.mates.at[chip],
            self.to_core,
        )

    def fetch(self, chip):
        self.net.arrive((self.name, "mate", chip), lambda: self.mates.at[chip])
        self.net.local((self.name, "load", chip), self.mates.at[chip], self.load.at[chip])

    def add(self, chip):
        self.net.ready((self.name, "load", chip))
        part = self.part(2 * chip)
        accumulate(part, part, self.load.at[chip])

    def far(self):
        for half, device in ((0, self.to_x), (1, self.to_y)):
            self.net.send(
                (self.name, "far", half),
                lambda: self.part(6, half),
                lambda: self.fars.at[half],
                device,
            )

    def near(self, chip, half, device):
        self.net.send(
            (self.name, "chip", chip, half),
            lambda: self.part(2 * chip, half),
            lambda: self.landed.at[chip - 1, self.half(half)],
            device,
        )

    def plain(self, chip):
        self.near(chip, *((1, self.to_y) if chip == 1 else (0, self.to_x)))

    def combined(self):
        for half, chip, device in ((0, 1, self.to_y), (1, 2, self.to_x)):
            self.net.arrive((self.name, "far", half), lambda: self.fars.at[half])
            self.net.local((self.name, "far", half), self.fars.at[half], self.load.at[3, self.half(half)])
            self.net.ready((self.name, "far", half))
            part = self.part(2 * chip, half)
            accumulate(part, part, self.load.at[3, self.half(half)])
            self.near(chip, half, device)

    def total(self, out, *more):
        for chip in (1, 2):
            for half in range(2):
                self.net.arrive(
                    (self.name, "chip", chip, half), lambda: self.landed.at[chip - 1, self.half(half)]
                )
            self.net.local((self.name, "last", chip), self.landed.at[chip - 1], self.load.at[chip])
        for chip in (1, 2):
            self.net.ready((self.name, "last", chip))
        accumulate(out, self.part(0), self.load.at[1], self.load.at[2], *more)

    def sent(self):
        for chip in range(4):
            self.net.sent((self.name, "mate", chip))
        for half in range(2):
            self.net.sent((self.name, "far", half))
            for chip in (1, 2):
                self.net.sent((self.name, "chip", chip, half))


def accumulate(out, *terms):
    total, columns = out.shape
    step = 32 if columns < 1024 and total % 32 == 0 else 16

    @pl.loop(0, total // step)
    def _(i):
        here = pl.ds(pl.multiple_of(i * step, step), step)
        value = terms[0][here, :].astype(F32)
        for term in terms[1:]:
            value = value + term[here, :].astype(F32)
        out[here, :] = value.astype(out.dtype)


def clear(out):
    @pl.loop(0, out.shape[0] // 16)
    def _(i):
        here = pl.ds(pl.multiple_of(i * 16, 16), 16)
        out[here, :] = jnp.zeros((16, out.shape[1]), out.dtype)


class LineScatter:
    def __init__(self, net, name, depth, z, block, landed, load):
        self.net, self.name, self.depth, self.z = net, name, depth, z
        self.block, self.landed, self.load = block, landed, load

        steps = range(1, depth)
        up = {s: (depth - s + z, z == 0, jnp.logical_and(z >= 1, z <= s - 1)) for s in steps}
        back = depth - 1 - z
        down = {s: (z + s - depth, back == 0, jnp.logical_and(back >= 1, back <= s - 1)) for s in steps}
        self.ways = (
            ("up", {"z": z + 1}, 0, z >= 1, z < 1, up),
            ("down", {"z": z - 1}, 1, back >= 1, back < 1, down),
        )

    def send(self, key, device, way, s, t, cond):
        self.net.send(
            key,
            lambda: self.block(t),
            lambda: self.landed.at[way, s - 1],
            device,
            cond,
            slot=(self.name, key[1], s),
        )

    def start(self):
        for s in range(1, self.depth):
            for tag, device, way, _, _, steps in self.ways:
                target, first, _ = steps[s]
                self.send((self.name, tag, s), device, way, s, target, first)

    def term(self, way, s):
        return self.landed.at[way, s - 1] if self.load is None else self.load.at[way]

    def take(self, tag, way, s):
        self.net.arrive((self.name, tag, s), lambda: self.landed.at[way, s - 1])
        if self.load is not None:
            pltpu.sync_copy(self.landed.at[way, s - 1], self.load.at[way])

    def step(self, s):
        for tag, device, way, _, _, steps in self.ways:
            t, _, cond = steps[s]

            def body():
                self.take(tag, way, s - 1)
                block = self.block(t)
                accumulate(block, block, self.term(way, s - 1))

            pl.when(cond)(body)
            self.send((self.name, tag, s, "on"), device, way, s, t, cond)

    def finish(self, *outs):
        last = self.depth - 1
        for tag, _, way, fed, unfed, _ in self.ways:
            pl.when(fed)(lambda: self.take(tag, way, last))
            pl.when(unfed)(lambda: clear(self.term(way, last)))
        rows = outs[0].shape[0]
        for i, out in enumerate(outs):
            here = pl.ds(i * rows, rows)
            accumulate(
                out, *(term.at[here, :] for term in (self.block(self.z), self.term(0, last), self.term(1, last)))
            )


class ExpertShare:
    def __init__(self, net, name, coords, result, dst):
        self.net, self.name, self.coords, self.result, self.dst = net, name, coords, result, dst
        x, y, c, _ = coords
        self.across = {4: {"x": 1 - x}, 2: {"y": 1 - y}, 1: {"c": 1 - c}}

    def place(self, flip):
        x, y, c, _ = self.coords
        fx = 1 - x if flip & 4 else x
        fy = 1 - y if flip & 2 else y
        fc = 1 - c if flip & 1 else c
        return self.dst.at[4 * fx + 2 * fy + fc]

    def put(self, flip, src, axis):
        self.net.send(
            (self.name, axis | flip), src, lambda: self.place(flip), self.across[axis]
        )

    def on(self, flip, axis):
        self.put(flip, lambda: self.place(flip), axis)

    def wait(self, flip):
        self.net.arrive((self.name, flip), lambda: self.place(flip))

    def start(self):
        x = self.coords[0]
        self.put(0, lambda: self.result.at[1 - x], 4)
        self.put(0, lambda: self.result.at[x], 2)
        self.put(0, lambda: self.result.at[x], 1)
        self.net.local((self.name, "own"), self.result.at[x], self.place(0))

    def pass_near(self):
        self.wait(4)
        self.on(4, 2)
        self.on(4, 1)
        self.wait(2)
        self.on(2, 1)

    def pass_far(self):
        self.wait(6)
        self.on(6, 1)

    def finish(self):
        self.net.ready((self.name, "own"))
        for flip in (1, 5, 3, 7):
            self.wait(flip)


class AttentionScatter:
    def __init__(self, net, name, depth, coords, grad, mates, chips, lines, dst, mate_load, chip_load, blocks, low):
        self.net, self.name, self.depth, self.coords = net, name, depth, coords
        self.grad, self.mates, self.chips, self.dst = grad, mates, chips, dst
        self.blocks, self.low = blocks, low
        self.columns = columns = grad.shape[1] // 4
        self.rows = grad.shape[0] // (2 * depth)
        self.mate_load, self.chip_load = mate_load.at[:, :columns], chip_load.at[:, :, :, :columns]
        x, y, c, z = coords
        self.line = LineScatter(net, name + " line", depth, z, lambda t: blocks.at[t], lines, None)

    def lanes(self, yi, ci):
        return pl.ds(pl.multiple_of((2 * yi + ci) * self.columns, LANES), self.columns)

    def quarter(self, yi, ci):
        return self.dst.at[:, self.lanes(yi, ci)]

    def part(self, zi, xi, yi):
        rows = pl.ds(pl.multiple_of((zi * 2 + xi) * self.rows, self.rows), self.rows)
        return self.grad.at[rows, self.lanes(yi, self.coords[2])]

    def to_mate(self, j, yi):
        c = self.coords[2]
        self.net.send(
            (self.name, "c", j),
            lambda: self.grad.at[:, self.lanes(yi, 1 - c)],
            lambda: self.mates.at[j],
            {"c": 1 - c},
        )

    def to_chip(self, key, zi, xi, yi, slot, device):
        self.net.send(
            (self.name, key, zi),
            lambda: self.part(zi, xi, yi),
            lambda: self.chips.at[slot, zi],
            device,
        )

    def start(self):
        y = self.coords[1]
        self.to_mate(1, 1 - y)
        self.to_mate(0, y)

    def add_mate(self, j, yi):
        self.net.arrive((self.name, "c", j), lambda: self.mates.at[j])
        pltpu.sync_copy(self.mates.at[j], self.mate_load)
        mine = self.grad.at[:, self.lanes(yi, self.coords[2])]
        accumulate(mine, mine, self.mate_load)

    def pass_c(self):
        x, y, c, z = self.coords
        half = self.depth // 2
        self.add_mate(1, 1 - y)
        for zi in range(self.depth):
            device = {"x": 1 - x} if zi < half else {"y": 1 - y}
            self.to_chip("far", zi, 1 - x, 1 - y, 2, device)
        for zi in range(half, self.depth):
            self.to_chip("y", zi, x, 1 - y, 0, {"y": 1 - y})
        self.add_mate(0, y)
        for zi in range(half):
            self.to_chip("x", zi, 1 - x, y, 1, {"x": 1 - x})

    def combined(self):
        x, y, c, z = self.coords
        half = self.depth // 2
        for first, key, xi, yi, slot, device in (
            (0, "y", x, 1 - y, 0, {"y": 1 - y}), (half, "x", 1 - x, y, 1, {"x": 1 - x})
        ):
            for zi in range(first, first + half):
                self.net.arrive((self.name, "far", zi), lambda: self.chips.at[2, zi])
            here = pl.ds(first, half)
            pltpu.sync_copy(self.chips.at[2, here], self.chip_load.at[2, here])
            for zi in range(first, first + half):
                part = self.part(zi, xi, yi)
                accumulate(part, part, self.chip_load.at[2, zi])
                self.to_chip(key, zi, xi, yi, slot, device)

    def pass_chips(self):
        x, y, c, z = self.coords
        for slot, key in enumerate(("y", "x")):
            for zi in range(self.depth):
                self.net.arrive((self.name, key, zi), lambda: self.chips.at[slot, zi])
            self.net.local((self.name, "load", slot), self.chips.at[slot], self.chip_load.at[slot])
        for slot in range(2):
            self.net.ready((self.name, "load", slot))
        for zi in range(self.depth):
            accumulate(
                self.blocks.at[zi],
                self.part(zi, x, y),
                self.chip_load.at[0, zi],
                self.chip_load.at[1, zi],
            )
        self.line.start()

    def total(self):
        x, y, c, z = self.coords
        self.line.finish(self.low)
        self.net.local((self.name, "own"), self.low, self.quarter(y, c))
        for key, device in (("ty", {"y": 1 - y}), ("tc", {"c": 1 - c})):
            self.net.send(
                (self.name, key), lambda: self.low, lambda: self.quarter(y, c), device
            )

    def pass_y(self):
        x, y, c, z = self.coords
        there = lambda: self.quarter(1 - y, c)
        self.net.arrive((self.name, "ty"), there)
        self.net.send((self.name, "tyc"), there, there, {"c": 1 - c})

    def finish(self):
        x, y, c, z = self.coords
        self.net.ready((self.name, "own"))
        self.net.arrive((self.name, "tc"), lambda: self.quarter(y, 1 - c))
        self.net.arrive((self.name, "tyc"), lambda: self.quarter(1 - y, 1 - c))


def norm_back(values, gain, upstream):
    inverse = inverse_rms(values)
    normal = values * inverse
    gain_grad = jnp.sum(upstream * normal, axis=0, keepdims=True)
    scaled = upstream * gain
    return (
        inverse * (scaled - normal * jnp.mean(scaled * normal, axis=-1, keepdims=True)),
        gain_grad,
    )


def layer_kernel(depth, shard_rows, *refs):
    (
        hidden, grad_out, mask, cosine, sine,
        gains_in, wq_in, wo_in, gate_in, up_in, down_in, share_in, grad_hbm,
        layer_out, grad_in, gain_total,
        gate_total, up_total, down_total, wq_total, wo_total,
        wq, wo, down_full, shares, probability,
        row_mates, row_fars, row_chips, out_mates, out_fars, out_chips,
        gate_lines, up_lines, down_lines, wq_mates, wq_chips, wo_mates, wo_chips,
        rows, grads, wide, down_grad, returned, wide_load, down_load, wide_low, down_low,
        mate_load, chip_load, wq_lines, wo_lines, wq_blocks, wo_blocks, wq_low, wo_low, gain_swap,
        gains, gain_rows, queries, keys, values, attended, mixed,
        send_sems, recv_sems, local_sems,
    ) = refs
    coords = x, y, c, z = tuple(lax.axis_index(n) for n in ("x", "y", "c", "z"))
    expert = 4 * x + 2 * y + c
    net = Net(send_sems, recv_sems, local_sems, c)
    length, width = hidden.shape
    units = gate_in.shape[2]
    tile, step = 256, 16
    factor = HEAD_DIM ** (-0.5)
    greet(depth, coords)

    wq_gather = AttentionGather(net, "wq", depth, coords, wq_in, wq)
    wo_gather = AttentionGather(net, "wo", depth, coords, wo_in, wo)
    gate_gather = ExpertGather(net, "gate", depth, coords, gate_in, wide.at[:, :units])
    up_gather = ExpertGather(net, "up", depth, coords, up_in, wide.at[:, units:])
    down_gather = ExpertGather(net, "down", depth, coords, down_in, down_full)
    gate_up = (gate_gather, up_gather)
    row_gather = SlabGather(net, "row", coords, rows, length)
    grad_gather = SlabGather(net, "grad", coords, grads, length)

    def wide_block(first):
        size = 2 * shard_rows
        return lambda t: wide.at[
            pl.ds(pl.multiple_of(t * size, size), size), pl.ds(first, units)
        ]

    def down_block(t):
        size = 2 * (units // (2 * depth))
        return down_grad.at[pl.ds(pl.multiple_of(t * size, size), size), :]

    gate_line = LineScatter(net, "gate line", depth, z, wide_block(0), gate_lines, wide_load)
    up_line = LineScatter(net, "up line", depth, z, wide_block(units), up_lines, wide_load)
    down_line = LineScatter(net, "down line", depth, z, down_block, down_lines, down_load)
    row_back = SlabReturn(net, "row back", coords, grads, length, row_mates, row_fars, row_chips, returned)
    out_back = SlabReturn(net, "out back", coords, rows, length, out_mates, out_fars, out_chips, returned)

    def simple_send(key, source, target, device, cond=None):
        net.send(key, lambda: source, lambda: target, device, cond)

    to_mate = {"c": 1 - c}

    me = z * 2 + x
    base = [net.slot(("gains", s)) for s in range(2 * depth)][0]

    def gain_copy(s, index):
        return pltpu.make_async_remote_copy(
            src_ref=gains_in,
            dst_ref=gains.at[me],
            send_sem=send_sems.at[index],
            recv_sem=recv_sems.at[base + me],
            device_id={"z": jnp.int32(s // 2), "x": jnp.int32(s % 2)},
            device_id_type=MESH,
        )

    wq_gather.start()
    net.local("gains", gains_in, gains.at[me])
    gain_sends = []
    for s in range(2 * depth):
        index = net.count
        net.count += 1
        gain_sends.append((s, index))
        pl.when(me != s)(lambda: gain_copy(s, index).start())
    wo_gather.start()
    for k in range(1, depth):
        wq_gather.pass_z(k)
        if k > 1:
            wo_gather.pass_z(k - 1)
    wo_gather.pass_z(depth - 1)
    for one in gate_up:
        one.start_x()
        one.start()
    wq_gather.pass_x(0)
    for k in range(1, depth):
        wq_gather.pass_x(k)
    down_gather.start()
    for k in range(1, depth):
        wq_gather.pass_y(k)
    for one in gate_up:
        one.pass_z(1, 0)
    wq_gather.finish()
    for k in range(depth):
        wo_gather.pass_x(k)
    grad_gather.start(grad_hbm)
    net.local("own grad", grad_hbm, grads.at[:length])
    x_share = {"x": 1 - x}
    for slot, device in (
        (1, {"c": 1 - c}), (2, {"y": 1 - y}), (4, x_share), (6, {"y": 1 - y, "x": 1 - x})
    ):
        simple_send(("share", slot), share_in, shares.at[slot], device)
    net.local("own share", share_in, shares.at[0])

    def attention_forward(wq_here, wo_here, chances):
        net.local("wq here", wq, wq_here)
        for s in range(2 * depth):
            pl.when(me != s)(lambda: net.arrive(("gains", s), lambda: gains.at[s]))
        net.ready("gains")
        wide_gain = None
        for s in range(2 * depth):
            rest = jnp.zeros((8, width - gains.shape[2]), F32)
            piece = jnp.concatenate([gains[s], rest], axis=1)
            piece = piece if s == 0 else pltpu.roll(piece, s * shard_rows, axis=1)
            wide_gain = piece if wide_gain is None else wide_gain + piece
        gain_rows[...] = wide_gain

        @pl.loop(0, length // step)
        def _(i):
            here = pl.ds(pl.multiple_of(i * step, step), step)
            one = hidden[here, :].astype(F32)
            rows[here, :] = (one * inverse_rms(one) * gain_rows[0:1, :]).astype(BF16)

        net.ready("wq here")
        cos, sin = cosine[...], sine[...]
        for start in range(0, wq.shape[1], tile):
            part = dot_nn(rows[:length, :], wq_here[:, start : start + tile])
            for at in range(start, start + tile, HEAD_DIM):
                head, one = at // HEAD_DIM, part[:, at - start : at - start + HEAD_DIM]
                if head < HEADS:
                    queries[head * length : (head + 1) * length, :] = turn(one, cos, sin).astype(BF16)
                elif head < HEADS + KV_HEADS:
                    at_row = (head - HEADS) * length
                    keys[at_row : at_row + length, :] = turn(one, cos, sin).astype(BF16)
                else:
                    at_row = (head - HEADS - KV_HEADS) * length
                    values[at_row : at_row + length, :] = one.astype(BF16)
        for one in gate_up:
            one.pass_x()
        for k in range(1, depth):
            wo_gather.pass_y(k)
        down_gather.start_x()
        for one in gate_up:
            one.pass_z(1, 1)
        allowed = mask[...] > 0.0
        for head in range(HEADS):
            kv = head // GROUP
            here = slice(head * length, (head + 1) * length)
            there = slice(kv * length, (kv + 1) * length)
            scores = dot_nt(queries[here, :], keys[there, :]) * factor
            scores = jnp.where(allowed, scores, masked_score)
            terms = jnp.exp(scores - jnp.max(scores, axis=-1, keepdims=True))
            chance = terms / jnp.sum(terms, axis=-1, keepdims=True)
            chances[here, :] = chance
            attended[:, head * HEAD_DIM : (head + 1) * HEAD_DIM] = dot_nn(
                chance.astype(BF16), values[there, :]
            ).astype(BF16)
        wo_gather.finish()
        net.local("wo here", wo, wo_here)
        net.local("keep chances", chances, probability)
        grad_gather.forward()
        net.ready("wo here")
        for start in range(0, width, tile):
            there = slice(start, start + tile)
            mixed[:, there] = hidden[:, there].astype(F32) + dot_nn(attended[...], wo_here[:, there])

        @pl.loop(0, length // step)
        def _(i):
            here = pl.ds(pl.multiple_of(i * step, step), step)
            total = mixed[here, :]
            rows[here, :] = (total * inverse_rms(total) * gain_rows[1:2, :]).astype(BF16)

        row_gather.start(rows.at[:length, :])
        net.ready("keep chances")

    pl.run_scoped(
        attention_forward,
        pltpu.VMEM(wq.shape, BF16),
        pltpu.VMEM(wo.shape, BF16),
        pltpu.VMEM((HEADS * length, length), F32),
    )

    def experts(down, hidden_act, both_grads, share_here):
        for k in range(2, depth):
            for j in range(2):
                for one in gate_up:
                    one.pass_z(k, j)
        down_gather.pass_x()
        grad_gather.forward_far()
        down_gather.pass_z(1, 0)
        for slot in (2, 4, 6):
            net.arrive(("share", slot), lambda: shares.at[slot])
            net.send(
                ("share", slot + 1),
                lambda slot=slot: shares.at[slot],
                lambda slot=slot: shares.at[slot + 1],
                to_mate,
            )
        row_gather.forward()
        down_gather.pass_z(1, 1)
        for slot in (1, 3, 5, 7):
            net.arrive(("share", slot), lambda: shares.at[slot])
        net.ready("own share")
        net.local("shares", shares, share_here)
        for one in gate_up:
            one.finish()
        net.ready("shares")
        net.ready("own grad")
        lane = lax.broadcasted_iota(jnp.int32, (length, LANES), 1)

        def share_of(r):
            return jnp.sum(jnp.where(lane == expert, share_here[r], 0.0), axis=1, keepdims=True)

        def first_half(first, count):
            @pl.loop(first, first + count)
            def _(r):
                here = pl.ds(pl.multiple_of(r * length, length), length)
                grads[here, :] = (share_of(r) * grads[here, :].astype(F32)).astype(BF16)
                for j in range(0, units, tile):
                    gate = dot_nn(rows[here, :], wide[:, j : j + tile])
                    up = dot_nn(rows[here, :], wide[:, units + j : units + j + tile])
                    sigmoid = 1.0 / (1.0 + jnp.exp(-gate))
                    silu = gate * sigmoid
                    hidden_act[here, j : j + tile] = (silu * up).astype(BF16)
                    both_grads[here, j : j + tile] = (
                        up * sigmoid * (1.0 + gate * (1.0 - sigmoid))
                    ).astype(BF16)
                    both_grads[here, units + j : units + j + tile] = silu.astype(BF16)

        row_gather.wait(1)
        grad_gather.wait(1)
        net.sent(("grad", 1, None))
        first_half(0, 2)
        row_gather.forward_far()
        for gather in (row_gather, grad_gather):
            gather.wait(3)
            gather.wait(5)
            for half in range(2):
                gather.wait(7, half)
            for slot, half in ((2, None), (4, None), (6, 0), (6, 1), (3, None), (5, None), (7, 0), (7, 1)):
                net.sent((gather.name, slot, half))
        first_half(2, 4)
        for k in range(2, depth):
            for j in range(2):
                down_gather.pass_z(k, j)
        first_half(6, 2)

        @pl.loop(0, units // tile)
        def _(i):
            at = pl.ds(pl.multiple_of(i * tile, tile), tile)
            for j in range(0, width, 512):
                down_grad[at, j : j + 512] = dot_tn(hidden_act[:, at], grads[:, j : j + 512]).astype(BF16)

        down_line.start()
        down_gather.finish()
        net.local("down here", down_full, down)
        net.ready("down here")

        @pl.loop(0, EXPERTS)
        def _(r):
            here = pl.ds(pl.multiple_of(r * length, length), length)
            for j in range(0, units, tile):
                back = dot_nt(grads[here, :], down[j : j + tile, :])
                for first in (j, units + j):
                    both_grads[here, first : first + tile] = (
                        back * both_grads[here, first : first + tile].astype(F32)
                    ).astype(BF16)

        def row_grad(slot):
            here = slice(slot * length, (slot + 1) * length)
            for j in range(0, width, 512):
                grads[here, j : j + 512] = dot_nt(both_grads[here, :], wide[j : j + 512, :]).astype(BF16)

        def out_rows(slot):
            here = slice(slot * length, (slot + 1) * length)
            share = share_of(slot)
            for j in range(0, width, 512):
                rows[here, j : j + 512] = (
                    share * dot_nn(hidden_act[here, :], down[:, j : j + 512])
                ).astype(BF16)

        def give_back(back, compute):
            for chip in (3, 1, 2, 0):
                compute(2 * chip + 1)
                back.to_mate(chip)
            for chip in (3, 1, 2, 0):
                compute(2 * chip)
                back.fetch(chip)
                if chip == 3:
                    back.add(3)
                    back.far()
                elif chip:
                    back.add(chip)
                    back.plain(chip)
            back.combined()
            back.add(0)

        give_back(row_back, row_grad)
        for s in range(2, depth):
            down_line.step(s)
        for one in gate_up:
            one.sent()

        def weight_grad(first):
            @pl.loop(0, width // tile)
            def _(i):
                at = pl.ds(pl.multiple_of(i * tile, tile), tile)
                wide[at, first : first + units] = dot_tn(
                    rows[:, at], both_grads[:, first : first + units]
                ).astype(BF16)

        weight_grad(0)
        gate_line.start()
        weight_grad(units)
        up_line.start()
        net.sent(("row", 1, None))
        give_back(out_back, out_rows)

    pl.run_scoped(
        experts,
        pltpu.VMEM((units, width), BF16),
        pltpu.VMEM((EXPERTS * length, units), BF16),
        pltpu.VMEM((EXPERTS * length, 2 * units), BF16),
        pltpu.VMEM((EXPERTS, length, LANES), F32),
    )

    def shared_out(name, line, low, dst):
        line.finish(low.at[0], low.at[1])
        share = ExpertShare(net, name, coords, low, dst)
        share.start()
        return share

    def attention_backward(weight, chances, wq_grad, upstream_two, mixed_grad, mixed_low, attended_grad, qkv_grad):
        net.local("wo again", wo, weight.at[:, :width])
        net.local("chance 0", probability.at[: GROUP * length], chances)
        row_back.total(upstream_two)
        gain_swap[0] = jnp.zeros(gain_swap.shape[1:], F32)

        @pl.loop(0, length // step)
        def _(i):
            here = pl.ds(pl.multiple_of(i * step, step), step)
            part, gain_two = norm_back(mixed[here, :], gain_rows[1:2, :], upstream_two[here, :])
            total = grad_out[here, :].astype(F32) + part
            mixed_grad[here, :] = total
            mixed_low[here, :] = total.astype(BF16)
            gain_swap[0, 1:2, :] += gain_two

        row_back.sent()
        for i in range(0, width, tile):
            for j in range(0, width, 512):
                grads[i : i + tile, j : j + 512] = dot_tn(
                    attended[:, i : i + tile], mixed_low[:, j : j + 512]
                ).astype(BF16)
        wo_net = AttentionScatter(
            net, "wo sum", depth, coords, grads.at[:width, :], wo_mates, wo_chips, wo_lines, wo_total,
            mate_load, chip_load, wo_blocks, wo_low,
        )
        wo_net.start()
        net.ready("wo again")
        for i in range(0, width, 512):
            attended_grad[:, i : i + 512] = dot_nt(
                mixed_low[...], weight[i : i + 512, :width]
            ).astype(BF16)
        net.local("wq again", wq, weight)
        wo_net.pass_c()
        gate_line.step(2)
        down_share = shared_out("down sum", down_line, down_low, down_total)
        cos, sin = cosine[...], -sine[...]
        for kv in range(KV_HEADS):
            net.ready("chance %d" % kv)
            there = slice(kv * length, (kv + 1) * length)
            value_sum = key_sum = None
            for g in range(GROUP):
                head = kv * GROUP + g
                here = slice(head * length, (head + 1) * length)
                cols = slice(head * HEAD_DIM, (head + 1) * HEAD_DIM)
                chance = chances[g * length : (g + 1) * length, :]
                back = attended_grad[:, cols]
                prob_grad = dot_nt(back, values[there, :])
                value_part = dot_tn(chance.astype(BF16), back)
                inner = jnp.sum(chance * prob_grad, axis=-1, keepdims=True)
                score_grad = (chance * (prob_grad - inner)).astype(BF16)
                query_grad = dot_nn(score_grad, keys[there, :]) * factor
                key_part = dot_tn(score_grad, queries[here, :])
                qkv_grad[:, cols] = turn(query_grad, cos, sin).astype(BF16)
                value_sum = value_part if value_sum is None else value_sum + value_part
                key_sum = key_part if key_sum is None else key_sum + key_part
            if kv + 1 < KV_HEADS:
                size = GROUP * length
                net.local("chance %d" % (kv + 1), probability.at[(kv + 1) * size : (kv + 2) * size], chances)
            first = (HEADS + kv) * HEAD_DIM
            qkv_grad[:, first : first + HEAD_DIM] = turn(key_sum * factor, cos, sin).astype(BF16)
            first = first + KV_HEADS * HEAD_DIM
            qkv_grad[:, first : first + HEAD_DIM] = value_sum.astype(BF16)

        @pl.loop(0, length // step)
        def _(i):
            here = pl.ds(pl.multiple_of(i * step, step), step)
            one = hidden[here, :].astype(F32)
            mixed_low[here, :] = (one * inverse_rms(one) * gain_rows[0:1, :]).astype(BF16)

        for i in range(0, width, tile):
            for j in range(0, wq_grad.shape[1], 512):
                wq_grad[i : i + tile, j : j + 512] = dot_tn(
                    mixed_low[:, i : i + tile], qkv_grad[:, j : j + 512]
                ).astype(BF16)
        wq_net = AttentionScatter(
            net, "wq sum", depth, coords, wq_grad, wq_mates, wq_chips, wq_lines, wq_total,
            mate_load, chip_load, wq_blocks, wq_low,
        )
        wq_net.start()
        wo_net.combined()
        for s in range(3, depth):
            gate_line.step(s)
        wq_net.pass_c()
        net.ready("wq again")
        for i in range(0, width, 512):
            upstream_two[:, i : i + 512] = dot_nt(qkv_grad[...], weight[i : i + 512, :])

        @pl.loop(0, length // step)
        def _(i):
            here = pl.ds(pl.multiple_of(i * step, step), step)
            part, gain_one = norm_back(
                hidden[here, :].astype(F32), gain_rows[0:1, :], upstream_two[here, :]
            )
            grad_in[here, :] = (mixed_grad[here, :] + part).astype(BF16)
            gain_swap[0, 0:1, :] += gain_one

        down_share.pass_near()
        wo_net.pass_chips()
        up_line.step(2)
        wq_net.combined()
        gate_share = shared_out("gate sum", gate_line, wide_low.at[0], gate_total)
        for i, (axis, device) in enumerate(
            (("c", {"c": 1 - c}), ("x", {"x": 1 - x}), ("y", {"y": 1 - y}))
        ):
            source, target = gain_swap.at[2 * i], gain_swap.at[2 * i + 1]
            simple_send(("gain", axis), source, target, device)
            net.arrive(("gain", axis), lambda: target)
            gain_swap[2 * i + 2] = gain_swap[2 * i] + gain_swap[2 * i + 1]
        for far in range(1, depth):
            simple_send(("gain", "up", far), gain_swap.at[6], gain_swap.at[5 + 2 * far], {"z": z + far}, z + far < depth)
            simple_send(("gain", "down", far), gain_swap.at[6], gain_swap.at[6 + 2 * far], {"z": z - far}, z - far >= 0)
        out_back.total(layer_out, mixed)
        down_share.pass_far()
        wq_net.pass_chips()
        for s in range(3, depth):
            up_line.step(s)
        for s in range(2, depth):
            wo_net.line.step(s)
            wq_net.line.step(s)
        gate_share.pass_near()
        gain_total[...] = gain_swap[6]
        for far in range(1, depth):
            for tag, slot, cond in (
                ("up", 5 + 2 * far, z - far >= 0), ("down", 6 + 2 * far, z + far < depth)
            ):

                def take():
                    net.arrive(("gain", tag, far), lambda: gain_swap.at[slot])
                    gain_total[...] += gain_swap[slot]

                pl.when(cond)(take)
        gate_share.pass_far()
        up_share = shared_out("up sum", up_line, wide_low.at[1], up_total)
        wo_net.total()
        wq_net.total()
        up_share.pass_near()
        wo_net.pass_y()
        wq_net.pass_y()
        up_share.pass_far()
        for one in (down_share, gate_share, up_share, wo_net, wq_net):
            one.finish()
        net.drain()

    pl.run_scoped(
        attention_backward,
        pltpu.VMEM(wq.shape, BF16),
        pltpu.VMEM((GROUP * length, length), F32),
        pltpu.VMEM(wq.shape, BF16),
        pltpu.VMEM((length, width), F32),
        pltpu.VMEM((length, width), F32),
        pltpu.VMEM((length, width), BF16),
        pltpu.VMEM((length, width), BF16),
        pltpu.VMEM((length, wq.shape[1]), BF16),
    )
    for s, index in gain_sends:
        pl.when(me != s)(lambda: gain_copy(s, index).wait_send())
    assert net.count <= send_sems.shape[0] and len(net.slots) <= recv_sems.shape[0]
    assert len(net.locals) <= local_sems.shape[0]


def layer_call(depth, shard_rows, hidden, grad_out, mask, cosine, sine, gains, wq_in, wo_in, gate_in, up_in, down_in, shares):
    length, width = hidden.shape
    wide, units, down_rows = wq_in.shape[1], gate_in.shape[2], down_in.shape[1]
    here, there = pl.BlockSpec(memory_space=pltpu.VMEM), pl.BlockSpec(memory_space=pltpu.HBM)

    def shape(*dims, dtype=BF16):
        return jax.ShapeDtypeStruct(dims, dtype)

    returns = [shape(4, length, width), shape(2, length // 2, width), shape(2, length, width)]
    out_shape = [
        shape(length, width), shape(length, width), shape(8, width, dtype=F32),
        shape(EXPERTS, shard_rows, units), shape(EXPERTS, shard_rows, units),
        shape(EXPERTS, down_rows, width),
        shape(shard_rows, wide), shape(shard_rows, width),
        shape(width, wide), shape(width, width), shape(units, width),
        shape(EXPERTS, length, LANES, dtype=F32), shape(HEADS * length, length, dtype=F32),
        *returns, *returns,
        shape(2, depth - 1, 2 * shard_rows, units), shape(2, depth - 1, 2 * shard_rows, units),
        shape(2, depth - 1, 2 * down_rows, width),
        shape(2, width, wide // 4), shape(3, depth, shard_rows, wide // 4),
        shape(2, width, width // 4), shape(3, depth, shard_rows, width // 4),
    ]
    sends = 110 * depth + 160
    return pl.pallas_call(
        functools.partial(layer_kernel, depth, shard_rows),
        out_shape=out_shape,
        in_specs=[here] * 5 + [there] * 8,
        out_specs=[here] * 3 + [there] * (len(out_shape) - 3),
        scratch_shapes=[
            pltpu.VMEM((EXPERTS * length, width), BF16),
            pltpu.VMEM((EXPERTS * length, width), BF16),
            pltpu.VMEM((width, 2 * units), BF16),
            pltpu.VMEM((units, width), BF16),
            pltpu.VMEM((4, length, width), BF16),
            pltpu.VMEM((2, 2 * shard_rows, units), BF16),
            pltpu.VMEM((2, 2 * down_rows, width), BF16),
            pltpu.VMEM((2, 2, shard_rows, units), BF16),
            pltpu.VMEM((2, down_rows, width), BF16),
            pltpu.VMEM((width, wide // 4), BF16),
            pltpu.VMEM((3, depth, shard_rows, wide // 4), BF16),
            pltpu.VMEM((2, depth - 1, shard_rows, wide // 4), BF16),
            pltpu.VMEM((2, depth - 1, shard_rows, width // 4), BF16),
            pltpu.VMEM((depth, shard_rows, wide // 4), BF16),
            pltpu.VMEM((depth, shard_rows, width // 4), BF16),
            pltpu.VMEM((shard_rows, wide // 4), BF16),
            pltpu.VMEM((shard_rows, width // 4), BF16),
            pltpu.VMEM((5 + 2 * depth, 8, width), F32),
            pltpu.VMEM((2 * depth, *gains.shape), F32),
            pltpu.VMEM((8, width), F32),
            pltpu.VMEM((HEADS * length, HEAD_DIM), BF16),
            pltpu.VMEM((KV_HEADS * length, HEAD_DIM), BF16),
            pltpu.VMEM((KV_HEADS * length, HEAD_DIM), BF16),
            pltpu.VMEM((length, width), BF16),
            pltpu.VMEM((length, width), F32),
            pltpu.SemaphoreType.DMA((sends,)),
            pltpu.SemaphoreType.DMA((sends,)),
            pltpu.SemaphoreType.DMA((80,)),
        ],
        compiler_params=pltpu.CompilerParams(
            collective_id=1, has_side_effects=True, vmem_limit_bytes=VMEM_LIMIT
        ),
    )(hidden, grad_out, mask, cosine, sine, gains, wq_in, wo_in, gate_in, up_in, down_in, shares, grad_out)


def rotary_tables(length, head_width):
    half_width = head_width // 2
    frequency = rotary_base ** (-2.0 * jnp.arange(half_width, dtype=jnp.float32) / head_width)
    angles = jnp.arange(length, dtype=jnp.float32)[:, None] * frequency[None, :]
    cosine, sine = jnp.cos(angles), jnp.sin(angles)
    return (
        jnp.concatenate([cosine, cosine], axis=1),
        jnp.concatenate([-sine, sine], axis=1),
    )


def make_shards(sizes):
    depth = sizes["z"]

    def shards(
        hidden_in,
        segments,
        routes,
        gate_weights,
        grad_out,
        attn_gain,
        query_weight,
        key_weight,
        value_weight,
        output_weight,
        ffn_gain,
        gate_weight,
        up_weight,
        down_weight,
    ):
        length, width = hidden_in.shape
        gains = jnp.stack([attn_gain, ffn_gain]).astype(F32)
        shard_rows = gains.shape[1]
        lanes = -(-shard_rows // LANES) * LANES
        gains = jnp.pad(gains, ((0, 6), (0, lanes - shard_rows)))
        wq_in = jnp.concatenate([query_weight, key_weight, value_weight], axis=1)
        onehot = routes[:, :, None] == jnp.arange(LANES, dtype=jnp.int32)
        shares = jnp.sum(jnp.where(onehot, gate_weights[:, :, None], 0.0), axis=1)
        segment = segments[0]
        position = jnp.arange(length, dtype=jnp.int32)
        allowed = (position[:, None] >= position[None, :]) & (segment[:, None] == segment[None, :])
        cosine, sine = rotary_tables(length, HEAD_DIM)
        layer_out, grad_in, gain_total, gate_total, up_total, down_total, wq_total, wo_total = (
            layer_call(
                depth, shard_rows, hidden_in, grad_out, allowed.astype(F32), cosine, sine, gains,
                wq_in, output_weight, gate_weight, up_weight, down_weight, shares,
            )[:8]
        )
        z, x = lax.axis_index("z"), lax.axis_index("x")
        gain_total = lax.dynamic_slice_in_dim(gain_total, (z * 2 + x) * shard_rows, shard_rows, 1)

        def whole(value):
            value = value.astype(F32)
            return lax.psum(value, "o") if sizes["o"] > 1 else value

        wq_total = whole(wq_total)
        queries_end = HEADS * HEAD_DIM
        keys_end = queries_end + KV_HEADS * HEAD_DIM
        gain_total = whole(gain_total)
        return (
            layer_out,
            grad_in,
            gain_total[0],
            wq_total[:, :queries_end],
            wq_total[:, queries_end:keys_end],
            wq_total[:, keys_end:],
            whole(wo_total),
            gain_total[1],
            whole(gate_total),
            whole(up_total),
            whole(down_total),
        )

    return shards


def solution(mesh):
    reps, shard_count = mesh.shape["rep"], mesh.shape["shard"]
    sizes = {"o": reps // 4, "y": 2, "c": 2, "z": shard_count // 2, "x": 2}
    fine = Mesh(mesh.devices.reshape(tuple(sizes.values())), tuple(sizes))
    tokens = P(("o", "y", "c", "z", "x"), None)
    first, second = P(("z", "x")), P(None, ("z", "x"), None)
    matrix = P(("z", "x"), None)
    return jax.shard_map(
        make_shards(sizes),
        mesh=fine,
        in_specs=(
            (tokens,) * 5 + (first, matrix, matrix, matrix, matrix, first) + (second,) * 3
        ),
        out_specs=(
            (tokens,) * 2 + (first, matrix, matrix, matrix, matrix, first) + (second,) * 3
        ),
        check_vma=False,
    )
```

```python
import functools

import jax
import jax.numpy as jnp
from jax import lax
from jax.experimental import pallas as pl
from jax.experimental.pallas import tpu as pltpu
from jax.sharding import Mesh
from jax.sharding import PartitionSpec as P

HEADS = 12
KV_HEADS = 2
GROUP = HEADS // KV_HEADS
HEAD_DIM = 128
EXPERTS = 8
LANES = 128

epsilon = 1e-06
rotary_base = 1000000.0
masked_score = -1e30

F32 = jnp.float32
BF16 = jnp.bfloat16
MESH = pl.DeviceIdType.MESH
VMEM_LIMIT = 62 * 2**20


def dot(a, b, dims):
    return lax.dot_general(a, b, (dims, ((), ())), preferred_element_type=F32)


def dot_nn(a, b):
    return dot(a, b, ((1,), (0,)))


def dot_nt(a, b):
    return dot(a, b, ((1,), (1,)))


def dot_tn(a, b):
    return dot(a, b, ((0,), (0,)))


def guarded(cond, body):
    if cond is None:
        body()
    else:
        pl.when(cond)(body)


def both(first, second):
    if first is None:
        return second
    if second is None:
        return first
    return jnp.logical_and(first, second)


class Net:
    def __init__(self, send_sems, recv_sems, local_sems, core):
        self.send_sems, self.recv_sems, self.local_sems = send_sems, recv_sems, local_sems
        self.away = {"c": 1 - core}
        self.slots, self.sends, self.locals, self.count, self.done = {}, {}, {}, 0, set()

    def slot(self, key):
        return self.slots.setdefault(key, len(self.slots))

    def send(self, key, src, dst, device, cond=None, slot=None):
        recv, index = self.slot(slot or key), self.count
        self.count += 1

        def build():
            return pltpu.make_async_remote_copy(
                src_ref=src(),
                dst_ref=dst(),
                send_sem=self.send_sems.at[index],
                recv_sem=self.recv_sems.at[recv],
                device_id=device,
                device_id_type=MESH,
            )

        guarded(cond, lambda: build().start())
        self.sends[key] = (cond, build)

    def sent(self, key):
        cond, build = self.sends.pop(key)
        guarded(cond, lambda: build().wait_send())

    def arrive(self, key, dst, cond=None):
        recv = self.slot(key)

        def wait():
            pltpu.make_async_remote_copy(
                src_ref=dst(),
                dst_ref=dst(),
                send_sem=self.send_sems.at[0],
                recv_sem=self.recv_sems.at[recv],
                device_id=self.away,
                device_id_type=MESH,
            ).wait_recv()

        guarded(cond, wait)

    def local(self, key, src, dst):
        index = len(self.locals)
        copy = pltpu.make_async_copy(src, dst, self.local_sems.at[index])
        copy.start()
        self.locals[key] = copy

    def ready(self, key):
        if key not in self.done:
            self.done.add(key)
            self.locals[key].wait()

    def drain(self):
        for key in list(self.sends):
            self.sent(key)
        for key in self.locals:
            self.ready(key)


def greet(depth, coords):
    x, y, c, z = coords
    barrier = pltpu.get_barrier_semaphore()
    for device in ({"y": 1 - y}, {"y": 1 - y, "x": 1 - x}, {"c": 1 - c}):
        pl.semaphore_signal(barrier, inc=1, device_id=device, device_id_type=MESH)
    for zi in range(depth):
        for xi in range(2):

            def tell(zi=zi, xi=xi):
                pl.semaphore_signal(
                    barrier,
                    inc=1,
                    device_id={"z": jnp.int32(zi), "x": jnp.int32(xi)},
                    device_id_type=MESH,
                )

            pl.when(jnp.logical_or(z != zi, x != xi))(tell)
    pl.semaphore_wait(barrier, 3 + 2 * depth - 1)


def along(depth, z):
    return (
        ("up", {"z": z + 1}, z + 1 < depth, lambda k: z - k, lambda k: z - k >= 0),
        ("down", {"z": z - 1}, z > 0, lambda k: z + k, lambda k: z + k < depth),
    )


class SlabGather:
    def __init__(self, net, name, coords, dst, length):
        self.net, self.name, self.dst, self.length = net, name, dst, length
        x, y, c, _ = coords
        self.to_x, self.to_y, self.to_mate = {"x": 1 - x}, {"y": 1 - y}, {"c": 1 - c}

    def slot(self, slot, half=None):
        first, size = slot * self.length, self.length
        if half is not None:
            size = size // 2
            first = first + half * size
        return self.dst.at[first : first + size, :]

    def put(self, slot, src, device, half=None):
        self.net.send(
            (self.name, slot, half), lambda: src, lambda: self.slot(slot, half), device
        )

    def wait(self, slot, half=None):
        self.net.arrive((self.name, slot, half), lambda: self.slot(slot, half))

    def start(self, src):
        self.put(2, src, self.to_y)
        self.put(4, src, self.to_x)
        self.put(1, src, self.to_mate)

    def forward(self):
        self.wait(2)
        self.put(6, self.slot(2, 0), self.to_x, 0)
        self.put(3, self.slot(2), self.to_mate)
        self.wait(4)
        self.put(6, self.slot(4, 1), self.to_y, 1)
        self.put(5, self.slot(4), self.to_mate)

    def forward_far(self):
        for half in range(2):
            self.wait(6, half)
            self.put(7, self.slot(6, half), self.to_mate, half)

    def sent(self):
        for slot, half in ((2, None), (4, None), (1, None), (6, 0), (6, 1), (3, None), (5, None), (7, 0), (7, 1)):
            self.net.sent((self.name, slot, half))


class AttentionGather:
    def __init__(self, net, name, depth, coords, src, dst):
        self.net, self.name, self.depth, self.src, self.dst = net, name, depth, src, dst
        self.x, self.y, self.c, self.z = x, y, c, z = coords
        self.nx, self.ny, self.nc = 1 - x, 1 - y, 1 - c
        self.rows, self.columns = src.shape[0], src.shape[1] // 4
        self.to_x, self.to_y, self.to_mate = {"x": self.nx}, {"y": self.ny}, {"c": self.nc}
        self.ways = [
            (tag, device, more, {k: (origin(k), there(k), both(there(k), more)) for k in range(1, depth)})
            for tag, device, more, origin, there in along(depth, z)
        ]

    def lanes(self, yi, ci):
        return pl.ds(pl.multiple_of((2 * yi + ci) * self.columns, LANES), self.columns)

    def block(self, zi, xi, yi, ci):
        return lambda: self.dst.at[
            pl.ds(pl.multiple_of((zi * 2 + xi) * self.rows, self.rows), self.rows), self.lanes(yi, ci)
        ]

    def put(self, key, place, device, cond=None, src=None):
        block = self.block(*place)
        self.net.send((self.name,) + key, src or block, block, device, cond)

    def wait(self, key, place, cond=None):
        self.net.arrive((self.name,) + key, self.block(*place), cond)

    def mine(self):
        return pl.ds(pl.multiple_of((self.z * 2 + self.x) * self.rows, self.rows), self.rows)

    def start(self):
        x, y, c, z = self.x, self.y, self.c, self.z
        own = lambda: self.src.at[:, self.lanes(y, c)]
        cross = lambda: self.src.at[:, self.lanes(self.ny, c)]
        for tag, device, more, _ in self.ways:
            self.put(("z", tag, 1), (z, x, y, c), device, more, own)
        self.put(("x", "same"), (z, x, y, c), self.to_x, None, own)
        self.put(("x", "cross"), (z, x, self.ny, c), self.to_x, None, cross)

    def pass_z(self, k):
        for tag, device, _, steps in self.ways:
            origin, cond, on = steps[k]
            place = (origin, self.x, self.y, self.c)
            self.wait(("z", tag, k), place, cond)
            if k + 1 < self.depth:
                self.put(("z", tag, k + 1), place, device, on)
            self.put(("x", tag, k), place, self.to_x, cond)
            self.put(("y", tag, k, 0), place, self.to_y, cond)
            self.put(("c", tag, k, 0), place, self.to_mate, cond)

    def pass_x(self, k):
        if k == 0:
            for tag, yi in (("same", self.y), ("cross", self.ny)):
                place = (self.z, self.nx, yi, self.c)
                self.wait(("x", tag), place)
                self.put(("c", tag), place, self.to_mate)
            return
        for tag, _, _, steps in self.ways:
            origin, cond, _ = steps[k]
            place = (origin, self.nx, self.y, self.c)
            self.wait(("x", tag, k), place, cond)
            self.put(("y", tag, k, 1), place, self.to_y, cond)
            self.put(("c", tag, k, 1), place, self.to_mate, cond)

    def pass_y(self, k):
        for tag, _, _, steps in self.ways:
            origin, cond, _ = steps[k]
            for j, xi in ((0, self.x), (1, self.nx)):
                place = (origin, xi, self.ny, self.c)
                self.wait(("y", tag, k, j), place, cond)
                self.put(("c", tag, k, 2 + j), place, self.to_mate, cond)

    def finish(self):
        for tag, yi in (("same", self.y), ("cross", self.ny)):
            self.wait(("c", tag), (self.z, self.nx, yi, self.nc))
        for k in range(1, self.depth):
            for tag, _, _, steps in self.ways:
                origin, cond, _ = steps[k]
                for j, (xi, yi) in enumerate(
                    ((self.x, self.y), (self.nx, self.y), (self.x, self.ny), (self.nx, self.ny))
                ):
                    self.wait(("c", tag, k, j), (origin, xi, yi, self.nc), cond)


class ExpertGather:
    def __init__(self, net, name, depth, coords, src, dst):
        self.net, self.name, self.depth, self.coords, self.src, self.dst = (
            net, name, depth, coords, src, dst,
        )
        self.rows = src.shape[1]
        x, y, c, z = coords
        self.own, self.away = 4 * x + 2 * y + c, 4 * (1 - x) + 2 * y + c
        self.xs = (x, 1 - x)
        self.to_x = {"x": self.xs[1]}
        self.ways = [
            (tag, device, more, {
                k: (origin(k), there(k), both(there(k), more), both(there(k), jnp.logical_not(more)))
                for k in range(1, depth)
            })
            for tag, device, more, origin, there in along(depth, z)
        ]

    def block(self, zi, xi):
        return lambda: self.dst.at[
            pl.ds(pl.multiple_of((zi * 2 + xi) * self.rows, self.rows), self.rows), :
        ]

    def put(self, key, place, device, cond=None, src=None):
        block = self.block(*place)
        self.net.send((self.name,) + key, src or block, block, device, cond)

    def start(self):
        x, _, _, z = self.coords
        for tag, device, more, _ in self.ways:
            self.put(("z", tag, 1, 0), (z, x), device, more, lambda: self.src.at[self.own])

    def start_x(self):
        x, _, _, z = self.coords
        self.put(("x",), (z, x), self.to_x, None, lambda: self.src.at[self.away])

    def pass_x(self):
        x, _, _, z = self.coords
        self.net.arrive((self.name, "x"), self.block(z, self.xs[1]))
        for tag, device, more, _ in self.ways:
            self.put(("z", tag, 1, 1), (z, self.xs[1]), device, more)

    def pass_z(self, k, j):
        if k + 1 >= self.depth:
            return
        for tag, device, _, steps in self.ways:
            origin, _, on, _ = steps[k]
            place = (origin, self.xs[j])
            self.net.arrive((self.name, "z", tag, k, j), self.block(*place), on)
            self.put(("z", tag, k + 1, j), place, device, on)

    def finish(self):
        for k in range(1, self.depth):
            for j in range(2):
                for tag, _, _, steps in self.ways:
                    origin, there, _, last = steps[k]
                    cond = there if k + 1 >= self.depth else last
                    self.net.arrive(
                        (self.name, "z", tag, k, j), self.block(origin, self.xs[j]), cond
                    )

    def sent(self):
        self.net.sent((self.name, "x"))
        for k in range(1, self.depth):
            for j in range(2):
                for tag, _, _, _ in self.ways:
                    self.net.sent((self.name, "z", tag, k, j))


def inverse_rms(values):
    return lax.rsqrt(jnp.mean(values * values, axis=-1, keepdims=True) + epsilon)


def turn(values, cosine, sine):
    return values * cosine + pltpu.roll(values, HEAD_DIM // 2, axis=1) * sine


class SlabReturn:
    def __init__(self, net, name, coords, parts, length, mates, fars, chips, load, by_x):
        self.net, self.name, self.parts, self.length = net, name, parts, length
        self.mates, self.fars, self.landed, self.load, self.by_x = mates, fars, chips, load, by_x
        x, y, c, _ = coords
        self.to_x, self.to_y, self.to_core = {"x": 1 - x}, {"y": 1 - y}, {"c": 1 - c}

    def part(self, slot, half=None):
        first, size = slot * self.length, self.length
        if half is not None:
            size = size // 2
            first = first + half * size
        return self.parts.at[first : first + size, :]

    def half(self, half):
        return pl.ds(half * (self.length // 2), self.length // 2)

    def to_mate(self, chip):
        self.net.send(
            (self.name, "mate", chip),
            lambda: self.part(2 * chip + 1),
            lambda: self.mates.at[chip],
            self.to_core,
        )

    def fetch(self, chip):
        self.net.arrive((self.name, "mate", chip), lambda: self.mates.at[chip])
        self.net.local((self.name, "load", chip), self.mates.at[chip], self.load.at[chip])

    def fetched(self, chip):
        self.net.ready((self.name, "load", chip))
        return self.load.at[chip]

    def far(self, half, device):
        self.net.send(
            (self.name, "far", half),
            lambda: self.part(6, half),
            lambda: self.fars.at[self.half(half)],
            device,
        )

    def near(self, chip, half, device):
        self.net.send(
            (self.name, "chip", chip, half),
            lambda: self.part(2 * chip, half),
            lambda: self.landed.at[chip - 1, self.half(half)],
            device,
        )

    def give(self, chip):
        if chip == 3:
            self.far(0, self.to_x)
            self.far(1, self.to_x if self.by_x else self.to_y)
        elif chip == 1 and not self.by_x:
            self.near(1, 1, self.to_y)
        elif chip == 2:
            self.near(2, 0, self.to_x)
            if self.by_x:
                self.near(2, 1, self.to_x)

    def combined(self):
        places = ((0, 1, self.to_y), (1, 1, self.to_y) if self.by_x else (1, 2, self.to_x))
        for half, _, _ in places:
            here = self.half(half)
            self.net.arrive((self.name, "far", half), lambda: self.fars.at[here])
            self.net.local((self.name, "far", half), self.fars.at[here], self.load.at[3, here])
        for half, chip, device in places:
            self.net.ready((self.name, "far", half))
            part = self.part(2 * chip, half)
            accumulate(part, part, self.load.at[3, self.half(half)])
            self.near(chip, half, device)

    def total(self, out, *more):
        for chip in (1, 2):
            for half in range(2):
                self.net.arrive(
                    (self.name, "chip", chip, half), lambda: self.landed.at[chip - 1, self.half(half)]
                )
            self.net.local((self.name, "last", chip), self.landed.at[chip - 1], self.load.at[chip])
        for chip in (1, 2):
            self.net.ready((self.name, "last", chip))
        accumulate(out, self.part(0), self.load.at[1], self.load.at[2], *more)

    def sent(self):
        for chip in range(4):
            self.net.sent((self.name, "mate", chip))
        for half in range(2):
            self.net.sent((self.name, "far", half))
            for chip in (1, 2):
                self.net.sent((self.name, "chip", chip, half))


def accumulate(out, *terms):
    total, columns = out.shape
    step = 32 if columns < 1024 and total % 32 == 0 else 16

    @pl.loop(0, total // step)
    def _(i):
        here = pl.ds(pl.multiple_of(i * step, step), step)
        value = terms[0][here, :].astype(F32)
        for term in terms[1:]:
            value = value + term[here, :].astype(F32)
        out[here, :] = value.astype(out.dtype)


def clear(out):
    @pl.loop(0, out.shape[0] // 16)
    def _(i):
        here = pl.ds(pl.multiple_of(i * 16, 16), 16)
        out[here, :] = jnp.zeros((16, out.shape[1]), out.dtype)


class LineScatter:
    def __init__(self, net, name, depth, z, block, landed, load):
        self.net, self.name, self.depth, self.z = net, name, depth, z
        self.block, self.landed, self.load = block, landed, load

        steps = range(1, depth)
        up = {s: (depth - s + z, z == 0, jnp.logical_and(z >= 1, z <= s - 1)) for s in steps}
        back = depth - 1 - z
        down = {s: (z + s - depth, back == 0, jnp.logical_and(back >= 1, back <= s - 1)) for s in steps}
        self.ways = (
            ("up", {"z": z + 1}, 0, z >= 1, z < 1, up),
            ("down", {"z": z - 1}, 1, back >= 1, back < 1, down),
        )

    def send(self, key, device, way, s, t, cond):
        self.net.send(
            key,
            lambda: self.block(t),
            lambda: self.landed.at[way, s - 1],
            device,
            cond,
            slot=(self.name, key[1], s),
        )

    def start(self):
        for s in range(1, self.depth):
            for tag, device, way, _, _, steps in self.ways:
                target, first, _ = steps[s]
                self.send((self.name, tag, s), device, way, s, target, first)

    def term(self, way, s):
        return self.landed.at[way, s - 1] if self.load is None else self.load.at[way]

    def take(self, tag, way, s):
        self.net.arrive((self.name, tag, s), lambda: self.landed.at[way, s - 1])
        if self.load is not None:
            pltpu.sync_copy(self.landed.at[way, s - 1], self.load.at[way])

    def step(self, s):
        for tag, device, way, _, _, steps in self.ways:
            t, _, cond = steps[s]

            def body():
                self.take(tag, way, s - 1)
                block = self.block(t)
                accumulate(block, block, self.term(way, s - 1))

            pl.when(cond)(body)
            self.send((self.name, tag, s, "on"), device, way, s, t, cond)

    def finish(self, *outs):
        last = self.depth - 1
        for tag, _, way, fed, unfed, _ in self.ways:
            pl.when(fed)(lambda: self.take(tag, way, last))
            pl.when(unfed)(lambda: clear(self.term(way, last)))
        rows = outs[0].shape[0]
        for i, out in enumerate(outs):
            here = pl.ds(i * rows, rows)
            accumulate(
                out, *(term.at[here, :] for term in (self.block(self.z), self.term(0, last), self.term(1, last)))
            )


class ExpertShare:
    def __init__(self, net, name, coords, result, dst):
        self.net, self.name, self.coords, self.result, self.dst = net, name, coords, result, dst
        x, y, c, _ = coords
        self.across = {4: {"x": 1 - x}, 2: {"y": 1 - y}, 1: {"c": 1 - c}}

    def place(self, flip):
        x, y, c, _ = self.coords
        fx = 1 - x if flip & 4 else x
        fy = 1 - y if flip & 2 else y
        fc = 1 - c if flip & 1 else c
        return self.dst.at[4 * fx + 2 * fy + fc]

    def put(self, flip, src, axis):
        self.net.send(
            (self.name, axis | flip), src, lambda: self.place(flip), self.across[axis]
        )

    def on(self, flip, axis):
        self.put(flip, lambda: self.place(flip), axis)

    def wait(self, flip):
        self.net.arrive((self.name, flip), lambda: self.place(flip))

    def start(self):
        x = self.coords[0]
        self.put(0, lambda: self.result.at[1 - x], 4)
        self.put(0, lambda: self.result.at[x], 2)
        self.put(0, lambda: self.result.at[x], 1)
        self.net.local((self.name, "own"), self.result.at[x], self.place(0))

    def pass_near(self):
        self.wait(4)
        self.on(4, 2)
        self.on(4, 1)
        self.wait(2)
        self.on(2, 1)

    def pass_far(self):
        self.wait(6)
        self.on(6, 1)

    def finish(self):
        self.net.ready((self.name, "own"))
        for flip in (1, 5, 3, 7):
            self.wait(flip)


class AttentionScatter:
    def __init__(self, net, name, depth, coords, grad, mates, chips, lines, dst, mate_load, chip_load, blocks, low):
        self.net, self.name, self.depth, self.coords = net, name, depth, coords
        self.grad, self.mates, self.chips, self.dst = grad, mates, chips, dst
        self.blocks, self.low = blocks, low
        self.columns = columns = grad.shape[1] // 4
        self.rows = grad.shape[0] // (2 * depth)
        self.mate_load, self.chip_load = mate_load.at[:, :columns], chip_load.at[:, :, :, :columns]
        x, y, c, z = coords
        self.line = LineScatter(net, name + " line", depth, z, lambda t: blocks.at[t], lines, None)

    def lanes(self, yi, ci):
        return pl.ds(pl.multiple_of((2 * yi + ci) * self.columns, LANES), self.columns)

    def quarter(self, yi, ci):
        return self.dst.at[:, self.lanes(yi, ci)]

    def part(self, zi, xi, yi):
        rows = pl.ds(pl.multiple_of((zi * 2 + xi) * self.rows, self.rows), self.rows)
        return self.grad.at[rows, self.lanes(yi, self.coords[2])]

    def to_mate(self, j, yi):
        c = self.coords[2]
        self.net.send(
            (self.name, "c", j),
            lambda: self.grad.at[:, self.lanes(yi, 1 - c)],
            lambda: self.mates.at[j],
            {"c": 1 - c},
        )

    def to_chip(self, key, zi, xi, yi, slot, device):
        self.net.send(
            (self.name, key, zi),
            lambda: self.part(zi, xi, yi),
            lambda: self.chips.at[slot, zi],
            device,
        )

    def start(self):
        y = self.coords[1]
        self.to_mate(1, 1 - y)
        self.to_mate(0, y)

    def add_mate(self, j, yi):
        self.net.arrive((self.name, "c", j), lambda: self.mates.at[j])
        pltpu.sync_copy(self.mates.at[j], self.mate_load)
        mine = self.grad.at[:, self.lanes(yi, self.coords[2])]
        accumulate(mine, mine, self.mate_load)

    def pass_c(self):
        x, y, c, z = self.coords
        half = self.depth // 2
        self.add_mate(1, 1 - y)
        for zi in range(self.depth):
            device = {"x": 1 - x} if zi < half else {"y": 1 - y}
            self.to_chip("far", zi, 1 - x, 1 - y, 2, device)
        for zi in range(half, self.depth):
            self.to_chip("y", zi, x, 1 - y, 0, {"y": 1 - y})
        self.add_mate(0, y)
        for zi in range(half):
            self.to_chip("x", zi, 1 - x, y, 1, {"x": 1 - x})

    def combined(self):
        x, y, c, z = self.coords
        half = self.depth // 2
        for first, key, xi, yi, slot, device in (
            (0, "y", x, 1 - y, 0, {"y": 1 - y}), (half, "x", 1 - x, y, 1, {"x": 1 - x})
        ):
            for zi in range(first, first + half):
                self.net.arrive((self.name, "far", zi), lambda: self.chips.at[2, zi])
            here = pl.ds(first, half)
            pltpu.sync_copy(self.chips.at[2, here], self.chip_load.at[2, here])
            for zi in range(first, first + half):
                part = self.part(zi, xi, yi)
                accumulate(part, part, self.chip_load.at[2, zi])
                self.to_chip(key, zi, xi, yi, slot, device)

    def pass_chips(self):
        x, y, c, z = self.coords
        for slot, key in enumerate(("y", "x")):
            for zi in range(self.depth):
                self.net.arrive((self.name, key, zi), lambda: self.chips.at[slot, zi])
            self.net.local((self.name, "load", slot), self.chips.at[slot], self.chip_load.at[slot])
        for slot in range(2):
            self.net.ready((self.name, "load", slot))
        for zi in range(self.depth):
            accumulate(
                self.blocks.at[zi],
                self.part(zi, x, y),
                self.chip_load.at[0, zi],
                self.chip_load.at[1, zi],
            )
        self.line.start()

    def total(self):
        x, y, c, z = self.coords
        self.line.finish(self.low)
        self.net.local((self.name, "own"), self.low, self.quarter(y, c))
        for key, device in (("ty", {"y": 1 - y}), ("tc", {"c": 1 - c})):
            self.net.send(
                (self.name, key), lambda: self.low, lambda: self.quarter(y, c), device
            )

    def pass_y(self):
        x, y, c, z = self.coords
        there = lambda: self.quarter(1 - y, c)
        self.net.arrive((self.name, "ty"), there)
        self.net.send((self.name, "tyc"), there, there, {"c": 1 - c})

    def finish(self):
        x, y, c, z = self.coords
        self.net.ready((self.name, "own"))
        self.net.arrive((self.name, "tc"), lambda: self.quarter(y, 1 - c))
        self.net.arrive((self.name, "tyc"), lambda: self.quarter(1 - y, 1 - c))


def norm_back(values, gain, upstream):
    inverse = inverse_rms(values)
    normal = values * inverse
    gain_grad = jnp.sum(upstream * normal, axis=0, keepdims=True)
    scaled = upstream * gain
    return (
        inverse * (scaled - normal * jnp.mean(scaled * normal, axis=-1, keepdims=True)),
        gain_grad,
    )


def layer_kernel(depth, shard_rows, *refs):
    (
        hidden, grad_out, mask, cosine, sine,
        gains_in, wq_in, wo_in, gate_in, up_in, down_in, share_in, grad_hbm,
        layer_out, grad_in, gain_total,
        gate_total, up_total, down_total, wq_total, wo_total,
        wq, wo, down_full, shares, probability,
        row_mates, row_fars, row_chips, out_mates, out_fars, out_chips,
        gate_lines, up_lines, down_lines, wq_mates, wq_chips, wo_mates, wo_chips,
        rows, grads, wide, down_grad, returned, wide_load, down_load, wide_low, down_low,
        mate_load, chip_load, wq_lines, wo_lines, wq_blocks, wo_blocks, wq_low, wo_low, gain_swap,
        gains, gain_rows, queries, keys, values, attended, mixed,
        send_sems, recv_sems, local_sems,
    ) = refs
    coords = x, y, c, z = tuple(lax.axis_index(n) for n in ("x", "y", "c", "z"))
    expert = 4 * x + 2 * y + c
    net = Net(send_sems, recv_sems, local_sems, c)
    length, width = hidden.shape
    units = gate_in.shape[2]
    tile, step = 256, 16
    factor = HEAD_DIM ** (-0.5)
    greet(depth, coords)

    wq_gather = AttentionGather(net, "wq", depth, coords, wq_in, wq)
    wo_gather = AttentionGather(net, "wo", depth, coords, wo_in, wo)
    gate_gather = ExpertGather(net, "gate", depth, coords, gate_in, wide.at[:, :units])
    up_gather = ExpertGather(net, "up", depth, coords, up_in, wide.at[:, units:])
    down_gather = ExpertGather(net, "down", depth, coords, down_in, down_full)
    gate_up = (gate_gather, up_gather)
    row_gather = SlabGather(net, "row", coords, rows, length)
    grad_gather = SlabGather(net, "grad", coords, grads, length)

    def wide_block(first):
        size = 2 * shard_rows
        return lambda t: wide.at[
            pl.ds(pl.multiple_of(t * size, size), size), pl.ds(first, units)
        ]

    def down_block(t):
        size = 2 * (units // (2 * depth))
        return down_grad.at[pl.ds(pl.multiple_of(t * size, size), size), :]

    gate_line = LineScatter(net, "gate line", depth, z, wide_block(0), gate_lines, wide_load)
    up_line = LineScatter(net, "up line", depth, z, wide_block(units), up_lines, wide_load)
    down_line = LineScatter(net, "down line", depth, z, down_block, down_lines, down_load)
    row_back = SlabReturn(net, "row back", coords, grads, length, row_mates, row_fars, row_chips, returned, False)
    out_back = SlabReturn(net, "out back", coords, rows, length, out_mates, out_fars, out_chips, returned, True)

    def simple_send(key, source, target, device, cond=None):
        net.send(key, lambda: source, lambda: target, device, cond)

    to_mate, to_x, to_y = {"c": 1 - c}, {"x": 1 - x}, {"y": 1 - y}
    to_xy = {**to_x, **to_y}

    me = z * 2 + x
    base = [net.slot(("gains", s)) for s in range(2 * depth)][0]

    def gain_copy(s, index):
        return pltpu.make_async_remote_copy(
            src_ref=gains_in,
            dst_ref=gains.at[me],
            send_sem=send_sems.at[index],
            recv_sem=recv_sems.at[base + me],
            device_id={"z": jnp.int32(s // 2), "x": jnp.int32(s % 2)},
            device_id_type=MESH,
        )

    def start_shares():
        net.local("own grad", grad_hbm, grads.at[:length])
        net.send(("share", 1), lambda: share_in, lambda: shares.at[1], to_mate)
        net.send(("share", 2), lambda: share_in, lambda: shares.at[2], to_y)
        net.send(("share", 4), lambda: share_in, lambda: shares.at[4], to_x)
        net.send(("share", 6), lambda: share_in, lambda: shares.at[6], to_xy)

    def pass_shares():
        for slot in (2, 4, 6):
            net.arrive(("share", slot), lambda: shares.at[slot])
            net.send(
                ("share", slot + 1),
                lambda slot=slot: shares.at[slot],
                lambda slot=slot: shares.at[slot + 1],
                to_mate,
            )

    quarter = wq_in.shape[1] // 4
    bounce = []
    for source, target in ((wq_in, wq), (wo_in, wo)):
        for j in range(0, source.shape[1], quarter):
            first = len(bounce) * shard_rows
            bounce.append((mate_load.at[first : first + shard_rows], source, target, j))
    wq_gather.start()
    net.local("gains", gains_in, gains.at[me])
    gain_sends = []
    for s in range(2 * depth):
        index = net.count
        net.count += 1
        gain_sends.append((s, index))
        pl.when(me != s)(lambda: gain_copy(s, index).start())
    for i, (middle, source, target, j) in enumerate(bounce):
        net.local(("in", i), source.at[:, j : j + quarter], middle)
    down_rows = down_in.shape[1]
    net.local("down in", down_in.at[expert], down_load.at[0, :down_rows])
    for gather in (gate_gather, up_gather):
        net.local((gather.name, "own"), gather.src.at[gather.own], gather.block(z, x)())
    for i, (middle, source, target, j) in enumerate(bounce):
        net.ready(("in", i))
        net.local(("out", i), middle, target.at[wq_gather.mine(), j : j + quarter])
    net.ready("down in")
    net.local("down out", down_load.at[0, :down_rows], down_gather.block(z, x)())
    wo_gather.start()
    wq_gather.pass_z(1)
    wo_gather.pass_z(1)
    gate_gather.start()
    up_gather.start()
    wo_gather.pass_z(2)
    wq_gather.pass_z(2)
    gate_gather.pass_z(1, 0)
    up_gather.pass_z(1, 0)
    wq_gather.pass_x(1)
    for k in range(3, depth):
        wo_gather.pass_z(k)
    wq_gather.pass_x(2)
    for k in range(3, depth):
        wq_gather.pass_z(k)
    for k in range(3, depth):
        wo_gather.pass_x(k)
    wo_gather.pass_x(1)
    for k in range(3, depth):
        wq_gather.pass_x(k)
    wq_gather.pass_x(0)
    wq_gather.pass_y(1)
    wo_gather.pass_x(2)
    for k in range(2, depth):
        gate_gather.pass_z(k, 0)
        up_gather.pass_z(k, 0)
    gate_gather.start_x()
    up_gather.start_x()
    wq_gather.pass_y(2)
    grad_gather.start(grad_hbm)
    start_shares()
    wo_gather.pass_y(1)
    down_gather.start_x()
    wo_gather.pass_x(0)
    down_gather.start()
    for k in range(3, depth):
        wo_gather.pass_y(k)
    for k in range(3, depth):
        wq_gather.pass_y(k)
    wo_gather.pass_y(2)
    wq_gather.finish()

    def attention_forward(wq_here, wo_here, chances):
        def project():
            for i in range(len(bounce)):
                net.ready(("out", i))
            net.local("wq here", wq, wq_here)
            gains_wide()
            project_heads()

        def gains_wide():
            for s in range(2 * depth):
                pl.when(me != s)(lambda: net.arrive(("gains", s), lambda: gains.at[s]))
            net.ready("gains")
            wide_gain = None
            for s in range(2 * depth):
                rest = jnp.zeros((8, width - gains.shape[2]), F32)
                piece = jnp.concatenate([gains[s], rest], axis=1)
                piece = piece if s == 0 else pltpu.roll(piece, s * shard_rows, axis=1)
                wide_gain = piece if wide_gain is None else wide_gain + piece
            gain_rows[...] = wide_gain

            @pl.loop(0, length // step)
            def _(i):
                here = pl.ds(pl.multiple_of(i * step, step), step)
                one = hidden[here, :].astype(F32)
                rows[here, :] = (one * inverse_rms(one) * gain_rows[0:1, :]).astype(BF16)

        def project_heads():
            net.ready("wq here")
            cos, sin = cosine[...], sine[...]
            for start in range(0, wq.shape[1], tile):
                part = dot_nn(rows[:length, :], wq_here[:, start : start + tile])
                for at in range(start, start + tile, HEAD_DIM):
                    head, one = at // HEAD_DIM, part[:, at - start : at - start + HEAD_DIM]
                    if head < HEADS:
                        queries[head * length : (head + 1) * length, :] = turn(one, cos, sin).astype(BF16)
                    elif head < HEADS + KV_HEADS:
                        at_row = (head - HEADS) * length
                        keys[at_row : at_row + length, :] = turn(one, cos, sin).astype(BF16)
                    else:
                        at_row = (head - HEADS - KV_HEADS) * length
                        values[at_row : at_row + length, :] = one.astype(BF16)

        def heads_forward():
            allowed = mask[...] > 0.0
            for head in range(HEADS):
                kv = head // GROUP
                here = slice(head * length, (head + 1) * length)
                there = slice(kv * length, (kv + 1) * length)
                scores = dot_nt(queries[here, :], keys[there, :]) * factor
                scores = jnp.where(allowed, scores, masked_score)
                terms = jnp.exp(scores - jnp.max(scores, axis=-1, keepdims=True))
                chance = terms / jnp.sum(terms, axis=-1, keepdims=True)
                chances[here, :] = chance
                attended[:, head * HEAD_DIM : (head + 1) * HEAD_DIM] = dot_nn(
                    chance.astype(BF16), values[there, :]
                ).astype(BF16)
            net.local("keep chances", chances, probability)

        def mix():
            net.local("wo here", wo, wo_here)
            net.ready("wo here")
            for start in range(0, width, tile):
                there = slice(start, start + tile)
                mixed[:, there] = hidden[:, there].astype(F32) + dot_nn(attended[...], wo_here[:, there])

            @pl.loop(0, length // step)
            def _(i):
                here = pl.ds(pl.multiple_of(i * step, step), step)
                total = mixed[here, :]
                rows[here, :] = (total * inverse_rms(total) * gain_rows[1:2, :]).astype(BF16)

        project()
        gate_gather.pass_x()
        up_gather.pass_x()
        wo_gather.finish()
        heads_forward()
        mix()
        row_gather.start(rows.at[:length, :])
        net.ready("keep chances")

    pl.run_scoped(
        attention_forward,
        pltpu.VMEM(wq.shape, BF16),
        pltpu.VMEM(wo.shape, BF16),
        pltpu.VMEM((HEADS * length, length), F32),
    )

    gate_gather.pass_z(1, 1)
    up_gather.pass_z(1, 1)
    for k in range(2, depth):
        gate_gather.pass_z(k, 1)
        up_gather.pass_z(k, 1)
    down_gather.pass_x()
    down_gather.pass_z(1, 0)
    grad_gather.forward()
    pass_shares()
    gate_gather.finish()
    up_gather.finish()
    row_gather.forward()

    def experts(down, hidden_act, both_grads, share_here):
        lane = lax.broadcasted_iota(jnp.int32, (length, LANES), 1)

        def share_of(r):
            return jnp.sum(jnp.where(lane == expert, share_here[r], 0.0), axis=1, keepdims=True)

        def first_half(first, count):
            @pl.loop(first, first + count)
            def _(r):
                here = pl.ds(pl.multiple_of(r * length, length), length)
                grads[here, :] = (share_of(r) * grads[here, :].astype(F32)).astype(BF16)
                for j in range(0, units, tile):
                    gate = dot_nn(rows[here, :], wide[:, j : j + tile])
                    up = dot_nn(rows[here, :], wide[:, units + j : units + j + tile])
                    sigmoid = 1.0 / (1.0 + jnp.exp(-gate))
                    silu = gate * sigmoid
                    hidden_act[here, j : j + tile] = (silu * up).astype(BF16)
                    both_grads[here, j : j + tile] = (
                        up * sigmoid * (1.0 + gate * (1.0 - sigmoid))
                    ).astype(BF16)
                    both_grads[here, units + j : units + j + tile] = silu.astype(BF16)

        def first_rows():
            net.local("own share", share_in, share_here.at[0])
            for slot in (1, 2, 3, 4, 5, 6, 7):
                if slot % 2:
                    net.arrive(("share", slot), lambda: shares.at[slot])
            net.local("shares", shares.at[1:], share_here.at[1:])
            row_gather.wait(1)
            grad_gather.wait(1)
            for name in ("own grad", "own share", "shares", ("gate", "own"), ("up", "own")):
                net.ready(name)
            first_half(0, 2)

        def gathered(*slots):
            for gather in (row_gather, grad_gather):
                for slot, half in slots:
                    gather.wait(slot, half)

        def left(*slots):
            for slot, half in slots:
                net.sent(("grad", slot, half))

        def middle_rows():
            gathered((3, None), (5, None))
            left((6, 0), (3, None), (6, 1), (5, None))
            first_half(2, 4)

        def last_rows():
            gathered((7, 0), (7, 1))
            left((7, 0), (7, 1))
            first_half(6, 2)

        def down_weight_grad():
            @pl.loop(0, units // tile)
            def _(i):
                at = pl.ds(pl.multiple_of(i * tile, tile), tile)
                for j in range(0, width, 512):
                    down_grad[at, j : j + 512] = dot_tn(hidden_act[:, at], grads[:, j : j + 512]).astype(BF16)

        def take_down():
            net.ready("down out")
            net.local("down here", down_full, down)
            net.ready("down here")

        def hidden_grads():
            @pl.loop(0, EXPERTS)
            def _(r):
                here = pl.ds(pl.multiple_of(r * length, length), length)
                for j in range(0, units, tile):
                    back = dot_nt(grads[here, :], down[j : j + tile, :])
                    for first in (j, units + j):
                        both_grads[here, first : first + tile] = (
                            back * both_grads[here, first : first + tile].astype(F32)
                        ).astype(BF16)

        def row_grad(slot, more=None):
            here = slice(slot * length, (slot + 1) * length)
            for j in range(0, width, 512):
                part = dot_nt(both_grads[here, :], wide[j : j + 512, :])
                if more is not None:
                    part = part + more[:, j : j + 512].astype(F32)
                grads[here, j : j + 512] = part.astype(BF16)

        def out_rows(slot, more=None):
            here = slice(slot * length, (slot + 1) * length)
            share = share_of(slot)
            for j in range(0, width, 512):
                part = share * dot_nn(hidden_act[here, :], down[:, j : j + 512])
                if more is not None:
                    part = part + more[:, j : j + 512].astype(F32)
                rows[here, j : j + 512] = part.astype(BF16)

        order = (3, 1, 2, 0)

        def give_mates(back, compute):
            if back is out_back:
                for slot, half in ((2, None), (4, None), (1, None), (6, 0), (6, 1), (3, None), (5, None), (7, 0), (7, 1)):
                    net.sent(("row", slot, half))
            for chip in order:
                compute(2 * chip + 1)
                back.to_mate(chip)

        def give_chips(back, compute):
            back.fetch(order[0])
            for i, chip in enumerate(order):
                if i + 1 < len(order):
                    back.fetch(order[i + 1])
                compute(2 * chip, back.fetched(chip))
                back.give(chip)

        def weight_grad(first):
            if first == 0:
                for one in gate_up:
                    one.sent()

            @pl.loop(0, width // tile)
            def _(i):
                at = pl.ds(pl.multiple_of(i * tile, tile), tile)
                wide[at, first : first + units] = dot_tn(
                    rows[:, at], both_grads[:, first : first + units]
                ).astype(BF16)

        first_rows()
        down_gather.pass_z(1, 1)
        middle_rows()
        for k in range(2, depth):
            down_gather.pass_z(k, 0)
        for k in range(2, depth):
            down_gather.pass_z(k, 1)
        grad_gather.forward_far()
        row_gather.forward_far()
        last_rows()
        down_weight_grad()
        down_line.start()
        down_gather.finish()
        take_down()
        hidden_grads()
        give_mates(row_back, row_grad)
        down_line.step(2)
        give_chips(row_back, row_grad)
        weight_grad(0)
        gate_line.start()
        row_back.combined()
        for s in range(3, depth):
            down_line.step(s)
        weight_grad(units)
        up_line.start()
        give_mates(out_back, out_rows)
        give_chips(out_back, out_rows)

    pl.run_scoped(
        experts,
        pltpu.VMEM((units, width), BF16),
        pltpu.VMEM((EXPERTS * length, units), BF16),
        pltpu.VMEM((EXPERTS * length, 2 * units), BF16),
        pltpu.VMEM((EXPERTS, length, LANES), F32),
    )

    def shared_out(name, line, low, dst):
        line.finish(low.at[0], low.at[1])
        share = ExpertShare(net, name, coords, low, dst)
        share.start()
        return share

    def attention_backward(weight, chances, wq_grad, upstream_two, mixed_grad, mixed_low, attended_grad, qkv_grad):
        net.local("wo again", wo, weight.at[:, :width])
        net.local("chance 0", probability.at[: GROUP * length], chances)
        wo_net = AttentionScatter(
            net, "wo sum", depth, coords, grads.at[:width, :], wo_mates, wo_chips, wo_lines, wo_total,
            mate_load, chip_load, wo_blocks, wo_low,
        )
        wq_net = AttentionScatter(
            net, "wq sum", depth, coords, wq_grad, wq_mates, wq_chips, wq_lines, wq_total,
            mate_load, chip_load, wq_blocks, wq_low,
        )

        def norm_two_back():
            row_back.total(upstream_two)
            gain_swap[0] = jnp.zeros(gain_swap.shape[1:], F32)

            @pl.loop(0, length // step)
            def _(i):
                here = pl.ds(pl.multiple_of(i * step, step), step)
                part, gain_two = norm_back(mixed[here, :], gain_rows[1:2, :], upstream_two[here, :])
                total = grad_out[here, :].astype(F32) + part
                mixed_grad[here, :] = total
                mixed_low[here, :] = total.astype(BF16)
                gain_swap[0, 1:2, :] += gain_two

        def output_weight_grad():
            row_back.sent()
            for i in range(0, width, tile):
                for j in range(0, width, 512):
                    grads[i : i + tile, j : j + 512] = dot_tn(
                        attended[:, i : i + tile], mixed_low[:, j : j + 512]
                    ).astype(BF16)

        def attended_back():
            net.ready("wo again")
            for i in range(0, width, 512):
                attended_grad[:, i : i + 512] = dot_nt(
                    mixed_low[...], weight[i : i + 512, :width]
                ).astype(BF16)
            net.local("wq again", wq, weight)

        def heads_back():
            cos, sin = cosine[...], -sine[...]
            for kv in range(KV_HEADS):
                net.ready("chance %d" % kv)
                there = slice(kv * length, (kv + 1) * length)
                value_sum = key_sum = None
                for g in range(GROUP):
                    head = kv * GROUP + g
                    here = slice(head * length, (head + 1) * length)
                    cols = slice(head * HEAD_DIM, (head + 1) * HEAD_DIM)
                    chance = chances[g * length : (g + 1) * length, :]
                    back = attended_grad[:, cols]
                    prob_grad = dot_nt(back, values[there, :])
                    value_part = dot_tn(chance.astype(BF16), back)
                    inner = jnp.sum(chance * prob_grad, axis=-1, keepdims=True)
                    score_grad = (chance * (prob_grad - inner)).astype(BF16)
                    query_grad = dot_nn(score_grad, keys[there, :]) * factor
                    key_part = dot_tn(score_grad, queries[here, :])
                    qkv_grad[:, cols] = turn(query_grad, cos, sin).astype(BF16)
                    value_sum = value_part if value_sum is None else value_sum + value_part
                    key_sum = key_part if key_sum is None else key_sum + key_part
                if kv + 1 < KV_HEADS:
                    size = GROUP * length
                    net.local("chance %d" % (kv + 1), probability.at[(kv + 1) * size : (kv + 2) * size], chances)
                first = (HEADS + kv) * HEAD_DIM
                qkv_grad[:, first : first + HEAD_DIM] = turn(key_sum * factor, cos, sin).astype(BF16)
                first = first + KV_HEADS * HEAD_DIM
                qkv_grad[:, first : first + HEAD_DIM] = value_sum.astype(BF16)

        def qkv_weight_grad():
            @pl.loop(0, length // step)
            def _(i):
                here = pl.ds(pl.multiple_of(i * step, step), step)
                one = hidden[here, :].astype(F32)
                mixed_low[here, :] = (one * inverse_rms(one) * gain_rows[0:1, :]).astype(BF16)

            for i in range(0, width, tile):
                for j in range(0, wq_grad.shape[1], 512):
                    wq_grad[i : i + tile, j : j + 512] = dot_tn(
                        mixed_low[:, i : i + tile], qkv_grad[:, j : j + 512]
                    ).astype(BF16)

        def norm_one_back():
            net.ready("wq again")
            for i in range(0, width, 512):
                upstream_two[:, i : i + 512] = dot_nt(qkv_grad[...], weight[i : i + 512, :])

            @pl.loop(0, length // step)
            def _(i):
                here = pl.ds(pl.multiple_of(i * step, step), step)
                part, gain_one = norm_back(
                    hidden[here, :].astype(F32), gain_rows[0:1, :], upstream_two[here, :]
                )
                grad_in[here, :] = (mixed_grad[here, :] + part).astype(BF16)
                gain_swap[0, 0:1, :] += gain_one

        axes = (("c", to_mate), ("x", to_x), ("y", to_y))

        def gain_start(i):
            net.send(
                ("gain", axes[i][0]),
                lambda: gain_swap.at[2 * i],
                lambda: gain_swap.at[2 * i + 1],
                axes[i][1],
            )

        def gain_add(i):
            net.arrive(("gain", axes[i][0]), lambda: gain_swap.at[2 * i + 1])
            gain_swap[2 * i + 2] = gain_swap[2 * i] + gain_swap[2 * i + 1]

        def gains_out():
            for far in range(1, depth):
                simple_send(("gain", "up", far), gain_swap.at[6], gain_swap.at[5 + 2 * far], {"z": z + far}, z + far < depth)
                simple_send(("gain", "down", far), gain_swap.at[6], gain_swap.at[6 + 2 * far], {"z": z - far}, z - far >= 0)

        def gains_in_all():
            gain_total[...] = gain_swap[6]
            for far in range(1, depth):
                for tag, slot, cond in (
                    ("up", 5 + 2 * far, z - far >= 0), ("down", 6 + 2 * far, z + far < depth)
                ):

                    def take():
                        net.arrive(("gain", tag, far), lambda: gain_swap.at[slot])
                        gain_total[...] += gain_swap[slot]

                    pl.when(cond)(take)

        norm_two_back()
        attended_back()
        down_share = shared_out("down_share", down_line, down_low, down_total)
        heads_back()
        out_back.combined()
        gate_line.step(2)
        output_weight_grad()
        wo_net.start()
        wo_net.pass_c()
        qkv_weight_grad()
        wq_net.start()
        up_line.step(2)
        wq_net.pass_c()
        norm_one_back()
        for s in range(3, depth):
            gate_line.step(s)
        wq_net.combined()
        for s in range(3, depth):
            up_line.step(s)
        gain_start(0)
        down_share.pass_near()
        wo_net.combined()
        out_back.total(layer_out, mixed)
        gain_add(0)
        wq_net.pass_chips()
        gate_share = shared_out("gate_share", gate_line, wide_low.at[0], gate_total)
        up_share = shared_out("up_share", up_line, wide_low.at[1], up_total)
        wq_net.line.step(2)
        for s in range(3, depth):
            wq_net.line.step(s)
        gain_start(1)
        wo_net.pass_chips()
        gate_share.pass_near()
        down_share.pass_far()
        wq_net.total()
        wo_net.line.step(2)
        gain_add(1)
        up_share.pass_near()
        for s in range(3, depth):
            wo_net.line.step(s)
        gate_share.pass_far()
        wo_net.total()
        gain_start(2)
        up_share.pass_far()
        wq_net.pass_y()
        wo_net.pass_y()
        gain_add(2)
        gains_out()
        gains_in_all()
        for one in (down_share, gate_share, up_share, wo_net, wq_net):
            one.finish()
        net.drain()

    pl.run_scoped(
        attention_backward,
        pltpu.VMEM(wq.shape, BF16),
        pltpu.VMEM((GROUP * length, length), F32),
        pltpu.VMEM(wq.shape, BF16),
        pltpu.VMEM((length, width), F32),
        pltpu.VMEM((length, width), F32),
        pltpu.VMEM((length, width), BF16),
        pltpu.VMEM((length, width), BF16),
        pltpu.VMEM((length, wq.shape[1]), BF16),
    )
    for s, index in gain_sends:
        pl.when(me != s)(lambda: gain_copy(s, index).wait_send())
    assert net.count <= send_sems.shape[0] and len(net.slots) <= recv_sems.shape[0]
    assert len(net.locals) <= local_sems.shape[0]


def layer_call(depth, shard_rows, hidden, grad_out, mask, cosine, sine, gains, wq_in, wo_in, gate_in, up_in, down_in, shares):
    length, width = hidden.shape
    wide, units, down_rows = wq_in.shape[1], gate_in.shape[2], down_in.shape[1]
    here, there = pl.BlockSpec(memory_space=pltpu.VMEM), pl.BlockSpec(memory_space=pltpu.HBM)

    def shape(*dims, dtype=BF16):
        return jax.ShapeDtypeStruct(dims, dtype)

    returns = [shape(4, length, width), shape(length, width), shape(2, length, width)]
    out_shape = [
        shape(length, width), shape(length, width), shape(8, width, dtype=F32),
        shape(EXPERTS, shard_rows, units), shape(EXPERTS, shard_rows, units),
        shape(EXPERTS, down_rows, width),
        shape(shard_rows, wide), shape(shard_rows, width),
        shape(width, wide), shape(width, width), shape(units, width),
        shape(EXPERTS, length, LANES, dtype=F32), shape(HEADS * length, length, dtype=F32),
        *returns, *returns,
        shape(2, depth - 1, 2 * shard_rows, units), shape(2, depth - 1, 2 * shard_rows, units),
        shape(2, depth - 1, 2 * down_rows, width),
        shape(2, width, wide // 4), shape(3, depth, shard_rows, wide // 4),
        shape(2, width, width // 4), shape(3, depth, shard_rows, width // 4),
    ]
    copies, arrivals = 74 * depth + 18, 64 * depth + 34
    return pl.pallas_call(
        functools.partial(layer_kernel, depth, shard_rows),
        out_shape=out_shape,
        in_specs=[here] * 5 + [there] * 8,
        out_specs=[here] * 3 + [there] * (len(out_shape) - 3),
        scratch_shapes=[
            pltpu.VMEM((EXPERTS * length, width), BF16),
            pltpu.VMEM((EXPERTS * length, width), BF16),
            pltpu.VMEM((width, 2 * units), BF16),
            pltpu.VMEM((units, width), BF16),
            pltpu.VMEM((4, length, width), BF16),
            pltpu.VMEM((2, 2 * shard_rows, units), BF16),
            pltpu.VMEM((2, 2 * down_rows, width), BF16),
            pltpu.VMEM((2, 2, shard_rows, units), BF16),
            pltpu.VMEM((2, down_rows, width), BF16),
            pltpu.VMEM((width, wide // 4), BF16),
            pltpu.VMEM((3, depth, shard_rows, wide // 4), BF16),
            pltpu.VMEM((2, depth - 1, shard_rows, wide // 4), BF16),
            pltpu.VMEM((2, depth - 1, shard_rows, width // 4), BF16),
            pltpu.VMEM((depth, shard_rows, wide // 4), BF16),
            pltpu.VMEM((depth, shard_rows, width // 4), BF16),
            pltpu.VMEM((shard_rows, wide // 4), BF16),
            pltpu.VMEM((shard_rows, width // 4), BF16),
            pltpu.VMEM((5 + 2 * depth, 8, width), F32),
            pltpu.VMEM((2 * depth, *gains.shape), F32),
            pltpu.VMEM((8, width), F32),
            pltpu.VMEM((HEADS * length, HEAD_DIM), BF16),
            pltpu.VMEM((KV_HEADS * length, HEAD_DIM), BF16),
            pltpu.VMEM((KV_HEADS * length, HEAD_DIM), BF16),
            pltpu.VMEM((length, width), BF16),
            pltpu.VMEM((length, width), F32),
            pltpu.SemaphoreType.DMA((copies,)),
            pltpu.SemaphoreType.DMA((arrivals,)),
            pltpu.SemaphoreType.DMA((56,)),
        ],
        compiler_params=pltpu.CompilerParams(
            collective_id=1, has_side_effects=True, vmem_limit_bytes=VMEM_LIMIT
        ),
    )(hidden, grad_out, mask, cosine, sine, gains, wq_in, wo_in, gate_in, up_in, down_in, shares, grad_out)


def rotary_tables(length, head_width):
    half_width = head_width // 2
    frequency = rotary_base ** (-2.0 * jnp.arange(half_width, dtype=jnp.float32) / head_width)
    angles = jnp.arange(length, dtype=jnp.float32)[:, None] * frequency[None, :]
    cosine, sine = jnp.cos(angles), jnp.sin(angles)
    return (
        jnp.concatenate([cosine, cosine], axis=1),
        jnp.concatenate([-sine, sine], axis=1),
    )


def make_shards(sizes):
    depth = sizes["z"]

    def shards(
        hidden_in,
        segments,
        routes,
        gate_weights,
        grad_out,
        attn_gain,
        query_weight,
        key_weight,
        value_weight,
        output_weight,
        ffn_gain,
        gate_weight,
        up_weight,
        down_weight,
    ):
        length, width = hidden_in.shape
        gains = jnp.stack([attn_gain, ffn_gain]).astype(F32)
        shard_rows = gains.shape[1]
        lanes = -(-shard_rows // LANES) * LANES
        gains = jnp.pad(gains, ((0, 6), (0, lanes - shard_rows)))
        wq_in = jnp.concatenate([query_weight, key_weight, value_weight], axis=1)
        onehot = routes[:, :, None] == jnp.arange(LANES, dtype=jnp.int32)
        shares = jnp.sum(jnp.where(onehot, gate_weights[:, :, None], 0.0), axis=1)
        segment = segments[0]
        position = jnp.arange(length, dtype=jnp.int32)
        allowed = (position[:, None] >= position[None, :]) & (segment[:, None] == segment[None, :])
        cosine, sine = rotary_tables(length, HEAD_DIM)
        layer_out, grad_in, gain_total, gate_total, up_total, down_total, wq_total, wo_total = (
            layer_call(
                depth, shard_rows, hidden_in, grad_out, allowed.astype(F32), cosine, sine, gains,
                wq_in, output_weight, gate_weight, up_weight, down_weight, shares,
            )[:8]
        )
        z, x = lax.axis_index("z"), lax.axis_index("x")
        gain_total = lax.dynamic_slice_in_dim(gain_total, (z * 2 + x) * shard_rows, shard_rows, 1)

        def whole(value):
            value = value.astype(F32)
            return lax.psum(value, "o") if sizes["o"] > 1 else value

        wq_total = whole(wq_total)
        queries_end = HEADS * HEAD_DIM
        keys_end = queries_end + KV_HEADS * HEAD_DIM
        gain_total = whole(gain_total)
        return (
            layer_out,
            grad_in,
            gain_total[0],
            wq_total[:, :queries_end],
            wq_total[:, queries_end:keys_end],
            wq_total[:, keys_end:],
            whole(wo_total),
            gain_total[1],
            whole(gate_total),
            whole(up_total),
            whole(down_total),
        )

    return shards


def solution(mesh):
    reps, shard_count = mesh.shape["rep"], mesh.shape["shard"]
    sizes = {"o": reps // 4, "y": 2, "c": 2, "z": shard_count // 2, "x": 2}
    fine = Mesh(mesh.devices.reshape(tuple(sizes.values())), tuple(sizes))
    tokens = P(("o", "y", "c", "z", "x"), None)
    first, second = P(("z", "x")), P(None, ("z", "x"), None)
    matrix = P(("z", "x"), None)
    return jax.shard_map(
        make_shards(sizes),
        mesh=fine,
        in_specs=(
            (tokens,) * 5 + (first, matrix, matrix, matrix, matrix, first) + (second,) * 3
        ),
        out_specs=(
            (tokens,) * 2 + (first, matrix, matrix, matrix, matrix, first) + (second,) * 3
        ),
        check_vma=False,
    )
```

```python
import functools

import jax
import jax.numpy as jnp
import numpy as np
from jax import lax
from jax.experimental import pallas as pl
from jax.experimental.pallas import tpu as pltpu
from jax.sharding import Mesh
from jax.sharding import PartitionSpec as P

HEADS = 12
KV_HEADS = 2
GROUP = HEADS // KV_HEADS
HEAD_DIM = 128
EXPERTS = 8
LANES = 128

epsilon = 1e-06
rotary_base = 1000000.0
masked_score = -1e30

F32 = jnp.float32
BF16 = jnp.bfloat16
MESH = pl.DeviceIdType.MESH
VMEM_LIMIT = 62 * 2**20


def dot(a, b, dims):
    return lax.dot_general(a, b, (dims, ((), ())), preferred_element_type=F32)


def dot_nn(a, b):
    return dot(a, b, ((1,), (0,)))


def dot_nt(a, b):
    return dot(a, b, ((1,), (1,)))


def dot_tn(a, b):
    return dot(a, b, ((0,), (0,)))


def guarded(cond, body):
    if cond is None:
        body()
    else:
        pl.when(cond)(body)


def both(first, second):
    if first is None:
        return second
    if second is None:
        return first
    return jnp.logical_and(first, second)


class Net:
    def __init__(self, send_sems, recv_sems, local_sems, core):
        self.send_sems, self.recv_sems, self.local_sems = send_sems, recv_sems, local_sems
        self.away = {"c": 1 - core}
        self.slots, self.sends, self.locals, self.count, self.done = {}, {}, {}, 0, set()
        self.later = []

    def slot(self, key):
        return self.slots.setdefault(key, len(self.slots))

    def send(self, key, src, dst, device, cond=None, slot=None):
        recv, index = self.slot(slot or key), self.count
        self.count += 1

        def build():
            return pltpu.make_async_remote_copy(
                src_ref=src(),
                dst_ref=dst(),
                send_sem=self.send_sems.at[index],
                recv_sem=self.recv_sems.at[recv],
                device_id=device,
                device_id_type=MESH,
            )

        guarded(cond, lambda: build().start())
        self.sends[key] = (cond, build)

    def sent(self, key):
        cond, build = self.sends.pop(key)
        guarded(cond, lambda: build().wait_send())

    def arrive(self, key, dst, cond=None):
        recv = self.slot(key)

        def wait():
            pltpu.make_async_remote_copy(
                src_ref=dst(),
                dst_ref=dst(),
                send_sem=self.send_sems.at[0],
                recv_sem=self.recv_sems.at[recv],
                device_id=self.away,
                device_id_type=MESH,
            ).wait_recv()

        guarded(cond, wait)

    def local(self, key, src, dst):
        index = len(self.locals)

        def build():
            return pltpu.make_async_copy(
                src() if callable(src) else src,
                dst() if callable(dst) else dst,
                self.local_sems.at[index],
            )

        build().start()
        self.locals[key] = build

    def ready(self, key):
        if key not in self.done:
            self.done.add(key)
            self.locals[key]().wait()

    def ready_later(self, key):
        self.later.append(key)

    def ready_all(self):
        for key in self.later:
            self.ready(key)
        self.later = []

    def drain(self):
        for key in list(self.sends):
            self.sent(key)
        for key in self.locals:
            self.ready(key)


def greet(depth, coords):
    x, y, c, z = coords
    barrier = pltpu.get_barrier_semaphore()
    for device in ({"y": 1 - y}, {"y": 1 - y, "x": 1 - x}, {"c": 1 - c}):
        pl.semaphore_signal(barrier, inc=1, device_id=device, device_id_type=MESH)
    for zi in range(depth):
        for xi in range(2):

            def tell(zi=zi, xi=xi):
                pl.semaphore_signal(
                    barrier,
                    inc=1,
                    device_id={"z": jnp.int32(zi), "x": jnp.int32(xi)},
                    device_id_type=MESH,
                )

            pl.when(jnp.logical_or(z != zi, x != xi))(tell)
    pl.semaphore_wait(barrier, 3 + 2 * depth - 1)


def along(depth, z):
    return (
        ("up", {"z": z + 1}, z + 1 < depth, lambda k: z - k, lambda k: z - k >= 0),
        ("down", {"z": z - 1}, z > 0, lambda k: z + k, lambda k: z + k < depth),
    )


class SlabGather:
    def __init__(self, net, name, coords, dst, length):
        self.net, self.name, self.dst, self.length = net, name, dst, length
        x, y, c, _ = coords
        self.to_x, self.to_y, self.to_mate = {"x": 1 - x}, {"y": 1 - y}, {"c": 1 - c}

    def slot(self, slot, half=None):
        first, size = slot * self.length, self.length
        if half is not None:
            size = size // 2
            first = first + half * size
        return self.dst.at[first : first + size, :]

    def put(self, slot, src, device, half=None):
        self.net.send(
            (self.name, slot, half), lambda: src, lambda: self.slot(slot, half), device
        )

    def wait(self, slot, half=None):
        self.net.arrive((self.name, slot, half), lambda: self.slot(slot, half))

    def start(self, src):
        self.put(2, src, self.to_y)
        self.put(4, src, self.to_x)
        self.put(1, src, self.to_mate)

    def forward(self):
        self.wait(2)
        self.put(6, self.slot(2, 0), self.to_x, 0)
        self.put(3, self.slot(2), self.to_mate)
        self.wait(4)
        self.put(6, self.slot(4, 1), self.to_y, 1)
        self.put(5, self.slot(4), self.to_mate)

    def forward_far(self):
        for half in range(2):
            self.wait(6, half)
            self.put(7, self.slot(6, half), self.to_mate, half)

    def sent(self):
        for slot, half in ((2, None), (4, None), (1, None), (6, 0), (6, 1), (3, None), (5, None), (7, 0), (7, 1)):
            self.net.sent((self.name, slot, half))


class AttentionGather:
    def __init__(self, net, name, depth, coords, src, dst, stacked=False):
        self.net, self.name, self.depth, self.src, self.dst = net, name, depth, src, dst
        self.stacked = stacked
        self.x, self.y, self.c, self.z = x, y, c, z = coords
        self.nx, self.ny, self.nc = 1 - x, 1 - y, 1 - c
        self.rows, self.columns = dst.shape[0] // (2 * depth), dst.shape[1] // 4
        self.to_x, self.to_y, self.to_mate = {"x": self.nx}, {"y": self.ny}, {"c": self.nc}
        self.ways = [
            (tag, device, more, {k: (origin(k), there(k), both(there(k), more)) for k in range(1, depth)})
            for tag, device, more, origin, there in along(depth, z)
        ]

    def lanes(self, yi, ci):
        return pl.ds(pl.multiple_of((2 * yi + ci) * self.columns, LANES), self.columns)

    def block(self, zi, xi, yi, ci):
        return lambda: self.dst.at[
            pl.ds(pl.multiple_of((zi * 2 + xi) * self.rows, self.rows), self.rows), self.lanes(yi, ci)
        ]

    def put(self, key, place, device, cond=None, src=None):
        block = self.block(*place)
        self.net.send((self.name,) + key, src or block, block, device, cond)

    def wait(self, key, place, cond=None):
        self.net.arrive((self.name,) + key, self.block(*place), cond)

    def own(self, yi):
        if self.stacked:
            first = pl.multiple_of((2 * yi + self.c) * self.rows, self.rows)
            return self.src.at[pl.ds(first, self.rows), :]
        return self.src.at[:, self.lanes(yi, self.c)]

    def mine(self):
        return pl.ds(pl.multiple_of((self.z * 2 + self.x) * self.rows, self.rows), self.rows)

    def start(self):
        x, y, c, z = self.x, self.y, self.c, self.z
        own = lambda: self.own(y)
        cross = lambda: self.own(self.ny)
        for tag, device, more, _ in self.ways:
            self.put(("z", tag, 1), (z, x, y, c), device, more, own)
        self.put(("x", "same"), (z, x, y, c), self.to_x, None, own)
        self.put(("x", "cross"), (z, x, self.ny, c), self.to_x, None, cross)

    def pass_z(self, k):
        for tag, device, _, steps in self.ways:
            origin, cond, on = steps[k]
            place = (origin, self.x, self.y, self.c)
            self.wait(("z", tag, k), place, cond)
            if k + 1 < self.depth:
                self.put(("z", tag, k + 1), place, device, on)
            self.put(("x", tag, k), place, self.to_x, cond)
            self.put(("y", tag, k, 0), place, self.to_y, cond)
            self.put(("c", tag, k, 0), place, self.to_mate, cond)

    def pass_x(self, k):
        if k == 0:
            for tag, yi in (("same", self.y), ("cross", self.ny)):
                place = (self.z, self.nx, yi, self.c)
                self.wait(("x", tag), place)
                self.put(("c", tag), place, self.to_mate)
            return
        for tag, _, _, steps in self.ways:
            origin, cond, _ = steps[k]
            place = (origin, self.nx, self.y, self.c)
            self.wait(("x", tag, k), place, cond)
            self.put(("y", tag, k, 1), place, self.to_y, cond)
            self.put(("c", tag, k, 1), place, self.to_mate, cond)

    def pass_y(self, k):
        for tag, _, _, steps in self.ways:
            origin, cond, _ = steps[k]
            for j, xi in ((0, self.x), (1, self.nx)):
                place = (origin, xi, self.ny, self.c)
                self.wait(("y", tag, k, j), place, cond)
                self.put(("c", tag, k, 2 + j), place, self.to_mate, cond)

    def finish(self):
        for tag, yi in (("same", self.y), ("cross", self.ny)):
            self.wait(("c", tag), (self.z, self.nx, yi, self.nc))
        for k in range(1, self.depth):
            for tag, _, _, steps in self.ways:
                origin, cond, _ = steps[k]
                for j, (xi, yi) in enumerate(
                    ((self.x, self.y), (self.nx, self.y), (self.x, self.ny), (self.nx, self.ny))
                ):
                    self.wait(("c", tag, k, j), (origin, xi, yi, self.nc), cond)


class ExpertGather:
    def __init__(self, net, name, depth, coords, src, dst):
        self.net, self.name, self.depth, self.coords, self.src, self.dst = (
            net, name, depth, coords, src, dst,
        )
        self.rows = src.shape[1]
        x, y, c, z = coords
        self.own, self.away = 4 * x + 2 * y + c, 4 * (1 - x) + 2 * y + c
        self.xs, self.z, self.half = (x, 1 - x), z, depth // 2
        self.to_x = {"x": self.xs[1]}
        self.ways = [
            (tag, device, more, {
                k: (origin(k), there(k), both(there(k), more), both(there(k), jnp.logical_not(more)))
                for k in range(1, depth)
            })
            for tag, device, more, origin, there in along(depth, z)
        ]

    def block(self, zi, xi):
        return lambda: self.dst.at[
            pl.ds(pl.multiple_of((zi * 2 + xi) * self.rows, self.rows), self.rows), :
        ]

    def put(self, key, place, device, cond=None, src=None):
        block = self.block(*place)
        self.net.send((self.name,) + key, src or block, block, device, cond)

    def start(self):
        x, _, _, z = self.coords
        for tag, device, more, _ in self.ways:
            self.put(("z", tag, 1, 0), (z, x), device, more, lambda: self.src.at[self.own])

    def start_x(self):
        x, _, _, z = self.coords
        self.put(("x",), (z, x), self.to_x, None, lambda: self.src.at[self.away])

    def pass_x(self):
        x, _, _, z = self.coords
        self.net.arrive((self.name, "x"), self.block(z, self.xs[1]))
        for tag, device, more, _ in self.ways:
            self.put(("z", tag, 1, 1), (z, self.xs[1]), device, more)

    def pass_z(self, k, j):
        if k + 1 >= self.depth:
            return
        for tag, device, _, steps in self.ways:
            origin, _, on, _ = steps[k]
            place = (origin, self.xs[j])
            self.net.arrive((self.name, "z", tag, k, j), self.block(*place), on)
            self.put(("z", tag, k + 1, j), place, device, on)

    def finish(self, near=None):
        for k in range(1, self.depth):
            for j in range(2):
                for tag, _, _, steps in self.ways:
                    origin, there, _, last = steps[k]
                    cond = there if k + 1 >= self.depth else last
                    if near is not None:
                        same = (origin >= self.half) == (self.z >= self.half)
                        cond = jnp.logical_and(cond, same if near else jnp.logical_not(same))
                    self.net.arrive(
                        (self.name, "z", tag, k, j), self.block(origin, self.xs[j]), cond
                    )

    def sent(self):
        self.net.sent((self.name, "x"))
        for k in range(1, self.depth):
            for j in range(2):
                for tag, _, _, _ in self.ways:
                    self.net.sent((self.name, "z", tag, k, j))


def inverse_rms(values):
    return lax.rsqrt(jnp.mean(values * values, axis=-1, keepdims=True) + epsilon)


def turn(values, cosine, sine):
    return values * cosine + pltpu.roll(values, HEAD_DIM // 2, axis=1) * sine


class SlabReturn:
    def __init__(self, net, name, coords, parts, length, mates, fars, chips, load, by_x):
        self.net, self.name, self.parts, self.length = net, name, parts, length
        self.mates, self.fars, self.landed, self.load, self.by_x = mates, fars, chips, load, by_x
        x, y, c, _ = coords
        self.to_x, self.to_y, self.to_core = {"x": 1 - x}, {"y": 1 - y}, {"c": 1 - c}

    def part(self, slot, half=None):
        first, size = slot * self.length, self.length
        if half is not None:
            size = size // 2
            first = first + half * size
        return self.parts.at[first : first + size, :]

    def half(self, half):
        return pl.ds(half * (self.length // 2), self.length // 2)

    def to_mate(self, chip):
        self.net.send(
            (self.name, "mate", chip),
            lambda: self.part(2 * chip + 1),
            lambda: self.mates.at[chip],
            self.to_core,
        )

    def fetch(self, chip):
        self.net.arrive((self.name, "mate", chip), lambda: self.mates.at[chip])
        self.net.local((self.name, "load", chip), self.mates.at[chip], self.load.at[chip])

    def fetched(self, chip):
        self.net.ready((self.name, "load", chip))
        return self.load.at[chip]

    def far(self, half, device):
        self.net.send(
            (self.name, "far", half),
            lambda: self.part(6, half),
            lambda: self.fars.at[self.half(half)],
            device,
        )

    def near(self, chip, half, device):
        self.net.send(
            (self.name, "chip", chip, half),
            lambda: self.part(2 * chip, half),
            lambda: self.landed.at[chip - 1, self.half(half)],
            device,
        )

    def give(self, chip):
        if chip == 3:
            self.far(0, self.to_x)
            self.far(1, self.to_x if self.by_x else self.to_y)
        elif chip == 1 and not self.by_x:
            self.near(1, 1, self.to_y)
        elif chip == 2:
            self.near(2, 0, self.to_x)
            if self.by_x:
                self.near(2, 1, self.to_x)

    def combined(self):
        places = ((0, 1, self.to_y), (1, 1, self.to_y) if self.by_x else (1, 2, self.to_x))
        for half, _, _ in places:
            here = self.half(half)
            self.net.arrive((self.name, "far", half), lambda: self.fars.at[here])
            self.net.local((self.name, "far", half), self.fars.at[here], self.load.at[3, here])
        for half, chip, device in places:
            self.net.ready((self.name, "far", half))
            part = self.part(2 * chip, half)
            accumulate(part, part, self.load.at[3, self.half(half)])
            self.near(chip, half, device)

    def total(self, out, *more):
        for chip in (1, 2):
            for half in range(2):
                self.net.arrive(
                    (self.name, "chip", chip, half), lambda: self.landed.at[chip - 1, self.half(half)]
                )
            self.net.local((self.name, "last", chip), self.landed.at[chip - 1], self.load.at[chip])
        for chip in (1, 2):
            self.net.ready((self.name, "last", chip))
        accumulate(out, self.part(0), self.load.at[1], self.load.at[2], *more)

    def sent(self):
        for chip in range(4):
            self.net.sent((self.name, "mate", chip))
        for half in range(2):
            self.net.sent((self.name, "far", half))
            for chip in (1, 2):
                self.net.sent((self.name, "chip", chip, half))


def accumulate(out, *terms):
    total, columns = out.shape
    step = 32 if columns < 1024 and total % 32 == 0 else 16

    @pl.loop(0, total // step)
    def _(i):
        here = pl.ds(pl.multiple_of(i * step, step), step)
        value = terms[0][here, :].astype(F32)
        for term in terms[1:]:
            value = value + term[here, :].astype(F32)
        out[here, :] = value.astype(out.dtype)


def clear(out):
    @pl.loop(0, out.shape[0] // 16)
    def _(i):
        here = pl.ds(pl.multiple_of(i * 16, 16), 16)
        out[here, :] = jnp.zeros((16, out.shape[1]), out.dtype)


class LineScatter:
    def __init__(self, net, name, depth, z, block, landed, load):
        self.net, self.name, self.depth, self.z = net, name, depth, z
        self.block, self.landed, self.load = block, landed, load

        steps = range(1, depth)
        up = {s: (depth - s + z, z == 0, jnp.logical_and(z >= 1, z <= s - 1)) for s in steps}
        back = depth - 1 - z
        down = {s: (z + s - depth, back == 0, jnp.logical_and(back >= 1, back <= s - 1)) for s in steps}
        self.ways = (
            ("up", {"z": z + 1}, 0, z >= 1, z < 1, up),
            ("down", {"z": z - 1}, 1, back >= 1, back < 1, down),
        )

    def send(self, key, device, way, s, t, cond):
        self.net.send(
            key,
            lambda: self.block(t),
            lambda: self.landed.at[way, s - 1],
            device,
            cond,
            slot=(self.name, key[1], s),
        )

    def start(self):
        for s in range(1, self.depth):
            for tag, device, way, _, _, steps in self.ways:
                target, first, _ = steps[s]
                self.send((self.name, tag, s), device, way, s, target, first)

    def term(self, way, s):
        return self.landed.at[way, s - 1] if self.load is None else self.load.at[way]

    def take(self, tag, way, s):
        self.net.arrive((self.name, tag, s), lambda: self.landed.at[way, s - 1])
        if self.load is not None:
            pltpu.sync_copy(self.landed.at[way, s - 1], self.load.at[way])

    def step(self, s):
        for tag, device, way, _, _, steps in self.ways:
            t, _, cond = steps[s]

            def body():
                self.take(tag, way, s - 1)
                block = self.block(t)
                accumulate(block, block, self.term(way, s - 1))

            pl.when(cond)(body)
            self.send((self.name, tag, s, "on"), device, way, s, t, cond)

    def finish(self, *outs):
        last = self.depth - 1
        for tag, _, way, fed, unfed, _ in self.ways:
            pl.when(fed)(lambda: self.take(tag, way, last))
            pl.when(unfed)(lambda: clear(self.term(way, last)))
        rows = outs[0].shape[0]
        for i, out in enumerate(outs):
            here = pl.ds(i * rows, rows)
            accumulate(
                out, *(term.at[here, :] for term in (self.block(self.z), self.term(0, last), self.term(1, last)))
            )


class ExpertShare:
    def __init__(self, net, name, coords, result, dst):
        self.net, self.name, self.coords, self.result, self.dst = net, name, coords, result, dst
        x, y, c, _ = coords
        self.across = {4: {"x": 1 - x}, 2: {"y": 1 - y}, 1: {"c": 1 - c}}
        self.expert = 4 * x + 2 * y + c

    def place(self, flip):
        x, y, c, _ = self.coords
        fx = 1 - x if flip & 4 else x
        fy = 1 - y if flip & 2 else y
        fc = 1 - c if flip & 1 else c
        return self.dst.at[4 * fx + 2 * fy + fc]

    def put(self, flip, src, axis):
        self.net.send(
            (self.name, axis | flip), src, lambda: self.place(flip), self.across[axis]
        )

    def on(self, flip, axis):
        self.put(flip, lambda: self.place(flip), axis)

    def wait(self, flip):
        self.net.arrive((self.name, flip), lambda: self.place(flip))

    def start(self):
        x = self.coords[0]
        self.put(0, lambda: self.result.at[1 - x], 4)
        self.put(0, lambda: self.result.at[x], 2)
        self.put(0, lambda: self.result.at[x], 1)
        self.net.local(
            (self.name, "own"), lambda: self.result.at[x], lambda: self.dst.at[self.expert]
        )

    def pass_near(self):
        self.wait(4)
        self.on(4, 2)
        self.on(4, 1)
        self.wait(2)
        self.on(2, 1)

    def pass_far(self):
        self.wait(6)
        self.on(6, 1)

    def finish(self):
        self.net.ready((self.name, "own"))
        for flip in (1, 5, 3, 7):
            self.wait(flip)


class AttentionScatter:
    def __init__(self, net, name, depth, coords, grad, part, by_x, mates, chips, lines, dst, mate_load, chip_load, blocks, low):
        self.net, self.name, self.depth, self.coords = net, name, depth, coords
        self.grad, self.compute, self.mates, self.chips, self.dst = grad, part, mates, chips, dst
        self.blocks, self.low, self.by_x = blocks, low, by_x
        self.columns = columns = grad.shape[1] // 4
        self.rows = grad.shape[0] // (2 * depth)
        self.mate_load, self.chip_load = mate_load.at[:, :columns], chip_load.at[:, :, :, :columns]
        x, y, c, z = coords
        self.to_x, self.to_y, self.to_core = {"x": 1 - x}, {"y": 1 - y}, {"c": 1 - c}
        self.ys = (y, 1 - y)
        self.line = LineScatter(net, name + " line", depth, z, lambda t: blocks.at[t], lines, None)

    def lanes(self, yi, ci):
        return pl.ds(pl.multiple_of((2 * yi + ci) * self.columns, LANES), self.columns)

    def quarter(self, yi, ci):
        return self.dst.at[:, self.lanes(yi, ci)]

    def part(self, zi, xi, yi):
        rows = pl.ds(pl.multiple_of((zi * 2 + xi) * self.rows, self.rows), self.rows)
        return self.grad.at[rows, self.lanes(yi, self.coords[2])]

    def fill(self, lanes, more=None):
        tile = 256
        for i in range(0, self.grad.shape[0], tile):
            value = self.compute(i, tile, lanes)
            if more is not None:
                value = value + more[i : i + tile, :].astype(F32)
            self.grad[i : i + tile, lanes] = value.astype(BF16)

    def start(self):
        c = self.coords[2]
        for j in (1, 0):
            lanes = self.lanes(self.ys[j], 1 - c)
            self.fill(lanes)
            self.net.send(
                (self.name, "c", j),
                lambda lanes=lanes: self.grad.at[:, lanes],
                lambda j=j: self.mates.at[j],
                self.to_core,
            )

    def fetch(self, j):
        self.net.arrive((self.name, "c", j), lambda: self.mates.at[j])
        self.net.local((self.name, "mate", j), self.mates.at[j], self.mate_load)

    def add_mate(self, j):
        self.net.ready((self.name, "mate", j))
        self.fill(self.lanes(self.ys[j], self.coords[2]), self.mate_load)

    def to_chip(self, key, zi, xi, yi, slot, device):
        self.net.send(
            (self.name, key, zi),
            lambda: self.part(zi, xi, yi),
            lambda: self.chips.at[slot, zi],
            device,
        )

    def pass_c(self):
        x, y, c, z = self.coords
        half = 0 if self.by_x else self.depth // 2
        self.add_mate(1)
        self.fetch(0)
        for zi in range(self.depth):
            far_by_x = self.by_x or zi < self.depth // 2
            self.to_chip("far", zi, 1 - x, self.ys[1], 2, self.to_x if far_by_x else self.to_y)
        if not self.by_x:
            for zi in range(self.depth // 2, self.depth):
                self.to_chip("y", zi, x, self.ys[1], 0, self.to_y)
        self.add_mate(0)
        for zi in range(self.depth if self.by_x else self.depth // 2):
            self.to_chip("x", zi, 1 - x, y, 1, self.to_x)

    def combined(self):
        x, y, c, z = self.coords
        half = self.depth // 2
        places = (
            (0, "y", x, self.ys[1], 0, self.to_y),
            (half, "y", x, self.ys[1], 0, self.to_y) if self.by_x else (half, "x", 1 - x, y, 1, self.to_x),
        )
        for first, _, _, _, _, _ in places:
            for zi in range(first, first + half):
                self.net.arrive((self.name, "far", zi), lambda: self.chips.at[2, zi])
            here = pl.ds(first, half)
            self.net.local((self.name, "far", first), self.chips.at[2, here], self.chip_load.at[2, here])
        for first, key, xi, yi, slot, device in places:
            self.net.ready((self.name, "far", first))
            for zi in range(first, first + half):
                part = self.part(zi, xi, yi)
                accumulate(part, part, self.chip_load.at[2, zi])
                self.to_chip(key, zi, xi, yi, slot, device)

    def pass_chips(self):
        x, y, c, z = self.coords
        for slot, key in ((1, "x"), (0, "y")):
            for zi in range(self.depth):
                self.net.arrive((self.name, key, zi), lambda: self.chips.at[slot, zi])
            self.net.local((self.name, "load", slot), self.chips.at[slot], self.chip_load.at[slot])
        for slot in range(2):
            self.net.ready((self.name, "load", slot))
        for zi in range(self.depth):
            accumulate(
                self.blocks.at[zi],
                self.part(zi, x, y),
                self.chip_load.at[0, zi],
                self.chip_load.at[1, zi],
            )
        self.line.start()

    def total(self):
        x, y, c, z = self.coords
        self.line.finish(self.low)
        self.net.local((self.name, "own"), self.low, self.quarter(y, c))
        for key, device in (("ty", self.to_y), ("tc", self.to_core)):
            self.net.send((self.name, key), lambda: self.low, lambda: self.quarter(y, c), device)

    def pass_y(self):
        x, y, c, z = self.coords
        there = lambda: self.quarter(1 - y, c)
        self.net.arrive((self.name, "ty"), there)
        self.net.send((self.name, "tyc"), there, there, self.to_core)

    def finish(self):
        x, y, c, z = self.coords
        self.net.ready((self.name, "own"))
        self.net.arrive((self.name, "tc"), lambda: self.quarter(y, 1 - c))
        self.net.arrive((self.name, "tyc"), lambda: self.quarter(1 - y, 1 - c))


def norm_back(values, gain, upstream):
    inverse = inverse_rms(values)
    normal = values * inverse
    gain_grad = jnp.sum(upstream * normal, axis=0, keepdims=True)
    scaled = upstream * gain
    return (
        inverse * (scaled - normal * jnp.mean(scaled * normal, axis=-1, keepdims=True)),
        gain_grad,
    )


def layer_kernel(depth, shard_rows, *refs):
    (
        hidden, grad_out, segment, routes, weights, cosine, sine,
        gains_in, query_in, key_in, value_in, wo_in, gate_in, up_in, down_in, grad_hbm,
        layer_out, grad_in, gain_total,
        gate_total, up_total, down_total, wq_total, wo_total,
        wq, wo, down_full, shares, probability,
        row_mates, row_fars, row_chips, out_mates, out_fars, out_chips,
        gate_lines, up_lines, down_lines, wq_mates, wq_chips, wo_mates, wo_chips,
        rows, grads, wide, down_grad, returned, wide_load, down_load, wide_low, down_low,
        mate_load, chip_load, wq_lines, wo_lines, wq_blocks, wo_blocks, wq_low, wo_low, gain_swap,
        gains, gain_rows, queries, keys, values, attended, mixed, share_in,
        send_sems, recv_sems, local_sems,
    ) = refs
    coords = x, y, c, z = tuple(lax.axis_index(n) for n in ("x", "y", "c", "z"))
    expert = 4 * x + 2 * y + c
    net = Net(send_sems, recv_sems, local_sems, c)
    length, width = hidden.shape
    units = gate_in.shape[2]
    tile, step = 256, 16
    factor = HEAD_DIM ** (-0.5)
    greet(depth, coords)

    wq_gather = AttentionGather(net, "wq", depth, coords, mate_load, wq, True)
    wo_gather = AttentionGather(net, "wo", depth, coords, wo_in, wo)
    gate_gather = ExpertGather(net, "gate", depth, coords, gate_in, wide.at[:, :units])
    up_gather = ExpertGather(net, "up", depth, coords, up_in, wide.at[:, units:])
    down_gather = ExpertGather(net, "down", depth, coords, down_in, down_full)
    gate_up = (gate_gather, up_gather)
    row_gather = SlabGather(net, "row", coords, rows, length)
    grad_gather = SlabGather(net, "grad", coords, grads, length)

    def wide_block(first):
        size = 2 * shard_rows
        return lambda t: wide.at[
            pl.ds(pl.multiple_of(t * size, size), size), pl.ds(first, units)
        ]

    def down_block(t):
        size = 2 * (units // (2 * depth))
        return down_grad.at[pl.ds(pl.multiple_of(t * size, size), size), :]

    gate_line = LineScatter(net, "gate line", depth, z, wide_block(0), gate_lines, wide_load)
    up_line = LineScatter(net, "up line", depth, z, wide_block(units), up_lines, wide_load)
    down_line = LineScatter(net, "down line", depth, z, down_block, down_lines, down_load)
    row_back = SlabReturn(net, "row back", coords, grads, length, row_mates, row_fars, row_chips, returned, False)

    down_share = ExpertShare(net, "down sum", coords, down_low, down_total)
    gate_share = ExpertShare(net, "gate sum", coords, wide_low.at[0], gate_total)
    up_share = ExpertShare(net, "up sum", coords, wide_low.at[1], up_total)

    def finish_line(line, share):
        line.finish(share.result.at[0], share.result.at[1])
        share.start()

    def simple_send(key, source, target, device, cond=None):
        net.send(key, lambda: source, lambda: target, device, cond)

    to_mate, to_x, to_y = {"c": 1 - c}, {"x": 1 - x}, {"y": 1 - y}
    to_xy = {**to_x, **to_y}

    me = z * 2 + x
    base = [net.slot(("gains", s)) for s in range(2 * depth)][0]

    def gain_copy(s, index):
        return pltpu.make_async_remote_copy(
            src_ref=gains_in,
            dst_ref=gains.at[me],
            send_sem=send_sems.at[index],
            recv_sem=recv_sems.at[base + me],
            device_id={"z": jnp.int32(s // 2), "x": jnp.int32(s % 2)},
            device_id_type=MESH,
        )

    def start_shares():
        net.local("own grad", grad_hbm, grads.at[:length])
        net.send(("share", 1), lambda: share_in, lambda: shares.at[1], to_mate)
        net.send(("share", 2), lambda: share_in, lambda: shares.at[2], to_y)
        net.send(("share", 4), lambda: share_in, lambda: shares.at[4], to_x)
        net.send(("share", 6), lambda: share_in, lambda: shares.at[6], to_xy)

    def pass_shares():
        for slot in (2, 4, 6):
            net.arrive(("share", slot), lambda: shares.at[slot])
            net.send(
                ("share", slot + 1),
                lambda slot=slot: shares.at[slot],
                lambda slot=slot: shares.at[slot + 1],
                to_mate,
            )

    quarter = wq.shape[1] // 4
    query_end, key_end = query_in.shape[1], query_in.shape[1] + key_in.shape[1]
    bounce = []

    def middle(i, first, size):
        return mate_load.at[i * shard_rows : (i + 1) * shard_rows, first : first + size]

    for i, j in enumerate(range(0, wq.shape[1], quarter)):
        for source, begin, end in (
            (query_in, 0, query_end), (key_in, query_end, key_end), (value_in, key_end, wq.shape[1])
        ):
            low, high = max(j, begin), min(j + quarter, end)
            if low < high:
                net.local(("in", i, low), source.at[:, low - begin : high - begin], middle(i, low - j, high - low))
                net.ready_later(("in", i, low))
        bounce.append((middle(i, 0, quarter), wq, j))
    for j in range(0, width, quarter):
        i = len(bounce)
        net.local(("in", i, 0), wo_in.at[:, j : j + quarter], middle(i, 0, quarter))
        net.ready_later(("in", i, 0))
        bounce.append((middle(i, 0, quarter), wo, j))
    net.ready_all()
    wq_gather.start()
    net.local("gains", gains_in, gains.at[me])
    gain_sends = []
    for s in range(2 * depth):
        index = net.count
        net.count += 1
        gain_sends.append((s, index))
        pl.when(me != s)(lambda: gain_copy(s, index).start())
    down_rows = down_in.shape[1]
    net.local("down in", down_in.at[expert], down_load.at[0, :down_rows])
    for gather in (gate_gather, up_gather):
        net.local((gather.name, "own"), gather.src.at[gather.own], gather.block(z, x)())
    for i, (source, target, j) in enumerate(bounce):
        net.local(("out", i), source, target.at[wq_gather.mine(), j : j + quarter])
    names = lax.broadcasted_iota(jnp.int32, (LANES, length), 0)
    share = jnp.zeros((LANES, length), F32)
    for i in range(routes.shape[0]):
        share = share + jnp.where(names == routes[i : i + 1, :], weights[i : i + 1, :], 0.0)
    share_in[...] = share.T
    net.ready("down in")
    net.local("down out", down_load.at[0, :down_rows], down_gather.block(z, x)())
    wo_gather.start()
    wq_gather.pass_z(1)
    wo_gather.pass_z(1)
    wq_gather.pass_z(2)
    gate_gather.start()
    up_gather.start()
    gate_gather.start_x()
    up_gather.start_x()
    wq_gather.pass_x(0)
    wq_gather.pass_x(1)
    gate_gather.pass_z(1, 0)
    up_gather.pass_z(1, 0)
    wo_gather.pass_x(1)
    wq_gather.pass_y(1)
    wo_gather.pass_z(2)
    for k in range(2, depth):
        gate_gather.pass_z(k, 0)
        up_gather.pass_z(k, 0)
    for k in range(3, depth):
        wq_gather.pass_z(k)
    wq_gather.pass_x(2)
    gate_gather.pass_x()
    up_gather.pass_x()
    for k in range(3, depth):
        wq_gather.pass_x(k)
    wq_gather.pass_y(2)
    for k in range(3, depth):
        wo_gather.pass_z(k)
    for k in range(3, depth):
        wq_gather.pass_y(k)
    wo_gather.pass_y(1)
    wq_gather.finish()
    for k in range(3, depth):
        wo_gather.pass_x(k)
    down_gather.start_x()
    down_gather.start()
    wo_gather.pass_x(2)
    grad_gather.start(grad_hbm)
    start_shares()

    def attention_forward(wq_here, wo_here, chances):
        def project():
            for i in range(len(bounce)):
                net.ready(("out", i))
            for key in (("z", "up", 1), ("z", "down", 1), ("x", "same"), ("x", "cross")):
                net.sent(("wq",) + key)
            net.local("wq here", wq, wq_here)
            gains_wide()
            project_heads()

        def gains_wide():
            for s in range(2 * depth):
                pl.when(me != s)(lambda: net.arrive(("gains", s), lambda: gains.at[s]))
            net.ready("gains")
            wide_gain = None
            for s in range(2 * depth):
                rest = jnp.zeros((8, width - gains.shape[2]), F32)
                piece = jnp.concatenate([gains[s], rest], axis=1)
                piece = piece if s == 0 else pltpu.roll(piece, s * shard_rows, axis=1)
                wide_gain = piece if wide_gain is None else wide_gain + piece
            gain_rows[...] = wide_gain

            @pl.loop(0, length // step)
            def _(i):
                here = pl.ds(pl.multiple_of(i * step, step), step)
                one = hidden[here, :].astype(F32)
                rows[here, :] = (one * inverse_rms(one) * gain_rows[0:1, :]).astype(BF16)

        def project_heads():
            net.ready("wq here")
            cos, sin = cosine[...], sine[...]
            for start in range(0, wq.shape[1], tile):
                part = dot_nn(rows[:length, :], wq_here[:, start : start + tile])
                for at in range(start, start + tile, HEAD_DIM):
                    head, one = at // HEAD_DIM, part[:, at - start : at - start + HEAD_DIM]
                    if head < HEADS:
                        queries[head * length : (head + 1) * length, :] = turn(one, cos, sin).astype(BF16)
                    elif head < HEADS + KV_HEADS:
                        at_row = (head - HEADS) * length
                        keys[at_row : at_row + length, :] = turn(one, cos, sin).astype(BF16)
                    else:
                        at_row = (head - HEADS - KV_HEADS) * length
                        values[at_row : at_row + length, :] = one.astype(BF16)

        def heads_forward():
            across = jnp.broadcast_to(segment[...].astype(F32), (length, length))
            order = lax.broadcasted_iota(jnp.int32, (length, length), 0)
            allowed = (across == across.T) & (order >= lax.broadcasted_iota(jnp.int32, (length, length), 1))
            for head in range(HEADS):
                kv = head // GROUP
                here = slice(head * length, (head + 1) * length)
                there = slice(kv * length, (kv + 1) * length)
                scores = dot_nt(queries[here, :], keys[there, :]) * factor
                scores = jnp.where(allowed, scores, masked_score)
                terms = jnp.exp(scores - jnp.max(scores, axis=-1, keepdims=True))
                chance = terms / jnp.sum(terms, axis=-1, keepdims=True)
                chances[here, :] = chance
                attended[:, head * HEAD_DIM : (head + 1) * HEAD_DIM] = dot_nn(
                    chance.astype(BF16), values[there, :]
                ).astype(BF16)
            net.local("keep chances", chances, probability)

        def mix():
            net.local("wo here", wo, wo_here)
            net.ready("wo here")
            for start in range(0, width, tile):
                there = slice(start, start + tile)
                mixed[:, there] = hidden[:, there].astype(F32) + dot_nn(attended[...], wo_here[:, there])

            @pl.loop(0, length // step)
            def _(i):
                here = pl.ds(pl.multiple_of(i * step, step), step)
                total = mixed[here, :]
                rows[here, :] = (total * inverse_rms(total) * gain_rows[1:2, :]).astype(BF16)

        project()
        wo_gather.pass_x(0)
        for k in range(3, depth):
            wo_gather.pass_y(k)
        heads_forward()
        wo_gather.pass_y(2)
        gate_gather.pass_z(1, 1)
        up_gather.pass_z(1, 1)
        wo_gather.finish()
        mix()
        row_gather.start(rows.at[:length, :])
        net.ready("keep chances")

    pl.run_scoped(
        attention_forward,
        pltpu.VMEM(wq.shape, BF16),
        pltpu.VMEM(wo.shape, BF16),
        pltpu.VMEM((HEADS * length, length), F32),
    )

    for k in range(2, depth):
        gate_gather.pass_z(k, 1)
        up_gather.pass_z(k, 1)
    down_gather.pass_x()
    grad_gather.forward()
    pass_shares()
    down_gather.pass_z(1, 1)
    row_gather.forward()
    down_gather.pass_z(1, 0)
    for k in range(2, depth):
        down_gather.pass_z(k, 1)
    gate_gather.finish()
    up_gather.finish()

    def experts(down, hidden_act, both_grads, share_here, parts_out):
        out_back = SlabReturn(net, "out back", coords, parts_out, length, out_mates, out_fars, out_chips, returned, False)
        lane = lax.broadcasted_iota(jnp.int32, (length, LANES), 1)

        def share_of(r):
            return jnp.sum(jnp.where(lane == expert, share_here[r], 0.0), axis=1, keepdims=True)

        def first_half(first, count):
            @pl.loop(first, first + count)
            def _(r):
                here = pl.ds(pl.multiple_of(r * length, length), length)
                grads[here, :] = (share_of(r) * grads[here, :].astype(F32)).astype(BF16)
                for j in range(0, units, tile):
                    gate = dot_nn(rows[here, :], wide[:, j : j + tile])
                    up = dot_nn(rows[here, :], wide[:, units + j : units + j + tile])
                    sigmoid = 1.0 / (1.0 + jnp.exp(-gate))
                    silu = gate * sigmoid
                    hidden_act[here, j : j + tile] = (silu * up).astype(BF16)
                    both_grads[here, j : j + tile] = (
                        up * sigmoid * (1.0 + gate * (1.0 - sigmoid))
                    ).astype(BF16)
                    both_grads[here, units + j : units + j + tile] = silu.astype(BF16)

        def first_rows():
            net.local("own share", share_in, share_here.at[0])
            for slot in (1, 2, 3, 4, 5, 6, 7):
                if slot % 2:
                    net.arrive(("share", slot), lambda: shares.at[slot])
            net.local("shares", shares.at[1:], share_here.at[1:])
            row_gather.wait(1)
            grad_gather.wait(1)
            for name in ("own grad", "own share", "shares", ("gate", "own"), ("up", "own")):
                net.ready(name)
            first_half(0, 2)

        def gathered(*slots):
            for gather in (row_gather, grad_gather):
                for slot, half in slots:
                    gather.wait(slot, half)

        def left(*slots):
            for slot, half in slots:
                net.sent(("grad", slot, half))

        def middle_rows():
            gathered((3, None), (5, None))
            left((6, 0), (3, None), (6, 1), (5, None))
            first_half(2, 4)

        def last_rows():
            gathered((7, 0), (7, 1))
            left((7, 0), (7, 1))
            first_half(6, 2)

        def down_weight_grad():
            @pl.loop(0, units // tile)
            def _(i):
                at = pl.ds(pl.multiple_of(i * tile, tile), tile)
                for j in range(0, width, 512):
                    down_grad[at, j : j + 512] = dot_tn(hidden_act[:, at], grads[:, j : j + 512]).astype(BF16)

        near_half = units // 2 * (z >= depth // 2).astype(jnp.int32)
        near = pl.multiple_of(near_half, LANES)
        far = pl.multiple_of(units // 2 - near_half, LANES)

        def take_down(first):
            if first is near:
                net.ready("down out")
            here = pl.ds(first, units // 2)
            name = "down near" if first is near else "down far"
            net.local(name, down_full.at[here, :], down.at[here, :])
            net.ready(name)

        def hidden_grads(first):
            @pl.loop(0, EXPERTS)
            def _(r):
                here = pl.ds(pl.multiple_of(r * length, length), length)
                for j in range(0, units // 2, tile):
                    size = min(tile, units // 2 - j)
                    at = pl.multiple_of(first + j, LANES)
                    back = dot_nt(grads[here, :], down[pl.ds(at, size), :])
                    for lane_first in (at, pl.multiple_of(units + at, LANES)):
                        lanes = pl.ds(lane_first, size)
                        both_grads[here, lanes] = (
                            back * both_grads[here, lanes].astype(F32)
                        ).astype(BF16)

        def row_grad(slot, more=None):
            here = slice(slot * length, (slot + 1) * length)
            for j in range(0, width, 512):
                part = dot_nt(both_grads[here, :], wide[j : j + 512, :])
                if more is not None:
                    part = part + more[:, j : j + 512].astype(F32)
                grads[here, j : j + 512] = part.astype(BF16)

        def out_rows(slot, more=None):
            here = slice(slot * length, (slot + 1) * length)
            share = share_of(slot)
            for j in range(0, width, 512):
                part = share * dot_nn(hidden_act[here, :], down[:, j : j + 512])
                if more is not None:
                    part = part + more[:, j : j + 512].astype(F32)
                parts_out[here, j : j + 512] = part.astype(BF16)

        order = (3, 1, 2, 0)

        def give_mates(back, compute):
            for chip in order:
                compute(2 * chip + 1)
                back.to_mate(chip)

        def give_chips(back, compute):
            back.fetch(order[0])
            for i, chip in enumerate(order):
                if i + 1 < len(order):
                    back.fetch(order[i + 1])
                compute(2 * chip, back.fetched(chip))
                back.give(chip)

        def weight_grad(first):
            if first == 0:
                for one in gate_up:
                    one.sent()

            @pl.loop(0, width // tile)
            def _(i):
                at = pl.ds(pl.multiple_of(i * tile, tile), tile)
                wide[at, first : first + units] = dot_tn(
                    rows[:, at], both_grads[:, first : first + units]
                ).astype(BF16)

        first_rows()
        grad_gather.forward_far()
        middle_rows()
        row_gather.forward_far()
        for k in range(2, depth):
            down_gather.pass_z(k, 0)
        down_gather.finish(True)
        take_down(near)
        last_rows()
        down_weight_grad()
        down_line.start()
        hidden_grads(near)
        down_gather.finish(False)
        take_down(far)
        give_mates(out_back, out_rows)
        give_chips(out_back, out_rows)
        hidden_grads(far)
        down_line.step(2)
        give_mates(row_back, row_grad)
        give_chips(row_back, row_grad)
        out_back.combined()
        for s in range(3, depth):
            down_line.step(s)
        weight_grad(0)
        gate_line.start()
        row_back.combined()
        weight_grad(units)
        up_line.start()
        finish_line(down_line, down_share)
        out_back.total(layer_out, mixed)
        gate_line.step(2)
        out_back.sent()

    pl.run_scoped(
        experts,
        pltpu.VMEM((units, width), BF16),
        pltpu.VMEM((EXPERTS * length, units), BF16),
        pltpu.VMEM((EXPERTS * length, 2 * units), BF16),
        pltpu.VMEM((EXPERTS, length, LANES), F32),
        pltpu.VMEM((EXPERTS * length, width), BF16),
    )

    def attention_backward(weight, chances, wq_grad, upstream_two, mixed_grad, mixed_low, attended_grad, qkv_grad):
        net.local("wo again", wo, weight.at[:, :width])
        net.local("chance 0", probability.at[: GROUP * length], chances)
        def output_part(first, size, lanes):
            return dot_tn(attended[:, first : first + size], mixed_low[:, lanes])

        def qkv_part(first, size, lanes):
            return dot_tn(attended_grad[:, first : first + size], qkv_grad[:, lanes])

        wo_net = AttentionScatter(
            net, "wo sum", depth, coords, grads.at[:width, :], output_part, False, wo_mates, wo_chips, wo_lines,
            wo_total, mate_load, chip_load, wo_blocks, wo_low,
        )
        wq_net = AttentionScatter(
            net, "wq sum", depth, coords, wq_grad, qkv_part, False, wq_mates, wq_chips, wq_lines,
            wq_total, mate_load, chip_load, wq_blocks, wq_low,
        )

        def norm_two_back():
            row_back.total(upstream_two)
            gain_swap[0] = jnp.zeros(gain_swap.shape[1:], F32)

            @pl.loop(0, length // step)
            def _(i):
                here = pl.ds(pl.multiple_of(i * step, step), step)
                part, gain_two = norm_back(mixed[here, :], gain_rows[1:2, :], upstream_two[here, :])
                total = grad_out[here, :].astype(F32) + part
                mixed_grad[here, :] = total
                mixed_low[here, :] = total.astype(BF16)
                gain_swap[0, 1:2, :] += gain_two

        def attended_back():
            net.ready("wo again")
            for i in range(0, width, 512):
                attended_grad[:, i : i + 512] = dot_nt(
                    mixed_low[...], weight[i : i + 512, :width]
                ).astype(BF16)
            net.local("wq again", wq, weight)

        def heads_back():
            cos, sin = cosine[...], -sine[...]
            for kv in range(KV_HEADS):
                net.ready("chance %d" % kv)
                there = slice(kv * length, (kv + 1) * length)
                value_sum = key_sum = None
                for g in range(GROUP):
                    head = kv * GROUP + g
                    here = slice(head * length, (head + 1) * length)
                    cols = slice(head * HEAD_DIM, (head + 1) * HEAD_DIM)
                    chance = chances[g * length : (g + 1) * length, :]
                    back = attended_grad[:, cols]
                    prob_grad = dot_nt(back, values[there, :])
                    value_part = dot_tn(chance.astype(BF16), back)
                    inner = jnp.sum(chance * prob_grad, axis=-1, keepdims=True)
                    score_grad = (chance * (prob_grad - inner)).astype(BF16)
                    query_grad = dot_nn(score_grad, keys[there, :]) * factor
                    key_part = dot_tn(score_grad, queries[here, :])
                    qkv_grad[:, cols] = turn(query_grad, cos, sin).astype(BF16)
                    value_sum = value_part if value_sum is None else value_sum + value_part
                    key_sum = key_part if key_sum is None else key_sum + key_part
                if kv + 1 < KV_HEADS:
                    size = GROUP * length
                    net.local("chance %d" % (kv + 1), probability.at[(kv + 1) * size : (kv + 2) * size], chances)
                first = (HEADS + kv) * HEAD_DIM
                qkv_grad[:, first : first + HEAD_DIM] = turn(key_sum * factor, cos, sin).astype(BF16)
                first = first + KV_HEADS * HEAD_DIM
                qkv_grad[:, first : first + HEAD_DIM] = value_sum.astype(BF16)

        def norm_again():
            @pl.loop(0, length // step)
            def _(i):
                here = pl.ds(pl.multiple_of(i * step, step), step)
                one = hidden[here, :].astype(F32)
                attended_grad[here, :] = (one * inverse_rms(one) * gain_rows[0:1, :]).astype(BF16)

        def norm_one_back():
            net.ready("wq again")
            for i in range(0, width, 512):
                upstream_two[:, i : i + 512] = dot_nt(qkv_grad[...], weight[i : i + 512, :])

            @pl.loop(0, length // step)
            def _(i):
                here = pl.ds(pl.multiple_of(i * step, step), step)
                part, gain_one = norm_back(
                    hidden[here, :].astype(F32), gain_rows[0:1, :], upstream_two[here, :]
                )
                grad_in[here, :] = (mixed_grad[here, :] + part).astype(BF16)
                gain_swap[0, 0:1, :] += gain_one

        axes = (("c", to_mate), ("x", to_x), ("y", to_y))

        def gain_start(i):
            net.send(
                ("gain", axes[i][0]),
                lambda: gain_swap.at[2 * i],
                lambda: gain_swap.at[2 * i + 1],
                axes[i][1],
            )

        def gain_add(i):
            net.arrive(("gain", axes[i][0]), lambda: gain_swap.at[2 * i + 1])
            gain_swap[2 * i + 2] = gain_swap[2 * i] + gain_swap[2 * i + 1]

        def gains_out():
            for far in range(1, depth):
                simple_send(("gain", "up", far), gain_swap.at[6], gain_swap.at[5 + 2 * far], {"z": z + far}, z + far < depth)
                simple_send(("gain", "down", far), gain_swap.at[6], gain_swap.at[6 + 2 * far], {"z": z - far}, z - far >= 0)

        def gains_in_all():
            for far in range(1, depth):
                for tag, slot, cond in (
                    ("up", 5 + 2 * far, z - far >= 0), ("down", 6 + 2 * far, z + far < depth)
                ):

                    def take():
                        net.arrive(("gain", tag, far), lambda: gain_swap.at[slot])
                        gain_swap[6] += gain_swap[slot]

                    pl.when(cond)(take)
            for s in range(2 * depth):

                def pick(s=s):
                    value = gain_swap[6]
                    if s:
                        value = pltpu.roll(value, width - s * shard_rows, axis=1)
                    gain_total[...] = value[:, : gain_total.shape[1]]

                pl.when(me == s)(pick)

        norm_two_back()
        row_back.sent()
        wo_net.start()
        down_share.pass_near()
        attended_back()
        wo_net.fetch(1)
        wo_net.pass_c()
        heads_back()
        norm_again()
        wq_net.start()
        for s in range(3, depth):
            gate_line.step(s)
        wo_net.combined()
        wq_net.fetch(1)
        wq_net.pass_c()
        up_line.step(2)
        norm_one_back()
        gain_start(0)
        wq_net.combined()
        gain_add(0)
        for s in range(3, depth):
            up_line.step(s)
        finish_line(gate_line, gate_share)
        wo_net.pass_chips()
        gain_start(1)
        down_share.pass_far()
        wq_net.pass_chips()
        wo_net.line.step(2)
        gate_share.pass_near()
        finish_line(up_line, up_share)
        for s in range(3, depth):
            wo_net.line.step(s)
        wq_net.line.step(2)
        wo_net.total()
        gate_share.pass_far()
        up_share.pass_near()
        for s in range(3, depth):
            wq_net.line.step(s)
        wo_net.pass_y()
        gain_add(1)
        wq_net.total()
        up_share.pass_far()
        gain_start(2)
        wq_net.pass_y()
        gain_add(2)
        gains_out()
        for key in [key for key in net.sends if key[0] == "gain"]:
            net.sent(key)
        gains_in_all()
        for one in (down_share, gate_share, up_share, wo_net, wq_net):
            one.finish()
        net.drain()

    pl.run_scoped(
        attention_backward,
        pltpu.VMEM(wq.shape, BF16),
        pltpu.VMEM((GROUP * length, length), F32),
        pltpu.VMEM(wq.shape, BF16),
        pltpu.VMEM((length, width), F32),
        pltpu.VMEM((length, width), F32),
        pltpu.VMEM((length, width), BF16),
        pltpu.VMEM((length, width), BF16),
        pltpu.VMEM((length, wq.shape[1]), BF16),
    )
    for s, index in gain_sends:
        pl.when(me != s)(lambda: gain_copy(s, index).wait_send())
    assert net.count <= send_sems.shape[0] and len(net.slots) <= recv_sems.shape[0]
    assert len(net.locals) <= local_sems.shape[0]


def layer_call(
    depth, shard_rows, hidden, grad_out, segments, routes, weights, cosine, sine, gains, query_in, key_in,
    value_in, wo_in, gate_in, up_in, down_in,
):
    length, width = hidden.shape
    wide = query_in.shape[1] + key_in.shape[1] + value_in.shape[1]
    units, down_rows = gate_in.shape[2], down_in.shape[1]
    here, there = pl.BlockSpec(memory_space=pltpu.VMEM), pl.BlockSpec(memory_space=pltpu.HBM)

    def shape(*dims, dtype=BF16):
        return jax.ShapeDtypeStruct(dims, dtype)

    returns = [shape(4, length, width), shape(length, width), shape(2, length, width)]
    out_shape = [
        shape(length, width), shape(length, width), shape(*gains.shape, dtype=F32),
        shape(EXPERTS, shard_rows, units), shape(EXPERTS, shard_rows, units),
        shape(EXPERTS, down_rows, width),
        shape(shard_rows, wide), shape(shard_rows, width),
        shape(width, wide), shape(width, width), shape(units, width),
        shape(EXPERTS, length, LANES, dtype=F32), shape(HEADS * length, length, dtype=F32),
        *returns, *returns,
        shape(2, depth - 1, 2 * shard_rows, units), shape(2, depth - 1, 2 * shard_rows, units),
        shape(2, depth - 1, 2 * down_rows, width),
        shape(2, width, wide // 4), shape(3, depth, shard_rows, wide // 4),
        shape(2, width, width // 4), shape(3, depth, shard_rows, width // 4),
    ]
    copies, arrivals = 74 * depth + 14, 64 * depth + 34
    return pl.pallas_call(
        functools.partial(layer_kernel, depth, shard_rows),
        out_shape=out_shape,
        in_specs=[here] * 7 + [there] * 9,
        out_specs=[here] * 3 + [there] * (len(out_shape) - 3),
        scratch_shapes=[
            pltpu.VMEM((EXPERTS * length, width), BF16),
            pltpu.VMEM((EXPERTS * length, width), BF16),
            pltpu.VMEM((width, 2 * units), BF16),
            pltpu.VMEM((units, width), BF16),
            pltpu.VMEM((4, length, width), BF16),
            pltpu.VMEM((2, 2 * shard_rows, units), BF16),
            pltpu.VMEM((2, 2 * down_rows, width), BF16),
            pltpu.VMEM((2, 2, shard_rows, units), BF16),
            pltpu.VMEM((2, down_rows, width), BF16),
            pltpu.VMEM((width, wide // 4), BF16),
            pltpu.VMEM((3, depth, shard_rows, wide // 4), BF16),
            pltpu.VMEM((2, depth - 1, shard_rows, wide // 4), BF16),
            pltpu.VMEM((2, depth - 1, shard_rows, width // 4), BF16),
            pltpu.VMEM((depth, shard_rows, wide // 4), BF16),
            pltpu.VMEM((depth, shard_rows, width // 4), BF16),
            pltpu.VMEM((shard_rows, wide // 4), BF16),
            pltpu.VMEM((shard_rows, width // 4), BF16),
            pltpu.VMEM((5 + 2 * depth, 8, width), F32),
            pltpu.VMEM((2 * depth, *gains.shape), F32),
            pltpu.VMEM((8, width), F32),
            pltpu.VMEM((HEADS * length, HEAD_DIM), BF16),
            pltpu.VMEM((KV_HEADS * length, HEAD_DIM), BF16),
            pltpu.VMEM((KV_HEADS * length, HEAD_DIM), BF16),
            pltpu.VMEM((length, width), BF16),
            pltpu.VMEM((length, width), F32),
            pltpu.VMEM((length, LANES), F32),
            pltpu.SemaphoreType.DMA((copies,)),
            pltpu.SemaphoreType.DMA((arrivals,)),
            pltpu.SemaphoreType.DMA((68,)),
        ],
        compiler_params=pltpu.CompilerParams(
            collective_id=1, has_side_effects=True, vmem_limit_bytes=VMEM_LIMIT
        ),
    )(
        hidden, grad_out, segments, routes, weights, cosine, sine, gains, query_in, key_in, value_in, wo_in,
        gate_in, up_in, down_in, grad_out,
    )


def rotary_tables(length, head_width):
    half_width = head_width // 2
    frequency = rotary_base ** (-2.0 * np.arange(half_width, dtype=np.float32) / head_width)
    angles = np.arange(length, dtype=np.float32)[:, None] * frequency.astype(np.float32)[None, :]
    cosine, sine = np.cos(angles), np.sin(angles)
    return (
        np.concatenate([cosine, cosine], axis=1).astype(np.float32),
        np.concatenate([-sine, sine], axis=1).astype(np.float32),
    )


def widen_kernel(*refs):
    wq, wo, gate, up, down, layer, grad = refs[:7]
    query_out, key_out, value_out, wo_out, gate_out, up_out, down_out, layer_out, grad_out = refs[7:16]
    low, high, same, in_sems, out_sems, same_sems = refs[16:]
    queries_end = HEADS * HEAD_DIM
    kv = KV_HEADS * HEAD_DIM
    rows = wq.shape[0]
    width = wo.shape[1]
    pieces = [
        (wq.at[:, :queries_end], query_out),
        (wo, wo_out),
    ]
    for source, target in ((gate, gate_out), (up, up_out), (down, down_out)):
        for e in range(EXPERTS):
            pieces.append((source.at[e], target.at[e]))
    pieces.append((wq.at[:, queries_end : queries_end + kv], key_out))
    pieces.append((wq.at[:, queries_end + kv :], value_out))
    depth = low.shape[0]

    def place(buffer, i):
        r, n = pieces[i][0].shape
        return buffer.at[i % depth, :r, :n]

    def read(i):
        return pltpu.make_async_copy(pieces[i][0], place(low, i), in_sems.at[i % depth])

    def write(i):
        return pltpu.make_async_copy(place(high, i), pieces[i][1], out_sems.at[i % depth])

    passed = ((layer, layer_out), (grad, grad_out))

    def take(i):
        return pltpu.make_async_copy(passed[i][0], same.at[i], same_sems.at[i])

    def put(i):
        return pltpu.make_async_copy(same.at[i], passed[i][1], same_sems.at[2 + i])

    for i in range(depth - 1):
        read(i).start()
    for i in range(2):
        take(i).start()
    for i in range(len(pieces)):
        if i + depth - 1 < len(pieces):
            read(i + depth - 1).start()
        read(i).wait()
        if i >= depth:
            write(i - depth).wait()
        place(high, i)[...] = place(low, i)[...].astype(F32)
        write(i).start()
        if i in (depth, depth + 1):
            take(i - depth).wait()
            put(i - depth).start()
    for i in range(2):
        put(i).wait()
    for i in range(max(0, len(pieces) - depth), len(pieces)):
        write(i).wait()


def widen_call(wq, wo, gate, up, down, layer, grad):
    rows, width = wo.shape
    there = pl.BlockSpec(memory_space=pltpu.HBM)
    queries_end, kv = HEADS * HEAD_DIM, KV_HEADS * HEAD_DIM

    def shape(*dims):
        return jax.ShapeDtypeStruct(dims, F32)

    buffers = 6
    return pl.pallas_call(
        widen_kernel,
        out_shape=[
            shape(rows, queries_end), shape(rows, kv), shape(rows, kv), shape(*wo.shape),
            shape(*gate.shape), shape(*up.shape), shape(*down.shape),
            jax.ShapeDtypeStruct(layer.shape, layer.dtype), jax.ShapeDtypeStruct(grad.shape, grad.dtype),
        ],
        in_specs=[there] * 7,
        out_specs=[there] * 9,
        scratch_shapes=[
            pltpu.VMEM((buffers, rows, width), BF16),
            pltpu.VMEM((buffers, rows, width), F32),
            pltpu.VMEM((2, *layer.shape), BF16),
            pltpu.SemaphoreType.DMA((buffers,)),
            pltpu.SemaphoreType.DMA((buffers,)),
            pltpu.SemaphoreType.DMA((4,)),
        ],
        compiler_params=pltpu.CompilerParams(vmem_limit_bytes=VMEM_LIMIT),
    )(wq, wo, gate, up, down, layer, grad)


def make_shards(sizes):
    depth = sizes["z"]

    def shards(
        hidden_in,
        segments,
        routes,
        gate_weights,
        grad_out,
        attn_gain,
        query_weight,
        key_weight,
        value_weight,
        output_weight,
        ffn_gain,
        gate_weight,
        up_weight,
        down_weight,
    ):
        length, width = hidden_in.shape
        shard_rows = attn_gain.shape[0]
        spare = -(-shard_rows // LANES) * LANES - shard_rows
        first, second = (jnp.pad(gain.astype(F32), (0, spare))[None, :] for gain in (attn_gain, ffn_gain))
        place = lax.broadcasted_iota(jnp.int32, (8, shard_rows + spare), 0)
        gains = jnp.where(place == 0, first, jnp.where(place == 1, second, 0.0))
        cosine, sine = rotary_tables(length, HEAD_DIM)
        layer_out, grad_in, gain_total, gate_total, up_total, down_total, wq_total, wo_total = (
            layer_call(
                depth, shard_rows, hidden_in, grad_out, segments, routes.T, gate_weights.T, cosine, sine,
                gains, query_weight, key_weight, value_weight, output_weight, gate_weight, up_weight,
                down_weight,
            )[:8]
        )
        def whole(value):
            return lax.psum(value.astype(F32), "o") if sizes["o"] > 1 else value

        wq_total = whole(wq_total)
        queries_end = HEADS * HEAD_DIM
        keys_end = queries_end + KV_HEADS * HEAD_DIM
        gain_total = gain_total[:, :shard_rows]
        gain_total = whole(gain_total)
        parts = (wq_total, whole(wo_total), whole(gate_total), whole(up_total), whole(down_total))
        if sizes["o"] == 1:
            *parts, layer_out, grad_in = widen_call(*parts, layer_out, grad_in)
        else:
            parts = (
                wq_total[:, :queries_end], wq_total[:, queries_end:keys_end], wq_total[:, keys_end:], *parts[1:]
            )
        query_grad, key_grad, value_grad, output_grad, gate_grad, up_grad, down_grad = parts
        return (
            layer_out,
            grad_in,
            gain_total[0],
            query_grad,
            key_grad,
            value_grad,
            output_grad,
            gain_total[1],
            gate_grad,
            up_grad,
            down_grad,
        )

    return shards


def solution(mesh):
    reps, shard_count = mesh.shape["rep"], mesh.shape["shard"]
    sizes = {"o": reps // 4, "y": 2, "c": 2, "z": shard_count // 2, "x": 2}
    fine = Mesh(mesh.devices.reshape(tuple(sizes.values())), tuple(sizes))
    tokens = P(("o", "y", "c", "z", "x"), None)
    first, second = P(("z", "x")), P(None, ("z", "x"), None)
    matrix = P(("z", "x"), None)
    return jax.shard_map(
        make_shards(sizes),
        mesh=fine,
        in_specs=(
            (tokens,) * 5 + (first, matrix, matrix, matrix, matrix, first) + (second,) * 3
        ),
        out_specs=(
            (tokens,) * 2 + (first, matrix, matrix, matrix, matrix, first) + (second,) * 3
        ),
        check_vma=False,
    )
```

```python
import functools

import jax
import jax.numpy as jnp
import numpy as np
from jax import lax
from jax.experimental import pallas as pl
from jax.experimental.pallas import tpu as pltpu
from jax.sharding import Mesh
from jax.sharding import PartitionSpec as P

HEADS = 12
KV_HEADS = 2
GROUP = HEADS // KV_HEADS
HEAD_DIM = 128
EXPERTS = 8
LANES = 128

epsilon = 1e-06
rotary_base = 1000000.0
masked_score = -1e30

F32 = jnp.float32
BF16 = jnp.bfloat16
MESH = pl.DeviceIdType.MESH
VMEM_LIMIT = 63 * 2**20


def dot(a, b, dims):
    return lax.dot_general(a, b, (dims, ((), ())), preferred_element_type=F32)


def dot_nn(a, b):
    return dot(a, b, ((1,), (0,)))


def dot_nt(a, b):
    return dot(a, b, ((1,), (1,)))


def dot_tn(a, b):
    return dot(a, b, ((0,), (0,)))


def guarded(cond, body):
    if cond is None:
        body()
    else:
        pl.when(cond)(body)


def both(first, second):
    if first is None:
        return second
    if second is None:
        return first
    return jnp.logical_and(first, second)


class Net:
    def __init__(self, send_sems, recv_sems, local_sems, core):
        self.send_sems, self.recv_sems, self.local_sems = send_sems, recv_sems, local_sems
        self.away = {"c": 1 - core}
        self.slots, self.sends, self.locals, self.count, self.done = {}, {}, {}, 0, set()
        self.later = []

    def slot(self, key):
        return self.slots.setdefault(key, len(self.slots))

    def send(self, key, src, dst, device, cond=None, slot=None):
        recv, index = self.slot(slot or key), self.count
        self.count += 1

        def build():
            return pltpu.make_async_remote_copy(
                src_ref=src(),
                dst_ref=dst(),
                send_sem=self.send_sems.at[index],
                recv_sem=self.recv_sems.at[recv],
                device_id=device,
                device_id_type=MESH,
            )

        guarded(cond, lambda: build().start())
        self.sends[key] = (cond, build)

    def sent(self, key):
        cond, build = self.sends.pop(key)
        guarded(cond, lambda: build().wait_send())

    def arrive(self, key, dst, cond=None):
        recv = self.slot(key)

        def wait():
            pltpu.make_async_remote_copy(
                src_ref=dst(),
                dst_ref=dst(),
                send_sem=self.send_sems.at[0],
                recv_sem=self.recv_sems.at[recv],
                device_id=self.away,
                device_id_type=MESH,
            ).wait_recv()

        guarded(cond, wait)

    def local(self, key, src, dst):
        index = len(self.locals)

        def build():
            return pltpu.make_async_copy(
                src() if callable(src) else src,
                dst() if callable(dst) else dst,
                self.local_sems.at[index],
            )

        build().start()
        self.locals[key] = build

    def ready(self, key):
        if key not in self.done:
            self.done.add(key)
            self.locals[key]().wait()

    def ready_later(self, key):
        self.later.append(key)

    def ready_all(self):
        for key in self.later:
            self.ready(key)
        self.later = []

    def drain(self):
        for key in list(self.sends):
            self.sent(key)
        for key in self.locals:
            self.ready(key)


def greet(depth, coords):
    x, y, c, z = coords
    barrier = pltpu.get_barrier_semaphore()
    for device in ({"y": 1 - y}, {"y": 1 - y, "x": 1 - x}, {"c": 1 - c}):
        pl.semaphore_signal(barrier, inc=1, device_id=device, device_id_type=MESH)
    for zi in range(depth):
        for xi in range(2):

            def tell(zi=zi, xi=xi):
                pl.semaphore_signal(
                    barrier,
                    inc=1,
                    device_id={"z": jnp.int32(zi), "x": jnp.int32(xi)},
                    device_id_type=MESH,
                )

            pl.when(jnp.logical_or(z != zi, x != xi))(tell)
    pl.semaphore_wait(barrier, 3 + 2 * depth - 1)


def along(depth, z):
    return (
        ("up", {"z": z + 1}, z + 1 < depth, lambda k: z - k, lambda k: z - k >= 0),
        ("down", {"z": z - 1}, z > 0, lambda k: z + k, lambda k: z + k < depth),
    )


class SlabGather:
    def __init__(self, net, name, coords, dst, length):
        self.net, self.name, self.dst, self.length = net, name, dst, length
        x, y, c, _ = coords
        self.to_x, self.to_y, self.to_mate = {"x": 1 - x}, {"y": 1 - y}, {"c": 1 - c}

    def slot(self, slot, half=None):
        first, size = slot * self.length, self.length
        if half is not None:
            size = size // 2
            first = first + half * size
        return self.dst.at[first : first + size, :]

    def put(self, slot, src, device, half=None):
        self.net.send(
            (self.name, slot, half), lambda: src, lambda: self.slot(slot, half), device
        )

    def wait(self, slot, half=None):
        self.net.arrive((self.name, slot, half), lambda: self.slot(slot, half))

    def start(self, src):
        self.put(2, src, self.to_y)
        self.put(4, src, self.to_x)
        self.put(1, src, self.to_mate)

    def forward(self):
        self.wait(2)
        self.put(6, self.slot(2, 0), self.to_x, 0)
        self.put(3, self.slot(2), self.to_mate)
        self.wait(4)
        self.put(6, self.slot(4, 1), self.to_y, 1)
        self.put(5, self.slot(4), self.to_mate)

    def forward_far(self):
        for half in range(2):
            self.wait(6, half)
            self.put(7, self.slot(6, half), self.to_mate, half)

    def sent(self):
        for slot, half in ((2, None), (4, None), (1, None), (6, 0), (6, 1), (3, None), (5, None), (7, 0), (7, 1)):
            self.net.sent((self.name, slot, half))


class AttentionGather:
    def __init__(self, net, name, depth, coords, src, dst, stacked=False):
        self.net, self.name, self.depth, self.src, self.dst = net, name, depth, src, dst
        self.stacked = stacked
        self.x, self.y, self.c, self.z = x, y, c, z = coords
        self.nx, self.ny, self.nc = 1 - x, 1 - y, 1 - c
        self.rows, self.columns = dst.shape[0] // (2 * depth), dst.shape[1] // 4
        self.to_x, self.to_y, self.to_mate = {"x": self.nx}, {"y": self.ny}, {"c": self.nc}
        self.ways = [
            (tag, device, more, {k: (origin(k), there(k), both(there(k), more)) for k in range(1, depth)})
            for tag, device, more, origin, there in along(depth, z)
        ]

    def lanes(self, yi, ci):
        return pl.ds(pl.multiple_of((2 * yi + ci) * self.columns, LANES), self.columns)

    def block(self, zi, xi, yi, ci):
        return lambda: self.dst.at[
            pl.ds(pl.multiple_of((zi * 2 + xi) * self.rows, self.rows), self.rows), self.lanes(yi, ci)
        ]

    def put(self, key, place, device, cond=None, src=None):
        block = self.block(*place)
        self.net.send((self.name,) + key, src or block, block, device, cond)

    def wait(self, key, place, cond=None):
        self.net.arrive((self.name,) + key, self.block(*place), cond)

    def own(self, yi):
        if self.stacked:
            first = pl.multiple_of((2 * yi + self.c) * self.rows, self.rows)
            return self.src.at[pl.ds(first, self.rows), :]
        return self.src.at[:, self.lanes(yi, self.c)]

    def mine(self):
        return pl.ds(pl.multiple_of((self.z * 2 + self.x) * self.rows, self.rows), self.rows)

    def start(self):
        x, y, c, z = self.x, self.y, self.c, self.z
        own = lambda: self.own(y)
        cross = lambda: self.own(self.ny)
        for tag, device, more, _ in self.ways:
            self.put(("z", tag, 1), (z, x, y, c), device, more, own)
        self.put(("x", "same"), (z, x, y, c), self.to_x, None, own)
        self.put(("x", "cross"), (z, x, self.ny, c), self.to_x, None, cross)

    def pass_z(self, k):
        for tag, device, _, steps in self.ways:
            origin, cond, on = steps[k]
            place = (origin, self.x, self.y, self.c)
            self.wait(("z", tag, k), place, cond)
            if k + 1 < self.depth:
                self.put(("z", tag, k + 1), place, device, on)
            self.put(("x", tag, k), place, self.to_x, cond)
            self.put(("y", tag, k, 0), place, self.to_y, cond)
            self.put(("c", tag, k, 0), place, self.to_mate, cond)

    def pass_x(self, k):
        if k == 0:
            for tag, yi in (("same", self.y), ("cross", self.ny)):
                place = (self.z, self.nx, yi, self.c)
                self.wait(("x", tag), place)
                self.put(("c", tag), place, self.to_mate)
            return
        for tag, _, _, steps in self.ways:
            origin, cond, _ = steps[k]
            place = (origin, self.nx, self.y, self.c)
            self.wait(("x", tag, k), place, cond)
            self.put(("y", tag, k, 1), place, self.to_y, cond)
            self.put(("c", tag, k, 1), place, self.to_mate, cond)

    def pass_y(self, k):
        for tag, _, _, steps in self.ways:
            origin, cond, _ = steps[k]
            for j, xi in ((0, self.x), (1, self.nx)):
                place = (origin, xi, self.ny, self.c)
                self.wait(("y", tag, k, j), place, cond)
                self.put(("c", tag, k, 2 + j), place, self.to_mate, cond)

    def finish(self):
        for tag, yi in (("same", self.y), ("cross", self.ny)):
            self.wait(("c", tag), (self.z, self.nx, yi, self.nc))
        for k in range(1, self.depth):
            for tag, _, _, steps in self.ways:
                origin, cond, _ = steps[k]
                for j, (xi, yi) in enumerate(
                    ((self.x, self.y), (self.nx, self.y), (self.x, self.ny), (self.nx, self.ny))
                ):
                    self.wait(("c", tag, k, j), (origin, xi, yi, self.nc), cond)


class ExpertGather:
    def __init__(self, net, name, depth, coords, src, dst):
        self.net, self.name, self.depth, self.coords, self.src, self.dst = (
            net, name, depth, coords, src, dst,
        )
        self.rows = src.shape[1]
        x, y, c, z = coords
        self.own, self.away = 4 * x + 2 * y + c, 4 * (1 - x) + 2 * y + c
        self.xs, self.z, self.half = (x, 1 - x), z, depth // 2
        self.to_x = {"x": self.xs[1]}
        self.ways = [
            (tag, device, more, {
                k: (origin(k), there(k), both(there(k), more), both(there(k), jnp.logical_not(more)))
                for k in range(1, depth)
            })
            for tag, device, more, origin, there in along(depth, z)
        ]

    def block(self, zi, xi):
        return lambda: self.dst.at[
            pl.ds(pl.multiple_of((zi * 2 + xi) * self.rows, self.rows), self.rows), :
        ]

    def put(self, key, place, device, cond=None, src=None):
        block = self.block(*place)
        self.net.send((self.name,) + key, src or block, block, device, cond)

    def start(self):
        x, _, _, z = self.coords
        for tag, device, more, _ in self.ways:
            self.put(("z", tag, 1, 0), (z, x), device, more, lambda: self.src.at[self.own])

    def start_x(self):
        x, _, _, z = self.coords
        self.put(("x",), (z, x), self.to_x, None, lambda: self.src.at[self.away])

    def pass_x(self):
        x, _, _, z = self.coords
        self.net.arrive((self.name, "x"), self.block(z, self.xs[1]))
        for tag, device, more, _ in self.ways:
            self.put(("z", tag, 1, 1), (z, self.xs[1]), device, more)

    def pass_z(self, k, j):
        if k + 1 >= self.depth:
            return
        for tag, device, _, steps in self.ways:
            origin, _, on, _ = steps[k]
            place = (origin, self.xs[j])
            self.net.arrive((self.name, "z", tag, k, j), self.block(*place), on)
            self.put(("z", tag, k + 1, j), place, device, on)

    def finish(self, near=None):
        for k in range(1, self.depth):
            for j in range(2):
                for tag, _, _, steps in self.ways:
                    origin, there, _, last = steps[k]
                    cond = there if k + 1 >= self.depth else last
                    if near is not None:
                        same = (origin >= self.half) == (self.z >= self.half)
                        cond = jnp.logical_and(cond, same if near else jnp.logical_not(same))
                    self.net.arrive(
                        (self.name, "z", tag, k, j), self.block(origin, self.xs[j]), cond
                    )

    def sent(self):
        self.net.sent((self.name, "x"))
        for k in range(1, self.depth):
            for j in range(2):
                for tag, _, _, _ in self.ways:
                    self.net.sent((self.name, "z", tag, k, j))


def inverse_rms(values):
    return lax.rsqrt(jnp.mean(values * values, axis=-1, keepdims=True) + epsilon)


def turn(values, cosine, sine):
    return values * cosine + pltpu.roll(values, HEAD_DIM // 2, axis=1) * sine


class SlabReturn:
    def __init__(self, net, name, coords, parts, length, mates, fars, chips, load, by_x):
        self.net, self.name, self.parts, self.length = net, name, parts, length
        self.mates, self.fars, self.landed, self.load, self.by_x = mates, fars, chips, load, by_x
        x, y, c, _ = coords
        self.to_x, self.to_y, self.to_core = {"x": 1 - x}, {"y": 1 - y}, {"c": 1 - c}

    def part(self, slot, half=None):
        first, size = slot * self.length, self.length
        if half is not None:
            size = size // 2
            first = first + half * size
        return self.parts.at[first : first + size, :]

    def half(self, half):
        return pl.ds(half * (self.length // 2), self.length // 2)

    def to_mate(self, chip):
        self.net.send(
            (self.name, "mate", chip),
            lambda: self.part(2 * chip + 1),
            lambda: self.mates.at[chip],
            self.to_core,
        )

    def fetch(self, chip):
        self.net.arrive((self.name, "mate", chip), lambda: self.mates.at[chip])
        self.net.local((self.name, "load", chip), self.mates.at[chip], self.load.at[chip])

    def fetched(self, chip):
        self.net.ready((self.name, "load", chip))
        return self.load.at[chip]

    def far(self, half, device):
        self.net.send(
            (self.name, "far", half),
            lambda: self.part(6, half),
            lambda: self.fars.at[self.half(half)],
            device,
        )

    def near(self, chip, half, device):
        self.net.send(
            (self.name, "chip", chip, half),
            lambda: self.part(2 * chip, half),
            lambda: self.landed.at[chip - 1, self.half(half)],
            device,
        )

    def give(self, chip):
        if chip == 3:
            self.far(0, self.to_x)
            self.far(1, self.to_x if self.by_x else self.to_y)
        elif chip == 1 and not self.by_x:
            self.near(1, 1, self.to_y)
        elif chip == 2:
            self.near(2, 0, self.to_x)
            if self.by_x:
                self.near(2, 1, self.to_x)

    def combined(self):
        places = ((0, 1, self.to_y), (1, 1, self.to_y) if self.by_x else (1, 2, self.to_x))
        for half, _, _ in places:
            here = self.half(half)
            self.net.arrive((self.name, "far", half), lambda: self.fars.at[here])
            self.net.local((self.name, "far", half), self.fars.at[here], self.load.at[3, here])
        for half, chip, device in places:
            self.net.ready((self.name, "far", half))
            part = self.part(2 * chip, half)
            accumulate(part, part, self.load.at[3, self.half(half)])
            self.near(chip, half, device)

    def total(self, out, *more):
        for chip in (1, 2):
            for half in range(2):
                self.net.arrive(
                    (self.name, "chip", chip, half), lambda: self.landed.at[chip - 1, self.half(half)]
                )
            self.net.local((self.name, "last", chip), self.landed.at[chip - 1], self.load.at[chip])
        for chip in (1, 2):
            self.net.ready((self.name, "last", chip))
        accumulate(out, self.part(0), self.load.at[1], self.load.at[2], *more)

    def sent(self):
        for chip in range(4):
            self.net.sent((self.name, "mate", chip))
        for half in range(2):
            self.net.sent((self.name, "far", half))
            for chip in (1, 2):
                self.net.sent((self.name, "chip", chip, half))


def accumulate(out, *terms):
    total, columns = out.shape
    step = 32 if columns < 1024 and total % 32 == 0 else 16

    @pl.loop(0, total // step)
    def _(i):
        here = pl.ds(pl.multiple_of(i * step, step), step)
        value = terms[0][here, :].astype(F32)
        for term in terms[1:]:
            value = value + term[here, :].astype(F32)
        out[here, :] = value.astype(out.dtype)


def clear(out):
    @pl.loop(0, out.shape[0] // 16)
    def _(i):
        here = pl.ds(pl.multiple_of(i * 16, 16), 16)
        out[here, :] = jnp.zeros((16, out.shape[1]), out.dtype)


class LineScatter:
    def __init__(self, net, name, depth, z, block, landed, load):
        self.net, self.name, self.depth, self.z = net, name, depth, z
        self.block, self.landed, self.load = block, landed, load

        steps = range(1, depth)
        up = {s: (depth - s + z, z == 0, jnp.logical_and(z >= 1, z <= s - 1)) for s in steps}
        back = depth - 1 - z
        down = {s: (z + s - depth, back == 0, jnp.logical_and(back >= 1, back <= s - 1)) for s in steps}
        self.ways = (
            ("up", {"z": z + 1}, 0, z >= 1, z < 1, up),
            ("down", {"z": z - 1}, 1, back >= 1, back < 1, down),
        )

    def send(self, key, device, way, s, t, cond):
        self.net.send(
            key,
            lambda: self.block(t),
            lambda: self.landed.at[way, s - 1],
            device,
            cond,
            slot=(self.name, key[1], s),
        )

    def start_step(self, s):
        for tag, device, way, _, _, steps in self.ways:
            target, first, _ = steps[s]
            self.send((self.name, tag, s), device, way, s, target, first)

    def start(self):
        for s in range(1, self.depth):
            self.start_step(s)

    def term(self, way, s):
        return self.landed.at[way, s - 1] if self.load is None else self.load.at[way]

    def take(self, tag, way, s):
        self.net.arrive((self.name, tag, s), lambda: self.landed.at[way, s - 1])
        if self.load is not None:
            pltpu.sync_copy(self.landed.at[way, s - 1], self.load.at[way])

    def step(self, s):
        for tag, device, way, _, _, steps in self.ways:
            t, _, cond = steps[s]

            def body():
                self.take(tag, way, s - 1)
                block = self.block(t)
                accumulate(block, block, self.term(way, s - 1))

            pl.when(cond)(body)
            self.send((self.name, tag, s, "on"), device, way, s, t, cond)

    def finish(self, *outs):
        last = self.depth - 1
        for tag, _, way, fed, unfed, _ in self.ways:
            pl.when(fed)(lambda: self.take(tag, way, last))
            pl.when(unfed)(lambda: clear(self.term(way, last)))
        rows = outs[0].shape[0]
        for i, out in enumerate(outs):
            here = pl.ds(i * rows, rows)
            accumulate(
                out, *(term.at[here, :] for term in (self.block(self.z), self.term(0, last), self.term(1, last)))
            )


class ExpertShare:
    def __init__(self, net, name, coords, result, dst):
        self.net, self.name, self.coords, self.result, self.dst = net, name, coords, result, dst
        x, y, c, _ = coords
        self.across = {4: {"x": 1 - x}, 2: {"y": 1 - y}, 1: {"c": 1 - c}}
        self.expert = 4 * x + 2 * y + c

    def place(self, flip):
        x, y, c, _ = self.coords
        fx = 1 - x if flip & 4 else x
        fy = 1 - y if flip & 2 else y
        fc = 1 - c if flip & 1 else c
        return self.dst.at[4 * fx + 2 * fy + fc]

    def put(self, flip, src, axis):
        self.net.send(
            (self.name, axis | flip), src, lambda: self.place(flip), self.across[axis]
        )

    def on(self, flip, axis):
        self.put(flip, lambda: self.place(flip), axis)

    def wait(self, flip):
        self.net.arrive((self.name, flip), lambda: self.place(flip))

    def start(self):
        x = self.coords[0]
        self.put(0, lambda: self.result.at[1 - x], 4)
        self.put(0, lambda: self.result.at[x], 2)
        self.put(0, lambda: self.result.at[x], 1)
        self.net.local(
            (self.name, "own"), lambda: self.result.at[x], lambda: self.dst.at[self.expert]
        )

    def pass_near(self):
        self.wait(4)
        self.on(4, 2)
        self.on(4, 1)
        self.wait(2)
        self.on(2, 1)

    def pass_far(self):
        self.wait(6)
        self.on(6, 1)

    def finish(self):
        self.net.ready((self.name, "own"))
        for flip in (1, 5, 3, 7):
            self.wait(flip)


class ParityGather:
    def __init__(self, net, name, coords, halves, dst, length):
        self.net, self.name, self.halves, self.dst, self.length = net, name, halves, dst, length
        self.x, y, c, _ = coords
        self.nx = 1 - self.x
        self.to_x, self.to_y, self.to_mate = {"x": self.nx}, {"y": 1 - y}, {"c": 1 - c}

    def slot(self, slot):
        return self.dst.at[slot * self.length : (slot + 1) * self.length, :]

    def put(self, slot, src, device):
        self.net.send((self.name, slot), src, lambda: self.slot(slot), device)

    def wait(self, slot):
        self.net.arrive((self.name, slot), lambda: self.slot(slot))

    def start(self):
        mine = lambda: self.halves(self.x)
        self.put(2, mine, self.to_y)
        self.put(4, lambda: self.halves(self.nx), self.to_x)
        self.put(1, mine, self.to_mate)
        self.net.local((self.name, "own"), mine, lambda: self.slot(0))

    def forward(self):
        self.wait(4)
        self.put(6, lambda: self.slot(4), self.to_y)
        self.put(5, lambda: self.slot(4), self.to_mate)
        self.wait(2)
        self.put(3, lambda: self.slot(2), self.to_mate)

    def forward_far(self):
        self.wait(6)
        self.put(7, lambda: self.slot(6), self.to_mate)

    def finish(self):
        self.net.ready((self.name, "own"))
        for slot in (1, 3, 5, 7):
            self.wait(slot)

    def left(self):
        for slot in (2, 4, 1):
            self.net.sent((self.name, slot))
        self.net.ready((self.name, "own"))


class AttentionScatter:
    def __init__(self, net, name, depth, coords, grad, left, pieces, blocks, lines, dst, low):
        self.net, self.name, self.depth, self.coords = net, name, depth, coords
        self.grad, self.left, self.pieces, self.blocks = grad, left, pieces, blocks
        self.dst, self.low = dst, low
        self.length, self.columns, self.rows = grad.shape[0], grad.shape[1] // 4, dst.shape[0]
        x, y, c, z = coords
        self.ys, self.cs = (y, 1 - y), (c, 1 - c)
        self.to_x, self.to_y, self.to_core = {"x": 1 - x}, {"y": self.ys[1]}, {"c": self.cs[1]}
        self.to_x_core = {"x": 1 - x, "c": self.cs[1]}
        self.to_y_core = {"y": self.ys[1], "c": self.cs[1]}
        self.line = LineScatter(net, name + " line", depth, z, self.block, lines, None)

    def block(self, t):
        return self.blocks.at[pl.ds(pl.multiple_of(t * self.rows, self.rows), self.rows), :]

    def lanes(self, yi, ci):
        return pl.ds(pl.multiple_of((2 * yi + ci) * self.columns, LANES), self.columns)

    def quarter(self, yi, ci):
        return self.dst.at[:, self.lanes(yi, ci)]

    def slot(self, slot):
        return self.pieces.at[slot * self.length : (slot + 1) * self.length, :]

    def put(self, slot, src, device):
        self.net.send((self.name, slot), src, lambda: self.slot(slot), device)

    def give(self, slot, fy, fc, device):
        self.put(slot, lambda: self.grad.at[:, self.lanes(self.ys[fy], self.cs[fc])], device)

    def start(self):
        self.give(2, 1, 0, self.to_y)
        self.give(3, 1, 1, self.to_y_core)
        self.give(4, 0, 0, self.to_x)
        self.give(5, 0, 1, self.to_x_core)
        self.give(1, 0, 1, self.to_core)
        self.net.local(
            (self.name, "own piece"),
            lambda: self.grad.at[:, self.lanes(self.ys[0], self.cs[0])],
            lambda: self.slot(0),
        )

    def forward(self):
        for slot in (2, 3):
            self.net.arrive((self.name, slot), lambda: self.slot(slot))
            self.put(slot + 4, lambda slot=slot: self.slot(slot), self.to_x)

    def take(self):
        for slot in (4, 5, 1, 6, 7):
            self.net.arrive((self.name, slot), lambda: self.slot(slot))
        self.net.ready((self.name, "own piece"))
        tile = 256
        for i in range(0, self.left.shape[1], tile):
            self.blocks[i : i + tile, :] = dot_tn(self.left[:, i : i + tile], self.pieces[...]).astype(BF16)
        self.line.start()

    def total(self):
        x, y, c, z = self.coords
        self.line.finish(self.low)
        self.net.local((self.name, "own"), self.low, self.quarter(y, c))
        for key, device in (("ty", self.to_y), ("tc", self.to_core)):
            self.net.send((self.name, key), lambda: self.low, lambda: self.quarter(y, c), device)

    def pass_y(self):
        x, y, c, z = self.coords
        there = lambda: self.quarter(1 - y, c)
        self.net.arrive((self.name, "ty"), there)
        self.net.send((self.name, "tyc"), there, there, self.to_core)

    def finish(self):
        x, y, c, z = self.coords
        self.net.ready((self.name, "own"))
        self.net.arrive((self.name, "tc"), lambda: self.quarter(y, 1 - c))
        self.net.arrive((self.name, "tyc"), lambda: self.quarter(1 - y, 1 - c))


def norm_back(values, gain, upstream):
    inverse = inverse_rms(values)
    normal = values * inverse
    gain_grad = jnp.sum(upstream * normal, axis=0, keepdims=True)
    scaled = upstream * gain
    return (
        inverse * (scaled - normal * jnp.mean(scaled * normal, axis=-1, keepdims=True)),
        gain_grad,
    )


def layer_kernel(depth, shard_rows, *refs):
    (
        hidden, grad_out, segment, routes, weights, cosine, sine,
        gains_in, query_in, key_in, value_in, wo_in, gate_in, up_in, down_in, grad_hbm,
        layer_out, grad_in, gain_total,
        gate_total, up_total, down_total, wq_total, wo_total,
        wq, wo, down_full, shares, probability,
        row_mates, row_fars, row_chips, out_mates, out_fars, out_chips,
        gate_lines, up_lines, down_lines, normed_all, attended_all,
        rows, grads, wide, gate_grad, down_grad, returned, wide_load, down_load, wide_low, down_low,
        wq_pieces, wo_pieces, wq_lines, wo_lines, wq_blocks, wo_blocks, wq_low, wo_low, gain_swap,
        gains, gain_rows, queries, keys, values, attended, mixed, share_in,
        send_sems, recv_sems, local_sems,
    ) = refs
    coords = x, y, c, z = tuple(lax.axis_index(n) for n in ("x", "y", "c", "z"))
    expert = 4 * x + 2 * y + c
    net = Net(send_sems, recv_sems, local_sems, c)
    length, width = hidden.shape
    units = gate_in.shape[2]
    tile, step = 256, 16
    factor = HEAD_DIM ** (-0.5)
    greet(depth, coords)

    wq_gather = AttentionGather(net, "wq", depth, coords, wq_pieces, wq, True)
    wo_gather = AttentionGather(net, "wo", depth, coords, wo_in, wo)
    gate_gather = ExpertGather(net, "gate", depth, coords, gate_in, wide.at[:, :units])
    up_gather = ExpertGather(net, "up", depth, coords, up_in, wide.at[:, units:])
    down_gather = ExpertGather(net, "down", depth, coords, down_in, down_full)
    gate_up = (gate_gather, up_gather)
    row_gather = SlabGather(net, "row", coords, rows, length)
    grad_gather = SlabGather(net, "grad", coords, grads, length)

    def gate_block(t):
        size = 2 * shard_rows
        return gate_grad.at[pl.ds(pl.multiple_of(t * size, size), size), :]

    def up_block(t):
        size = 2 * shard_rows
        return wide.at[pl.ds(pl.multiple_of(t * size, size), size), pl.ds(units, units)]

    def down_block(t):
        size = 2 * (units // (2 * depth))
        return down_grad.at[pl.ds(pl.multiple_of(t * size, size), size), :]

    gate_line = LineScatter(net, "gate line", depth, z, gate_block, gate_lines, wide_load)
    up_line = LineScatter(net, "up line", depth, z, up_block, up_lines, wide_load)
    down_line = LineScatter(net, "down line", depth, z, down_block, down_lines, down_load)
    row_back = SlabReturn(net, "row back", coords, grads, length, row_mates, row_fars, row_chips, returned, False)

    down_share = ExpertShare(net, "down sum", coords, down_low, down_total)
    gate_share = ExpertShare(net, "gate sum", coords, wide_low.at[0], gate_total)
    up_share = ExpertShare(net, "up sum", coords, wide_low.at[1], up_total)

    def finish_line(line, share):
        line.finish(share.result.at[0], share.result.at[1])
        share.start()

    def columns_of(i):
        return lambda parity: returned.at[
            i, :, pl.ds(pl.multiple_of(parity * (width // 2), LANES), width // 2)
        ]

    normed_gather = ParityGather(net, "normed", coords, columns_of(0), normed_all, length)
    attended_gather = ParityGather(net, "attended", coords, columns_of(1), attended_all, length)

    def simple_send(key, source, target, device, cond=None):
        net.send(key, lambda: source, lambda: target, device, cond)

    to_mate, to_x, to_y = {"c": 1 - c}, {"x": 1 - x}, {"y": 1 - y}
    to_xy = {**to_x, **to_y}

    me = z * 2 + x
    base = [net.slot(("gains", s)) for s in range(2 * depth)][0]

    def gain_copy(s, index):
        return pltpu.make_async_remote_copy(
            src_ref=gains_in,
            dst_ref=gains.at[me],
            send_sem=send_sems.at[index],
            recv_sem=recv_sems.at[base + me],
            device_id={"z": jnp.int32(s // 2), "x": jnp.int32(s % 2)},
            device_id_type=MESH,
        )

    def start_shares():
        net.local("own grad", grad_hbm, grads.at[:length])
        net.send(("share", 1), lambda: share_in, lambda: shares.at[1], to_mate)
        net.send(("share", 2), lambda: share_in, lambda: shares.at[2], to_y)
        net.send(("share", 4), lambda: share_in, lambda: shares.at[4], to_x)
        net.send(("share", 6), lambda: share_in, lambda: shares.at[6], to_xy)

    def pass_shares():
        for slot in (2, 4, 6):
            net.arrive(("share", slot), lambda: shares.at[slot])
            net.send(
                ("share", slot + 1),
                lambda slot=slot: shares.at[slot],
                lambda slot=slot: shares.at[slot + 1],
                to_mate,
            )

    quarter = wq.shape[1] // 4
    query_end, key_end = query_in.shape[1], query_in.shape[1] + key_in.shape[1]
    bounce = []

    def middle(i, first, size):
        return wq_pieces.at[i * shard_rows : (i + 1) * shard_rows, first : first + size]

    for i, j in enumerate(range(0, wq.shape[1], quarter)):
        for source, begin, end in (
            (query_in, 0, query_end), (key_in, query_end, key_end), (value_in, key_end, wq.shape[1])
        ):
            low, high = max(j, begin), min(j + quarter, end)
            if low < high:
                net.local(("in", i, low), source.at[:, low - begin : high - begin], middle(i, low - j, high - low))
                net.ready_later(("in", i, low))
        bounce.append((middle(i, 0, quarter), wq, j))
    for j in range(0, width, quarter):
        i = len(bounce)
        net.local(("in", i, 0), wo_in.at[:, j : j + quarter], middle(i, 0, quarter))
        net.ready_later(("in", i, 0))
        bounce.append((middle(i, 0, quarter), wo, j))
    net.ready_all()
    wq_gather.start()
    net.local("gains", gains_in, gains.at[me])
    gain_sends = []
    for s in range(2 * depth):
        index = net.count
        net.count += 1
        gain_sends.append((s, index))
        pl.when(me != s)(lambda: gain_copy(s, index).start())
    down_rows = down_in.shape[1]
    net.local("down in", down_in.at[expert], down_load.at[0, :down_rows])
    for gather in (gate_gather, up_gather):
        net.local((gather.name, "own"), gather.src.at[gather.own], gather.block(z, x)())
    for i, (source, target, j) in enumerate(bounce):
        net.local(("out", i), source, target.at[wq_gather.mine(), j : j + quarter])
    names = lax.broadcasted_iota(jnp.int32, (LANES, length), 0)
    share = jnp.zeros((LANES, length), F32)
    for i in range(routes.shape[0]):
        share = share + jnp.where(names == routes[i : i + 1, :], weights[i : i + 1, :], 0.0)
    share_in[...] = share.T
    net.ready("down in")
    net.local("down out", down_load.at[0, :down_rows], down_gather.block(z, x)())
    wo_gather.start()
    wo_gather.pass_z(1)
    wq_gather.pass_z(1)
    wo_gather.pass_z(2)
    wq_gather.pass_z(2)
    for k in range(3, depth):
        wo_gather.pass_z(k)
    gate_gather.start()
    up_gather.start()
    wq_gather.pass_x(1)
    wo_gather.pass_x(1)
    for k in range(3, depth):
        wq_gather.pass_z(k)
    gate_gather.start_x()
    up_gather.start_x()
    wo_gather.pass_x(0)
    for k in range(3, depth):
        wo_gather.pass_x(k)
    down_gather.start()
    for k in range(3, depth):
        wq_gather.pass_x(k)
    wq_gather.pass_y(1)
    wq_gather.pass_x(2)
    down_gather.start_x()
    gate_gather.pass_z(1, 0)
    up_gather.pass_z(1, 0)
    wo_gather.pass_x(2)
    for k in range(3, depth):
        wo_gather.pass_y(k)
    wq_gather.pass_y(2)
    wq_gather.pass_x(0)
    grad_gather.start(grad_hbm)
    start_shares()
    for k in range(3, depth):
        wq_gather.pass_y(k)
    wo_gather.pass_y(2)
    wo_gather.pass_y(1)
    wq_gather.finish()
    gate_gather.pass_x()
    up_gather.pass_x()

    def attention_forward(wq_here, wo_here, chances, order, normed):
        def project():
            for i in range(len(bounce)):
                net.ready(("out", i))
            for key in (("z", "up", 1), ("z", "down", 1), ("x", "same"), ("x", "cross")):
                net.sent(("wq",) + key)
            net.local("wq here", wq, wq_here)
            gains_wide()
            project_heads()

        def gains_wide():
            for s in range(2 * depth):
                pl.when(me != s)(lambda: net.arrive(("gains", s), lambda: gains.at[s]))
            net.ready("gains")
            wide_gain = None
            for s in range(2 * depth):
                rest = jnp.zeros((8, width - gains.shape[2]), F32)
                piece = jnp.concatenate([gains[s], rest], axis=1)
                piece = piece if s == 0 else pltpu.roll(piece, s * shard_rows, axis=1)
                wide_gain = piece if wide_gain is None else wide_gain + piece
            gain_rows[...] = wide_gain

            @pl.loop(0, length // step)
            def _(i):
                here = pl.ds(pl.multiple_of(i * step, step), step)
                one = hidden[here, :].astype(F32)
                normed[here, :] = (one * inverse_rms(one) * gain_rows[0:1, :]).astype(BF16)

        def project_heads():
            net.ready("wq here")
            cos, sin = cosine[...], sine[...]
            for start in range(0, wq.shape[1], tile):
                part = dot_nn(normed[...], wq_here[:, start : start + tile])
                for at in range(start, start + tile, HEAD_DIM):
                    head, one = at // HEAD_DIM, part[:, at - start : at - start + HEAD_DIM]
                    if head < HEADS:
                        queries[head * length : (head + 1) * length, :] = turn(one, cos, sin).astype(BF16)
                    elif head < HEADS + KV_HEADS:
                        at_row = (head - HEADS) * length
                        keys[at_row : at_row + length, :] = turn(one, cos, sin).astype(BF16)
                    else:
                        at_row = (head - HEADS - KV_HEADS) * length
                        values[at_row : at_row + length, :] = one.astype(BF16)

        def heads_forward():
            across = jnp.broadcast_to(segment[...].astype(F32), (length, length))
            later = lax.broadcasted_iota(jnp.int32, (length, length), 0)
            allowed = (across == across.T) & (later >= lax.broadcasted_iota(jnp.int32, (length, length), 1))
            for head in range(HEADS):
                kv = head // GROUP
                here = slice(head * length, (head + 1) * length)
                there = slice(kv * length, (kv + 1) * length)
                scores = dot_nt(queries[here, :], keys[there, :]) * factor
                scores = jnp.where(allowed, scores, masked_score)
                terms = jnp.exp(scores - jnp.max(scores, axis=-1, keepdims=True))
                chance = terms / jnp.sum(terms, axis=-1, keepdims=True)
                chances[here, :] = chance
                attended[:, head * HEAD_DIM : (head + 1) * HEAD_DIM] = dot_nn(
                    chance.astype(BF16), values[there, :]
                ).astype(BF16)
            net.local("keep chances", chances, probability)

        def mix():
            net.local("wo here", wo, wo_here)
            net.ready("wo here")
            for start in range(0, width, tile):
                there = slice(start, start + tile)
                mixed[:, there] = hidden[:, there].astype(F32) + dot_nn(attended[...], wo_here[:, there])

            @pl.loop(0, length // step)
            def _(i):
                here = pl.ds(pl.multiple_of(i * step, step), step)
                total = mixed[here, :]
                rows[here, :] = (total * inverse_rms(total) * gain_rows[1:2, :]).astype(BF16)

        def by_parity():
            for s in range(2 * depth):
                size = (shard_rows, width)
                first = (s % 2) * (width // 2) + (s // 2) * shard_rows
                hit = lax.broadcasted_iota(jnp.int32, size, 1) - first == lax.broadcasted_iota(jnp.int32, size, 0)
                order[s * shard_rows : (s + 1) * shard_rows, :] = hit.astype(F32).astype(BF16)
            for i, source in enumerate((normed, attended)):
                for j in range(0, width, 512):
                    returned[i, :, j : j + 512] = dot_nn(source[...], order[:, j : j + 512]).astype(BF16)

        project()
        wo_gather.finish()
        heads_forward()
        for k in range(2, depth):
            gate_gather.pass_z(k, 0)
            up_gather.pass_z(k, 0)
        mix()
        row_gather.start(rows.at[:length, :])
        by_parity()
        net.ready("keep chances")

    pl.run_scoped(
        attention_forward,
        pltpu.VMEM(wq.shape, BF16),
        pltpu.VMEM(wo.shape, BF16),
        pltpu.VMEM((HEADS * length, length), F32),
        pltpu.VMEM((width, width), BF16),
        pltpu.VMEM((length, width), BF16),
    )

    grad_gather.forward()
    pass_shares()
    gate_gather.pass_z(1, 1)
    up_gather.pass_z(1, 1)
    for k in range(2, depth):
        gate_gather.pass_z(k, 1)
        up_gather.pass_z(k, 1)
    row_gather.forward()
    down_gather.pass_x()
    down_gather.pass_z(1, 0)
    down_gather.pass_z(1, 1)
    attended_gather.start()
    gate_gather.finish()
    up_gather.finish()

    def experts(down, hidden_act, both_grads, share_here, parts_out):
        out_back = SlabReturn(net, "out back", coords, parts_out, length, out_mates, out_fars, out_chips, returned, False)
        lane = lax.broadcasted_iota(jnp.int32, (length, LANES), 1)

        def share_of(r):
            return jnp.sum(jnp.where(lane == expert, share_here[r], 0.0), axis=1, keepdims=True)

        def first_half(first, count):
            @pl.loop(first, first + count)
            def _(r):
                here = pl.ds(pl.multiple_of(r * length, length), length)
                grads[here, :] = (share_of(r) * grads[here, :].astype(F32)).astype(BF16)
                for j in range(0, units, tile):
                    gate = dot_nn(rows[here, :], wide[:, j : j + tile])
                    up = dot_nn(rows[here, :], wide[:, units + j : units + j + tile])
                    sigmoid = 1.0 / (1.0 + jnp.exp(-gate))
                    silu = gate * sigmoid
                    hidden_act[here, j : j + tile] = (silu * up).astype(BF16)
                    both_grads[here, j : j + tile] = (
                        up * sigmoid * (1.0 + gate * (1.0 - sigmoid))
                    ).astype(BF16)
                    both_grads[here, units + j : units + j + tile] = silu.astype(BF16)

        def first_rows():
            net.local("own share", share_in, share_here.at[0])
            for slot in (1, 2, 3, 4, 5, 6, 7):
                if slot % 2:
                    net.arrive(("share", slot), lambda: shares.at[slot])
            net.local("shares", shares.at[1:], share_here.at[1:])
            row_gather.wait(1)
            grad_gather.wait(1)
            for name in ("own grad", "own share", "shares", ("gate", "own"), ("up", "own")):
                net.ready(name)
            first_half(0, 2)

        def gathered(*slots):
            for gather in (row_gather, grad_gather):
                for slot, half in slots:
                    gather.wait(slot, half)

        def left(*slots):
            for slot, half in slots:
                net.sent(("grad", slot, half))

        def middle_rows():
            gathered((3, None), (5, None))
            left((6, 0), (3, None), (6, 1), (5, None))
            first_half(2, 4)

        def last_rows():
            gathered((7, 0), (7, 1))
            left((7, 0), (7, 1))
            first_half(6, 2)

        def down_weight_grad():
            @pl.loop(0, units // tile)
            def _(i):
                at = pl.ds(pl.multiple_of(i * tile, tile), tile)
                for j in range(0, width, 512):
                    down_grad[at, j : j + 512] = dot_tn(hidden_act[:, at], grads[:, j : j + 512]).astype(BF16)

        near_half = units // 2 * (z >= depth // 2).astype(jnp.int32)
        near = pl.multiple_of(near_half, LANES)
        far = pl.multiple_of(units // 2 - near_half, LANES)

        def take_down(first):
            if first is near:
                net.ready("down out")
            here = pl.ds(first, units // 2)
            name = "down near" if first is near else "down far"
            net.local(name, down_full.at[here, :], down.at[here, :])
            net.ready(name)

        def hidden_grads(first):
            @pl.loop(0, EXPERTS)
            def _(r):
                here = pl.ds(pl.multiple_of(r * length, length), length)
                for j in range(0, units // 2, tile):
                    size = min(tile, units // 2 - j)
                    at = pl.multiple_of(first + j, LANES)
                    back = dot_nt(grads[here, :], down[pl.ds(at, size), :])
                    for lane_first in (at, pl.multiple_of(units + at, LANES)):
                        lanes = pl.ds(lane_first, size)
                        both_grads[here, lanes] = (
                            back * both_grads[here, lanes].astype(F32)
                        ).astype(BF16)

        def row_grad(slot, more=None):
            here = slice(slot * length, (slot + 1) * length)
            for j in range(0, width, 512):
                part = dot_nt(both_grads[here, :], wide[j : j + 512, :])
                if more is not None:
                    part = part + more[:, j : j + 512].astype(F32)
                grads[here, j : j + 512] = part.astype(BF16)

        def out_rows(slot, more=None):
            here = slice(slot * length, (slot + 1) * length)
            share = share_of(slot)
            for j in range(0, width, 512):
                part = share * dot_nn(hidden_act[here, :], down[:, j : j + 512])
                if more is not None:
                    part = part + more[:, j : j + 512].astype(F32)
                parts_out[here, j : j + 512] = part.astype(BF16)

        order = (3, 1, 2, 0)

        def give_mates(back, compute):
            for chip in order:
                compute(2 * chip + 1)
                back.to_mate(chip)

        def give_chips(back, compute):
            if back is out_back:
                normed_gather.left()
                attended_gather.left()
            back.fetch(order[0])
            for i, chip in enumerate(order):
                if i + 1 < len(order):
                    back.fetch(order[i + 1])
                compute(2 * chip, back.fetched(chip))
                back.give(chip)

        def weight_grad(first, target):
            @pl.loop(0, width // tile)
            def _(i):
                at = pl.ds(pl.multiple_of(i * tile, tile), tile)
                target[at, :] = dot_tn(rows[:, at], both_grads[:, first : first + units]).astype(BF16)

        first_rows()
        grad_gather.forward_far()
        middle_rows()
        row_gather.forward_far()
        normed_gather.start()
        for k in range(2, depth):
            down_gather.pass_z(k, 1)
        last_rows()
        for k in range(2, depth):
            down_gather.pass_z(k, 0)
        down_weight_grad()
        down_line.start()
        down_gather.finish(True)
        take_down(near)
        attended_gather.forward()
        normed_gather.forward()
        hidden_grads(near)
        down_gather.finish(False)
        take_down(far)
        give_mates(out_back, out_rows)
        attended_gather.forward_far()
        give_chips(out_back, out_rows)
        hidden_grads(far)
        down_line.step(2)
        weight_grad(0, gate_grad)
        gate_line.start_step(1)
        out_back.combined()
        give_mates(row_back, row_grad)
        give_chips(row_back, row_grad)
        for s in range(3, depth):
            down_line.step(s)
        up_gather.sent()
        weight_grad(units, wide.at[:, units:])
        up_line.start_step(1)
        for s in range(2, depth):
            gate_line.start_step(s)
            up_line.start_step(s)
        row_back.combined()
        gate_line.step(2)
        out_back.total(layer_out, mixed)
        finish_line(down_line, down_share)
        up_line.step(2)
        out_back.sent()

    pl.run_scoped(
        experts,
        pltpu.VMEM((units, width), BF16),
        pltpu.VMEM((EXPERTS * length, units), BF16),
        pltpu.VMEM((EXPERTS * length, 2 * units), BF16),
        pltpu.VMEM((EXPERTS, length, LANES), F32),
        pltpu.VMEM((EXPERTS * length, width), BF16),
    )

    def attention_backward(weight, chances, normed_here, attended_here, upstream_two, mixed_grad, mixed_low, attended_grad, qkv_grad):
        net.local("wo again", wo, weight.at[:, :width])
        net.local("chance 0", probability.at[: GROUP * length], chances)
        wo_net = AttentionScatter(
            net, "wo sum", depth, coords, mixed_low, attended_here, wo_pieces, wo_blocks, wo_lines, wo_total, wo_low
        )
        wq_net = AttentionScatter(
            net, "wq sum", depth, coords, qkv_grad, normed_here, wq_pieces, wq_blocks, wq_lines, wq_total, wq_low
        )

        def take_normed():
            normed_gather.finish()
            net.local("normed here", normed_all, normed_here)

        def take_attended():
            attended_gather.finish()
            net.local("attended here", attended_all, attended_here)

        def norm_two_back():
            row_back.total(upstream_two)
            gain_swap[0] = jnp.zeros(gain_swap.shape[1:], F32)

            @pl.loop(0, length // step)
            def _(i):
                here = pl.ds(pl.multiple_of(i * step, step), step)
                part, gain_two = norm_back(mixed[here, :], gain_rows[1:2, :], upstream_two[here, :])
                total = grad_out[here, :].astype(F32) + part
                mixed_grad[here, :] = total
                mixed_low[here, :] = total.astype(BF16)
                gain_swap[0, 1:2, :] += gain_two

        def attended_back():
            net.ready("wo again")
            for i in range(0, width, 512):
                attended_grad[:, i : i + 512] = dot_nt(
                    mixed_low[...], weight[i : i + 512, :width]
                ).astype(BF16)
            net.local("wq again", wq, weight)

        def heads_back():
            cos, sin = cosine[...], -sine[...]
            for kv in range(KV_HEADS):
                net.ready("chance %d" % kv)
                there = slice(kv * length, (kv + 1) * length)
                value_sum = key_sum = None
                for g in range(GROUP):
                    head = kv * GROUP + g
                    here = slice(head * length, (head + 1) * length)
                    cols = slice(head * HEAD_DIM, (head + 1) * HEAD_DIM)
                    chance = chances[g * length : (g + 1) * length, :]
                    back = attended_grad[:, cols]
                    prob_grad = dot_nt(back, values[there, :])
                    value_part = dot_tn(chance.astype(BF16), back)
                    inner = jnp.sum(chance * prob_grad, axis=-1, keepdims=True)
                    score_grad = (chance * (prob_grad - inner)).astype(BF16)
                    query_grad = dot_nn(score_grad, keys[there, :]) * factor
                    key_part = dot_tn(score_grad, queries[here, :])
                    qkv_grad[:, cols] = turn(query_grad, cos, sin).astype(BF16)
                    value_sum = value_part if value_sum is None else value_sum + value_part
                    key_sum = key_part if key_sum is None else key_sum + key_part
                if kv + 1 < KV_HEADS:
                    size = GROUP * length
                    net.local("chance %d" % (kv + 1), probability.at[(kv + 1) * size : (kv + 2) * size], chances)
                first = (HEADS + kv) * HEAD_DIM
                qkv_grad[:, first : first + HEAD_DIM] = turn(key_sum * factor, cos, sin).astype(BF16)
                first = first + KV_HEADS * HEAD_DIM
                qkv_grad[:, first : first + HEAD_DIM] = value_sum.astype(BF16)

        def norm_one_back():
            net.ready("wq again")
            for i in range(0, width, 512):
                upstream_two[:, i : i + 512] = dot_nt(qkv_grad[...], weight[i : i + 512, :])

            @pl.loop(0, length // step)
            def _(i):
                here = pl.ds(pl.multiple_of(i * step, step), step)
                part, gain_one = norm_back(
                    hidden[here, :].astype(F32), gain_rows[0:1, :], upstream_two[here, :]
                )
                grad_in[here, :] = (mixed_grad[here, :] + part).astype(BF16)
                gain_swap[0, 0:1, :] += gain_one

        axes = (("c", to_mate), ("x", to_x), ("y", to_y))

        def gain_start(i):
            net.send(
                ("gain", axes[i][0]),
                lambda: gain_swap.at[2 * i],
                lambda: gain_swap.at[2 * i + 1],
                axes[i][1],
            )

        def gain_add(i):
            net.arrive(("gain", axes[i][0]), lambda: gain_swap.at[2 * i + 1])
            gain_swap[2 * i + 2] = gain_swap[2 * i] + gain_swap[2 * i + 1]

        def gains_out():
            for far in range(1, depth):
                simple_send(("gain", "up", far), gain_swap.at[6], gain_swap.at[5 + 2 * far], {"z": z + far}, z + far < depth)
                simple_send(("gain", "down", far), gain_swap.at[6], gain_swap.at[6 + 2 * far], {"z": z - far}, z - far >= 0)

        def gains_in_all():
            for far in range(1, depth):
                for tag, slot, cond in (
                    ("up", 5 + 2 * far, z - far >= 0), ("down", 6 + 2 * far, z + far < depth)
                ):

                    def take():
                        net.arrive(("gain", tag, far), lambda: gain_swap.at[slot])
                        gain_swap[6] += gain_swap[slot]

                    pl.when(cond)(take)
            for s in range(2 * depth):

                def pick(s=s):
                    value = gain_swap[6]
                    if s:
                        value = pltpu.roll(value, width - s * shard_rows, axis=1)
                    gain_total[...] = value[:, : gain_total.shape[1]]

                pl.when(me == s)(pick)

        norm_two_back()
        wo_net.start()
        normed_gather.forward_far()
        attended_back()
        heads_back()
        wq_net.start()
        for s in range(3, depth):
            gate_line.step(s)
        norm_one_back()
        wq_net.forward()
        for s in range(3, depth):
            up_line.step(s)
        wo_net.forward()
        finish_line(gate_line, gate_share)
        take_normed()
        net.ready("normed here")
        wq_net.take()
        down_share.pass_near()
        gain_start(0)
        take_attended()
        finish_line(up_line, up_share)
        wq_net.line.step(2)
        gain_add(0)
        net.ready("attended here")
        wo_net.take()
        gain_start(1)
        gate_share.pass_near()
        for s in range(3, depth):
            wq_net.line.step(s)
        down_share.pass_far()
        up_share.pass_near()
        wo_net.line.step(2)
        gain_add(1)
        wq_net.total()
        for s in range(3, depth):
            wo_net.line.step(s)
        wo_net.total()
        gain_start(2)
        up_share.pass_far()
        wq_net.pass_y()
        gate_share.pass_far()
        wo_net.pass_y()
        gain_add(2)
        gains_out()
        for key in [key for key in net.sends if key[0] == "gain"]:
            net.sent(key)
        gains_in_all()
        for one in (down_share, gate_share, up_share, wo_net, wq_net):
            one.finish()
        net.drain()

    pl.run_scoped(
        attention_backward,
        pltpu.VMEM(wq.shape, BF16),
        pltpu.VMEM((GROUP * length, length), F32),
        pltpu.VMEM((EXPERTS * length, width // 2), BF16),
        pltpu.VMEM((EXPERTS * length, width // 2), BF16),
        pltpu.VMEM((length, width), F32),
        pltpu.VMEM((length, width), F32),
        pltpu.VMEM((length, width), BF16),
        pltpu.VMEM((length, width), BF16),
        pltpu.VMEM((length, wq.shape[1]), BF16),
    )
    for s, index in gain_sends:
        pl.when(me != s)(lambda: gain_copy(s, index).wait_send())
    assert net.count <= send_sems.shape[0] and len(net.slots) <= recv_sems.shape[0]
    assert len(net.locals) <= local_sems.shape[0]


def layer_call(
    depth, shard_rows, hidden, grad_out, segments, routes, weights, cosine, sine, gains, query_in, key_in,
    value_in, wo_in, gate_in, up_in, down_in,
):
    length, width = hidden.shape
    wide = query_in.shape[1] + key_in.shape[1] + value_in.shape[1]
    units, down_rows = gate_in.shape[2], down_in.shape[1]
    here, there = pl.BlockSpec(memory_space=pltpu.VMEM), pl.BlockSpec(memory_space=pltpu.HBM)

    def shape(*dims, dtype=BF16):
        return jax.ShapeDtypeStruct(dims, dtype)

    returns = [shape(4, length, width), shape(length, width), shape(2, length, width)]
    out_shape = [
        shape(length, width), shape(length, width), shape(*gains.shape, dtype=F32),
        shape(EXPERTS, shard_rows, units), shape(EXPERTS, shard_rows, units),
        shape(EXPERTS, down_rows, width),
        shape(shard_rows, wide), shape(shard_rows, width),
        shape(width, wide), shape(width, width), shape(units, width),
        shape(EXPERTS, length, LANES, dtype=F32), shape(HEADS * length, length, dtype=F32),
        *returns, *returns,
        shape(2, depth - 1, 2 * shard_rows, units), shape(2, depth - 1, 2 * shard_rows, units),
        shape(2, depth - 1, 2 * down_rows, width),
        shape(EXPERTS * length, width // 2), shape(EXPERTS * length, width // 2),
    ]
    copies, arrivals = 68 * depth + 38, 58 * depth + 58
    return pl.pallas_call(
        functools.partial(layer_kernel, depth, shard_rows),
        out_shape=out_shape,
        in_specs=[here] * 7 + [there] * 9,
        out_specs=[here] * 3 + [there] * (len(out_shape) - 3),
        scratch_shapes=[
            pltpu.VMEM((EXPERTS * length, width), BF16),
            pltpu.VMEM((EXPERTS * length, width), BF16),
            pltpu.VMEM((width, 2 * units), BF16),
            pltpu.VMEM((width, units), BF16),
            pltpu.VMEM((units, width), BF16),
            pltpu.VMEM((4, length, width), BF16),
            pltpu.VMEM((2, 2 * shard_rows, units), BF16),
            pltpu.VMEM((2, 2 * down_rows, width), BF16),
            pltpu.VMEM((2, 2, shard_rows, units), BF16),
            pltpu.VMEM((2, down_rows, width), BF16),
            pltpu.VMEM((EXPERTS * length, wide // 4), BF16),
            pltpu.VMEM((EXPERTS * length, width // 4), BF16),
            pltpu.VMEM((2, depth - 1, shard_rows, wide // 4), BF16),
            pltpu.VMEM((2, depth - 1, shard_rows, width // 4), BF16),
            pltpu.VMEM((depth * shard_rows, wide // 4), BF16),
            pltpu.VMEM((depth * shard_rows, width // 4), BF16),
            pltpu.VMEM((shard_rows, wide // 4), BF16),
            pltpu.VMEM((shard_rows, width // 4), BF16),
            pltpu.VMEM((5 + 2 * depth, 8, width), F32),
            pltpu.VMEM((2 * depth, *gains.shape), F32),
            pltpu.VMEM((8, width), F32),
            pltpu.VMEM((HEADS * length, HEAD_DIM), BF16),
            pltpu.VMEM((KV_HEADS * length, HEAD_DIM), BF16),
            pltpu.VMEM((KV_HEADS * length, HEAD_DIM), BF16),
            pltpu.VMEM((length, width), BF16),
            pltpu.VMEM((length, width), F32),
            pltpu.VMEM((length, LANES), F32),
            pltpu.SemaphoreType.DMA((copies,)),
            pltpu.SemaphoreType.DMA((arrivals,)),
            pltpu.SemaphoreType.DMA((60,)),
        ],
        compiler_params=pltpu.CompilerParams(
            collective_id=1, has_side_effects=True, vmem_limit_bytes=VMEM_LIMIT
        ),
    )(
        hidden, grad_out, segments, routes, weights, cosine, sine, gains, query_in, key_in, value_in, wo_in,
        gate_in, up_in, down_in, grad_out,
    )


def rotary_tables(length, head_width):
    half_width = head_width // 2
    frequency = rotary_base ** (-2.0 * np.arange(half_width, dtype=np.float32) / head_width)
    angles = np.arange(length, dtype=np.float32)[:, None] * frequency.astype(np.float32)[None, :]
    cosine, sine = np.cos(angles), np.sin(angles)
    return (
        np.concatenate([cosine, cosine], axis=1).astype(np.float32),
        np.concatenate([-sine, sine], axis=1).astype(np.float32),
    )


def widen_kernel(*refs):
    wq, wo, gate, up, down, layer, grad = refs[:7]
    query_out, key_out, value_out, wo_out, gate_out, up_out, down_out, layer_out, grad_out = refs[7:16]
    low, high, same, in_sems, out_sems, same_sems = refs[16:]
    queries_end = HEADS * HEAD_DIM
    kv = KV_HEADS * HEAD_DIM
    rows = wq.shape[0]
    width = wo.shape[1]
    pieces = [
        (wq.at[:, :queries_end], query_out),
        (wo, wo_out),
    ]
    for source, target in ((gate, gate_out), (up, up_out), (down, down_out)):
        for e in range(EXPERTS):
            pieces.append((source.at[e], target.at[e]))
    pieces.append((wq.at[:, queries_end : queries_end + kv], key_out))
    pieces.append((wq.at[:, queries_end + kv :], value_out))
    depth = low.shape[0]

    def place(buffer, i):
        r, n = pieces[i][0].shape
        return buffer.at[i % depth, :r, :n]

    def read(i):
        return pltpu.make_async_copy(pieces[i][0], place(low, i), in_sems.at[i % depth])

    def write(i):
        return pltpu.make_async_copy(place(high, i), pieces[i][1], out_sems.at[i % depth])

    passed = ((layer, layer_out), (grad, grad_out))

    def take(i):
        return pltpu.make_async_copy(passed[i][0], same.at[i], same_sems.at[i])

    def put(i):
        return pltpu.make_async_copy(same.at[i], passed[i][1], same_sems.at[2 + i])

    for i in range(depth - 1):
        read(i).start()
    for i in range(2):
        take(i).start()
    for i in range(len(pieces)):
        if i + depth - 1 < len(pieces):
            read(i + depth - 1).start()
        read(i).wait()
        if i >= depth:
            write(i - depth).wait()
        place(high, i)[...] = place(low, i)[...].astype(F32)
        write(i).start()
        if i in (depth, depth + 1):
            take(i - depth).wait()
            put(i - depth).start()
    for i in range(2):
        put(i).wait()
    for i in range(max(0, len(pieces) - depth), len(pieces)):
        write(i).wait()


def widen_call(wq, wo, gate, up, down, layer, grad):
    rows, width = wo.shape
    there = pl.BlockSpec(memory_space=pltpu.HBM)
    queries_end, kv = HEADS * HEAD_DIM, KV_HEADS * HEAD_DIM

    def shape(*dims):
        return jax.ShapeDtypeStruct(dims, F32)

    buffers = 6
    return pl.pallas_call(
        widen_kernel,
        out_shape=[
            shape(rows, queries_end), shape(rows, kv), shape(rows, kv), shape(*wo.shape),
            shape(*gate.shape), shape(*up.shape), shape(*down.shape),
            jax.ShapeDtypeStruct(layer.shape, layer.dtype), jax.ShapeDtypeStruct(grad.shape, grad.dtype),
        ],
        in_specs=[there] * 7,
        out_specs=[there] * 9,
        scratch_shapes=[
            pltpu.VMEM((buffers, rows, width), BF16),
            pltpu.VMEM((buffers, rows, width), F32),
            pltpu.VMEM((2, *layer.shape), BF16),
            pltpu.SemaphoreType.DMA((buffers,)),
            pltpu.SemaphoreType.DMA((buffers,)),
            pltpu.SemaphoreType.DMA((4,)),
        ],
        compiler_params=pltpu.CompilerParams(vmem_limit_bytes=VMEM_LIMIT),
    )(wq, wo, gate, up, down, layer, grad)


def make_shards(sizes):
    depth = sizes["z"]

    def shards(
        hidden_in,
        segments,
        routes,
        gate_weights,
        grad_out,
        attn_gain,
        query_weight,
        key_weight,
        value_weight,
        output_weight,
        ffn_gain,
        gate_weight,
        up_weight,
        down_weight,
    ):
        length, width = hidden_in.shape
        shard_rows = attn_gain.shape[0]
        spare = -(-shard_rows // LANES) * LANES - shard_rows
        first, second = (jnp.pad(gain.astype(F32), (0, spare))[None, :] for gain in (attn_gain, ffn_gain))
        place = lax.broadcasted_iota(jnp.int32, (8, shard_rows + spare), 0)
        gains = jnp.where(place == 0, first, jnp.where(place == 1, second, 0.0))
        cosine, sine = rotary_tables(length, HEAD_DIM)
        layer_out, grad_in, gain_total, gate_total, up_total, down_total, wq_total, wo_total = (
            layer_call(
                depth, shard_rows, hidden_in, grad_out, segments, routes.T, gate_weights.T, cosine, sine,
                gains, query_weight, key_weight, value_weight, output_weight, gate_weight, up_weight,
                down_weight,
            )[:8]
        )
        def whole(value):
            return lax.psum(value.astype(F32), "o") if sizes["o"] > 1 else value

        wq_total = whole(wq_total)
        queries_end = HEADS * HEAD_DIM
        keys_end = queries_end + KV_HEADS * HEAD_DIM
        gain_total = gain_total[:, :shard_rows]
        gain_total = whole(gain_total)
        parts = (wq_total, whole(wo_total), whole(gate_total), whole(up_total), whole(down_total))
        if sizes["o"] == 1:
            *parts, layer_out, grad_in = widen_call(*parts, layer_out, grad_in)
        else:
            parts = (
                wq_total[:, :queries_end], wq_total[:, queries_end:keys_end], wq_total[:, keys_end:], *parts[1:]
            )
        query_grad, key_grad, value_grad, output_grad, gate_grad, up_grad, down_grad = parts
        return (
            layer_out,
            grad_in,
            gain_total[0],
            query_grad,
            key_grad,
            value_grad,
            output_grad,
            gain_total[1],
            gate_grad,
            up_grad,
            down_grad,
        )

    return shards


def solution(mesh):
    reps, shard_count = mesh.shape["rep"], mesh.shape["shard"]
    sizes = {"o": reps // 4, "y": 2, "c": 2, "z": shard_count // 2, "x": 2}
    fine = Mesh(mesh.devices.reshape(tuple(sizes.values())), tuple(sizes))
    tokens = P(("o", "y", "c", "z", "x"), None)
    first, second = P(("z", "x")), P(None, ("z", "x"), None)
    matrix = P(("z", "x"), None)
    return jax.shard_map(
        make_shards(sizes),
        mesh=fine,
        in_specs=(
            (tokens,) * 5 + (first, matrix, matrix, matrix, matrix, first) + (second,) * 3
        ),
        out_specs=(
            (tokens,) * 2 + (first, matrix, matrix, matrix, matrix, first) + (second,) * 3
        ),
        check_vma=False,
    )
```

```python
import functools

import jax
import jax.numpy as jnp
import numpy as np
from jax import lax
from jax.experimental import pallas as pl
from jax.experimental.pallas import tpu as pltpu
from jax.sharding import Mesh
from jax.sharding import PartitionSpec as P

HEADS = 12
KV_HEADS = 2
GROUP = HEADS // KV_HEADS
HEAD_DIM = 128
EXPERTS = 8
LANES = 128

epsilon = 1e-06
rotary_base = 1000000.0
masked_score = -1e30

F32 = jnp.float32
BF16 = jnp.bfloat16
MESH = pl.DeviceIdType.MESH
VMEM_LIMIT = 63 * 2**20


def dot(a, b, dims):
    return lax.dot_general(a, b, (dims, ((), ())), preferred_element_type=F32)


def dot_nn(a, b):
    return dot(a, b, ((1,), (0,)))


def dot_nt(a, b):
    return dot(a, b, ((1,), (1,)))


def dot_tn(a, b):
    return dot(a, b, ((0,), (0,)))


def guarded(cond, body):
    if cond is None:
        body()
    else:
        pl.when(cond)(body)


def both(first, second):
    if first is None:
        return second
    if second is None:
        return first
    return jnp.logical_and(first, second)


class Net:
    def __init__(self, send_sems, recv_sems, local_sems, core):
        self.send_sems, self.recv_sems, self.local_sems = send_sems, recv_sems, local_sems
        self.away = {"c": 1 - core}
        self.slots, self.sends, self.locals, self.count, self.done = {}, {}, {}, 0, set()
        self.later, self.free = [], []

    def slot(self, key):
        return self.slots.setdefault(key, len(self.slots))

    def send(self, key, src, dst, device, cond=None, slot=None):
        recv, index = self.slot(slot or key), self.index()

        def build():
            return pltpu.make_async_remote_copy(
                src_ref=src(),
                dst_ref=dst(),
                send_sem=self.send_sems.at[index],
                recv_sem=self.recv_sems.at[recv],
                device_id=device,
                device_id_type=MESH,
            )

        guarded(cond, lambda: build().start())
        self.sends[key] = (cond, build, index)

    def index(self):
        if self.free:
            return self.free.pop()
        self.count += 1
        return self.count - 1

    def sent(self, key):
        if key not in self.sends:
            return
        cond, build, index = self.sends.pop(key)
        guarded(cond, lambda: build().wait_send())
        self.free.append(index)

    def settle(self, *names):
        for key in [key for key in self.sends if key[0] in names]:
            self.sent(key)

    def arrive(self, key, dst, cond=None):
        recv = self.slot(key)

        def wait():
            pltpu.make_async_remote_copy(
                src_ref=dst(),
                dst_ref=dst(),
                send_sem=self.send_sems.at[0],
                recv_sem=self.recv_sems.at[recv],
                device_id=self.away,
                device_id_type=MESH,
            ).wait_recv()

        guarded(cond, wait)

    def local(self, key, src, dst):
        index = len(self.locals)

        def build():
            return pltpu.make_async_copy(
                src() if callable(src) else src,
                dst() if callable(dst) else dst,
                self.local_sems.at[index],
            )

        build().start()
        self.locals[key] = build

    def ready(self, key):
        if key not in self.done:
            self.done.add(key)
            self.locals[key]().wait()

    def ready_later(self, key):
        self.later.append(key)

    def ready_all(self):
        for key in self.later:
            self.ready(key)
        self.later = []

    def drain(self):
        for key in list(self.sends):
            self.sent(key)
        for key in self.locals:
            self.ready(key)


def greet(depth, coords):
    x, y, c, z = coords
    barrier = pltpu.get_barrier_semaphore()
    for device in ({"y": 1 - y}, {"y": 1 - y, "x": 1 - x}, {"c": 1 - c}):
        pl.semaphore_signal(barrier, inc=1, device_id=device, device_id_type=MESH)
    for zi in range(depth):
        for xi in range(2):

            def tell(zi=zi, xi=xi):
                pl.semaphore_signal(
                    barrier,
                    inc=1,
                    device_id={"z": jnp.int32(zi), "x": jnp.int32(xi)},
                    device_id_type=MESH,
                )

            pl.when(jnp.logical_or(z != zi, x != xi))(tell)
    pl.semaphore_wait(barrier, 3 + 2 * depth - 1)


def along(depth, z):
    return (
        ("up", {"z": z + 1}, z + 1 < depth, lambda k: z - k, lambda k: z - k >= 0),
        ("down", {"z": z - 1}, z > 0, lambda k: z + k, lambda k: z + k < depth),
    )


class SlabGather:
    def __init__(self, net, name, coords, dst, length):
        self.net, self.name, self.dst, self.length = net, name, dst, length
        x, y, c, _ = coords
        self.to_x, self.to_y, self.to_mate = {"x": 1 - x}, {"y": 1 - y}, {"c": 1 - c}

    def slot(self, slot, half=None):
        first, size = slot * self.length, self.length
        if half is not None:
            size = size // 2
            first = first + half * size
        return self.dst.at[first : first + size, :]

    def put(self, slot, src, device, half=None):
        self.net.send(
            (self.name, slot, half), lambda: src, lambda: self.slot(slot, half), device
        )

    def wait(self, slot, half=None):
        self.net.arrive((self.name, slot, half), lambda: self.slot(slot, half))

    def start(self, src):
        self.put(2, src, self.to_y)
        self.put(4, src, self.to_x)
        self.put(1, src, self.to_mate)

    def forward(self):
        self.wait(2)
        self.put(6, self.slot(2, 0), self.to_x, 0)
        self.put(3, self.slot(2), self.to_mate)
        self.wait(4)
        self.put(6, self.slot(4, 1), self.to_y, 1)
        self.put(5, self.slot(4), self.to_mate)

    def forward_far(self):
        for half in range(2):
            self.wait(6, half)
            self.put(7, self.slot(6, half), self.to_mate, half)

    def sent(self):
        for slot, half in ((2, None), (4, None), (1, None), (6, 0), (6, 1), (3, None), (5, None), (7, 0), (7, 1)):
            self.net.sent((self.name, slot, half))


class AttentionGather:
    def __init__(self, net, name, depth, coords, src, dst, stacked=False):
        self.net, self.name, self.depth, self.src, self.dst = net, name, depth, src, dst
        self.stacked = stacked
        self.x, self.y, self.c, self.z = x, y, c, z = coords
        self.nx, self.ny, self.nc = 1 - x, 1 - y, 1 - c
        self.rows, self.columns = dst.shape[0] // (2 * depth), dst.shape[1] // 4
        self.to_x, self.to_y, self.to_mate = {"x": self.nx}, {"y": self.ny}, {"c": self.nc}
        self.ways = [
            (tag, device, more, {k: (origin(k), there(k), both(there(k), more)) for k in range(1, depth)})
            for tag, device, more, origin, there in along(depth, z)
        ]

    def lanes(self, yi, ci):
        return pl.ds(pl.multiple_of((2 * yi + ci) * self.columns, LANES), self.columns)

    def block(self, zi, xi, yi, ci):
        return lambda: self.dst.at[
            pl.ds(pl.multiple_of((zi * 2 + xi) * self.rows, self.rows), self.rows), self.lanes(yi, ci)
        ]

    def put(self, key, place, device, cond=None, src=None):
        block = self.block(*place)
        self.net.send((self.name,) + key, src or block, block, device, cond)

    def wait(self, key, place, cond=None):
        self.net.arrive((self.name,) + key, self.block(*place), cond)

    def own(self, yi):
        if self.stacked:
            first = pl.multiple_of((2 * yi + self.c) * self.rows, self.rows)
            return self.src.at[pl.ds(first, self.rows), :]
        return self.src.at[:, self.lanes(yi, self.c)]

    def mine(self):
        return pl.ds(pl.multiple_of((self.z * 2 + self.x) * self.rows, self.rows), self.rows)

    def start(self):
        x, y, c, z = self.x, self.y, self.c, self.z
        own = lambda: self.own(y)
        cross = lambda: self.own(self.ny)
        for tag, device, more, _ in self.ways:
            self.put(("z", tag, 1), (z, x, y, c), device, more, own)
        self.put(("x", "same"), (z, x, y, c), self.to_x, None, own)
        self.put(("x", "cross"), (z, x, self.ny, c), self.to_x, None, cross)

    def pass_z(self, k):
        for tag, device, _, steps in self.ways:
            origin, cond, on = steps[k]
            place = (origin, self.x, self.y, self.c)
            self.wait(("z", tag, k), place, cond)
            if k + 1 < self.depth:
                self.put(("z", tag, k + 1), place, device, on)
            self.put(("x", tag, k), place, self.to_x, cond)
            self.put(("y", tag, k, 0), place, self.to_y, cond)
            self.put(("c", tag, k, 0), place, self.to_mate, cond)

    def pass_x(self, k):
        if k == 0:
            for tag, yi in (("same", self.y), ("cross", self.ny)):
                place = (self.z, self.nx, yi, self.c)
                self.wait(("x", tag), place)
                self.put(("c", tag), place, self.to_mate)
            return
        for tag, _, _, steps in self.ways:
            origin, cond, _ = steps[k]
            place = (origin, self.nx, self.y, self.c)
            self.wait(("x", tag, k), place, cond)
            self.put(("y", tag, k, 1), place, self.to_y, cond)
            self.put(("c", tag, k, 1), place, self.to_mate, cond)

    def pass_y(self, k):
        for tag, _, _, steps in self.ways:
            origin, cond, _ = steps[k]
            for j, xi in ((0, self.x), (1, self.nx)):
                place = (origin, xi, self.ny, self.c)
                self.wait(("y", tag, k, j), place, cond)
                self.put(("c", tag, k, 2 + j), place, self.to_mate, cond)

    def finish(self):
        for tag, yi in (("same", self.y), ("cross", self.ny)):
            self.wait(("c", tag), (self.z, self.nx, yi, self.nc))
        for k in range(1, self.depth):
            for tag, _, _, steps in self.ways:
                origin, cond, _ = steps[k]
                for j, (xi, yi) in enumerate(
                    ((self.x, self.y), (self.nx, self.y), (self.x, self.ny), (self.nx, self.ny))
                ):
                    self.wait(("c", tag, k, j), (origin, xi, yi, self.nc), cond)


class ExpertGather:
    def __init__(self, net, name, depth, coords, src, dst):
        self.net, self.name, self.depth, self.coords, self.src, self.dst = (
            net, name, depth, coords, src, dst,
        )
        self.rows = src.shape[1]
        x, y, c, z = coords
        self.own, self.away = 4 * x + 2 * y + c, 4 * (1 - x) + 2 * y + c
        self.xs, self.z, self.half = (x, 1 - x), z, depth // 2
        self.to_x = {"x": self.xs[1]}
        self.ways = [
            (tag, device, more, {
                k: (origin(k), there(k), both(there(k), more), both(there(k), jnp.logical_not(more)))
                for k in range(1, depth)
            })
            for tag, device, more, origin, there in along(depth, z)
        ]

    def block(self, zi, xi):
        return lambda: self.dst.at[
            pl.ds(pl.multiple_of((zi * 2 + xi) * self.rows, self.rows), self.rows), :
        ]

    def put(self, key, place, device, cond=None, src=None):
        block = self.block(*place)
        self.net.send((self.name,) + key, src or block, block, device, cond)

    def start(self):
        x, _, _, z = self.coords
        for tag, device, more, _ in self.ways:
            self.put(("z", tag, 1, 0), (z, x), device, more, lambda: self.src.at[self.own])

    def start_x(self):
        x, _, _, z = self.coords
        self.put(("x",), (z, x), self.to_x, None, lambda: self.src.at[self.away])

    def pass_x(self):
        x, _, _, z = self.coords
        self.net.arrive((self.name, "x"), self.block(z, self.xs[1]))
        for tag, device, more, _ in self.ways:
            self.put(("z", tag, 1, 1), (z, self.xs[1]), device, more)

    def pass_z(self, k, j):
        if k + 1 >= self.depth:
            return
        for tag, device, _, steps in self.ways:
            origin, _, on, _ = steps[k]
            place = (origin, self.xs[j])
            self.net.arrive((self.name, "z", tag, k, j), self.block(*place), on)
            self.put(("z", tag, k + 1, j), place, device, on)

    def finish(self, near=None):
        for k in range(1, self.depth):
            for j in range(2):
                for tag, _, _, steps in self.ways:
                    origin, there, _, last = steps[k]
                    cond = there if k + 1 >= self.depth else last
                    if near is not None:
                        same = (origin >= self.half) == (self.z >= self.half)
                        cond = jnp.logical_and(cond, same if near else jnp.logical_not(same))
                    self.net.arrive(
                        (self.name, "z", tag, k, j), self.block(origin, self.xs[j]), cond
                    )

    def sent(self):
        self.net.sent((self.name, "x"))
        for k in range(1, self.depth):
            for j in range(2):
                for tag, _, _, _ in self.ways:
                    self.net.sent((self.name, "z", tag, k, j))


def inverse_rms(values):
    return lax.rsqrt(jnp.mean(values * values, axis=-1, keepdims=True) + epsilon)


def turn(values, cosine, sine):
    return values * cosine + pltpu.roll(values, HEAD_DIM // 2, axis=1) * sine


class SlabReturn:
    def __init__(self, net, name, coords, parts, length, mates, fars, chips, load, by_x):
        self.net, self.name, self.parts, self.length = net, name, parts, length
        self.mates, self.fars, self.landed, self.load, self.by_x = mates, fars, chips, load, by_x
        x, y, c, _ = coords
        self.to_x, self.to_y, self.to_core = {"x": 1 - x}, {"y": 1 - y}, {"c": 1 - c}

    def part(self, slot, half=None):
        first, size = slot * self.length, self.length
        if half is not None:
            size = size // 2
            first = first + half * size
        return self.parts.at[first : first + size, :]

    def half(self, half):
        return pl.ds(half * (self.length // 2), self.length // 2)

    def to_mate(self, chip):
        self.net.send(
            (self.name, "mate", chip),
            lambda: self.part(2 * chip + 1),
            lambda: self.mates.at[chip],
            self.to_core,
        )

    def fetch(self, chip):
        self.net.arrive((self.name, "mate", chip), lambda: self.mates.at[chip])
        self.net.local((self.name, "load", chip), self.mates.at[chip], self.load.at[chip])

    def fetched(self, chip):
        self.net.ready((self.name, "load", chip))
        return self.load.at[chip]

    def far(self, half, device):
        self.net.send(
            (self.name, "far", half),
            lambda: self.part(6, half),
            lambda: self.fars.at[self.half(half)],
            device,
        )

    def near(self, chip, half, device):
        self.net.send(
            (self.name, "chip", chip, half),
            lambda: self.part(2 * chip, half),
            lambda: self.landed.at[chip - 1, self.half(half)],
            device,
        )

    def give(self, chip):
        if chip == 3:
            self.far(0, self.to_x)
            self.far(1, self.to_x if self.by_x else self.to_y)
        elif chip == 1 and not self.by_x:
            self.near(1, 1, self.to_y)
        elif chip == 2:
            self.near(2, 0, self.to_x)
            if self.by_x:
                self.near(2, 1, self.to_x)

    def combined(self):
        places = ((0, 1, self.to_y), (1, 1, self.to_y) if self.by_x else (1, 2, self.to_x))
        for half, _, _ in places:
            here = self.half(half)
            self.net.arrive((self.name, "far", half), lambda: self.fars.at[here])
            self.net.local((self.name, "far", half), self.fars.at[here], self.load.at[3, here])
        for half, chip, device in places:
            self.net.ready((self.name, "far", half))
            part = self.part(2 * chip, half)
            accumulate(part, part, self.load.at[3, self.half(half)])
            self.near(chip, half, device)

    def total(self, out, *more):
        for chip in (1, 2):
            for half in range(2):
                self.net.arrive(
                    (self.name, "chip", chip, half), lambda: self.landed.at[chip - 1, self.half(half)]
                )
            self.net.local((self.name, "last", chip), self.landed.at[chip - 1], self.load.at[chip])
        for chip in (1, 2):
            self.net.ready((self.name, "last", chip))
        accumulate(out, self.part(0), self.load.at[1], self.load.at[2], *more)

    def sent(self):
        for chip in range(4):
            self.net.sent((self.name, "mate", chip))
        for half in range(2):
            self.net.sent((self.name, "far", half))
            for chip in (1, 2):
                self.net.sent((self.name, "chip", chip, half))


def accumulate(out, *terms):
    total, columns = out.shape
    step = 32 if columns < 1024 and total % 32 == 0 else 16

    @pl.loop(0, total // step)
    def _(i):
        here = pl.ds(pl.multiple_of(i * step, step), step)
        value = terms[0][here, :].astype(F32)
        for term in terms[1:]:
            value = value + term[here, :].astype(F32)
        out[here, :] = value.astype(out.dtype)


def clear(out):
    @pl.loop(0, out.shape[0] // 16)
    def _(i):
        here = pl.ds(pl.multiple_of(i * 16, 16), 16)
        out[here, :] = jnp.zeros((16, out.shape[1]), out.dtype)


class LineScatter:
    def __init__(self, net, name, depth, z, block, landed, load):
        self.net, self.name, self.depth, self.z = net, name, depth, z
        self.block, self.landed, self.load = block, landed, load

        steps = range(1, depth)
        up = {s: (depth - s + z, z == 0, jnp.logical_and(z >= 1, z <= s - 1)) for s in steps}
        back = depth - 1 - z
        down = {s: (z + s - depth, back == 0, jnp.logical_and(back >= 1, back <= s - 1)) for s in steps}
        self.ways = (
            ("up", {"z": z + 1}, 0, z >= 1, z < 1, up),
            ("down", {"z": z - 1}, 1, back >= 1, back < 1, down),
        )

    def send(self, key, device, way, s, t, cond):
        self.net.send(
            key,
            lambda: self.block(t),
            lambda: self.landed.at[way, s - 1],
            device,
            cond,
            slot=(self.name, key[1], s),
        )

    def start_step(self, s):
        for tag, device, way, _, _, steps in self.ways:
            target, first, _ = steps[s]
            self.send((self.name, tag, s), device, way, s, target, first)

    def start(self):
        for s in range(1, self.depth):
            self.start_step(s)

    def term(self, way, s):
        return self.landed.at[way, s - 1] if self.load is None else self.load.at[way]

    def take(self, tag, way, s):
        self.net.arrive((self.name, tag, s), lambda: self.landed.at[way, s - 1])
        if self.load is not None:
            pltpu.sync_copy(self.landed.at[way, s - 1], self.load.at[way])

    def step(self, s):
        for tag, device, way, _, _, steps in self.ways:
            t, _, cond = steps[s]

            def body():
                self.take(tag, way, s - 1)
                block = self.block(t)
                accumulate(block, block, self.term(way, s - 1))

            pl.when(cond)(body)
            self.send((self.name, tag, s, "on"), device, way, s, t, cond)

    def finish(self, *outs):
        last = self.depth - 1
        for tag, _, way, fed, unfed, _ in self.ways:
            pl.when(fed)(lambda: self.take(tag, way, last))
            pl.when(unfed)(lambda: clear(self.term(way, last)))
        rows = outs[0].shape[0]
        for i, out in enumerate(outs):
            here = pl.ds(i * rows, rows)
            accumulate(
                out, *(term.at[here, :] for term in (self.block(self.z), self.term(0, last), self.term(1, last)))
            )


class ExpertShare:
    def __init__(self, net, name, coords, result, dst):
        self.net, self.name, self.coords, self.result, self.dst = net, name, coords, result, dst
        x, y, c, _ = coords
        self.across = {4: {"x": 1 - x}, 2: {"y": 1 - y}, 1: {"c": 1 - c}}
        self.expert = 4 * x + 2 * y + c

    def place(self, flip):
        x, y, c, _ = self.coords
        fx = 1 - x if flip & 4 else x
        fy = 1 - y if flip & 2 else y
        fc = 1 - c if flip & 1 else c
        return self.dst.at[4 * fx + 2 * fy + fc]

    def put(self, flip, src, axis):
        self.net.send(
            (self.name, axis | flip), src, lambda: self.place(flip), self.across[axis]
        )

    def on(self, flip, axis):
        self.put(flip, lambda: self.place(flip), axis)

    def wait(self, flip):
        self.net.arrive((self.name, flip), lambda: self.place(flip))

    def start(self):
        x = self.coords[0]
        self.put(0, lambda: self.result.at[1 - x], 4)
        self.put(0, lambda: self.result.at[x], 2)
        self.put(0, lambda: self.result.at[x], 1)
        self.net.local(
            (self.name, "own"), lambda: self.result.at[x], lambda: self.dst.at[self.expert]
        )

    def pass_near(self):
        self.wait(4)
        self.on(4, 2)
        self.on(4, 1)
        self.wait(2)
        self.on(2, 1)

    def pass_far(self):
        self.wait(6)
        self.on(6, 1)

    def finish(self):
        self.net.ready((self.name, "own"))
        for flip in (1, 5, 3, 7):
            self.wait(flip)


class ParityGather:
    def __init__(self, net, name, coords, halves, dst, length):
        self.net, self.name, self.halves, self.dst, self.length = net, name, halves, dst, length
        self.x, y, c, _ = coords
        self.nx = 1 - self.x
        self.to_x, self.to_y, self.to_mate = {"x": self.nx}, {"y": 1 - y}, {"c": 1 - c}

    def slot(self, slot):
        return self.dst.at[slot * self.length : (slot + 1) * self.length, :]

    def put(self, slot, src, device):
        self.net.send((self.name, slot), src, lambda: self.slot(slot), device)

    def wait(self, slot):
        self.net.arrive((self.name, slot), lambda: self.slot(slot))

    def start(self):
        mine = lambda: self.halves(self.x)
        self.put(2, mine, self.to_y)
        self.put(4, lambda: self.halves(self.nx), self.to_x)
        self.put(1, mine, self.to_mate)
        self.net.local((self.name, "own"), mine, lambda: self.slot(0))

    def forward(self):
        self.wait(4)
        self.put(6, lambda: self.slot(4), self.to_y)
        self.put(5, lambda: self.slot(4), self.to_mate)
        self.wait(2)
        self.put(3, lambda: self.slot(2), self.to_mate)

    def forward_far(self):
        self.wait(6)
        self.put(7, lambda: self.slot(6), self.to_mate)

    def finish(self):
        self.net.ready((self.name, "own"))
        for slot in (1, 3, 5, 7):
            self.wait(slot)

    def left(self):
        for slot in (2, 4, 1):
            self.net.sent((self.name, slot))
        self.net.ready((self.name, "own"))


class AttentionScatter:
    def __init__(self, net, name, depth, coords, grad, left, pieces, blocks, lines, dst, low):
        self.net, self.name, self.depth, self.coords = net, name, depth, coords
        self.grad, self.left, self.pieces, self.blocks = grad, left, pieces, blocks
        self.dst, self.low = dst, low
        self.length, self.columns, self.rows = grad.shape[0], grad.shape[1] // 4, dst.shape[0]
        x, y, c, z = coords
        self.ys, self.cs = (y, 1 - y), (c, 1 - c)
        self.to_x, self.to_y, self.to_core = {"x": 1 - x}, {"y": self.ys[1]}, {"c": self.cs[1]}
        self.to_x_core = {"x": 1 - x, "c": self.cs[1]}
        self.to_y_core = {"y": self.ys[1], "c": self.cs[1]}
        self.line = LineScatter(net, name + " line", depth, z, self.block, lines, None)

    def block(self, t):
        return self.blocks.at[pl.ds(pl.multiple_of(t * self.rows, self.rows), self.rows), :]

    def lanes(self, yi, ci):
        return pl.ds(pl.multiple_of((2 * yi + ci) * self.columns, LANES), self.columns)

    def quarter(self, yi, ci):
        return self.dst.at[:, self.lanes(yi, ci)]

    def slot(self, slot):
        return self.pieces.at[slot * self.length : (slot + 1) * self.length, :]

    def put(self, slot, src, device):
        self.net.send((self.name, slot), src, lambda: self.slot(slot), device)

    def give(self, slot, fy, fc, device):
        self.put(slot, lambda: self.grad.at[:, self.lanes(self.ys[fy], self.cs[fc])], device)

    def start(self):
        self.give(2, 1, 0, self.to_y)
        self.give(3, 1, 1, self.to_y_core)
        self.give(4, 0, 0, self.to_x)
        self.give(5, 0, 1, self.to_x_core)
        self.give(1, 0, 1, self.to_core)
        self.net.local(
            (self.name, "own piece"),
            lambda: self.grad.at[:, self.lanes(self.ys[0], self.cs[0])],
            lambda: self.slot(0),
        )

    def forward(self):
        for slot in (2, 3):
            self.net.arrive((self.name, slot), lambda: self.slot(slot))
            self.put(slot + 4, lambda slot=slot: self.slot(slot), self.to_x)

    def take(self):
        for slot in (4, 5, 1, 6, 7):
            self.net.arrive((self.name, slot), lambda: self.slot(slot))
        self.net.ready((self.name, "own piece"))
        tile = 256
        for i in range(0, self.left.shape[1], tile):
            self.blocks[i : i + tile, :] = dot_tn(self.left[:, i : i + tile], self.pieces[...]).astype(BF16)
        self.line.start()

    def total(self):
        x, y, c, z = self.coords
        self.line.finish(self.low)
        self.net.local((self.name, "own"), self.low, self.quarter(y, c))
        for key, device in (("ty", self.to_y), ("tc", self.to_core)):
            self.net.send((self.name, key), lambda: self.low, lambda: self.quarter(y, c), device)

    def pass_y(self):
        x, y, c, z = self.coords
        there = lambda: self.quarter(1 - y, c)
        self.net.arrive((self.name, "ty"), there)
        self.net.send((self.name, "tyc"), there, there, self.to_core)

    def finish(self):
        x, y, c, z = self.coords
        self.net.ready((self.name, "own"))
        self.net.arrive((self.name, "tc"), lambda: self.quarter(y, 1 - c))
        self.net.arrive((self.name, "tyc"), lambda: self.quarter(1 - y, 1 - c))


def norm_back(values, gain, upstream):
    inverse = inverse_rms(values)
    normal = values * inverse
    gain_grad = jnp.sum(upstream * normal, axis=0, keepdims=True)
    scaled = upstream * gain
    return (
        inverse * (scaled - normal * jnp.mean(scaled * normal, axis=-1, keepdims=True)),
        gain_grad,
    )


def layer_kernel(depth, shard_rows, *refs):
    (
        hidden, grad_out, segment, routes, weights, cosine, sine,
        gains_in, query_in, key_in, value_in, wo_in, gate_in, up_in, down_in, grad_hbm,
        layer_out, grad_in, gain_total,
        gate_total, up_total, down_total, wq_total, wo_total,
        wq, wo, down_full, shares, probability,
        row_mates, row_fars, row_chips, out_mates, out_fars, out_chips,
        gate_lines, up_lines, down_lines, normed_all, attended_all,
        rows, grads, wide, gate_grad, down_grad, returned, wide_load, down_load, wide_low, down_low,
        wq_pieces, wo_pieces, wq_lines, wo_lines, wq_blocks, wo_blocks, wq_low, wo_low, gain_swap,
        gains, gain_rows, queries, keys, values, attended, mixed, share_in,
        send_sems, recv_sems, local_sems,
    ) = refs
    coords = x, y, c, z = tuple(lax.axis_index(n) for n in ("x", "y", "c", "z"))
    expert = 4 * x + 2 * y + c
    net = Net(send_sems, recv_sems, local_sems, c)
    length, width = hidden.shape
    units = gate_in.shape[2]
    tile, step = 256, 16
    factor = HEAD_DIM ** (-0.5)
    greet(depth, coords)

    wq_gather = AttentionGather(net, "wq", depth, coords, wq_pieces, wq, True)
    wo_gather = AttentionGather(net, "wo", depth, coords, wo_in, wo)
    gate_gather = ExpertGather(net, "gate", depth, coords, gate_in, wide.at[:, :units])
    up_gather = ExpertGather(net, "up", depth, coords, up_in, wide.at[:, units:])
    down_gather = ExpertGather(net, "down", depth, coords, down_in, down_full)
    gate_up = (gate_gather, up_gather)
    row_gather = SlabGather(net, "row", coords, rows, length)
    grad_gather = SlabGather(net, "grad", coords, grads, length)

    def gate_block(t):
        size = 2 * shard_rows
        return gate_grad.at[pl.ds(pl.multiple_of(t * size, size), size), :]

    def up_block(t):
        size = 2 * shard_rows
        return wide.at[pl.ds(pl.multiple_of(t * size, size), size), pl.ds(units, units)]

    def down_block(t):
        size = 2 * (units // (2 * depth))
        return down_grad.at[pl.ds(pl.multiple_of(t * size, size), size), :]

    gate_line = LineScatter(net, "gate line", depth, z, gate_block, gate_lines, wide_load)
    up_line = LineScatter(net, "up line", depth, z, up_block, up_lines, wide_load)
    down_line = LineScatter(net, "down line", depth, z, down_block, down_lines, down_load)
    row_back = SlabReturn(net, "row back", coords, grads, length, row_mates, row_fars, row_chips, returned, False)

    down_share = ExpertShare(net, "down sum", coords, down_low, down_total)
    gate_share = ExpertShare(net, "gate sum", coords, wide_low.at[0], gate_total)
    up_share = ExpertShare(net, "up sum", coords, wide_low.at[1], up_total)

    def finish_line(line, share):
        line.finish(share.result.at[0], share.result.at[1])
        share.start()

    def columns_of(i):
        return lambda parity: returned.at[
            i, :, pl.ds(pl.multiple_of(parity * (width // 2), LANES), width // 2)
        ]

    normed_gather = ParityGather(net, "normed", coords, columns_of(0), normed_all, length)
    attended_gather = ParityGather(net, "attended", coords, columns_of(1), attended_all, length)

    def simple_send(key, source, target, device, cond=None):
        net.send(key, lambda: source, lambda: target, device, cond)

    to_mate, to_x, to_y = {"c": 1 - c}, {"x": 1 - x}, {"y": 1 - y}
    to_xy = {**to_x, **to_y}

    me = z * 2 + x
    base = [net.slot(("gains", s)) for s in range(2 * depth)][0]

    def gain_copy(s, index):
        return pltpu.make_async_remote_copy(
            src_ref=gains_in,
            dst_ref=gains.at[me],
            send_sem=send_sems.at[index],
            recv_sem=recv_sems.at[base + me],
            device_id={"z": jnp.int32(s // 2), "x": jnp.int32(s % 2)},
            device_id_type=MESH,
        )

    def start_shares():
        net.local("own grad", grad_hbm, grads.at[:length])
        net.send(("share", 1), lambda: share_in, lambda: shares.at[1], to_mate)
        net.send(("share", 2), lambda: share_in, lambda: shares.at[2], to_y)
        net.send(("share", 4), lambda: share_in, lambda: shares.at[4], to_x)
        net.send(("share", 6), lambda: share_in, lambda: shares.at[6], to_xy)

    def pass_shares():
        for slot in (2, 4, 6):
            net.arrive(("share", slot), lambda: shares.at[slot])
            net.send(
                ("share", slot + 1),
                lambda slot=slot: shares.at[slot],
                lambda slot=slot: shares.at[slot + 1],
                to_mate,
            )

    quarter = wq.shape[1] // 4
    query_end, key_end = query_in.shape[1], query_in.shape[1] + key_in.shape[1]
    bounce = []

    def middle(i, first, size):
        return wq_pieces.at[i * shard_rows : (i + 1) * shard_rows, first : first + size]

    for i, j in enumerate(range(0, wq.shape[1], quarter)):
        for source, begin, end in (
            (query_in, 0, query_end), (key_in, query_end, key_end), (value_in, key_end, wq.shape[1])
        ):
            low, high = max(j, begin), min(j + quarter, end)
            if low < high:
                net.local(("in", i, low), source.at[:, low - begin : high - begin], middle(i, low - j, high - low))
                net.ready_later(("in", i, low))
        bounce.append((middle(i, 0, quarter), wq, j))
    for j in range(0, width, quarter):
        i = len(bounce)
        net.local(("in", i, 0), wo_in.at[:, j : j + quarter], middle(i, 0, quarter))
        net.ready_later(("in", i, 0))
        bounce.append((middle(i, 0, quarter), wo, j))
    net.ready_all()
    wq_gather.start()
    net.local("gains", gains_in, gains.at[me])
    gain_sends = []
    for s in range(2 * depth):
        index = net.index()
        gain_sends.append((s, index))
        pl.when(me != s)(lambda: gain_copy(s, index).start())
    down_rows = down_in.shape[1]
    net.local("down in", down_in.at[expert], down_load.at[0, :down_rows])
    for gather in (gate_gather, up_gather):
        net.local((gather.name, "own"), gather.src.at[gather.own], gather.block(z, x)())
    for i, (source, target, j) in enumerate(bounce):
        net.local(("out", i), source, target.at[wq_gather.mine(), j : j + quarter])
    names = lax.broadcasted_iota(jnp.int32, (LANES, length), 0)
    share = jnp.zeros((LANES, length), F32)
    for i in range(routes.shape[0]):
        share = share + jnp.where(names == routes[i : i + 1, :], weights[i : i + 1, :], 0.0)
    share_in[...] = share.T
    net.ready("down in")
    net.local("down out", down_load.at[0, :down_rows], down_gather.block(z, x)())
    wo_gather.start()
    wq_gather.pass_z(1)
    wo_gather.pass_z(1)
    wq_gather.pass_z(2)
    gate_gather.start_x()
    up_gather.start_x()
    wo_gather.pass_z(2)
    gate_gather.start()
    up_gather.start()
    wq_gather.pass_x(1)
    for k in range(3, depth):
        wq_gather.pass_z(k)
    grad_gather.start(grad_hbm)
    start_shares()
    gate_gather.pass_z(1, 0)
    up_gather.pass_z(1, 0)
    for k in range(3, depth):
        wo_gather.pass_z(k)
    wq_gather.pass_x(2)
    wq_gather.pass_x(0)
    gate_gather.pass_x()
    up_gather.pass_x()
    for k in range(3, depth):
        wq_gather.pass_x(k)
    down_gather.start_x()
    wq_gather.pass_y(1)
    wo_gather.pass_x(1)
    wo_gather.pass_x(0)
    gate_gather.pass_z(1, 1)
    up_gather.pass_z(1, 1)
    for k in range(3, depth):
        wq_gather.pass_y(k)
    wo_gather.pass_x(2)
    wq_gather.pass_y(2)
    wq_gather.finish()

    def attention_forward(wq_here, wo_here, chances, order, normed):
        def project():
            for i in range(len(bounce)):
                net.ready(("out", i))
            for key in (("z", "up", 1), ("z", "down", 1), ("x", "same"), ("x", "cross")):
                net.sent(("wq",) + key)
            net.local("wq here", wq, wq_here)
            gains_wide()
            project_heads()

        def gains_wide():
            for s in range(2 * depth):
                pl.when(me != s)(lambda: net.arrive(("gains", s), lambda: gains.at[s]))
            net.ready("gains")
            wide_gain = None
            for s in range(2 * depth):
                rest = jnp.zeros((8, width - gains.shape[2]), F32)
                piece = jnp.concatenate([gains[s], rest], axis=1)
                piece = piece if s == 0 else pltpu.roll(piece, s * shard_rows, axis=1)
                wide_gain = piece if wide_gain is None else wide_gain + piece
            gain_rows[...] = wide_gain

            @pl.loop(0, length // step)
            def _(i):
                here = pl.ds(pl.multiple_of(i * step, step), step)
                one = hidden[here, :].astype(F32)
                normed[here, :] = (one * inverse_rms(one) * gain_rows[0:1, :]).astype(BF16)

        def project_heads():
            net.ready("wq here")
            cos, sin = cosine[...], sine[...]
            for start in range(0, wq.shape[1], tile):
                part = dot_nn(normed[...], wq_here[:, start : start + tile])
                for at in range(start, start + tile, HEAD_DIM):
                    head, one = at // HEAD_DIM, part[:, at - start : at - start + HEAD_DIM]
                    if head < HEADS:
                        queries[head * length : (head + 1) * length, :] = turn(one, cos, sin).astype(BF16)
                    elif head < HEADS + KV_HEADS:
                        at_row = (head - HEADS) * length
                        keys[at_row : at_row + length, :] = turn(one, cos, sin).astype(BF16)
                    else:
                        at_row = (head - HEADS - KV_HEADS) * length
                        values[at_row : at_row + length, :] = one.astype(BF16)

        def heads_forward():
            across = jnp.broadcast_to(segment[...].astype(F32), (length, length))
            later = lax.broadcasted_iota(jnp.int32, (length, length), 0)
            allowed = (across == across.T) & (later >= lax.broadcasted_iota(jnp.int32, (length, length), 1))
            for head in range(HEADS):
                kv = head // GROUP
                here = slice(head * length, (head + 1) * length)
                there = slice(kv * length, (kv + 1) * length)
                scores = dot_nt(queries[here, :], keys[there, :]) * factor
                scores = jnp.where(allowed, scores, masked_score)
                terms = jnp.exp(scores - jnp.max(scores, axis=-1, keepdims=True))
                chance = terms / jnp.sum(terms, axis=-1, keepdims=True)
                chances[here, :] = chance
                attended[:, head * HEAD_DIM : (head + 1) * HEAD_DIM] = dot_nn(
                    chance.astype(BF16), values[there, :]
                ).astype(BF16)
            net.local("keep chances", chances, probability)

        def mix():
            net.local("wo here", wo, wo_here)
            net.ready("wo here")
            for start in range(0, width, tile):
                there = slice(start, start + tile)
                mixed[:, there] = hidden[:, there].astype(F32) + dot_nn(attended[...], wo_here[:, there])

            @pl.loop(0, length // step)
            def _(i):
                here = pl.ds(pl.multiple_of(i * step, step), step)
                total = mixed[here, :]
                rows[here, :] = (total * inverse_rms(total) * gain_rows[1:2, :]).astype(BF16)

        def by_parity():
            for s in range(2 * depth):
                size = (shard_rows, width)
                first = (s % 2) * (width // 2) + (s // 2) * shard_rows
                hit = lax.broadcasted_iota(jnp.int32, size, 1) - first == lax.broadcasted_iota(jnp.int32, size, 0)
                order[s * shard_rows : (s + 1) * shard_rows, :] = hit.astype(F32).astype(BF16)
            for i, source in enumerate((normed, attended)):
                for j in range(0, width, 512):
                    returned[i, :, j : j + 512] = dot_nn(source[...], order[:, j : j + 512]).astype(BF16)

        project()
        for k in range(3, depth):
            wo_gather.pass_x(k)
        grad_gather.forward()
        pass_shares()
        for k in range(2, depth):
            gate_gather.pass_z(k, 1)
            up_gather.pass_z(k, 1)
        heads_forward()
        down_gather.start()
        for k in range(3, depth):
            wo_gather.pass_y(k)
        for k in range(2, depth):
            gate_gather.pass_z(k, 0)
            up_gather.pass_z(k, 0)
        wo_gather.pass_y(1)
        down_gather.pass_x()
        wo_gather.pass_y(2)
        wo_gather.finish()
        mix()
        row_gather.start(rows.at[:length, :])
        by_parity()
        net.ready("keep chances")

    pl.run_scoped(
        attention_forward,
        pltpu.VMEM(wq.shape, BF16),
        pltpu.VMEM(wo.shape, BF16),
        pltpu.VMEM((HEADS * length, length), F32),
        pltpu.VMEM((width, width), BF16),
        pltpu.VMEM((length, width), BF16),
    )

    down_gather.pass_z(1, 0)
    down_gather.pass_z(1, 1)
    gate_gather.finish()
    up_gather.finish()
    row_gather.forward()

    def experts(down, hidden_act, both_grads, share_here, parts_out):
        out_back = SlabReturn(net, "out back", coords, parts_out, length, out_mates, out_fars, out_chips, returned, False)
        lane = lax.broadcasted_iota(jnp.int32, (length, LANES), 1)

        def share_of(r):
            return jnp.sum(jnp.where(lane == expert, share_here[r], 0.0), axis=1, keepdims=True)

        def first_half(first, count):
            @pl.loop(first, first + count)
            def _(r):
                here = pl.ds(pl.multiple_of(r * length, length), length)
                grads[here, :] = (share_of(r) * grads[here, :].astype(F32)).astype(BF16)
                for j in range(0, units, tile):
                    gate = dot_nn(rows[here, :], wide[:, j : j + tile])
                    up = dot_nn(rows[here, :], wide[:, units + j : units + j + tile])
                    sigmoid = 1.0 / (1.0 + jnp.exp(-gate))
                    silu = gate * sigmoid
                    hidden_act[here, j : j + tile] = (silu * up).astype(BF16)
                    both_grads[here, j : j + tile] = (
                        up * sigmoid * (1.0 + gate * (1.0 - sigmoid))
                    ).astype(BF16)
                    both_grads[here, units + j : units + j + tile] = silu.astype(BF16)

        def first_rows():
            net.local("own share", share_in, share_here.at[0])
            for slot in (1, 2, 3, 4, 5, 6, 7):
                if slot % 2:
                    net.arrive(("share", slot), lambda: shares.at[slot])
            net.local("shares", shares.at[1:], share_here.at[1:])
            row_gather.wait(1)
            grad_gather.wait(1)
            for name in ("own grad", "own share", "shares", ("gate", "own"), ("up", "own")):
                net.ready(name)
            first_half(0, 2)

        def gathered(*slots):
            for gather in (row_gather, grad_gather):
                for slot, half in slots:
                    gather.wait(slot, half)

        def left(*slots):
            for slot, half in slots:
                net.sent(("grad", slot, half))

        def middle_rows():
            gathered((3, None), (5, None))
            left((6, 0), (3, None), (6, 1), (5, None))
            first_half(2, 4)

        def last_rows():
            gathered((7, 0), (7, 1))
            left((7, 0), (7, 1))
            first_half(6, 2)

        def down_weight_grad():
            @pl.loop(0, units // tile)
            def _(i):
                at = pl.ds(pl.multiple_of(i * tile, tile), tile)
                for j in range(0, width, 512):
                    down_grad[at, j : j + 512] = dot_tn(hidden_act[:, at], grads[:, j : j + 512]).astype(BF16)

        near_half = units // 2 * (z >= depth // 2).astype(jnp.int32)
        near = pl.multiple_of(near_half, LANES)
        far = pl.multiple_of(units // 2 - near_half, LANES)

        def take_down(first):
            if first is near:
                net.ready("down out")
            here = pl.ds(first, units // 2)
            name = "down near" if first is near else "down far"
            net.local(name, down_full.at[here, :], down.at[here, :])
            net.ready(name)

        def hidden_grads(first):
            @pl.loop(0, EXPERTS)
            def _(r):
                here = pl.ds(pl.multiple_of(r * length, length), length)
                for j in range(0, units // 2, tile):
                    size = min(tile, units // 2 - j)
                    at = pl.multiple_of(first + j, LANES)
                    back = dot_nt(grads[here, :], down[pl.ds(at, size), :])
                    for lane_first in (at, pl.multiple_of(units + at, LANES)):
                        lanes = pl.ds(lane_first, size)
                        both_grads[here, lanes] = (
                            back * both_grads[here, lanes].astype(F32)
                        ).astype(BF16)

        def row_grad(slot, more=None):
            here = slice(slot * length, (slot + 1) * length)
            for j in range(0, width, 512):
                part = dot_nt(both_grads[here, :], wide[j : j + 512, :])
                if more is not None:
                    part = part + more[:, j : j + 512].astype(F32)
                grads[here, j : j + 512] = part.astype(BF16)

        def out_rows(slot, more=None):
            here = slice(slot * length, (slot + 1) * length)
            share = share_of(slot)
            for j in range(0, width, 512):
                part = share * dot_nn(hidden_act[here, :], down[:, j : j + 512])
                if more is not None:
                    part = part + more[:, j : j + 512].astype(F32)
                parts_out[here, j : j + 512] = part.astype(BF16)

        order = (3, 1, 2, 0)

        def give_mates(back, compute):
            for chip in order:
                compute(2 * chip + 1)
                back.to_mate(chip)

        def give_chips(back, compute):
            normed_gather.left()
            attended_gather.left()
            back.fetch(order[0])
            for i, chip in enumerate(order):
                if i + 1 < len(order):
                    back.fetch(order[i + 1])
                compute(2 * chip, back.fetched(chip))
                back.give(chip)

        def weight_grad(first, target):
            @pl.loop(0, width // tile)
            def _(i):
                at = pl.ds(pl.multiple_of(i * tile, tile), tile)
                target[at, :] = dot_tn(rows[:, at], both_grads[:, first : first + units]).astype(BF16)

        net.settle("wq", "wo")
        first_rows()
        normed_gather.start()
        for k in range(2, depth):
            down_gather.pass_z(k, 1)
        attended_gather.start()
        grad_gather.forward_far()
        middle_rows()
        for k in range(2, depth):
            down_gather.pass_z(k, 0)
        row_gather.forward_far()
        down_gather.finish(True)
        take_down(near)
        last_rows()
        down_weight_grad()
        down_line.start()
        normed_gather.forward()
        hidden_grads(near)
        attended_gather.forward()
        down_gather.finish(False)
        take_down(far)
        give_mates(out_back, out_rows)
        give_chips(out_back, out_rows)
        down_line.step(2)
        hidden_grads(far)
        give_mates(row_back, row_grad)
        out_back.combined()
        weight_grad(0, gate_grad)
        gate_line.start_step(1)
        for s in range(3, depth):
            down_line.step(s)
        give_chips(row_back, row_grad)
        up_gather.sent()
        weight_grad(units, wide.at[:, units:])
        up_line.start_step(1)
        for s in range(2, depth):
            gate_line.start_step(s)
            up_line.start_step(s)
        attended_gather.forward_far()
        row_back.combined()
        gate_line.step(2)
        finish_line(down_line, down_share)
        normed_gather.forward_far()
        net.settle("gate", "up", "down", "row", "grad", "share", "normed", "attended")
        out_back.total(layer_out, mixed)
        up_line.step(2)
        out_back.sent()

    pl.run_scoped(
        experts,
        pltpu.VMEM((units, width), BF16),
        pltpu.VMEM((EXPERTS * length, units), BF16),
        pltpu.VMEM((EXPERTS * length, 2 * units), BF16),
        pltpu.VMEM((EXPERTS, length, LANES), F32),
        pltpu.VMEM((EXPERTS * length, width), BF16),
    )

    def attention_backward(weight, chances, normed_here, attended_here, upstream_two, mixed_grad, mixed_low, attended_grad, qkv_grad):
        net.local("wo again", wo, weight.at[:, :width])
        net.local("chance 0", probability.at[: GROUP * length], chances)
        wo_net = AttentionScatter(
            net, "wo sum", depth, coords, mixed_low, attended_here, wo_pieces, wo_blocks, wo_lines, wo_total, wo_low
        )
        wq_net = AttentionScatter(
            net, "wq sum", depth, coords, qkv_grad, normed_here, wq_pieces, wq_blocks, wq_lines, wq_total, wq_low
        )

        def take_normed():
            normed_gather.finish()
            net.local("normed here", normed_all, normed_here)

        def take_attended():
            attended_gather.finish()
            net.local("attended here", attended_all, attended_here)

        def norm_two_back():
            row_back.total(upstream_two)
            gain_swap[0] = jnp.zeros(gain_swap.shape[1:], F32)

            @pl.loop(0, length // step)
            def _(i):
                here = pl.ds(pl.multiple_of(i * step, step), step)
                part, gain_two = norm_back(mixed[here, :], gain_rows[1:2, :], upstream_two[here, :])
                total = grad_out[here, :].astype(F32) + part
                mixed_grad[here, :] = total
                mixed_low[here, :] = total.astype(BF16)
                gain_swap[0, 1:2, :] += gain_two

        def attended_back():
            net.ready("wo again")
            for i in range(0, width, 512):
                attended_grad[:, i : i + 512] = dot_nt(
                    mixed_low[...], weight[i : i + 512, :width]
                ).astype(BF16)
            net.local("wq again", wq, weight)

        def heads_back():
            cos, sin = cosine[...], -sine[...]
            for kv in range(KV_HEADS):
                net.ready("chance %d" % kv)
                there = slice(kv * length, (kv + 1) * length)
                value_sum = key_sum = None
                for g in range(GROUP):
                    head = kv * GROUP + g
                    here = slice(head * length, (head + 1) * length)
                    cols = slice(head * HEAD_DIM, (head + 1) * HEAD_DIM)
                    chance = chances[g * length : (g + 1) * length, :]
                    back = attended_grad[:, cols]
                    prob_grad = dot_nt(back, values[there, :])
                    value_part = dot_tn(chance.astype(BF16), back)
                    inner = jnp.sum(chance * prob_grad, axis=-1, keepdims=True)
                    score_grad = (chance * (prob_grad - inner)).astype(BF16)
                    query_grad = dot_nn(score_grad, keys[there, :]) * factor
                    key_part = dot_tn(score_grad, queries[here, :])
                    qkv_grad[:, cols] = turn(query_grad, cos, sin).astype(BF16)
                    value_sum = value_part if value_sum is None else value_sum + value_part
                    key_sum = key_part if key_sum is None else key_sum + key_part
                if kv + 1 < KV_HEADS:
                    size = GROUP * length
                    net.local("chance %d" % (kv + 1), probability.at[(kv + 1) * size : (kv + 2) * size], chances)
                first = (HEADS + kv) * HEAD_DIM
                qkv_grad[:, first : first + HEAD_DIM] = turn(key_sum * factor, cos, sin).astype(BF16)
                first = first + KV_HEADS * HEAD_DIM
                qkv_grad[:, first : first + HEAD_DIM] = value_sum.astype(BF16)

        def norm_one_back():
            net.ready("wq again")
            for i in range(0, width, 512):
                upstream_two[:, i : i + 512] = dot_nt(qkv_grad[...], weight[i : i + 512, :])

            @pl.loop(0, length // step)
            def _(i):
                here = pl.ds(pl.multiple_of(i * step, step), step)
                part, gain_one = norm_back(
                    hidden[here, :].astype(F32), gain_rows[0:1, :], upstream_two[here, :]
                )
                grad_in[here, :] = (mixed_grad[here, :] + part).astype(BF16)
                gain_swap[0, 0:1, :] += gain_one

        axes = (("c", to_mate), ("x", to_x), ("y", to_y))

        def gain_start(i):
            net.send(
                ("gain", axes[i][0]),
                lambda: gain_swap.at[2 * i],
                lambda: gain_swap.at[2 * i + 1],
                axes[i][1],
            )

        def gain_add(i):
            net.arrive(("gain", axes[i][0]), lambda: gain_swap.at[2 * i + 1])
            gain_swap[2 * i + 2] = gain_swap[2 * i] + gain_swap[2 * i + 1]

        def gains_out():
            for far in range(1, depth):
                simple_send(("gain", "up", far), gain_swap.at[6], gain_swap.at[5 + 2 * far], {"z": z + far}, z + far < depth)
                simple_send(("gain", "down", far), gain_swap.at[6], gain_swap.at[6 + 2 * far], {"z": z - far}, z - far >= 0)

        def gains_in_all():
            for far in range(1, depth):
                for tag, slot, cond in (
                    ("up", 5 + 2 * far, z - far >= 0), ("down", 6 + 2 * far, z + far < depth)
                ):

                    def take():
                        net.arrive(("gain", tag, far), lambda: gain_swap.at[slot])
                        gain_swap[6] += gain_swap[slot]

                    pl.when(cond)(take)
            for s in range(2 * depth):

                def pick(s=s):
                    value = gain_swap[6]
                    if s:
                        value = pltpu.roll(value, width - s * shard_rows, axis=1)
                    gain_total[...] = value[:, : gain_total.shape[1]]

                pl.when(me == s)(pick)

        norm_two_back()
        take_attended()
        wo_net.start()
        attended_back()
        for s in range(3, depth):
            gate_line.step(s)
        wo_net.forward()
        heads_back()
        wq_net.start()
        down_share.pass_near()
        for s in range(3, depth):
            up_line.step(s)
        take_normed()
        norm_one_back()
        wq_net.forward()
        finish_line(gate_line, gate_share)
        net.ready("attended here")
        wo_net.take()
        down_share.pass_far()
        finish_line(up_line, up_share)
        gain_start(0)
        wo_net.line.step(2)
        net.ready("normed here")
        wq_net.take()
        gate_share.pass_near()
        gain_add(0)
        for s in range(3, depth):
            wo_net.line.step(s)
        wq_net.line.step(2)
        gain_start(1)
        up_share.pass_near()
        gate_share.pass_far()
        for s in range(3, depth):
            wq_net.line.step(s)
        gain_add(1)
        gain_start(2)
        wo_net.total()
        wq_net.total()
        up_share.pass_far()
        wo_net.pass_y()
        gain_add(2)
        gains_out()
        wq_net.pass_y()
        for key in [key for key in net.sends if key[0] == "gain"]:
            net.sent(key)
        gains_in_all()
        for one in (down_share, gate_share, up_share, wo_net, wq_net):
            one.finish()
        net.drain()

    pl.run_scoped(
        attention_backward,
        pltpu.VMEM(wq.shape, BF16),
        pltpu.VMEM((GROUP * length, length), F32),
        pltpu.VMEM((EXPERTS * length, width // 2), BF16),
        pltpu.VMEM((EXPERTS * length, width // 2), BF16),
        pltpu.VMEM((length, width), F32),
        pltpu.VMEM((length, width), F32),
        pltpu.VMEM((length, width), BF16),
        pltpu.VMEM((length, width), BF16),
        pltpu.VMEM((length, wq.shape[1]), BF16),
    )
    for s, index in gain_sends:
        pl.when(me != s)(lambda: gain_copy(s, index).wait_send())
    assert net.count <= send_sems.shape[0] and len(net.slots) <= recv_sems.shape[0]
    assert len(net.locals) <= local_sems.shape[0]


def layer_call(
    depth, shard_rows, hidden, grad_out, segments, routes, weights, cosine, sine, gains, query_in, key_in,
    value_in, wo_in, gate_in, up_in, down_in,
):
    length, width = hidden.shape
    wide = query_in.shape[1] + key_in.shape[1] + value_in.shape[1]
    units, down_rows = gate_in.shape[2], down_in.shape[1]
    here, there = pl.BlockSpec(memory_space=pltpu.VMEM), pl.BlockSpec(memory_space=pltpu.HBM)

    def shape(*dims, dtype=BF16):
        return jax.ShapeDtypeStruct(dims, dtype)

    returns = [shape(4, length, width), shape(length, width), shape(2, length, width)]
    out_shape = [
        shape(length, width), shape(length, width), shape(*gains.shape, dtype=F32),
        shape(EXPERTS, shard_rows, units), shape(EXPERTS, shard_rows, units),
        shape(EXPERTS, down_rows, width),
        shape(shard_rows, wide), shape(shard_rows, width),
        shape(width, wide), shape(width, width), shape(units, width),
        shape(EXPERTS, length, LANES, dtype=F32), shape(HEADS * length, length, dtype=F32),
        *returns, *returns,
        shape(2, depth - 1, 2 * shard_rows, units), shape(2, depth - 1, 2 * shard_rows, units),
        shape(2, depth - 1, 2 * down_rows, width),
        shape(EXPERTS * length, width // 2), shape(EXPERTS * length, width // 2),
    ]
    copies, arrivals = 42 * depth, 58 * depth + 58
    return pl.pallas_call(
        functools.partial(layer_kernel, depth, shard_rows),
        out_shape=out_shape,
        in_specs=[here] * 7 + [there] * 9,
        out_specs=[here] * 3 + [there] * (len(out_shape) - 3),
        scratch_shapes=[
            pltpu.VMEM((EXPERTS * length, width), BF16),
            pltpu.VMEM((EXPERTS * length, width), BF16),
            pltpu.VMEM((width, 2 * units), BF16),
            pltpu.VMEM((width, units), BF16),
            pltpu.VMEM((units, width), BF16),
            pltpu.VMEM((4, length, width), BF16),
            pltpu.VMEM((2, 2 * shard_rows, units), BF16),
            pltpu.VMEM((2, 2 * down_rows, width), BF16),
            pltpu.VMEM((2, 2, shard_rows, units), BF16),
            pltpu.VMEM((2, down_rows, width), BF16),
            pltpu.VMEM((EXPERTS * length, wide // 4), BF16),
            pltpu.VMEM((EXPERTS * length, width // 4), BF16),
            pltpu.VMEM((2, depth - 1, shard_rows, wide // 4), BF16),
            pltpu.VMEM((2, depth - 1, shard_rows, width // 4), BF16),
            pltpu.VMEM((depth * shard_rows, wide // 4), BF16),
            pltpu.VMEM((depth * shard_rows, width // 4), BF16),
            pltpu.VMEM((shard_rows, wide // 4), BF16),
            pltpu.VMEM((shard_rows, width // 4), BF16),
            pltpu.VMEM((5 + 2 * depth, 8, width), F32),
            pltpu.VMEM((2 * depth, *gains.shape), F32),
            pltpu.VMEM((8, width), F32),
            pltpu.VMEM((HEADS * length, HEAD_DIM), BF16),
            pltpu.VMEM((KV_HEADS * length, HEAD_DIM), BF16),
            pltpu.VMEM((KV_HEADS * length, HEAD_DIM), BF16),
            pltpu.VMEM((length, width), BF16),
            pltpu.VMEM((length, width), F32),
            pltpu.VMEM((length, LANES), F32),
            pltpu.SemaphoreType.DMA((copies,)),
            pltpu.SemaphoreType.DMA((arrivals,)),
            pltpu.SemaphoreType.DMA((60,)),
        ],
        compiler_params=pltpu.CompilerParams(
            collective_id=1, has_side_effects=True, vmem_limit_bytes=VMEM_LIMIT
        ),
    )(
        hidden, grad_out, segments, routes, weights, cosine, sine, gains, query_in, key_in, value_in, wo_in,
        gate_in, up_in, down_in, grad_out,
    )


def rotary_tables(length, head_width):
    half_width = head_width // 2
    frequency = rotary_base ** (-2.0 * np.arange(half_width, dtype=np.float32) / head_width)
    angles = np.arange(length, dtype=np.float32)[:, None] * frequency.astype(np.float32)[None, :]
    cosine, sine = np.cos(angles), np.sin(angles)
    return (
        np.concatenate([cosine, cosine], axis=1).astype(np.float32),
        np.concatenate([-sine, sine], axis=1).astype(np.float32),
    )


def widen_kernel(*refs):
    wq, wo, gate, up, down, layer, grad = refs[:7]
    query_out, key_out, value_out, wo_out, gate_out, up_out, down_out, layer_out, grad_out = refs[7:16]
    low, high, same, in_sems, out_sems, same_sems = refs[16:]
    queries_end = HEADS * HEAD_DIM
    kv = KV_HEADS * HEAD_DIM
    rows = wq.shape[0]
    width = wo.shape[1]
    pieces = [
        (wq.at[:, :queries_end], query_out),
        (wo, wo_out),
    ]
    for source, target in ((gate, gate_out), (up, up_out), (down, down_out)):
        for e in range(EXPERTS):
            pieces.append((source.at[e], target.at[e]))
    pieces.append((wq.at[:, queries_end : queries_end + kv], key_out))
    pieces.append((wq.at[:, queries_end + kv :], value_out))
    depth = low.shape[0]

    def place(buffer, i):
        r, n = pieces[i][0].shape
        return buffer.at[i % depth, :r, :n]

    def read(i):
        return pltpu.make_async_copy(pieces[i][0], place(low, i), in_sems.at[i % depth])

    def write(i):
        return pltpu.make_async_copy(place(high, i), pieces[i][1], out_sems.at[i % depth])

    passed = ((layer, layer_out), (grad, grad_out))

    def take(i):
        return pltpu.make_async_copy(passed[i][0], same.at[i], same_sems.at[i])

    def put(i):
        return pltpu.make_async_copy(same.at[i], passed[i][1], same_sems.at[2 + i])

    for i in range(depth - 1):
        read(i).start()
    for i in range(2):
        take(i).start()
    for i in range(len(pieces)):
        if i + depth - 1 < len(pieces):
            read(i + depth - 1).start()
        read(i).wait()
        if i >= depth:
            write(i - depth).wait()
        place(high, i)[...] = place(low, i)[...].astype(F32)
        write(i).start()
        if i in (depth, depth + 1):
            take(i - depth).wait()
            put(i - depth).start()
    for i in range(2):
        put(i).wait()
    for i in range(max(0, len(pieces) - depth), len(pieces)):
        write(i).wait()


def widen_call(wq, wo, gate, up, down, layer, grad):
    rows, width = wo.shape
    there = pl.BlockSpec(memory_space=pltpu.HBM)
    queries_end, kv = HEADS * HEAD_DIM, KV_HEADS * HEAD_DIM

    def shape(*dims):
        return jax.ShapeDtypeStruct(dims, F32)

    buffers = 6
    return pl.pallas_call(
        widen_kernel,
        out_shape=[
            shape(rows, queries_end), shape(rows, kv), shape(rows, kv), shape(*wo.shape),
            shape(*gate.shape), shape(*up.shape), shape(*down.shape),
            jax.ShapeDtypeStruct(layer.shape, layer.dtype), jax.ShapeDtypeStruct(grad.shape, grad.dtype),
        ],
        in_specs=[there] * 7,
        out_specs=[there] * 9,
        scratch_shapes=[
            pltpu.VMEM((buffers, rows, width), BF16),
            pltpu.VMEM((buffers, rows, width), F32),
            pltpu.VMEM((2, *layer.shape), BF16),
            pltpu.SemaphoreType.DMA((buffers,)),
            pltpu.SemaphoreType.DMA((buffers,)),
            pltpu.SemaphoreType.DMA((4,)),
        ],
        compiler_params=pltpu.CompilerParams(vmem_limit_bytes=VMEM_LIMIT),
    )(wq, wo, gate, up, down, layer, grad)


def make_shards(sizes):
    depth = sizes["z"]

    def shards(
        hidden_in,
        segments,
        routes,
        gate_weights,
        grad_out,
        attn_gain,
        query_weight,
        key_weight,
        value_weight,
        output_weight,
        ffn_gain,
        gate_weight,
        up_weight,
        down_weight,
    ):
        length, width = hidden_in.shape
        shard_rows = attn_gain.shape[0]
        spare = -(-shard_rows // LANES) * LANES - shard_rows
        first, second = (jnp.pad(gain.astype(F32), (0, spare))[None, :] for gain in (attn_gain, ffn_gain))
        place = lax.broadcasted_iota(jnp.int32, (8, shard_rows + spare), 0)
        gains = jnp.where(place == 0, first, jnp.where(place == 1, second, 0.0))
        cosine, sine = rotary_tables(length, HEAD_DIM)
        layer_out, grad_in, gain_total, gate_total, up_total, down_total, wq_total, wo_total = (
            layer_call(
                depth, shard_rows, hidden_in, grad_out, segments, routes.T, gate_weights.T, cosine, sine,
                gains, query_weight, key_weight, value_weight, output_weight, gate_weight, up_weight,
                down_weight,
            )[:8]
        )
        def whole(value):
            return lax.psum(value.astype(F32), "o") if sizes["o"] > 1 else value

        wq_total = whole(wq_total)
        queries_end = HEADS * HEAD_DIM
        keys_end = queries_end + KV_HEADS * HEAD_DIM
        gain_total = gain_total[:, :shard_rows]
        gain_total = whole(gain_total)
        parts = (wq_total, whole(wo_total), whole(gate_total), whole(up_total), whole(down_total))
        if sizes["o"] == 1:
            *parts, layer_out, grad_in = widen_call(*parts, layer_out, grad_in)
        else:
            parts = (
                wq_total[:, :queries_end], wq_total[:, queries_end:keys_end], wq_total[:, keys_end:], *parts[1:]
            )
        query_grad, key_grad, value_grad, output_grad, gate_grad, up_grad, down_grad = parts
        return (
            layer_out,
            grad_in,
            gain_total[0],
            query_grad,
            key_grad,
            value_grad,
            output_grad,
            gain_total[1],
            gate_grad,
            up_grad,
            down_grad,
        )

    return shards


def solution(mesh):
    reps, shard_count = mesh.shape["rep"], mesh.shape["shard"]
    sizes = {"o": reps // 4, "y": 2, "c": 2, "z": shard_count // 2, "x": 2}
    fine = Mesh(mesh.devices.reshape(tuple(sizes.values())), tuple(sizes))
    tokens = P(("o", "y", "c", "z", "x"), None)
    first, second = P(("z", "x")), P(None, ("z", "x"), None)
    matrix = P(("z", "x"), None)
    return jax.shard_map(
        make_shards(sizes),
        mesh=fine,
        in_specs=(
            (tokens,) * 5 + (first, matrix, matrix, matrix, matrix, first) + (second,) * 3
        ),
        out_specs=(
            (tokens,) * 2 + (first, matrix, matrix, matrix, matrix, first) + (second,) * 3
        ),
        check_vma=False,
    )
```

```python
import functools

import jax
import jax.numpy as jnp
import numpy as np
from jax import lax
from jax.experimental import pallas as pl
from jax.experimental.pallas import tpu as pltpu
from jax.sharding import Mesh
from jax.sharding import PartitionSpec as P

HEADS = 12
KV_HEADS = 2
GROUP = HEADS // KV_HEADS
HEAD_DIM = 128
EXPERTS = 8
LANES = 128

epsilon = 1e-06
rotary_base = 1000000.0
masked_score = -1e30

F32 = jnp.float32
BF16 = jnp.bfloat16
MESH = pl.DeviceIdType.MESH
VMEM_LIMIT = 63 * 2**20


def dot(a, b, dims):
    return lax.dot_general(a, b, (dims, ((), ())), preferred_element_type=F32)


def dot_nn(a, b):
    return dot(a, b, ((1,), (0,)))


def dot_nt(a, b):
    return dot(a, b, ((1,), (1,)))


def dot_tn(a, b):
    return dot(a, b, ((0,), (0,)))


def guarded(cond, body):
    if cond is None:
        body()
    else:
        pl.when(cond)(body)


def both(first, second):
    if first is None:
        return second
    if second is None:
        return first
    return jnp.logical_and(first, second)


class Net:
    def __init__(self, send_sems, recv_sems, local_sems, core):
        self.send_sems, self.recv_sems, self.local_sems = send_sems, recv_sems, local_sems
        self.away = {"c": 1 - core}
        self.slots, self.sends, self.locals, self.count, self.done = {}, {}, {}, 0, set()
        self.later, self.free = [], []

    def slot(self, key):
        return self.slots.setdefault(key, len(self.slots))

    def send(self, key, src, dst, device, cond=None, slot=None):
        recv, index = self.slot(slot or key), self.index()

        def build():
            return pltpu.make_async_remote_copy(
                src_ref=src(),
                dst_ref=dst(),
                send_sem=self.send_sems.at[index],
                recv_sem=self.recv_sems.at[recv],
                device_id=device,
                device_id_type=MESH,
            )

        guarded(cond, lambda: build().start())
        self.sends[key] = (cond, build, index)

    def index(self):
        if self.free:
            return self.free.pop()
        self.count += 1
        return self.count - 1

    def sent(self, key):
        if key not in self.sends:
            return
        cond, build, index = self.sends.pop(key)
        guarded(cond, lambda: build().wait_send())
        self.free.append(index)

    def settle(self, *names):
        for key in [key for key in self.sends if key[0] in names]:
            self.sent(key)

    def arrive(self, key, dst, cond=None):
        recv = self.slot(key)

        def wait():
            pltpu.make_async_remote_copy(
                src_ref=dst(),
                dst_ref=dst(),
                send_sem=self.send_sems.at[0],
                recv_sem=self.recv_sems.at[recv],
                device_id=self.away,
                device_id_type=MESH,
            ).wait_recv()

        guarded(cond, wait)

    def local(self, key, src, dst):
        index = len(self.locals)

        def build():
            return pltpu.make_async_copy(
                src() if callable(src) else src,
                dst() if callable(dst) else dst,
                self.local_sems.at[index],
            )

        build().start()
        self.locals[key] = build

    def ready(self, key):
        if key not in self.done:
            self.done.add(key)
            self.locals[key]().wait()

    def ready_later(self, key):
        self.later.append(key)

    def ready_all(self):
        for key in self.later:
            self.ready(key)
        self.later = []

    def drain(self):
        for key in list(self.sends):
            self.sent(key)
        for key in self.locals:
            self.ready(key)


def greet(depth, coords):
    x, y, c, z = coords
    barrier = pltpu.get_barrier_semaphore()
    for device in ({"y": 1 - y}, {"y": 1 - y, "x": 1 - x}, {"c": 1 - c}):
        pl.semaphore_signal(barrier, inc=1, device_id=device, device_id_type=MESH)
    for zi in range(depth):
        for xi in range(2):

            def tell(zi=zi, xi=xi):
                pl.semaphore_signal(
                    barrier,
                    inc=1,
                    device_id={"z": jnp.int32(zi), "x": jnp.int32(xi)},
                    device_id_type=MESH,
                )

            pl.when(jnp.logical_or(z != zi, x != xi))(tell)
    pl.semaphore_wait(barrier, 3 + 2 * depth - 1)


def along(depth, z):
    return (
        ("up", {"z": z + 1}, z + 1 < depth, lambda k: z - k, lambda k: z - k >= 0),
        ("down", {"z": z - 1}, z > 0, lambda k: z + k, lambda k: z + k < depth),
    )


class SlabGather:
    def __init__(self, net, name, coords, dst, length):
        self.net, self.name, self.dst, self.length = net, name, dst, length
        x, y, c, _ = coords
        self.to_x, self.to_y, self.to_mate = {"x": 1 - x}, {"y": 1 - y}, {"c": 1 - c}

    def slot(self, slot, half=None):
        first, size = slot * self.length, self.length
        if half is not None:
            size = size // 2
            first = first + half * size
        return self.dst.at[first : first + size, :]

    def put(self, slot, src, device, half=None):
        self.net.send(
            (self.name, slot, half), lambda: src, lambda: self.slot(slot, half), device
        )

    def wait(self, slot, half=None):
        self.net.arrive((self.name, slot, half), lambda: self.slot(slot, half))

    def start(self, src):
        self.put(2, src, self.to_y)
        self.put(4, src, self.to_x)
        self.put(1, src, self.to_mate)

    def forward(self):
        self.wait(2)
        self.put(6, self.slot(2, 0), self.to_x, 0)
        self.put(3, self.slot(2), self.to_mate)
        self.wait(4)
        self.put(6, self.slot(4, 1), self.to_y, 1)
        self.put(5, self.slot(4), self.to_mate)

    def forward_far(self):
        for half in range(2):
            self.wait(6, half)
            self.put(7, self.slot(6, half), self.to_mate, half)

    def sent(self):
        for slot, half in ((2, None), (4, None), (1, None), (6, 0), (6, 1), (3, None), (5, None), (7, 0), (7, 1)):
            self.net.sent((self.name, slot, half))


class AttentionGather:
    def __init__(self, net, name, depth, coords, src, dst, stacked=False):
        self.net, self.name, self.depth, self.src, self.dst = net, name, depth, src, dst
        self.stacked = stacked
        self.x, self.y, self.c, self.z = x, y, c, z = coords
        self.nx, self.ny, self.nc = 1 - x, 1 - y, 1 - c
        self.rows, self.columns = dst.shape[0] // (2 * depth), dst.shape[1] // 4
        self.to_x, self.to_y, self.to_mate = {"x": self.nx}, {"y": self.ny}, {"c": self.nc}
        self.ways = [
            (tag, device, more, {k: (origin(k), there(k), both(there(k), more)) for k in range(1, depth)})
            for tag, device, more, origin, there in along(depth, z)
        ]

    def lanes(self, yi, ci):
        return pl.ds(pl.multiple_of((2 * yi + ci) * self.columns, LANES), self.columns)

    def block(self, zi, xi, yi, ci):
        return lambda: self.dst.at[
            pl.ds(pl.multiple_of((zi * 2 + xi) * self.rows, self.rows), self.rows), self.lanes(yi, ci)
        ]

    def put(self, key, place, device, cond=None, src=None):
        block = self.block(*place)
        self.net.send((self.name,) + key, src or block, block, device, cond)

    def wait(self, key, place, cond=None):
        self.net.arrive((self.name,) + key, self.block(*place), cond)

    def own(self, yi):
        if self.stacked:
            first = pl.multiple_of((2 * yi + self.c) * self.rows, self.rows)
            return self.src.at[pl.ds(first, self.rows), :]
        return self.src.at[:, self.lanes(yi, self.c)]

    def mine(self):
        return pl.ds(pl.multiple_of((self.z * 2 + self.x) * self.rows, self.rows), self.rows)

    def start(self):
        x, y, c, z = self.x, self.y, self.c, self.z
        own = lambda: self.own(y)
        cross = lambda: self.own(self.ny)
        for tag, device, more, _ in self.ways:
            self.put(("z", tag, 1), (z, x, y, c), device, more, own)
        self.put(("x", "same"), (z, x, y, c), self.to_x, None, own)
        self.put(("x", "cross"), (z, x, self.ny, c), self.to_x, None, cross)

    def pass_z(self, k):
        for tag, device, _, steps in self.ways:
            origin, cond, on = steps[k]
            place = (origin, self.x, self.y, self.c)
            self.wait(("z", tag, k), place, cond)
            if k + 1 < self.depth:
                self.put(("z", tag, k + 1), place, device, on)
            self.put(("x", tag, k), place, self.to_x, cond)
            self.put(("y", tag, k, 0), place, self.to_y, cond)
            self.put(("c", tag, k, 0), place, self.to_mate, cond)

    def pass_x(self, k):
        if k == 0:
            for tag, yi in (("same", self.y), ("cross", self.ny)):
                place = (self.z, self.nx, yi, self.c)
                self.wait(("x", tag), place)
                self.put(("c", tag), place, self.to_mate)
            return
        for tag, _, _, steps in self.ways:
            origin, cond, _ = steps[k]
            place = (origin, self.nx, self.y, self.c)
            self.wait(("x", tag, k), place, cond)
            self.put(("y", tag, k, 1), place, self.to_y, cond)
            self.put(("c", tag, k, 1), place, self.to_mate, cond)

    def pass_y(self, k):
        for tag, _, _, steps in self.ways:
            origin, cond, _ = steps[k]
            for j, xi in ((0, self.x), (1, self.nx)):
                place = (origin, xi, self.ny, self.c)
                self.wait(("y", tag, k, j), place, cond)
                self.put(("c", tag, k, 2 + j), place, self.to_mate, cond)

    def finish(self):
        for tag, yi in (("same", self.y), ("cross", self.ny)):
            self.wait(("c", tag), (self.z, self.nx, yi, self.nc))
        for k in range(1, self.depth):
            for tag, _, _, steps in self.ways:
                origin, cond, _ = steps[k]
                for j, (xi, yi) in enumerate(
                    ((self.x, self.y), (self.nx, self.y), (self.x, self.ny), (self.nx, self.ny))
                ):
                    self.wait(("c", tag, k, j), (origin, xi, yi, self.nc), cond)


class ExpertGather:
    def __init__(self, net, name, depth, coords, src, dst):
        self.net, self.name, self.depth, self.coords, self.src, self.dst = (
            net, name, depth, coords, src, dst,
        )
        self.rows = src.shape[1]
        x, y, c, z = coords
        self.own, self.away = 4 * x + 2 * y + c, 4 * (1 - x) + 2 * y + c
        self.xs, self.z, self.half = (x, 1 - x), z, depth // 2
        self.to_x = {"x": self.xs[1]}
        self.ways = [
            (tag, device, more, {
                k: (origin(k), there(k), both(there(k), more), both(there(k), jnp.logical_not(more)))
                for k in range(1, depth)
            })
            for tag, device, more, origin, there in along(depth, z)
        ]

    def block(self, zi, xi):
        return lambda: self.dst.at[
            pl.ds(pl.multiple_of((zi * 2 + xi) * self.rows, self.rows), self.rows), :
        ]

    def put(self, key, place, device, cond=None, src=None):
        block = self.block(*place)
        self.net.send((self.name,) + key, src or block, block, device, cond)

    def start(self):
        x, _, _, z = self.coords
        for tag, device, more, _ in self.ways:
            self.put(("z", tag, 1, 0), (z, x), device, more, lambda: self.src.at[self.own])

    def start_x(self):
        x, _, _, z = self.coords
        self.put(("x",), (z, x), self.to_x, None, lambda: self.src.at[self.away])

    def pass_x(self):
        x, _, _, z = self.coords
        self.net.arrive((self.name, "x"), self.block(z, self.xs[1]))
        for tag, device, more, _ in self.ways:
            self.put(("z", tag, 1, 1), (z, self.xs[1]), device, more)

    def pass_z(self, k, j):
        if k + 1 >= self.depth:
            return
        for tag, device, _, steps in self.ways:
            origin, _, on, _ = steps[k]
            place = (origin, self.xs[j])
            self.net.arrive((self.name, "z", tag, k, j), self.block(*place), on)
            self.put(("z", tag, k + 1, j), place, device, on)

    def finish(self, near=None):
        for k in range(1, self.depth):
            for j in range(2):
                for tag, _, _, steps in self.ways:
                    origin, there, _, last = steps[k]
                    cond = there if k + 1 >= self.depth else last
                    if near is not None:
                        same = (origin >= self.half) == (self.z >= self.half)
                        cond = jnp.logical_and(cond, same if near else jnp.logical_not(same))
                    self.net.arrive(
                        (self.name, "z", tag, k, j), self.block(origin, self.xs[j]), cond
                    )

    def sent(self):
        self.net.sent((self.name, "x"))
        for k in range(1, self.depth):
            for j in range(2):
                for tag, _, _, _ in self.ways:
                    self.net.sent((self.name, "z", tag, k, j))


def inverse_rms(values):
    return lax.rsqrt(jnp.mean(values * values, axis=-1, keepdims=True) + epsilon)


def turn(values, cosine, sine):
    return values * cosine + pltpu.roll(values, HEAD_DIM // 2, axis=1) * sine


class SlabReturn:
    def __init__(self, net, name, coords, parts, length, mates, fars, chips, load, by_x):
        self.net, self.name, self.parts, self.length = net, name, parts, length
        self.mates, self.fars, self.landed, self.load, self.by_x = mates, fars, chips, load, by_x
        x, y, c, _ = coords
        self.to_x, self.to_y, self.to_core = {"x": 1 - x}, {"y": 1 - y}, {"c": 1 - c}

    def part(self, slot, half=None):
        first, size = slot * self.length, self.length
        if half is not None:
            size = size // 2
            first = first + half * size
        return self.parts.at[first : first + size, :]

    def half(self, half):
        return pl.ds(half * (self.length // 2), self.length // 2)

    def to_mate(self, chip):
        self.net.send(
            (self.name, "mate", chip),
            lambda: self.part(2 * chip + 1),
            lambda: self.mates.at[chip],
            self.to_core,
        )

    def fetch(self, chip):
        self.net.arrive((self.name, "mate", chip), lambda: self.mates.at[chip])
        self.net.local((self.name, "load", chip), self.mates.at[chip], self.load.at[chip])

    def fetched(self, chip):
        self.net.ready((self.name, "load", chip))
        return self.load.at[chip]

    def far(self, half, device):
        self.net.send(
            (self.name, "far", half),
            lambda: self.part(6, half),
            lambda: self.fars.at[self.half(half)],
            device,
        )

    def near(self, chip, half, device):
        self.net.send(
            (self.name, "chip", chip, half),
            lambda: self.part(2 * chip, half),
            lambda: self.landed.at[chip - 1, self.half(half)],
            device,
        )

    def give(self, chip):
        if chip == 3:
            self.far(0, self.to_x)
            self.far(1, self.to_x if self.by_x else self.to_y)
        elif chip == 1 and not self.by_x:
            self.near(1, 1, self.to_y)
        elif chip == 2:
            self.near(2, 0, self.to_x)
            if self.by_x:
                self.near(2, 1, self.to_x)

    def combined(self):
        places = ((0, 1, self.to_y), (1, 1, self.to_y) if self.by_x else (1, 2, self.to_x))
        for half, _, _ in places:
            here = self.half(half)
            self.net.arrive((self.name, "far", half), lambda: self.fars.at[here])
            self.net.local((self.name, "far", half), self.fars.at[here], self.load.at[3, here])
        for half, chip, device in places:
            self.net.ready((self.name, "far", half))
            part = self.part(2 * chip, half)
            accumulate(part, part, self.load.at[3, self.half(half)])
            self.near(chip, half, device)

    def total(self, out, *more):
        for chip in (1, 2):
            for half in range(2):
                self.net.arrive(
                    (self.name, "chip", chip, half), lambda: self.landed.at[chip - 1, self.half(half)]
                )
            self.net.local((self.name, "last", chip), self.landed.at[chip - 1], self.load.at[chip])
        for chip in (1, 2):
            self.net.ready((self.name, "last", chip))
        accumulate(out, self.part(0), self.load.at[1], self.load.at[2], *more)

    def sent(self):
        for chip in range(4):
            self.net.sent((self.name, "mate", chip))
        for half in range(2):
            self.net.sent((self.name, "far", half))
            for chip in (1, 2):
                self.net.sent((self.name, "chip", chip, half))


def accumulate(out, *terms):
    total, columns = out.shape
    step = 32 if columns < 1024 and total % 32 == 0 else 16

    @pl.loop(0, total // step)
    def _(i):
        here = pl.ds(pl.multiple_of(i * step, step), step)
        value = terms[0][here, :].astype(F32)
        for term in terms[1:]:
            value = value + term[here, :].astype(F32)
        out[here, :] = value.astype(out.dtype)


def clear(out):
    @pl.loop(0, out.shape[0] // 16)
    def _(i):
        here = pl.ds(pl.multiple_of(i * 16, 16), 16)
        out[here, :] = jnp.zeros((16, out.shape[1]), out.dtype)


class LineScatter:
    def __init__(self, net, name, depth, z, block, landed, load):
        self.net, self.name, self.depth, self.z = net, name, depth, z
        self.block, self.landed, self.load = block, landed, load

        steps = range(1, depth)
        up = {s: (depth - s + z, z == 0, jnp.logical_and(z >= 1, z <= s - 1)) for s in steps}
        back = depth - 1 - z
        down = {s: (z + s - depth, back == 0, jnp.logical_and(back >= 1, back <= s - 1)) for s in steps}
        self.ways = (
            ("up", {"z": z + 1}, 0, z >= 1, z < 1, up),
            ("down", {"z": z - 1}, 1, back >= 1, back < 1, down),
        )

    def send(self, key, device, way, s, t, cond):
        self.net.send(
            key,
            lambda: self.block(t),
            lambda: self.landed.at[way, s - 1],
            device,
            cond,
            slot=(self.name, key[1], s),
        )

    def start_step(self, s):
        for tag, device, way, _, _, steps in self.ways:
            target, first, _ = steps[s]
            self.send((self.name, tag, s), device, way, s, target, first)

    def start(self):
        for s in range(1, self.depth):
            self.start_step(s)

    def term(self, way, s):
        return self.landed.at[way, s - 1] if self.load is None else self.load.at[way]

    def take(self, tag, way, s):
        self.net.arrive((self.name, tag, s), lambda: self.landed.at[way, s - 1])
        if self.load is not None:
            pltpu.sync_copy(self.landed.at[way, s - 1], self.load.at[way])

    def step(self, s):
        for tag, device, way, _, _, steps in self.ways:
            t, _, cond = steps[s]

            def body():
                self.take(tag, way, s - 1)
                block = self.block(t)
                accumulate(block, block, self.term(way, s - 1))

            pl.when(cond)(body)
            self.send((self.name, tag, s, "on"), device, way, s, t, cond)

    def finish(self, *outs):
        last = self.depth - 1
        for tag, _, way, fed, unfed, _ in self.ways:
            pl.when(fed)(lambda: self.take(tag, way, last))
            pl.when(unfed)(lambda: clear(self.term(way, last)))
        rows = outs[0].shape[0]
        for i, out in enumerate(outs):
            here = pl.ds(i * rows, rows)
            accumulate(
                out, *(term.at[here, :] for term in (self.block(self.z), self.term(0, last), self.term(1, last)))
            )


class ExpertShare:
    def __init__(self, net, name, coords, result, dst):
        self.net, self.name, self.coords, self.result, self.dst = net, name, coords, result, dst
        x, y, c, _ = coords
        self.across = {4: {"x": 1 - x}, 2: {"y": 1 - y}, 1: {"c": 1 - c}}
        self.expert = 4 * x + 2 * y + c

    def place(self, flip):
        x, y, c, _ = self.coords
        fx = 1 - x if flip & 4 else x
        fy = 1 - y if flip & 2 else y
        fc = 1 - c if flip & 1 else c
        return self.dst.at[4 * fx + 2 * fy + fc]

    def put(self, flip, src, axis):
        self.net.send(
            (self.name, axis | flip), src, lambda: self.place(flip), self.across[axis]
        )

    def on(self, flip, axis):
        self.put(flip, lambda: self.place(flip), axis)

    def wait(self, flip):
        self.net.arrive((self.name, flip), lambda: self.place(flip))

    def start(self):
        x = self.coords[0]
        self.put(0, lambda: self.result.at[1 - x], 4)
        self.put(0, lambda: self.result.at[x], 2)
        self.put(0, lambda: self.result.at[x], 1)
        self.net.local(
            (self.name, "own"), lambda: self.result.at[x], lambda: self.dst.at[self.expert]
        )

    def pass_near(self):
        self.wait(4)
        self.on(4, 2)
        self.on(4, 1)
        self.wait(2)
        self.on(2, 1)

    def pass_far(self):
        self.wait(6)
        self.on(6, 1)

    def finish(self):
        self.net.ready((self.name, "own"))
        for flip in (1, 5, 3, 7):
            self.wait(flip)


class ParityGather:
    def __init__(self, net, name, coords, halves, dst, length):
        self.net, self.name, self.halves, self.dst, self.length = net, name, halves, dst, length
        self.x, y, c, _ = coords
        self.nx = 1 - self.x
        self.to_x, self.to_y, self.to_mate = {"x": self.nx}, {"y": 1 - y}, {"c": 1 - c}

    def slot(self, slot):
        return self.dst.at[slot * self.length : (slot + 1) * self.length, :]

    def put(self, slot, src, device):
        self.net.send((self.name, slot), src, lambda: self.slot(slot), device)

    def wait(self, slot):
        self.net.arrive((self.name, slot), lambda: self.slot(slot))

    def start(self):
        mine = lambda: self.halves(self.x)
        self.put(2, mine, self.to_y)
        self.put(4, lambda: self.halves(self.nx), self.to_x)
        self.put(1, mine, self.to_mate)
        self.net.local((self.name, "own"), mine, lambda: self.slot(0))

    def forward(self):
        self.wait(4)
        self.put(6, lambda: self.slot(4), self.to_y)
        self.put(5, lambda: self.slot(4), self.to_mate)
        self.wait(2)
        self.put(3, lambda: self.slot(2), self.to_mate)

    def forward_far(self):
        self.wait(6)
        self.put(7, lambda: self.slot(6), self.to_mate)

    def finish(self):
        self.net.ready((self.name, "own"))
        for slot in (1, 3, 5, 7):
            self.wait(slot)

    def left(self):
        for slot in (2, 4, 1):
            self.net.sent((self.name, slot))
        self.net.ready((self.name, "own"))


class AttentionScatter:
    def __init__(self, net, name, depth, coords, grad, left, pieces, blocks, lines, dst, low):
        self.net, self.name, self.depth, self.coords = net, name, depth, coords
        self.grad, self.left, self.pieces, self.blocks = grad, left, pieces, blocks
        self.dst, self.low = dst, low
        self.length, self.columns, self.rows = grad.shape[0], grad.shape[1] // 4, dst.shape[0]
        x, y, c, z = coords
        self.ys, self.cs = (y, 1 - y), (c, 1 - c)
        self.to_x, self.to_y, self.to_core = {"x": 1 - x}, {"y": self.ys[1]}, {"c": self.cs[1]}
        self.to_x_core = {"x": 1 - x, "c": self.cs[1]}
        self.to_y_core = {"y": self.ys[1], "c": self.cs[1]}
        self.line = LineScatter(net, name + " line", depth, z, self.block, lines, None)

    def block(self, t):
        return self.blocks.at[pl.ds(pl.multiple_of(t * self.rows, self.rows), self.rows), :]

    def lanes(self, yi, ci):
        return pl.ds(pl.multiple_of((2 * yi + ci) * self.columns, LANES), self.columns)

    def quarter(self, yi, ci):
        return self.dst.at[:, self.lanes(yi, ci)]

    def slot(self, slot):
        return self.pieces.at[slot * self.length : (slot + 1) * self.length, :]

    def put(self, slot, src, device):
        self.net.send((self.name, slot), src, lambda: self.slot(slot), device)

    def give(self, slot, fy, fc, device):
        self.put(slot, lambda: self.grad.at[:, self.lanes(self.ys[fy], self.cs[fc])], device)

    def start(self):
        self.give(2, 1, 0, self.to_y)
        self.give(3, 1, 1, self.to_y_core)
        self.give(4, 0, 0, self.to_x)
        self.give(5, 0, 1, self.to_x_core)
        self.give(1, 0, 1, self.to_core)
        self.net.local(
            (self.name, "own piece"),
            lambda: self.grad.at[:, self.lanes(self.ys[0], self.cs[0])],
            lambda: self.slot(0),
        )

    def forward(self):
        for slot in (2, 3):
            self.net.arrive((self.name, slot), lambda: self.slot(slot))
            self.put(slot + 4, lambda slot=slot: self.slot(slot), self.to_x)

    def take(self):
        for slot in (4, 5, 1, 6, 7):
            self.net.arrive((self.name, slot), lambda: self.slot(slot))
        self.net.ready((self.name, "own piece"))
        tile = 256
        for i in range(0, self.left.shape[1], tile):
            self.blocks[i : i + tile, :] = dot_tn(self.left[:, i : i + tile], self.pieces[...]).astype(BF16)
        self.line.start()

    def total(self):
        x, y, c, z = self.coords
        self.line.finish(self.low)
        self.net.local((self.name, "own"), self.low, self.quarter(y, c))
        for key, device in (("ty", self.to_y), ("tc", self.to_core)):
            self.net.send((self.name, key), lambda: self.low, lambda: self.quarter(y, c), device)

    def pass_y(self):
        x, y, c, z = self.coords
        there = lambda: self.quarter(1 - y, c)
        self.net.arrive((self.name, "ty"), there)
        self.net.send((self.name, "tyc"), there, there, self.to_core)

    def finish(self):
        x, y, c, z = self.coords
        self.net.ready((self.name, "own"))
        self.net.arrive((self.name, "tc"), lambda: self.quarter(y, 1 - c))
        self.net.arrive((self.name, "tyc"), lambda: self.quarter(1 - y, 1 - c))


def norm_back(values, gain, upstream):
    inverse = inverse_rms(values)
    normal = values * inverse
    gain_grad = jnp.sum(upstream * normal, axis=0, keepdims=True)
    scaled = upstream * gain
    return (
        inverse * (scaled - normal * jnp.mean(scaled * normal, axis=-1, keepdims=True)),
        gain_grad,
    )


def layer_kernel(depth, shard_rows, *refs):
    (
        hidden, grad_out, segment, routes, weights, cosine, sine,
        gains_in, query_in, key_in, value_in, wo_in, gate_in, up_in, down_in, grad_hbm,
        layer_out, grad_in, gain_total,
        gate_total, up_total, down_total, wq_total, wo_total,
        wq, wo, down_full, shares, probability,
        row_mates, row_fars, row_chips, out_mates, out_fars, out_chips,
        gate_lines, up_lines, down_lines, normed_all, attended_all,
        rows, grads, wide, gate_grad, down_grad, returned, wide_load, down_load, wide_low, down_low,
        wq_pieces, wo_pieces, wq_lines, wo_lines, wq_blocks, wo_blocks, wq_low, wo_low, gain_swap,
        gains, gain_rows, queries, keys, values, attended, mixed, share_in,
        send_sems, recv_sems, local_sems,
    ) = refs
    coords = x, y, c, z = tuple(lax.axis_index(n) for n in ("x", "y", "c", "z"))
    expert = 4 * x + 2 * y + c
    net = Net(send_sems, recv_sems, local_sems, c)
    length, width = hidden.shape
    units = gate_in.shape[2]
    tile, step = 256, 16
    factor = HEAD_DIM ** (-0.5)

    wq_gather = AttentionGather(net, "wq", depth, coords, wq_pieces, wq, True)
    wo_gather = AttentionGather(net, "wo", depth, coords, wo_in, wo)
    gate_gather = ExpertGather(net, "gate", depth, coords, gate_in, wide.at[:, :units])
    up_gather = ExpertGather(net, "up", depth, coords, up_in, wide.at[:, units:])
    down_gather = ExpertGather(net, "down", depth, coords, down_in, down_full)
    gate_up = (gate_gather, up_gather)
    row_gather = SlabGather(net, "row", coords, rows, length)
    grad_gather = SlabGather(net, "grad", coords, grads, length)

    def gate_block(t):
        size = 2 * shard_rows
        return gate_grad.at[pl.ds(pl.multiple_of(t * size, size), size), :]

    def up_block(t):
        size = 2 * shard_rows
        return wide.at[pl.ds(pl.multiple_of(t * size, size), size), pl.ds(units, units)]

    def down_block(t):
        size = 2 * (units // (2 * depth))
        return down_grad.at[pl.ds(pl.multiple_of(t * size, size), size), :]

    gate_line = LineScatter(net, "gate line", depth, z, gate_block, gate_lines, wide_load)
    up_line = LineScatter(net, "up line", depth, z, up_block, up_lines, wide_load)
    down_line = LineScatter(net, "down line", depth, z, down_block, down_lines, down_load)
    row_back = SlabReturn(net, "row back", coords, grads, length, row_mates, row_fars, row_chips, returned, False)

    down_share = ExpertShare(net, "down sum", coords, down_low, down_total)
    gate_share = ExpertShare(net, "gate sum", coords, wide_low.at[0], gate_total)
    up_share = ExpertShare(net, "up sum", coords, wide_low.at[1], up_total)

    def finish_line(line, share):
        line.finish(share.result.at[0], share.result.at[1])
        share.start()

    def columns_of(i):
        return lambda parity: returned.at[
            i, :, pl.ds(pl.multiple_of(parity * (width // 2), LANES), width // 2)
        ]

    normed_gather = ParityGather(net, "normed", coords, columns_of(0), normed_all, length)
    attended_gather = ParityGather(net, "attended", coords, columns_of(1), attended_all, length)

    def simple_send(key, source, target, device, cond=None):
        net.send(key, lambda: source, lambda: target, device, cond)

    to_mate, to_x, to_y = {"c": 1 - c}, {"x": 1 - x}, {"y": 1 - y}
    to_xy = {**to_x, **to_y}

    me = z * 2 + x
    base = [net.slot(("gains", s)) for s in range(2 * depth)][0]

    def gain_copy(s, index):
        return pltpu.make_async_remote_copy(
            src_ref=gains_in,
            dst_ref=gains.at[me],
            send_sem=send_sems.at[index],
            recv_sem=recv_sems.at[base + me],
            device_id={"z": jnp.int32(s // 2), "x": jnp.int32(s % 2)},
            device_id_type=MESH,
        )

    def start_shares():
        net.local("own grad", grad_hbm, grads.at[:length])
        net.send(("share", 1), lambda: share_in, lambda: shares.at[1], to_mate)
        net.send(("share", 2), lambda: share_in, lambda: shares.at[2], to_y)
        net.send(("share", 4), lambda: share_in, lambda: shares.at[4], to_x)
        net.send(("share", 6), lambda: share_in, lambda: shares.at[6], to_xy)

    def pass_shares():
        for slot in (2, 4, 6):
            net.arrive(("share", slot), lambda: shares.at[slot])
            net.send(
                ("share", slot + 1),
                lambda slot=slot: shares.at[slot],
                lambda slot=slot: shares.at[slot + 1],
                to_mate,
            )

    quarter = wq.shape[1] // 4
    query_end, key_end = query_in.shape[1], query_in.shape[1] + key_in.shape[1]
    bounce = []

    def middle(i, first, size):
        return wq_pieces.at[i * shard_rows : (i + 1) * shard_rows, first : first + size]

    for i, j in enumerate(range(0, wq.shape[1], quarter)):
        for source, begin, end in (
            (query_in, 0, query_end), (key_in, query_end, key_end), (value_in, key_end, wq.shape[1])
        ):
            low, high = max(j, begin), min(j + quarter, end)
            if low < high:
                net.local(("in", i, low), source.at[:, low - begin : high - begin], middle(i, low - j, high - low))
                net.ready_later(("in", i, low))
        bounce.append((middle(i, 0, quarter), wq, j))
    for j in range(0, width, quarter):
        i = len(bounce)
        net.local(("in", i, 0), wo_in.at[:, j : j + quarter], middle(i, 0, quarter))
        net.ready_later(("in", i, 0))
        bounce.append((middle(i, 0, quarter), wo, j))
    greet(depth, coords)
    net.ready_all()
    wq_gather.start()
    net.local("gains", gains_in, gains.at[me])
    gain_sends = []
    for s in range(2 * depth):
        index = net.index()
        gain_sends.append((s, index))
        pl.when(me != s)(lambda: gain_copy(s, index).start())
    down_rows = down_in.shape[1]
    net.local("down in", down_in.at[expert], down_load.at[0, :down_rows])
    for gather in (gate_gather, up_gather):
        net.local((gather.name, "own"), gather.src.at[gather.own], gather.block(z, x)())
    for i, (source, target, j) in enumerate(bounce):
        net.local(("out", i), source, target.at[wq_gather.mine(), j : j + quarter])
    names = lax.broadcasted_iota(jnp.int32, (LANES, length), 0)
    share = jnp.zeros((LANES, length), F32)
    for i in range(routes.shape[0]):
        share = share + jnp.where(names == routes[i : i + 1, :], weights[i : i + 1, :], 0.0)
    share_in[...] = share.T
    net.ready("down in")
    net.local("down out", down_load.at[0, :down_rows], down_gather.block(z, x)())
    wo_gather.start()
    wq_gather.pass_z(1)
    wo_gather.pass_z(1)
    wq_gather.pass_z(2)
    gate_gather.start_x()
    up_gather.start_x()
    wo_gather.pass_z(2)
    gate_gather.start()
    up_gather.start()
    wq_gather.pass_x(1)
    for k in range(3, depth):
        wq_gather.pass_z(k)
    grad_gather.start(grad_hbm)
    start_shares()
    gate_gather.pass_z(1, 0)
    up_gather.pass_z(1, 0)
    for k in range(3, depth):
        wo_gather.pass_z(k)
    wq_gather.pass_x(2)
    wq_gather.pass_x(0)
    gate_gather.pass_x()
    up_gather.pass_x()
    for k in range(3, depth):
        wq_gather.pass_x(k)
    down_gather.start_x()
    wq_gather.pass_y(1)
    wo_gather.pass_x(1)
    wo_gather.pass_x(0)
    gate_gather.pass_z(1, 1)
    up_gather.pass_z(1, 1)
    for k in range(3, depth):
        wq_gather.pass_y(k)
    wo_gather.pass_x(2)
    wq_gather.pass_y(2)
    wq_gather.finish()

    def attention_forward(wq_here, wo_here, chances, order, normed):
        def project():
            for i in range(len(bounce)):
                net.ready(("out", i))
            for key in (("z", "up", 1), ("z", "down", 1), ("x", "same"), ("x", "cross")):
                net.sent(("wq",) + key)
            net.local("wq here", wq, wq_here)
            gains_wide()
            project_heads()

        def gains_wide():
            for s in range(2 * depth):
                pl.when(me != s)(lambda: net.arrive(("gains", s), lambda: gains.at[s]))
            net.ready("gains")
            wide_gain = None
            for s in range(2 * depth):
                rest = jnp.zeros((8, width - gains.shape[2]), F32)
                piece = jnp.concatenate([gains[s], rest], axis=1)
                piece = piece if s == 0 else pltpu.roll(piece, s * shard_rows, axis=1)
                wide_gain = piece if wide_gain is None else wide_gain + piece
            gain_rows[...] = wide_gain

            @pl.loop(0, length // step)
            def _(i):
                here = pl.ds(pl.multiple_of(i * step, step), step)
                one = hidden[here, :].astype(F32)
                normed[here, :] = (one * inverse_rms(one) * gain_rows[0:1, :]).astype(BF16)

        def project_heads():
            net.ready("wq here")
            cos, sin = cosine[...], sine[...]
            for start in range(0, wq.shape[1], tile):
                part = dot_nn(normed[...], wq_here[:, start : start + tile])
                for at in range(start, start + tile, HEAD_DIM):
                    head, one = at // HEAD_DIM, part[:, at - start : at - start + HEAD_DIM]
                    if head < HEADS:
                        queries[head * length : (head + 1) * length, :] = turn(one, cos, sin).astype(BF16)
                    elif head < HEADS + KV_HEADS:
                        at_row = (head - HEADS) * length
                        keys[at_row : at_row + length, :] = turn(one, cos, sin).astype(BF16)
                    else:
                        at_row = (head - HEADS - KV_HEADS) * length
                        values[at_row : at_row + length, :] = one.astype(BF16)

        def heads_forward():
            across = jnp.broadcast_to(segment[...].astype(F32), (length, length))
            later = lax.broadcasted_iota(jnp.int32, (length, length), 0)
            allowed = (across == across.T) & (later >= lax.broadcasted_iota(jnp.int32, (length, length), 1))
            for head in range(HEADS):
                kv = head // GROUP
                here = slice(head * length, (head + 1) * length)
                there = slice(kv * length, (kv + 1) * length)
                scores = dot_nt(queries[here, :], keys[there, :]) * factor
                scores = jnp.where(allowed, scores, masked_score)
                terms = jnp.exp(scores - jnp.max(scores, axis=-1, keepdims=True))
                chance = terms / jnp.sum(terms, axis=-1, keepdims=True)
                chances[here, :] = chance
                attended[:, head * HEAD_DIM : (head + 1) * HEAD_DIM] = dot_nn(
                    chance.astype(BF16), values[there, :]
                ).astype(BF16)
            net.local("keep chances", chances, probability)

        def mix():
            net.local("wo here", wo, wo_here)
            net.ready("wo here")
            for start in range(0, width, tile):
                there = slice(start, start + tile)
                mixed[:, there] = hidden[:, there].astype(F32) + dot_nn(attended[...], wo_here[:, there])

            @pl.loop(0, length // step)
            def _(i):
                here = pl.ds(pl.multiple_of(i * step, step), step)
                total = mixed[here, :]
                rows[here, :] = (total * inverse_rms(total) * gain_rows[1:2, :]).astype(BF16)

        def by_parity():
            for s in range(2 * depth):
                size = (shard_rows, width)
                first = (s % 2) * (width // 2) + (s // 2) * shard_rows
                hit = lax.broadcasted_iota(jnp.int32, size, 1) - first == lax.broadcasted_iota(jnp.int32, size, 0)
                order[s * shard_rows : (s + 1) * shard_rows, :] = hit.astype(F32).astype(BF16)
            for i, source in enumerate((normed, attended)):
                for j in range(0, width, 512):
                    returned[i, :, j : j + 512] = dot_nn(source[...], order[:, j : j + 512]).astype(BF16)

        project()
        for k in range(3, depth):
            wo_gather.pass_x(k)
        grad_gather.forward()
        pass_shares()
        for k in range(2, depth):
            gate_gather.pass_z(k, 1)
            up_gather.pass_z(k, 1)
        heads_forward()
        down_gather.start()
        for k in range(3, depth):
            wo_gather.pass_y(k)
        for k in range(2, depth):
            gate_gather.pass_z(k, 0)
            up_gather.pass_z(k, 0)
        wo_gather.pass_y(1)
        down_gather.pass_x()
        wo_gather.pass_y(2)
        wo_gather.finish()
        mix()
        row_gather.start(rows.at[:length, :])
        by_parity()
        net.ready("keep chances")

    pl.run_scoped(
        attention_forward,
        pltpu.VMEM(wq.shape, BF16),
        pltpu.VMEM(wo.shape, BF16),
        pltpu.VMEM((HEADS * length, length), F32),
        pltpu.VMEM((width, width), BF16),
        pltpu.VMEM((length, width), BF16),
    )

    down_gather.pass_z(1, 0)
    down_gather.pass_z(1, 1)
    gate_gather.finish()
    up_gather.finish()
    row_gather.forward()

    def experts(down, hidden_act, both_grads, share_here, parts_out):
        out_back = SlabReturn(net, "out back", coords, parts_out, length, out_mates, out_fars, out_chips, returned, False)
        lane = lax.broadcasted_iota(jnp.int32, (length, LANES), 1)

        def share_of(r):
            return jnp.sum(jnp.where(lane == expert, share_here[r], 0.0), axis=1, keepdims=True)

        def first_half(first, count):
            @pl.loop(first, first + count)
            def _(r):
                here = pl.ds(pl.multiple_of(r * length, length), length)
                grads[here, :] = (share_of(r) * grads[here, :].astype(F32)).astype(BF16)
                for j in range(0, units, tile):
                    gate = dot_nn(rows[here, :], wide[:, j : j + tile])
                    up = dot_nn(rows[here, :], wide[:, units + j : units + j + tile])
                    sigmoid = 1.0 / (1.0 + jnp.exp(-gate))
                    silu = gate * sigmoid
                    hidden_act[here, j : j + tile] = (silu * up).astype(BF16)
                    both_grads[here, j : j + tile] = (
                        up * sigmoid * (1.0 + gate * (1.0 - sigmoid))
                    ).astype(BF16)
                    both_grads[here, units + j : units + j + tile] = silu.astype(BF16)

        def first_rows():
            net.local("own share", share_in, share_here.at[0])
            for slot in (1, 2, 3, 4, 5, 6, 7):
                if slot % 2:
                    net.arrive(("share", slot), lambda: shares.at[slot])
            net.local("shares", shares.at[1:], share_here.at[1:])
            row_gather.wait(1)
            grad_gather.wait(1)
            for name in ("own grad", "own share", "shares", ("gate", "own"), ("up", "own")):
                net.ready(name)
            first_half(0, 2)

        def gathered(*slots):
            for gather in (row_gather, grad_gather):
                for slot, half in slots:
                    gather.wait(slot, half)

        def left(*slots):
            for slot, half in slots:
                net.sent(("grad", slot, half))

        def middle_rows():
            gathered((3, None), (5, None))
            left((6, 0), (3, None), (6, 1), (5, None))
            first_half(2, 4)

        def last_rows():
            gathered((7, 0), (7, 1))
            left((7, 0), (7, 1))
            first_half(6, 2)

        def down_weight_grad():
            @pl.loop(0, units // tile)
            def _(i):
                at = pl.ds(pl.multiple_of(i * tile, tile), tile)
                for j in range(0, width, 512):
                    down_grad[at, j : j + 512] = dot_tn(hidden_act[:, at], grads[:, j : j + 512]).astype(BF16)

        near_half = units // 2 * (z >= depth // 2).astype(jnp.int32)
        near = pl.multiple_of(near_half, LANES)
        far = pl.multiple_of(units // 2 - near_half, LANES)

        def take_down(first):
            if first is near:
                net.ready("down out")
            here = pl.ds(first, units // 2)
            name = "down near" if first is near else "down far"
            net.local(name, down_full.at[here, :], down.at[here, :])
            net.ready(name)

        def hidden_grads(first):
            @pl.loop(0, EXPERTS)
            def _(r):
                here = pl.ds(pl.multiple_of(r * length, length), length)
                for j in range(0, units // 2, tile):
                    size = min(tile, units // 2 - j)
                    at = pl.multiple_of(first + j, LANES)
                    back = dot_nt(grads[here, :], down[pl.ds(at, size), :])
                    for lane_first in (at, pl.multiple_of(units + at, LANES)):
                        lanes = pl.ds(lane_first, size)
                        both_grads[here, lanes] = (
                            back * both_grads[here, lanes].astype(F32)
                        ).astype(BF16)

        def row_grad(slot, more=None):
            here = slice(slot * length, (slot + 1) * length)
            for j in range(0, width, 512):
                part = dot_nt(both_grads[here, :], wide[j : j + 512, :])
                if more is not None:
                    part = part + more[:, j : j + 512].astype(F32)
                grads[here, j : j + 512] = part.astype(BF16)

        def out_rows(slot, more=None):
            here = slice(slot * length, (slot + 1) * length)
            share = share_of(slot)
            for j in range(0, width, 512):
                part = share * dot_nn(hidden_act[here, :], down[:, j : j + 512])
                if more is not None:
                    part = part + more[:, j : j + 512].astype(F32)
                parts_out[here, j : j + 512] = part.astype(BF16)

        order = (3, 1, 2, 0)

        def give_mates(back, compute):
            for chip in order:
                compute(2 * chip + 1)
                back.to_mate(chip)

        def give_chips(back, compute):
            normed_gather.left()
            attended_gather.left()
            back.fetch(order[0])
            for i, chip in enumerate(order):
                if i + 1 < len(order):
                    back.fetch(order[i + 1])
                compute(2 * chip, back.fetched(chip))
                back.give(chip)

        def weight_grad(first, target):
            @pl.loop(0, width // tile)
            def _(i):
                at = pl.ds(pl.multiple_of(i * tile, tile), tile)
                target[at, :] = dot_tn(rows[:, at], both_grads[:, first : first + units]).astype(BF16)

        net.settle("wq", "wo")
        first_rows()
        normed_gather.start()
        for k in range(2, depth):
            down_gather.pass_z(k, 1)
        attended_gather.start()
        grad_gather.forward_far()
        middle_rows()
        for k in range(2, depth):
            down_gather.pass_z(k, 0)
        row_gather.forward_far()
        down_gather.finish(True)
        take_down(near)
        last_rows()
        down_weight_grad()
        down_line.start()
        normed_gather.forward()
        hidden_grads(near)
        attended_gather.forward()
        down_gather.finish(False)
        take_down(far)
        give_mates(out_back, out_rows)
        give_chips(out_back, out_rows)
        down_line.step(2)
        hidden_grads(far)
        give_mates(row_back, row_grad)
        out_back.combined()
        weight_grad(0, gate_grad)
        gate_line.start_step(1)
        for s in range(3, depth):
            down_line.step(s)
        give_chips(row_back, row_grad)
        up_gather.sent()
        weight_grad(units, wide.at[:, units:])
        up_line.start_step(1)
        for s in range(2, depth):
            gate_line.start_step(s)
            up_line.start_step(s)
        attended_gather.forward_far()
        row_back.combined()
        gate_line.step(2)
        finish_line(down_line, down_share)
        normed_gather.forward_far()
        net.settle("gate", "up", "down", "row", "grad", "share", "normed", "attended")
        out_back.total(layer_out, mixed)
        up_line.step(2)
        out_back.sent()

    pl.run_scoped(
        experts,
        pltpu.VMEM((units, width), BF16),
        pltpu.VMEM((EXPERTS * length, units), BF16),
        pltpu.VMEM((EXPERTS * length, 2 * units), BF16),
        pltpu.VMEM((EXPERTS, length, LANES), F32),
        pltpu.VMEM((EXPERTS * length, width), BF16),
    )

    def attention_backward(weight, chances, normed_here, attended_here, upstream_two, mixed_grad, mixed_low, attended_grad, qkv_grad):
        net.local("wo again", wo, weight.at[:, :width])
        net.local("chance 0", probability.at[: GROUP * length], chances)
        wo_net = AttentionScatter(
            net, "wo sum", depth, coords, mixed_low, attended_here, wo_pieces, wo_blocks, wo_lines, wo_total, wo_low
        )
        wq_net = AttentionScatter(
            net, "wq sum", depth, coords, qkv_grad, normed_here, wq_pieces, wq_blocks, wq_lines, wq_total, wq_low
        )

        def take_normed():
            normed_gather.finish()
            net.local("normed here", normed_all, normed_here)

        def take_attended():
            attended_gather.finish()
            net.local("attended here", attended_all, attended_here)

        def norm_two_back():
            row_back.total(upstream_two)
            gain_swap[0] = jnp.zeros(gain_swap.shape[1:], F32)

            @pl.loop(0, length // step)
            def _(i):
                here = pl.ds(pl.multiple_of(i * step, step), step)
                part, gain_two = norm_back(mixed[here, :], gain_rows[1:2, :], upstream_two[here, :])
                total = grad_out[here, :].astype(F32) + part
                mixed_grad[here, :] = total
                mixed_low[here, :] = total.astype(BF16)
                gain_swap[0, 1:2, :] += gain_two

        def attended_back():
            net.ready("wo again")
            for i in range(0, width, 512):
                attended_grad[:, i : i + 512] = dot_nt(
                    mixed_low[...], weight[i : i + 512, :width]
                ).astype(BF16)
            net.local("wq again", wq, weight)

        def heads_back():
            cos, sin = cosine[...], -sine[...]
            for kv in range(KV_HEADS):
                net.ready("chance %d" % kv)
                there = slice(kv * length, (kv + 1) * length)
                value_sum = key_sum = None
                for g in range(GROUP):
                    head = kv * GROUP + g
                    here = slice(head * length, (head + 1) * length)
                    cols = slice(head * HEAD_DIM, (head + 1) * HEAD_DIM)
                    chance = chances[g * length : (g + 1) * length, :]
                    back = attended_grad[:, cols]
                    prob_grad = dot_nt(back, values[there, :])
                    value_part = dot_tn(chance.astype(BF16), back)
                    inner = jnp.sum(chance * prob_grad, axis=-1, keepdims=True)
                    score_grad = (chance * (prob_grad - inner)).astype(BF16)
                    query_grad = dot_nn(score_grad, keys[there, :]) * factor
                    key_part = dot_tn(score_grad, queries[here, :])
                    qkv_grad[:, cols] = turn(query_grad, cos, sin).astype(BF16)
                    value_sum = value_part if value_sum is None else value_sum + value_part
                    key_sum = key_part if key_sum is None else key_sum + key_part
                if kv + 1 < KV_HEADS:
                    size = GROUP * length
                    net.local("chance %d" % (kv + 1), probability.at[(kv + 1) * size : (kv + 2) * size], chances)
                first = (HEADS + kv) * HEAD_DIM
                qkv_grad[:, first : first + HEAD_DIM] = turn(key_sum * factor, cos, sin).astype(BF16)
                first = first + KV_HEADS * HEAD_DIM
                qkv_grad[:, first : first + HEAD_DIM] = value_sum.astype(BF16)

        def norm_one_back():
            net.ready("wq again")
            for i in range(0, width, 512):
                upstream_two[:, i : i + 512] = dot_nt(qkv_grad[...], weight[i : i + 512, :])

            @pl.loop(0, length // step)
            def _(i):
                here = pl.ds(pl.multiple_of(i * step, step), step)
                part, gain_one = norm_back(
                    hidden[here, :].astype(F32), gain_rows[0:1, :], upstream_two[here, :]
                )
                grad_in[here, :] = (mixed_grad[here, :] + part).astype(BF16)
                gain_swap[0, 0:1, :] += gain_one

        axes = (("c", to_mate), ("x", to_x), ("y", to_y))

        def gain_start(i):
            net.send(
                ("gain", axes[i][0]),
                lambda: gain_swap.at[2 * i],
                lambda: gain_swap.at[2 * i + 1],
                axes[i][1],
            )

        def gain_add(i):
            net.arrive(("gain", axes[i][0]), lambda: gain_swap.at[2 * i + 1])
            gain_swap[2 * i + 2] = gain_swap[2 * i] + gain_swap[2 * i + 1]

        def gains_out():
            for far in range(1, depth):
                simple_send(("gain", "up", far), gain_swap.at[6], gain_swap.at[5 + 2 * far], {"z": z + far}, z + far < depth)
                simple_send(("gain", "down", far), gain_swap.at[6], gain_swap.at[6 + 2 * far], {"z": z - far}, z - far >= 0)

        def gains_in_all():
            for far in range(1, depth):
                for tag, slot, cond in (
                    ("up", 5 + 2 * far, z - far >= 0), ("down", 6 + 2 * far, z + far < depth)
                ):

                    def take():
                        net.arrive(("gain", tag, far), lambda: gain_swap.at[slot])
                        gain_swap[6] += gain_swap[slot]

                    pl.when(cond)(take)
            for s in range(2 * depth):

                def pick(s=s):
                    value = gain_swap[6]
                    if s:
                        value = pltpu.roll(value, width - s * shard_rows, axis=1)
                    gain_total[...] = value[:, : gain_total.shape[1]]

                pl.when(me == s)(pick)

        norm_two_back()
        take_attended()
        wo_net.start()
        attended_back()
        for s in range(3, depth):
            gate_line.step(s)
        wo_net.forward()
        heads_back()
        wq_net.start()
        down_share.pass_near()
        for s in range(3, depth):
            up_line.step(s)
        take_normed()
        norm_one_back()
        wq_net.forward()
        finish_line(gate_line, gate_share)
        net.ready("attended here")
        wo_net.take()
        down_share.pass_far()
        finish_line(up_line, up_share)
        gain_start(0)
        wo_net.line.step(2)
        net.ready("normed here")
        wq_net.take()
        gate_share.pass_near()
        gain_add(0)
        for s in range(3, depth):
            wo_net.line.step(s)
        wq_net.line.step(2)
        gain_start(1)
        up_share.pass_near()
        gate_share.pass_far()
        for s in range(3, depth):
            wq_net.line.step(s)
        gain_add(1)
        gain_start(2)
        wo_net.total()
        wq_net.total()
        up_share.pass_far()
        wo_net.pass_y()
        gain_add(2)
        gains_out()
        wq_net.pass_y()
        for key in [key for key in net.sends if key[0] == "gain"]:
            net.sent(key)
        gains_in_all()
        for one in (down_share, gate_share, up_share, wo_net, wq_net):
            one.finish()
        net.drain()

    pl.run_scoped(
        attention_backward,
        pltpu.VMEM(wq.shape, BF16),
        pltpu.VMEM((GROUP * length, length), F32),
        pltpu.VMEM((EXPERTS * length, width // 2), BF16),
        pltpu.VMEM((EXPERTS * length, width // 2), BF16),
        pltpu.VMEM((length, width), F32),
        pltpu.VMEM((length, width), F32),
        pltpu.VMEM((length, width), BF16),
        pltpu.VMEM((length, width), BF16),
        pltpu.VMEM((length, wq.shape[1]), BF16),
    )
    for s, index in gain_sends:
        pl.when(me != s)(lambda: gain_copy(s, index).wait_send())
    assert net.count <= send_sems.shape[0] and len(net.slots) <= recv_sems.shape[0]
    assert len(net.locals) <= local_sems.shape[0]


def layer_call(
    depth, shard_rows, hidden, grad_out, segments, routes, weights, cosine, sine, gains, query_in, key_in,
    value_in, wo_in, gate_in, up_in, down_in,
):
    length, width = hidden.shape
    wide = query_in.shape[1] + key_in.shape[1] + value_in.shape[1]
    units, down_rows = gate_in.shape[2], down_in.shape[1]
    here, there = pl.BlockSpec(memory_space=pltpu.VMEM), pl.BlockSpec(memory_space=pltpu.HBM)

    def shape(*dims, dtype=BF16):
        return jax.ShapeDtypeStruct(dims, dtype)

    returns = [shape(4, length, width), shape(length, width), shape(2, length, width)]
    out_shape = [
        shape(length, width), shape(length, width), shape(*gains.shape, dtype=F32),
        shape(EXPERTS, shard_rows, units), shape(EXPERTS, shard_rows, units),
        shape(EXPERTS, down_rows, width),
        shape(shard_rows, wide), shape(shard_rows, width),
        shape(width, wide), shape(width, width), shape(units, width),
        shape(EXPERTS, length, LANES, dtype=F32), shape(HEADS * length, length, dtype=F32),
        *returns, *returns,
        shape(2, depth - 1, 2 * shard_rows, units), shape(2, depth - 1, 2 * shard_rows, units),
        shape(2, depth - 1, 2 * down_rows, width),
        shape(EXPERTS * length, width // 2), shape(EXPERTS * length, width // 2),
    ]
    copies, arrivals = 42 * depth, 58 * depth + 58
    return pl.pallas_call(
        functools.partial(layer_kernel, depth, shard_rows),
        out_shape=out_shape,
        in_specs=[here] * 7 + [there] * 9,
        out_specs=[here] * 3 + [there] * (len(out_shape) - 3),
        scratch_shapes=[
            pltpu.VMEM((EXPERTS * length, width), BF16),
            pltpu.VMEM((EXPERTS * length, width), BF16),
            pltpu.VMEM((width, 2 * units), BF16),
            pltpu.VMEM((width, units), BF16),
            pltpu.VMEM((units, width), BF16),
            pltpu.VMEM((4, length, width), BF16),
            pltpu.VMEM((2, 2 * shard_rows, units), BF16),
            pltpu.VMEM((2, 2 * down_rows, width), BF16),
            pltpu.VMEM((2, 2, shard_rows, units), BF16),
            pltpu.VMEM((2, down_rows, width), BF16),
            pltpu.VMEM((EXPERTS * length, wide // 4), BF16),
            pltpu.VMEM((EXPERTS * length, width // 4), BF16),
            pltpu.VMEM((2, depth - 1, shard_rows, wide // 4), BF16),
            pltpu.VMEM((2, depth - 1, shard_rows, width // 4), BF16),
            pltpu.VMEM((depth * shard_rows, wide // 4), BF16),
            pltpu.VMEM((depth * shard_rows, width // 4), BF16),
            pltpu.VMEM((shard_rows, wide // 4), BF16),
            pltpu.VMEM((shard_rows, width // 4), BF16),
            pltpu.VMEM((5 + 2 * depth, 8, width), F32),
            pltpu.VMEM((2 * depth, *gains.shape), F32),
            pltpu.VMEM((8, width), F32),
            pltpu.VMEM((HEADS * length, HEAD_DIM), BF16),
            pltpu.VMEM((KV_HEADS * length, HEAD_DIM), BF16),
            pltpu.VMEM((KV_HEADS * length, HEAD_DIM), BF16),
            pltpu.VMEM((length, width), BF16),
            pltpu.VMEM((length, width), F32),
            pltpu.VMEM((length, LANES), F32),
            pltpu.SemaphoreType.DMA((copies,)),
            pltpu.SemaphoreType.DMA((arrivals,)),
            pltpu.SemaphoreType.DMA((60,)),
        ],
        compiler_params=pltpu.CompilerParams(
            collective_id=1, has_side_effects=True, vmem_limit_bytes=VMEM_LIMIT
        ),
    )(
        hidden, grad_out, segments, routes, weights, cosine, sine, gains, query_in, key_in, value_in, wo_in,
        gate_in, up_in, down_in, grad_out,
    )


def rotary_tables(length, head_width):
    half_width = head_width // 2
    frequency = rotary_base ** (-2.0 * np.arange(half_width, dtype=np.float32) / head_width)
    angles = np.arange(length, dtype=np.float32)[:, None] * frequency.astype(np.float32)[None, :]
    cosine, sine = np.cos(angles), np.sin(angles)
    return (
        np.concatenate([cosine, cosine], axis=1).astype(np.float32),
        np.concatenate([-sine, sine], axis=1).astype(np.float32),
    )


def widen_kernel(*refs):
    wq, wo, gate, up, down, layer, grad = refs[:7]
    query_out, key_out, value_out, wo_out, gate_out, up_out, down_out, layer_out, grad_out = refs[7:16]
    low, high, same, in_sems, out_sems, same_sems = refs[16:]
    queries_end = HEADS * HEAD_DIM
    kv = KV_HEADS * HEAD_DIM
    rows = wq.shape[0]
    width = wo.shape[1]
    pieces = [
        (wq.at[:, :queries_end], query_out),
        (wo, wo_out),
    ]
    for source, target in ((gate, gate_out), (up, up_out), (down, down_out)):
        for e in range(EXPERTS):
            pieces.append((source.at[e], target.at[e]))
    pieces.append((wq.at[:, queries_end : queries_end + kv], key_out))
    pieces.append((wq.at[:, queries_end + kv :], value_out))
    depth = low.shape[0]

    def place(buffer, i):
        r, n = pieces[i][0].shape
        return buffer.at[i % depth, :r, :n]

    def read(i):
        return pltpu.make_async_copy(pieces[i][0], place(low, i), in_sems.at[i % depth])

    def write(i):
        return pltpu.make_async_copy(place(high, i), pieces[i][1], out_sems.at[i % depth])

    passed = ((layer, layer_out), (grad, grad_out))

    def take(i):
        return pltpu.make_async_copy(passed[i][0], same.at[i], same_sems.at[i])

    def put(i):
        return pltpu.make_async_copy(same.at[i], passed[i][1], same_sems.at[2 + i])

    for i in range(depth - 1):
        read(i).start()
    for i in range(2):
        take(i).start()
    for i in range(len(pieces)):
        if i + depth - 1 < len(pieces):
            read(i + depth - 1).start()
        read(i).wait()
        if i >= depth:
            write(i - depth).wait()
        place(high, i)[...] = place(low, i)[...].astype(F32)
        write(i).start()
        if i in (depth, depth + 1):
            take(i - depth).wait()
            put(i - depth).start()
    for i in range(2):
        put(i).wait()
    for i in range(max(0, len(pieces) - depth), len(pieces)):
        write(i).wait()


def widen_call(wq, wo, gate, up, down, layer, grad):
    rows, width = wo.shape
    there = pl.BlockSpec(memory_space=pltpu.HBM)
    queries_end, kv = HEADS * HEAD_DIM, KV_HEADS * HEAD_DIM

    def shape(*dims):
        return jax.ShapeDtypeStruct(dims, F32)

    buffers = 6
    return pl.pallas_call(
        widen_kernel,
        out_shape=[
            shape(rows, queries_end), shape(rows, kv), shape(rows, kv), shape(*wo.shape),
            shape(*gate.shape), shape(*up.shape), shape(*down.shape),
            jax.ShapeDtypeStruct(layer.shape, layer.dtype), jax.ShapeDtypeStruct(grad.shape, grad.dtype),
        ],
        in_specs=[there] * 7,
        out_specs=[there] * 9,
        scratch_shapes=[
            pltpu.VMEM((buffers, rows, width), BF16),
            pltpu.VMEM((buffers, rows, width), F32),
            pltpu.VMEM((2, *layer.shape), BF16),
            pltpu.SemaphoreType.DMA((buffers,)),
            pltpu.SemaphoreType.DMA((buffers,)),
            pltpu.SemaphoreType.DMA((4,)),
        ],
        compiler_params=pltpu.CompilerParams(vmem_limit_bytes=VMEM_LIMIT),
    )(wq, wo, gate, up, down, layer, grad)


def make_shards(sizes):
    depth = sizes["z"]

    def shards(
        hidden_in,
        segments,
        routes,
        gate_weights,
        grad_out,
        attn_gain,
        query_weight,
        key_weight,
        value_weight,
        output_weight,
        ffn_gain,
        gate_weight,
        up_weight,
        down_weight,
    ):
        length, width = hidden_in.shape
        shard_rows = attn_gain.shape[0]
        spare = -(-shard_rows // LANES) * LANES - shard_rows
        first, second = (jnp.pad(gain.astype(F32), (0, spare))[None, :] for gain in (attn_gain, ffn_gain))
        place = lax.broadcasted_iota(jnp.int32, (8, shard_rows + spare), 0)
        gains = jnp.where(place == 0, first, jnp.where(place == 1, second, 0.0))
        cosine, sine = rotary_tables(length, HEAD_DIM)
        layer_out, grad_in, gain_total, gate_total, up_total, down_total, wq_total, wo_total = (
            layer_call(
                depth, shard_rows, hidden_in, grad_out, segments, routes.T, gate_weights.T, cosine, sine,
                gains, query_weight, key_weight, value_weight, output_weight, gate_weight, up_weight,
                down_weight,
            )[:8]
        )
        def whole(value):
            return lax.psum(value.astype(F32), "o") if sizes["o"] > 1 else value

        wq_total = whole(wq_total)
        queries_end = HEADS * HEAD_DIM
        keys_end = queries_end + KV_HEADS * HEAD_DIM
        gain_total = gain_total[:, :shard_rows]
        gain_total = whole(gain_total)
        parts = (wq_total, whole(wo_total), whole(gate_total), whole(up_total), whole(down_total))
        if sizes["o"] == 1:
            *parts, layer_out, grad_in = widen_call(*parts, layer_out, grad_in)
        else:
            parts = (
                wq_total[:, :queries_end], wq_total[:, queries_end:keys_end], wq_total[:, keys_end:], *parts[1:]
            )
        query_grad, key_grad, value_grad, output_grad, gate_grad, up_grad, down_grad = parts
        return (
            layer_out,
            grad_in,
            gain_total[0],
            query_grad,
            key_grad,
            value_grad,
            output_grad,
            gain_total[1],
            gate_grad,
            up_grad,
            down_grad,
        )

    return shards


def solution(mesh):
    reps, shard_count = mesh.shape["rep"], mesh.shape["shard"]
    sizes = {"o": reps // 4, "y": 2, "c": 2, "z": shard_count // 2, "x": 2}
    fine = Mesh(mesh.devices.reshape(tuple(sizes.values())), tuple(sizes))
    tokens = P(("o", "y", "c", "z", "x"), None)
    first, second = P(("z", "x")), P(None, ("z", "x"), None)
    matrix = P(("z", "x"), None)
    return jax.shard_map(
        make_shards(sizes),
        mesh=fine,
        in_specs=(
            (tokens,) * 5 + (first, matrix, matrix, matrix, matrix, first) + (second,) * 3
        ),
        out_specs=(
            (tokens,) * 2 + (first, matrix, matrix, matrix, matrix, first) + (second,) * 3
        ),
        check_vma=False,
    )
```
